32 devices in a mesh: dp: 4 (over y, x), seq: 4 (over z), head: 2 (over core).
Axes of the slice: x: 2, y: 2, z: 4, core: 2. Of those that a mesh axis runs over, the one named last changes fastest.
Arguments:
- tokens_in: bfloat16 [4, 1024, 2048], P('dp', 'seq', 'head'), may hold values from -6 to 6
- lengths: int32 [4], P('dp'), may hold values from 256 to 1024, as said below
- first_gain: bfloat16 [2048], P('head'), may hold values from 0.25 to 1.75
- query_weight: bfloat16 [2048, 2048], P(None, 'head'), may hold values from -0.125 to 0.125
- key_weight: bfloat16 [2048, 2048], P(None, 'head'), may hold values from -0.125 to 0.125
- value_weight: bfloat16 [2048, 2048], P(None, 'head'), may hold values from -0.125 to 0.125
- beta_weight: bfloat16 [2048, 16], P(None, 'head'), may hold values from -0.125 to 0.125
- query_conv: bfloat16 [4, 2048], P(None, 'head'), may hold values from -3 to 3
- key_conv: bfloat16 [4, 2048], P(None, 'head'), may hold values from -3 to 3
- value_conv: bfloat16 [4, 2048], P(None, 'head'), may hold values from -3 to 3
- mixer_gain: bfloat16 [128], replicated, may hold values from 0.25 to 1.75
- output_weight: bfloat16 [2048, 2048], P('head'), may hold values from -0.125 to 0.125
- second_gain: bfloat16 [2048], P('head'), may hold values from 0.25 to 1.75
- gate_weight: bfloat16 [2048, 5632], P(None, 'head'), may hold values from -0.125 to 0.125
- up_weight: bfloat16 [2048, 5632], P(None, 'head'), may hold values from -0.125 to 0.125
- down_weight: bfloat16 [5632, 2048], P('head'), may hold values from -0.078125 to 0.078125
- upstream: bfloat16 [4, 1024, 2048], P('dp', 'seq', 'head'), may hold values from -6 to 6
Outputs:
- layer_out: bfloat16 [4, 1024, 2048], P('dp', 'seq', 'head')
- grad_tokens: float32 [4, 1024, 2048], P('dp', 'seq', 'head')
- grad_first_gain: float32 [2048], P('head')
- grad_query_weight: float32 [2048, 2048], P(('dp', 'seq'), 'head')
- grad_key_weight: float32 [2048, 2048], P(('dp', 'seq'), 'head')
- grad_value_weight: float32 [2048, 2048], P(('dp', 'seq'), 'head')
- grad_beta_weight: float32 [2048, 16], P(('dp', 'seq'), 'head')
- grad_query_conv: float32 [4, 2048], P(None, 'head')
- grad_key_conv: float32 [4, 2048], P(None, 'head')
- grad_value_conv: float32 [4, 2048], P(None, 'head')
- grad_mixer_gain: float32 [128], replicated
- grad_output_weight: float32 [2048, 2048], P('head', ('dp', 'seq'))
- grad_second_gain: float32 [2048], P('head')
- grad_gate_weight: float32 [2048, 5632], P(('dp', 'seq'), 'head')
- grad_up_weight: float32 [2048, 5632], P(('dp', 'seq'), 'head')
- grad_down_weight: float32 [5632, 2048], P('head', ('dp', 'seq'))
The draws below stay inside these ranges and needn't reach their ends.
Inputs may be any that keep to these rules, and one draw needn't show every extreme that they name: `lengths`: among the 1 row of each index of dp, one holds a sequence of 1024 tokens; every row's positions from its length on are padding.
All inputs are finite; a program needn't handle non-finite values.
Results may differ from the reference program's by a relative error of at most 0.025.
Values may be sent and summed in bfloat16 or wider, within the bound.
A program may use at most 256 MiB of HBM per device.

```python
import jax
import jax.numpy as jnp
from jax import lax

D = 2048
HEADS = 16
HEAD_DIM = 128
FF = 5632
STRETCH = 64
TAPS = 4
ROWS_DEV = 1
ROWS = 4
ROW_LEN = 1024
SHORTEST = 256


def draw_lengths(key, part):
    key = jax.random.fold_in(key, 11)
    pick_key, length_key = jax.random.split(key)
    groups = ROWS // ROWS_DEV
    chosen = jax.random.randint(pick_key, (groups, 1), 0, ROWS_DEV)
    drawn = jax.random.randint(length_key, (groups, ROWS_DEV), SHORTEST, ROW_LEN + 1)
    slots = jnp.arange(ROWS_DEV, dtype=jnp.int32)[None, :]
    filled = jnp.where(slots == chosen, ROW_LEN, drawn)
    return filled.reshape(ROWS).astype(jnp.int32)


def shard_levels(rng, dims, pieces, smallest, high):
    factor_of = 1.0
    for dim, shards_of in pieces:
        heights = jax.random.uniform(jax.random.fold_in(jax.random.fold_in(rng, 6), dim), (shards_of,), jnp.float32, smallest / len(pieces), high / len(pieces))
        factor_of = factor_of * jnp.repeat(jnp.exp(heights), dims[dim] // shards_of).reshape((-1,) + (1,) * (len(dims) - 1 - dim))
    return factor_of


def normal_values(rng, extent, deviation, bound, shards=(), kind=jnp.bfloat16):
    array = deviation * jax.random.normal(rng, extent, jnp.float32)
    if shards:
        array = array * shard_levels(rng, extent, shards, -0.22, 0.18)
    return jnp.clip(array, -bound, bound).astype(kind)


def setup_inputs(seed: int = 0) -> dict:
    streams_of = jax.random.split(jax.random.key(seed), 18)
    tokens_in = normal_values(streams_of[0], (ROWS, ROW_LEN, D), 1.0, 6.0, ((0, 4), (1, 4), (2, 2)))
    lengths = draw_lengths(jax.random.fold_in(streams_of[17], 71), 0)
    first_gain = jnp.clip(1.0 + 0.15 * jax.random.normal(streams_of[2], (D,), jnp.float32), 0.25, 1.75).astype(jnp.bfloat16)
    query_weight = normal_values(streams_of[3], (D, D), D ** -0.5, 0.125, ((1, 2),))
    key_weight = normal_values(streams_of[4], (D, D), D ** -0.5, 0.125, ((1, 2),))
    value_weight = normal_values(streams_of[5], (D, D), D ** -0.5, 0.125, ((1, 2),))
    beta_weight = normal_values(streams_of[6], (D, HEADS), D ** -0.5, 0.125, ((1, 2),))
    query_conv = normal_values(streams_of[7], (TAPS, D), TAPS ** -0.5, 3.0, ((1, 2),))
    key_conv = normal_values(streams_of[8], (TAPS, D), TAPS ** -0.5, 3.0, ((1, 2),))
    value_conv = normal_values(streams_of[9], (TAPS, D), TAPS ** -0.5, 3.0, ((1, 2),))
    mixer_gain = jnp.clip(1.0 + 0.15 * jax.random.normal(streams_of[10], (HEAD_DIM,), jnp.float32), 0.25, 1.75).astype(jnp.bfloat16)
    output_weight = normal_values(streams_of[11], (D, D), D ** -0.5, 0.125, ((0, 2),))
    second_gain = jnp.clip(1.0 + 0.15 * jax.random.normal(streams_of[12], (D,), jnp.float32), 0.25, 1.75).astype(jnp.bfloat16)
    gate_weight = normal_values(streams_of[13], (D, FF), D ** -0.5, 0.125, ((1, 2),))
    up_weight = normal_values(streams_of[14], (D, FF), D ** -0.5, 0.125, ((1, 2),))
    down_weight = normal_values(streams_of[15], (FF, D), FF ** -0.5, 0.078125, ((0, 2),))
    upstream = normal_values(streams_of[16], (ROWS, ROW_LEN, D), 1.0, 6.0, ((0, 4), (1, 4), (2, 2)))
    return dict(tokens_in=tokens_in, lengths=lengths, first_gain=first_gain, query_weight=query_weight, key_weight=key_weight, value_weight=value_weight, beta_weight=beta_weight, query_conv=query_conv, key_conv=key_conv, value_conv=value_conv, mixer_gain=mixer_gain, output_weight=output_weight, second_gain=second_gain, gate_weight=gate_weight, up_weight=up_weight, down_weight=down_weight, upstream=upstream)


HIGH = lax.Precision.HIGHEST
EPSILON = 1e-05
UNIT_EPSILON = 1e-06

@jax.custom_vjp
def low(v):
    return lax.optimization_barrier(v.astype(jnp.bfloat16)).astype(jnp.float32)

@jax.custom_vjp
def low_back(v):
    return v

def low_keep(v):
    return (low(v), None)

def low_pass(kept, grad):
    return (grad,)

def back_keep(v):
    return (v, None)

def back_low(kept, grad):
    return (low(grad),)
low.defvjp(low_keep, low_pass)
low_back.defvjp(back_keep, back_low)

def matmul_high(left, right):
    return jnp.dot(left.astype(jnp.float32), right.astype(jnp.float32), precision=HIGH, preferred_element_type=jnp.float32)

def inverse_rms(values):
    return lax.rsqrt(lax.optimization_barrier(jnp.mean(values * values, axis=-1, keepdims=True)) + EPSILON)

def unit_rows(values):
    return values * lax.rsqrt(lax.optimization_barrier(jnp.sum(values * values, axis=-1, keepdims=True)) + UNIT_EPSILON)

def mixer_inputs(padded, beta_logit, kernels, live_mask, head_size):
    local_len = live_mask.shape[-1]
    tap_count = kernels.shape[0]
    seq_axis = padded.ndim - 2
    summed = kernels[0] * lax.slice_in_dim(padded, 0, local_len, axis=seq_axis)
    for tap_index in range(1, tap_count):
        summed = summed + kernels[tap_index] * lax.slice_in_dim(padded, tap_index, tap_index + local_len, axis=seq_axis)
    active = jax.nn.silu(summed)
    channels = active.shape[-1] // 3
    head_shape = active.shape[:-1] + (channels // head_size, head_size)
    query = unit_rows(active[..., :channels].reshape(head_shape))
    key_rows = unit_rows(active[..., channels:2 * channels].reshape(head_shape)) * live_mask[..., None, None]
    value_rows = active[..., 2 * channels:].reshape(head_shape)
    beta = jax.nn.sigmoid(beta_logit) * live_mask[..., None]
    return (query, key_rows, value_rows, beta)

def prepare(key_rows, value_rows, beta):
    block_size = key_rows.shape[-2]
    head_size = key_rows.shape[-1]
    gram = jnp.einsum('...cd,...ed->...ce', key_rows, key_rows, precision=HIGH)
    strict = jnp.tril(jnp.ones((block_size, block_size), jnp.float32), -1)
    system = jnp.eye(block_size, dtype=jnp.float32) + beta[..., :, None] * gram * strict
    weighted = beta[..., :, None] * jnp.concatenate([key_rows, value_rows], -1)
    solved = lax.linalg.triangular_solve(system, weighted, left_side=True, lower=True, unit_diagonal=True)
    return (solved[..., :head_size], solved[..., head_size:])

def block_step(state, block):
    query, key_rows, wy_keys, wy_values = block
    block_size = query.shape[-2]
    causal = jnp.tril(jnp.ones((block_size, block_size), jnp.float32))
    fresh = wy_values - jnp.einsum('...cd,...de->...ce', wy_keys, state, precision=HIGH)
    scores = jnp.einsum('...cd,...ed->...ce', query, key_rows, precision=HIGH) * causal
    mixed = jnp.einsum('...cd,...de->...ce', query, state, precision=HIGH) + jnp.einsum('...ce,...ed->...cd', scores, fresh, precision=HIGH)
    state = state + jnp.einsum('...cd,...ce->...de', key_rows, fresh, precision=HIGH)
    return (state, mixed)

def run_blocks(query, key_rows, wy_keys, wy_values, state):
    moved = tuple((jnp.moveaxis(item, -3, 0) for item in (query, key_rows, wy_keys, wy_values)))
    state, mixed = lax.scan(jax.checkpoint(block_step), state, moved)
    return (jnp.moveaxis(mixed, 0, -3), state)

def layer(stream_row, live_mask, first_gain, query_weight, key_weight, value_weight, beta_weight, query_conv, key_conv, value_conv, mixer_gain, output_weight, second_gain, gate_weight, up_weight, down_weight):
    length = stream_row.shape[0]
    blocks = length // STRETCH
    normed_one = low(stream_row * inverse_rms(stream_row) * first_gain)
    projection = jnp.concatenate([query_weight, key_weight, value_weight], 1)
    pre_act = low_back(low(matmul_high(normed_one, projection)))
    beta_logit = low_back(matmul_high(normed_one, beta_weight))
    kernels = jnp.concatenate([query_conv, key_conv, value_conv], 1)
    padded = jnp.concatenate([jnp.zeros((kernels.shape[0] - 1, pre_act.shape[1]), jnp.float32), pre_act], 0)
    query, key_rows, value_rows, beta = mixer_inputs(padded, beta_logit, kernels, live_mask, HEAD_DIM)
    query = low(query)
    key_rows = low(key_rows)
    value_rows = low(value_rows)

    def to_blocks(values):
        return values.reshape(blocks, STRETCH, HEADS, HEAD_DIM).transpose(2, 0, 1, 3)
    query_blk = to_blocks(query)
    key_blk = to_blocks(key_rows)
    value_blk = to_blocks(value_rows)
    beta_blk = beta.reshape(blocks, STRETCH, HEADS).transpose(2, 0, 1)
    wy_keys, wy_values = prepare(key_blk, value_blk, beta_blk)
    start = jnp.zeros((HEADS, HEAD_DIM, HEAD_DIM), jnp.float32)
    mixed, unused = run_blocks(query_blk, key_blk, wy_keys, wy_values, start)
    mixed = mixed.transpose(1, 2, 0, 3).reshape(length, HEADS, HEAD_DIM)
    head_out = low((mixed * inverse_rms(mixed) * mixer_gain).reshape(length, HEADS * HEAD_DIM))
    stream = stream_row + low_back(matmul_high(head_out, output_weight))
    normed_two = low(stream * inverse_rms(stream) * second_gain)
    gate = low_back(matmul_high(normed_two, gate_weight))
    up_part = low_back(matmul_high(normed_two, up_weight))
    hidden = low(jax.nn.silu(gate) * up_part)
    return stream + low_back(matmul_high(hidden, down_weight))

def reference(tokens_in, lengths, first_gain, query_weight, key_weight, value_weight, beta_weight, query_conv, key_conv, value_conv, mixer_gain, output_weight, second_gain, gate_weight, up_weight, down_weight, upstream):
    weights = tuple((item.astype(jnp.float32) for item in (first_gain, query_weight, key_weight, value_weight, beta_weight, query_conv, key_conv, value_conv, mixer_gain, output_weight, second_gain, gate_weight, up_weight, down_weight)))
    positions = jnp.arange(tokens_in.shape[1], dtype=jnp.int32)

    def per_row(running, row_data):
        row_tokens, row_length, row_upstream = row_data
        live_mask = (positions < row_length).astype(jnp.float32)

        def forward(stream_row, *params):
            return layer(stream_row, live_mask, *params)
        layer_row, pull_back = jax.vjp(forward, row_tokens.astype(jnp.float32), *weights)
        gradients = pull_back(row_upstream.astype(jnp.float32) * live_mask[:, None])
        running = tuple((total + addend for total, addend in zip(running, gradients[1:])))
        return (running, (layer_row.astype(jnp.bfloat16), gradients[0]))
    zeros = tuple((jnp.zeros_like(item) for item in weights))
    running, outputs = lax.scan(per_row, zeros, (tokens_in, lengths, upstream))
    return (outputs[0], outputs[1]) + running
```

```python
import jax
import jax.numpy as jnp
from jax import lax
from jax.sharding import PartitionSpec as P

HEAD_DIM = 128
STRETCH = 64


HIGH = lax.Precision.HIGHEST
EPSILON = 1e-05
UNIT_EPSILON = 1e-06


def passed_along(value, axis, by):
    peers = lax.axis_size(axis)
    pairs = [(i, i + by) for i in range(peers) if 0 <= i + by < peers]
    return lax.ppermute(value, axis, pairs)


def swap_pairs(axis, by):
    peers = lax.axis_size(axis)
    return [(i, i ^ by) for i in range(peers)]


def exchanged(values, axis):
    peers = lax.axis_size(axis)
    own = lax.axis_index(axis)
    parts = [lax.dynamic_index_in_dim(values, own, 0, keepdims=False)]
    for by in range(1, peers):
        out = lax.dynamic_index_in_dim(values, own ^ by, 0, keepdims=False)
        parts.append(lax.ppermute(out, axis, swap_pairs(axis, by)))
    return parts


def spread(value, axis):
    peers = lax.axis_size(axis)
    return [value] + [
        lax.ppermute(value, axis, swap_pairs(axis, by)) for by in range(1, peers)
    ]


def in_order(parts, axis):
    stacked = jnp.stack(parts, 0)
    own = lax.axis_index(axis)
    return [
        lax.dynamic_index_in_dim(stacked, own ^ k, 0, keepdims=False) for k in range(len(parts))
    ]


def gather_head(value, axis):
    if lax.axis_size("head") == 2:
        other = lax.ppermute(value, "head", [(0, 1), (1, 0)])
        first = lax.axis_index("head") == 0
        return jnp.concatenate(
            [jnp.where(first, value, other), jnp.where(first, other, value)], axis
        )
    return lax.all_gather(value, "head", axis=axis, tiled=True)


def sum_head(value):
    low = value.astype(jnp.bfloat16)
    if lax.axis_size("head") == 2:
        other = lax.ppermute(low, "head", [(0, 1), (1, 0)])
        return low.astype(jnp.float32) + other.astype(jnp.float32)
    return lax.psum(low, "head").astype(jnp.float32)


def sum_doubling(value, axes):
    for axis in axes:
        by = 1
        while by < lax.axis_size(axis):
            value = value + lax.ppermute(value, axis, swap_pairs(axis, by))
            by *= 2
    return value


def own_half(value, width):
    return lax.dynamic_slice_in_dim(value, lax.axis_index("head") * width, width, value.ndim - 1)


def chain_state(maps, shifts, reverse):
    peers, position = lax.axis_size("seq"), lax.axis_index("seq")
    by = -1 if reverse else 1
    state = jnp.zeros_like(shifts)
    for step in range(peers - 1):
        out = (
            jnp.einsum("...ij,...jk->...ik", maps, state, precision=HIGH) + shifts
        ).astype(jnp.bfloat16)
        state = passed_along(out, "seq", by).astype(jnp.float32)
    return state


def inverse_rms(values):
    return lax.rsqrt(jnp.mean(values * values, axis=-1, keepdims=True) + EPSILON)


def unit_rows(values):
    return values * lax.rsqrt(jnp.sum(values * values, axis=-1, keepdims=True) + UNIT_EPSILON)


def round_trip(values):
    return lax.optimization_barrier(values.astype(jnp.bfloat16)).astype(jnp.float32)


def mixer_inputs(padded, beta_logit, kernels, live_mask, head_size):
    local_len = live_mask.shape[-1]
    tap_count = kernels.shape[0]
    seq_axis = padded.ndim - 2
    summed = kernels[0] * lax.slice_in_dim(padded, 0, local_len, axis=seq_axis)
    for tap_index in range(1, tap_count):
        summed = summed + kernels[tap_index] * lax.slice_in_dim(
            padded, tap_index, tap_index + local_len, axis=seq_axis
        )
    active = jax.nn.silu(summed)
    channels = active.shape[-1] // 3
    head_shape = active.shape[:-1] + (channels // head_size, head_size)
    query = unit_rows(active[..., :channels].reshape(head_shape))
    key_rows = (
        unit_rows(active[..., channels : 2 * channels].reshape(head_shape))
        * live_mask[..., None, None]
    )
    value_rows = active[..., 2 * channels :].reshape(head_shape)
    beta = jax.nn.sigmoid(beta_logit) * live_mask[..., None]
    return (query, key_rows, value_rows, beta)


def prepare(key_rows, value_rows, beta):
    block_size = key_rows.shape[-2]
    head_size = key_rows.shape[-1]
    gram = jnp.einsum("...cd,...ed->...ce", key_rows, key_rows, precision=HIGH)
    strict = jnp.tril(jnp.ones((block_size, block_size), jnp.float32), -1)
    system = jnp.eye(block_size, dtype=jnp.float32) + beta[..., :, None] * gram * strict
    weighted = beta[..., :, None] * jnp.concatenate([key_rows, value_rows], -1)
    solved = lax.linalg.triangular_solve(
        system, weighted, left_side=True, lower=True, unit_diagonal=True
    )
    return (solved[..., :head_size], solved[..., head_size:])


def block_step(state, block):
    query, key_rows, wy_keys, wy_values = block
    block_size = query.shape[-2]
    causal = jnp.tril(jnp.ones((block_size, block_size), jnp.float32))
    fresh = wy_values - jnp.einsum("...cd,...de->...ce", wy_keys, state, precision=HIGH)
    scores = jnp.einsum("...cd,...ed->...ce", query, key_rows, precision=HIGH) * causal
    mixed = jnp.einsum("...cd,...de->...ce", query, state, precision=HIGH) + jnp.einsum(
        "...ce,...ed->...cd", scores, fresh, precision=HIGH
    )
    state = state + jnp.einsum("...cd,...ce->...de", key_rows, fresh, precision=HIGH)
    return (state, mixed)


def run_blocks(query, key_rows, wy_keys, wy_values, state):
    moved = tuple((jnp.moveaxis(item, -3, 0) for item in (query, key_rows, wy_keys, wy_values)))
    state, mixed = lax.scan(block_step, state, moved)
    return (jnp.moveaxis(mixed, 0, -3), state)


def compose(earlier, later):
    first_map, first_shift = earlier
    next_map, next_shift = later
    joined_map = jnp.einsum("...ij,...jk->...ik", next_map, first_map, precision=HIGH)
    joined_shift = (
        jnp.einsum("...ij,...jk->...ik", next_map, first_shift, precision=HIGH) + next_shift
    )
    return (joined_map, joined_shift)


def device_map(key_rows, wy_keys, wy_values):
    head_size = key_rows.shape[-1]
    unit = jnp.eye(head_size, dtype=jnp.float32)
    block_maps = unit - jnp.einsum("...cd,...ce->...de", key_rows, wy_keys, precision=HIGH)
    block_shifts = jnp.einsum("...cd,...ce->...de", key_rows, wy_values, precision=HIGH)
    lead_shape = block_maps.shape[:-3] + (head_size, head_size)
    start = (jnp.broadcast_to(unit, lead_shape), jnp.zeros(lead_shape, jnp.float32))

    def fold_block(carry, block):
        return (compose(carry, block), None)

    total, unused = lax.scan(
        fold_block, start, (jnp.moveaxis(block_maps, -3, 0), jnp.moveaxis(block_shifts, -3, 0))
    )
    return total


def head_blocks(values):
    num_rows, local_len, local_heads, head_size = values.shape
    shaped = values.reshape(num_rows, local_len // STRETCH, STRETCH, local_heads, head_size)
    return shaped.transpose(0, 3, 1, 2, 4)


def seq_layout(values):
    num_rows, local_heads, blocks, block_size, head_size = values.shape
    return values.transpose(0, 2, 3, 1, 4).reshape(
        num_rows, blocks * block_size, local_heads, head_size
    )


def beta_blocks(values):
    num_rows, local_len, local_heads = values.shape
    return values.reshape(num_rows, local_len // STRETCH, STRETCH, local_heads).transpose(
        0, 3, 1, 2
    )


def beta_layout(values):
    num_rows, local_heads, blocks, block_size = values.shape
    return values.transpose(0, 2, 3, 1).reshape(num_rows, blocks * block_size, local_heads)


def mixer_norm(mixed_seq, gain):
    return mixed_seq * inverse_rms(mixed_seq) * gain


def shards(
    tokens_in,
    lengths,
    first_gain,
    query_weight,
    key_weight,
    value_weight,
    beta_weight,
    query_conv,
    key_conv,
    value_conv,
    mixer_gain,
    output_weight,
    second_gain,
    gate_weight,
    up_weight,
    down_weight,
    upstream,
):
    num_rows, local_len, local_width = tokens_in.shape
    full_width = query_weight.shape[0]
    channels = query_weight.shape[1]
    local_heads = beta_weight.shape[1]
    groups = lax.axis_size("head")
    ways = lax.axis_size("dp")
    spans = lax.axis_size("seq")
    rim_len = query_conv.shape[0] - 1
    positions = lax.axis_index("seq") * local_len + jnp.arange(local_len, dtype=jnp.int32)
    live_mask = (positions[None, :] < lengths[:, None]).astype(jnp.float32)
    masked_up = upstream * live_mask[..., None].astype(jnp.bfloat16)
    gathered = gather_head(tokens_in, 2)
    upstream_full = gather_head(masked_up, 2)
    gains = gather_head(jnp.stack([first_gain, second_gain]), 1).astype(jnp.float32)
    gain_one, gain_two = gains[0], gains[1]
    stream_full = gathered.astype(jnp.float32)
    scale_one = inverse_rms(stream_full)
    normed_one = (stream_full * scale_one * gain_one).astype(jnp.bfloat16)

    def tokens_of_plane(value):
        parts = spread(own_half(value, local_width)[0], "dp")
        part = gather_head(jnp.concatenate(parts, 0), 1)
        return part.reshape(part.shape[0], ways, spans, -1).transpose(2, 0, 1, 3).reshape(
            spans, part.shape[0], -1
        )

    def columns_of_plane(values):
        turned = values.T
        turned = turned.reshape(ways, turned.shape[0] // ways, turned.shape[1])
        return turned

    def reduced_piece(left, right):
        part = jnp.einsum("ct,stk->sck", left, right, preferred_element_type=jnp.float32)
        return lax.psum_scatter(
            part.astype(jnp.bfloat16), "seq", scatter_dimension=0, tiled=False
        )

    def to_owner(piece):
        c = piece.shape[0]
        blocks = piece.reshape(c, ways, -1).transpose(1, 0, 2)
        return jnp.stack(in_order(exchanged(blocks, "dp"), "dp"), 0)

    tokens_one = tokens_of_plane(normed_one)
    tokens_up = tokens_of_plane(upstream_full)
    pre_act = jnp.concatenate(
        [
            jnp.dot(normed_one, query_weight, preferred_element_type=jnp.float32),
            jnp.dot(normed_one, key_weight, preferred_element_type=jnp.float32),
            jnp.dot(normed_one, value_weight, preferred_element_type=jnp.float32),
        ],
        2,
    ).astype(jnp.bfloat16)
    beta_logit = jnp.dot(normed_one, beta_weight, preferred_element_type=jnp.float32)
    carried_rim = passed_along(pre_act[:, local_len - rim_len :, :], "seq", 1)
    pre_ext = jnp.concatenate([carried_rim, pre_act], 1).astype(jnp.float32)
    kernels = jnp.concatenate([query_conv, key_conv, value_conv], 1).astype(jnp.float32)

    def inputs_fn(padded, logits, weights):
        return mixer_inputs(padded, logits, weights, live_mask, HEAD_DIM)

    mixer_in, pull_inputs = jax.vjp(inputs_fn, pre_ext, beta_logit, kernels)
    query_blk = head_blocks(round_trip(mixer_in[0]))
    key_blk = head_blocks(round_trip(mixer_in[1]))
    value_blk = head_blocks(round_trip(mixer_in[2]))
    beta_blk = beta_blocks(mixer_in[3])
    wy_pair, pull_prep = jax.vjp(prepare, key_blk, value_blk, beta_blk)
    device_maps = device_map(key_blk, wy_pair[0], wy_pair[1])
    entering = chain_state(device_maps[0], device_maps[1], False)
    mixed_pair, pull_blocks = jax.vjp(
        run_blocks, query_blk, key_blk, wy_pair[0], wy_pair[1], entering
    )
    mixed_seq = seq_layout(mixed_pair[0])
    normed_mix, pull_norm = jax.vjp(mixer_norm, mixed_seq, mixer_gain.astype(jnp.float32))
    head_out = normed_mix.reshape(num_rows, local_len, channels).astype(jnp.bfloat16)
    mixer_part = jnp.dot(head_out, output_weight, preferred_element_type=jnp.float32)
    stream_mid = stream_full + sum_head(mixer_part)
    scale_two = inverse_rms(stream_mid)
    normed_two = (stream_mid * scale_two * gain_two).astype(jnp.bfloat16)
    gate_pre = jnp.dot(normed_two, gate_weight, preferred_element_type=jnp.float32)
    up_pre = jnp.dot(normed_two, up_weight, preferred_element_type=jnp.float32)
    hidden = (jax.nn.silu(gate_pre) * up_pre).astype(jnp.bfloat16)
    feed_part = jnp.dot(hidden, down_weight, preferred_element_type=jnp.float32)
    layer_out = own_half(stream_mid + sum_head(feed_part), local_width).astype(jnp.bfloat16)
    tokens_two = tokens_of_plane(normed_two)
    d_hidden = jnp.einsum(
        "rsd,fd->rsf", upstream_full, down_weight, preferred_element_type=jnp.float32
    )
    gate_sig = jax.nn.sigmoid(gate_pre)
    d_gate = (d_hidden * up_pre * gate_sig * (1.0 + gate_pre * (1.0 - gate_sig))).astype(
        jnp.bfloat16
    )
    d_up = (d_hidden * gate_pre * gate_sig).astype(jnp.bfloat16)
    d_normed_two = jnp.einsum(
        "rsf,df->rsd", d_gate, gate_weight, preferred_element_type=jnp.float32
    ) + jnp.einsum("rsf,df->rsd", d_up, up_weight, preferred_element_type=jnp.float32)
    feed_cols = exchanged(
        jnp.concatenate(
            [columns_of_plane(hidden[0]), columns_of_plane(d_gate[0]), columns_of_plane(d_up[0])], 1
        ),
        "dp",
    )
    feed_cols = jnp.concatenate(feed_cols, 1)
    units = feed_cols.shape[0] // 3
    down_piece = reduced_piece(feed_cols[:units], tokens_up)
    gate_piece = reduced_piece(feed_cols[units : 2 * units], tokens_two)
    up_piece = reduced_piece(feed_cols[2 * units :], tokens_two)
    d_two = sum_head(d_normed_two)
    d_stream = (
        upstream_full.astype(jnp.float32)
        + scale_two * gain_two * d_two
        - stream_mid
        * scale_two
        * scale_two
        * scale_two
        * (jnp.sum(d_two * gain_two * stream_mid, axis=-1, keepdims=True) / full_width)
    )
    grad_second = own_half(jnp.sum(d_two * stream_mid * scale_two, axis=(0, 1)), local_width)
    residual_full = d_stream.astype(jnp.bfloat16)
    tokens_res = tokens_of_plane(residual_full)
    d_head_out = jnp.einsum(
        "rsd,cd->rsc", residual_full, output_weight, preferred_element_type=jnp.float32
    )
    out_cols = jnp.concatenate(exchanged(columns_of_plane(head_out[0]), "dp"), 1)
    out_piece = reduced_piece(out_cols, tokens_res)
    d_mixed_seq, grad_gain_part = pull_norm(
        d_head_out.reshape(num_rows, local_len, local_heads, HEAD_DIM)
    )
    d_mixed_blk = head_blocks(d_mixed_seq)
    first_pass = pull_blocks((d_mixed_blk, jnp.zeros_like(entering)))
    leaving = chain_state(jnp.swapaxes(device_maps[0], -1, -2), first_pass[4], True)
    second_pass = pull_blocks((jnp.zeros_like(d_mixed_blk), leaving))
    d_query_blk = first_pass[0] + second_pass[0]
    d_key_blk = first_pass[1] + second_pass[1]
    d_wy_keys = first_pass[2] + second_pass[2]
    d_wy_values = first_pass[3] + second_pass[3]
    d_key_prep, d_value_blk, d_beta_blk = pull_prep((d_wy_keys, d_wy_values))
    d_mixer_in = (
        seq_layout(d_query_blk),
        seq_layout(d_key_blk + d_key_prep),
        seq_layout(d_value_blk),
        beta_layout(d_beta_blk),
    )
    d_pre_ext, d_beta_logit, grad_kernels = pull_inputs(d_mixer_in)
    rim_grad = passed_along(d_pre_ext[:, :rim_len, :], "seq", -1)
    d_pre_own = d_pre_ext[:, rim_len:, :]
    d_pre = jnp.concatenate(
        [d_pre_own[:, : local_len - rim_len, :], d_pre_own[:, local_len - rim_len :, :] + rim_grad],
        1,
    ).astype(jnp.bfloat16)
    d_logit_low = d_beta_logit.astype(jnp.bfloat16)
    d_pre_query = d_pre[..., :channels]
    d_pre_key = d_pre[..., channels : 2 * channels]
    d_pre_value = d_pre[..., 2 * channels :]
    d_normed_one = (
        jnp.einsum("rsc,dc->rsd", d_pre_query, query_weight, preferred_element_type=jnp.float32)
        + jnp.einsum("rsc,dc->rsd", d_pre_key, key_weight, preferred_element_type=jnp.float32)
        + jnp.einsum("rsc,dc->rsd", d_pre_value, value_weight, preferred_element_type=jnp.float32)
        + jnp.einsum("rsh,dh->rsd", d_logit_low, beta_weight, preferred_element_type=jnp.float32)
    )
    mix_cols = exchanged(
        jnp.concatenate(
            [
                columns_of_plane(d_pre_query[0]),
                columns_of_plane(d_pre_key[0]),
                columns_of_plane(d_pre_value[0]),
            ],
            1,
        ),
        "dp",
    )
    mix_piece = reduced_piece(jnp.concatenate(mix_cols, 1), tokens_one)
    grad_beta_part = jnp.einsum(
        "rsd,rsh->dh", normed_one, d_logit_low, preferred_element_type=jnp.float32
    )
    d_one = sum_head(d_normed_one)
    grad_tokens = own_half(
        d_stream
        + scale_one * gain_one * d_one
        - stream_full
        * scale_one
        * scale_one
        * scale_one
        * (jnp.sum(d_one * gain_one * stream_full, axis=-1, keepdims=True) / full_width),
        local_width,
    )
    grad_first = own_half(jnp.sum(d_one * stream_full * scale_one, axis=(0, 1)), local_width)
    small = [grad_first, grad_second, grad_kernels.reshape(-1), grad_beta_part.reshape(-1)]
    total = sum_doubling(jnp.concatenate(small), ("dp", "seq"))
    gain_total = sum_doubling(grad_gain_part, ("dp", "seq"))
    gain_total = sum_doubling(gain_total, ("head",))
    grad_first = total[:local_width]
    grad_second = total[local_width : 2 * local_width]
    kernel_end = 2 * local_width + grad_kernels.size
    kernel_sum = total[2 * local_width : kernel_end].reshape(grad_kernels.shape)
    share = lax.axis_index("dp") * spans + lax.axis_index("seq")
    rows = full_width // (ways * spans)
    grad_beta = lax.dynamic_slice_in_dim(
        total[kernel_end:].reshape(full_width, local_heads), share * rows, rows, 0
    )
    down = to_owner(down_piece).reshape(-1, rows).astype(jnp.float32)
    gate = to_owner(gate_piece).reshape(-1, rows).astype(jnp.float32)
    up = to_owner(up_piece).reshape(-1, rows).astype(jnp.float32)
    out = to_owner(out_piece).reshape(-1, rows).astype(jnp.float32)
    mix = to_owner(mix_piece).astype(jnp.float32)
    third = mix.shape[1] // 3
    return (
        layer_out,
        grad_tokens,
        grad_first,
        mix[:, :third].reshape(-1, rows).T,
        mix[:, third : 2 * third].reshape(-1, rows).T,
        mix[:, 2 * third :].reshape(-1, rows).T,
        grad_beta,
        kernel_sum[:, :channels],
        kernel_sum[:, channels : 2 * channels],
        kernel_sum[:, 2 * channels :],
        gain_total,
        out,
        grad_second,
        gate.T,
        up.T,
        down,
    )


def solution(mesh):
    placed = (
        P("dp", "seq", "head"),
        P("dp"),
        P("head"),
        P(None, "head"),
        P(None, "head"),
        P(None, "head"),
        P(None, "head"),
        P(None, "head"),
        P(None, "head"),
        P(None, "head"),
        P(),
        P("head", None),
        P("head"),
        P(None, "head"),
        P(None, "head"),
        P("head", None),
        P("dp", "seq", "head"),
    )
    return jax.shard_map(
        shards,
        mesh=mesh,
        in_specs=placed,
        out_specs=(
            P("dp", "seq", "head"),
            P("dp", "seq", "head"),
            P("head"),
            P(("dp", "seq"), "head"),
            P(("dp", "seq"), "head"),
            P(("dp", "seq"), "head"),
            P(("dp", "seq"), "head"),
            P(None, "head"),
            P(None, "head"),
            P(None, "head"),
            P(),
            P("head", ("dp", "seq")),
            P("head"),
            P(("dp", "seq"), "head"),
            P(("dp", "seq"), "head"),
            P("head", ("dp", "seq")),
        ),
        check_vma=False,
    )
```

```python
import functools

import jax
import jax.numpy as jnp
from jax import lax
from jax.experimental import pallas as pl
from jax.experimental.pallas import tpu as pltpu
from jax.sharding import PartitionSpec as P

HEAD_DIM = 128


HIGH = lax.Precision.HIGHEST
EPSILON = 1e-05
UNIT_EPSILON = 1e-06


def passed_along(value, axis, by):
    peers = lax.axis_size(axis)
    pairs = [(i, i + by) for i in range(peers) if 0 <= i + by < peers]
    return lax.ppermute(value, axis, pairs)


def swap_pairs(axis, by):
    peers = lax.axis_size(axis)
    return [(i, i ^ by) for i in range(peers)]


def exchanged(values, axis):
    peers = lax.axis_size(axis)
    own = lax.axis_index(axis)
    parts = [lax.dynamic_index_in_dim(values, own, 0, keepdims=False)]
    for by in range(1, peers):
        out = lax.dynamic_index_in_dim(values, own ^ by, 0, keepdims=False)
        parts.append(lax.ppermute(out, axis, swap_pairs(axis, by)))
    return parts


def spread(value, axis):
    peers = lax.axis_size(axis)
    return [value] + [
        lax.ppermute(value, axis, swap_pairs(axis, by)) for by in range(1, peers)
    ]


def in_order(parts, axis):
    stacked = jnp.stack(parts, 0)
    own = lax.axis_index(axis)
    return [
        lax.dynamic_index_in_dim(stacked, own ^ k, 0, keepdims=False) for k in range(len(parts))
    ]


def gather_head(value, axis):
    if lax.axis_size("head") == 2:
        other = lax.ppermute(value, "head", [(0, 1), (1, 0)])
        first = lax.axis_index("head") == 0
        return jnp.concatenate(
            [jnp.where(first, value, other), jnp.where(first, other, value)], axis
        )
    return lax.all_gather(value, "head", axis=axis, tiled=True)


def sum_head(value):
    low = value.astype(jnp.bfloat16)
    if lax.axis_size("head") == 2:
        other = lax.ppermute(low, "head", [(0, 1), (1, 0)])
        return low.astype(jnp.float32) + other.astype(jnp.float32)
    return lax.psum(low, "head").astype(jnp.float32)


def sum_doubling(value, axes):
    for axis in axes:
        by = 1
        while by < lax.axis_size(axis):
            value = value + lax.ppermute(value, axis, swap_pairs(axis, by))
            by *= 2
    return value


def own_half(value, width):
    return lax.dynamic_slice_in_dim(value, lax.axis_index("head") * width, width, value.ndim - 1)


def chain_state(maps, shifts, reverse):
    peers = lax.axis_size("seq")
    by = -1 if reverse else 1
    states = [passed_along(shifts.astype(jnp.bfloat16), "seq", by)]
    for step in range(peers - 2):
        out = (
            jnp.einsum("hij,hjk->hik", maps, states[-1].astype(jnp.float32), precision=HIGH)
            + shifts
        )
        states.append(passed_along(out.astype(jnp.bfloat16), "seq", by))
    return states[-1]


def inverse_rms(values):
    return lax.rsqrt(jnp.mean(values * values, axis=-1, keepdims=True) + EPSILON)


def halves(a):
    top = a.astype(jnp.bfloat16)
    return top, (a - top.astype(jnp.float32)).astype(jnp.bfloat16)


def dot_low(a, b, dims=(1, 0)):
    return lax.dot_general(
        a, b, (((dims[0],), (dims[1],)), ((), ())), preferred_element_type=jnp.float32
    )


def dot_left(a, b, dims=(1, 0)):
    top, rest = halves(a)
    return dot_low(top, b, dims) + dot_low(rest, b, dims)


def dot_right(a, b, dims=(1, 0)):
    top, rest = halves(b)
    return dot_low(a, top, dims) + dot_low(a, rest, dims)


def dot_both(a, b, dims=(1, 0)):
    a_top, a_rest = halves(a)
    b_top, b_rest = halves(b)
    return dot_low(a_top, b_top, dims) + (
        dot_low(a_top, b_rest, dims) + dot_low(a_rest, b_top, dims)
    )


def grid_marks(size):
    row = lax.broadcasted_iota(jnp.int32, (size, size), 0)
    col = lax.broadcasted_iota(jnp.int32, (size, size), 1)
    return row, col


def unit_lower_inverses(tiles):
    size = tiles[0].shape[0]
    row, col = grid_marks(size)
    unit = (row == col).astype(jnp.float32)
    base = 8
    near = (row // base == col // base) & (row > col)
    cores = [jnp.where(near, tile, 0.0) for tile in tiles]
    squares = [dot_both(core, core) for core in cores]
    fourths = [dot_both(square, square) for square in squares]
    found = [dot_both(unit - core, unit + square) for core, square in zip(cores, squares)]
    found = [dot_both(part, unit + fourth) for part, fourth in zip(found, fourths)]
    while base < size:
        wide = 2 * base
        near = (row // wide == col // wide) & (row // base > col // base)
        links = [jnp.where(near, tile, 0.0) for tile in tiles]
        steps = [dot_both(part, link) for part, link in zip(found, links)]
        found = [part - dot_both(step, part) for part, step in zip(found, steps)]
        base = wide
    return found


def lower_inverses(systems, tile):
    size = systems[0].shape[0]
    if size <= tile:
        return unit_lower_inverses(systems)
    half = size // 2
    diagonals = [s[:half, :half] for s in systems] + [s[half:, half:] for s in systems]
    found = lower_inverses(diagonals, tile)
    firsts, seconds = found[: len(systems)], found[len(systems) :]
    steps = [dot_both(second, s[half:, :half]) for second, s in zip(seconds, systems)]
    corners = [-dot_both(step, first) for step, first in zip(steps, firsts)]
    empty = jnp.zeros((half, half), jnp.float32)
    return [
        jnp.concatenate(
            [jnp.concatenate([first, empty], 1), jnp.concatenate([corner, second], 1)], 0
        )
        for first, corner, second in zip(firsts, corners, seconds)
    ]


RIM = 16


def conv_sum(ext, pre, rim, weights, taps, length):
    ext[:RIM, :] = rim.astype(jnp.float32)
    ext[RIM : RIM + length, :] = pre.astype(jnp.float32)
    first = RIM - taps + 1
    summed = weights[0:1, :] * ext[first : first + length, :]
    for tap in range(1, taps):
        summed = summed + weights[tap : tap + 1, :] * ext[first + tap : first + tap + length, :]
    return summed


def head_columns(refs, index):
    span = slice(index * HEAD_DIM, (index + 1) * HEAD_DIM)
    return [ref[:, span] for ref in refs]


def unit_scale(rows):
    return lax.rsqrt(jnp.sum(rows * rows, axis=-1, keepdims=True) + UNIT_EPSILON)


def column_of(values, index):
    lane = lax.broadcasted_iota(jnp.int32, values.shape, 1)
    return jnp.sum(jnp.where(lane == index, values, 0.0), axis=-1, keepdims=True)


def row_of(values, index):
    place = lax.broadcasted_iota(jnp.int32, values.shape, 0)
    return jnp.sum(jnp.where(place == index, values, 0.0), axis=0, keepdims=True)


def mixer_local_kernel(
    per_step, taps, *refs
):
    (q_pre, k_pre, v_pre, q_rim, k_rim, v_rim, q_w, k_w, v_w, logit, logit_t, live, live_t) = refs[:13]
    q_out, k_out, v_out, wy_out, inv_out, mix_out, end_out, ext = refs[13:]
    length = q_pre.shape[0]
    step = pl.program_id(0)
    row, col = grid_marks(length)
    live_col = live[...]
    queries, keys, values, systems, beta_rows = [], [], [], [], []
    for i in range(per_step):
        pres = head_columns((q_pre, k_pre, v_pre), i)
        rims = head_columns((q_rim, k_rim, v_rim), i)
        weights = head_columns((q_w, k_w, v_w), i)
        active = []
        for pre, rim, weight in zip(pres, rims, weights):
            summed = conv_sum(ext, pre, rim, weight.astype(jnp.float32), taps, length)
            active.append(summed * jax.nn.sigmoid(summed))
        q, k, v = active
        q = (q * unit_scale(q)).astype(jnp.bfloat16)
        k = (k * unit_scale(k) * live_col).astype(jnp.bfloat16)
        v = v.astype(jnp.bfloat16)
        beta = jax.nn.sigmoid(column_of(logit[...], step * per_step + i)) * live_col
        beta_rows.append(jax.nn.sigmoid(row_of(logit_t[...], step * per_step + i)) * live_t[...])
        gram = dot_low(k, k, (1, 1))
        systems.append(jnp.where(row > col, beta * gram, 0.0))
        span = slice(i * HEAD_DIM, (i + 1) * HEAD_DIM)
        q_out[:, span] = q
        k_out[:, span] = k
        v_out[:, span] = v
        queries.append(q)
        keys.append(k)
        values.append(v)
    inverses = lower_inverses(systems, 128)
    wys = [
        dot_left(inverse * beta_row, jnp.concatenate([k, v], 1))
        for inverse, beta_row, k, v in zip(inverses, beta_rows, keys, values)
    ]
    unit = (lax.broadcasted_iota(jnp.int32, (HEAD_DIM, 2 * HEAD_DIM), 0)
            == lax.broadcasted_iota(jnp.int32, (HEAD_DIM, 2 * HEAD_DIM), 1)).astype(jnp.float32)
    left = (lax.broadcasted_iota(jnp.int32, (HEAD_DIM, 2 * HEAD_DIM), 1) < HEAD_DIM)
    for i in range(per_step):
        wy_out[i] = wys[i]
        inv_out[i] = inverses[i]
        ends = dot_right(keys[i], wys[i], (0, 0))
        end_out[i] = unit + jnp.where(left, -ends, ends)
        scores = jnp.where(row >= col, dot_low(queries[i], keys[i], (1, 1)), 0.0)
        seen = dot_both(scores, wys[i])
        mix_out[i, :, :HEAD_DIM] = queries[i].astype(jnp.float32) - seen[:, :HEAD_DIM]
        mix_out[i, :, HEAD_DIM:] = seen[:, HEAD_DIM:]


def mixer_finish_kernel(per_step, mix, state, gain, token, mixed_out, head_out):
    for i in range(per_step):
        span = slice(i * HEAD_DIM, (i + 1) * HEAD_DIM)
        mixed = mix[i, :, HEAD_DIM:] + dot_left(mix[i, :, :HEAD_DIM], state[i])
        scale = lax.rsqrt(jnp.mean(mixed * mixed, axis=-1, keepdims=True) + EPSILON)
        mixed_out[:, span] = mixed
        head_out[:, span] = (mixed * scale * gain[...]).astype(jnp.bfloat16)


def mixer_back_local_kernel(
    per_step, d_head, mixed_ref, gain_ref, q_ref, k_ref, wy, token,
    d_mixed_out, d_fresh_out, end_out, gain_out,
):
    length = q_ref.shape[0]
    row, col = grid_marks(length)
    gain = gain_ref[...]
    gain_total = jnp.zeros((1, HEAD_DIM), jnp.float32)
    for i in range(per_step):
        d_out, mixed, q, k = head_columns((d_head, mixed_ref, q_ref, k_ref), i)
        scale = lax.rsqrt(jnp.mean(mixed * mixed, axis=-1, keepdims=True) + EPSILON)
        weighted = gain * d_out
        inner = jnp.sum(weighted * mixed, axis=-1, keepdims=True)
        d_mixed = scale * weighted - mixed * (scale * scale * scale * inner / HEAD_DIM)
        gain_total += jnp.sum(d_out * mixed * scale, axis=0, keepdims=True)
        scores_t = jnp.where(col >= row, dot_low(k, q, (1, 1)), 0.0)
        d_fresh = dot_both(scores_t, d_mixed)
        d_mixed_out[i] = d_mixed
        d_fresh_out[i] = d_fresh
        end_out[i] = dot_right(q, d_mixed, (0, 0)) - dot_both(wy[i, :, :HEAD_DIM], d_fresh, (0, 0))

    @pl.when(pl.program_id(0) == 0)
    def _():
        gain_out[...] = jnp.zeros_like(gain_out)

    gain_out[...] += jnp.broadcast_to(gain_total, gain_out.shape)


def mixer_back_kernel(per_step, taps, *refs):
    (q_pre, k_pre, v_pre, q_rim, k_rim, v_rim, q_w, k_w, v_w, logit, live) = refs[:11]
    (q_ref, k_ref, v_ref, wy, inv, state, d_mixed_ref, d_fresh_ref, d_state) = refs[11:20]
    d_q_out, d_k_out, d_v_out, tail_out, rim_out, conv_out, d_logit_out, ext, ext_back = refs[20:]
    length = q_pre.shape[0]
    step = pl.program_id(0)
    row, col = grid_marks(length)
    live_col = live[...]

    @pl.when(step == 0)
    def _():
        d_logit_out[...] = jnp.zeros_like(d_logit_out)

    for i in range(per_step):
        q, k, v = head_columns((q_ref, k_ref, v_ref), i)
        entering, leaving = state[i], d_state[i]
        wy_both = wy[i]
        d_mixed = d_mixed_ref[i]
        d_fresh = d_fresh_ref[i] + dot_low(k, leaving)
        fresh = wy_both[:, HEAD_DIM:] - dot_left(wy_both[:, :HEAD_DIM], entering)
        d_scores = jnp.where(row >= col, dot_both(d_mixed, fresh, (1, 1)), 0.0)
        d_q = dot_left(d_mixed, entering, (1, 1)) + dot_left(d_scores, k)
        d_k = dot_left(d_scores, q, (0, 0)) + dot_left(fresh, leaving, (1, 1))
        d_wy = jnp.concatenate([-dot_left(d_fresh, entering, (1, 1)), d_fresh], 1)
        d_rhs = dot_both(inv[i], d_wy, (0, 0))
        edges = jnp.where(row > col, -dot_both(d_rhs, wy_both, (1, 1)), 0.0)
        logits = column_of(logit[...], step * per_step + i)
        sig = jax.nn.sigmoid(logits)
        beta = sig * live_col
        both = jnp.concatenate([k, v], 1).astype(jnp.float32)
        gram = dot_low(k, k, (1, 1))
        d_beta = jnp.sum(d_rhs * both, axis=-1, keepdims=True) + jnp.sum(
            edges * gram, axis=-1, keepdims=True
        )
        scaled = beta * edges
        d_k = d_k + beta * d_rhs[:, :HEAD_DIM] + dot_left(scaled, k) + dot_left(scaled, k, (0, 0))
        d_v = beta * d_rhs[:, HEAD_DIM:]
        d_k = d_k * live_col
        d_logit = d_beta * live_col * sig * (1.0 - sig)
        lane = lax.broadcasted_iota(jnp.int32, d_logit_out.shape, 1)
        d_logit_out[...] += jnp.where(lane == step * per_step + i, d_logit, 0.0)
        span = slice(i * HEAD_DIM, (i + 1) * HEAD_DIM)
        pres = head_columns((q_pre, k_pre, v_pre), i)
        rims = head_columns((q_rim, k_rim, v_rim), i)
        weights = head_columns((q_w, k_w, v_w), i)
        outs = (d_q_out, d_k_out, d_v_out)
        for part, (pre, rim, weight, grad) in enumerate(zip(pres, rims, weights, (d_q, d_k, d_v))):
            weight = weight.astype(jnp.float32)
            summed = conv_sum(ext, pre, rim, weight, taps, length)
            gate = jax.nn.sigmoid(summed)
            if part < 2:
                active = summed * gate
                scale = unit_scale(active)
                inner = jnp.sum(active * grad, axis=-1, keepdims=True)
                grad = scale * grad - active * (scale * scale * scale * inner)
            d_conv = grad * gate * (1.0 + summed * (1.0 - gate))
            first = RIM - taps + 1
            rows = [
                jnp.sum(d_conv * ext[first + tap : first + tap + length, :], axis=0, keepdims=True)
                for tap in range(taps)
            ]
            conv_out[part, :, span] = jnp.concatenate(rows, 0)
            ext_back[:8, :] = jnp.zeros((8, HEAD_DIM), jnp.float32)
            ext_back[8 : 8 + length, :] = d_conv
            ext_back[8 + length :, :] = jnp.zeros((8, HEAD_DIM), jnp.float32)
            own = jnp.zeros((length, HEAD_DIM), jnp.float32)
            before = jnp.zeros((8, HEAD_DIM), jnp.float32)
            for tap in range(taps):
                shift = taps - 1 - tap
                own = own + weight[tap : tap + 1, :] * ext_back[8 + shift : 8 + shift + length, :]
                before = before + weight[tap : tap + 1, :] * ext_back[shift : shift + 8, :]
            outs[part][:, span] = own.astype(jnp.bfloat16)
            tail_out[part, :, span] = own[length - 8 :, :]
            rim_out[part, :, span] = before


def mixer_specs(length, heads, per_step):
    width = per_step * HEAD_DIM

    def flat(rows):
        return pl.BlockSpec((rows, width), lambda h: (0, h))

    def whole(*shape):
        return pl.BlockSpec(shape, lambda h: (0,) * len(shape))

    def by_head(*shape):
        return pl.BlockSpec((per_step,) + shape, lambda h: (h,) + (0,) * len(shape))

    return flat, whole, by_head


def mixer_call(kernel, heads, per_step, ins, outs, scratch, flops, args):
    moved = sum(a.size * a.dtype.itemsize for a in args)
    return pl.pallas_call(
        kernel,
        grid=(heads // per_step,),
        in_specs=ins,
        out_specs=[spec for spec, _ in outs],
        out_shape=[shape for _, shape in outs],
        scratch_shapes=scratch,
        compiler_params=pltpu.CompilerParams(vmem_limit_bytes=40 * 1024 * 1024),
        cost_estimate=pl.CostEstimate(flops=flops, bytes_accessed=moved, transcendentals=0),
    )(*args)


def f32(*shape):
    return jax.ShapeDtypeStruct(shape, jnp.float32)


def b16(*shape):
    return jax.ShapeDtypeStruct(shape, jnp.bfloat16)


def mixer_local(pres, rims, convs, logit, live, per_step):
    length, channels = pres[0].shape
    heads = channels // HEAD_DIM
    taps = convs[0].shape[0]
    flat, whole, by_head = mixer_specs(length, heads, per_step)
    args = (*pres, *rims, *convs, logit, logit.T, live, live.T)
    return mixer_call(
        functools.partial(mixer_local_kernel, per_step, taps),
        heads,
        per_step,
        [flat(length)] * 3
        + [flat(RIM)] * 3
        + [flat(taps)] * 3
        + [whole(length, heads), whole(heads, length), whole(length, 1), whole(1, length)],
        [(flat(length), b16(length, channels))] * 3
        + [
            (by_head(length, 2 * HEAD_DIM), f32(heads, length, 2 * HEAD_DIM)),
            (by_head(length, length), f32(heads, length, length)),
            (by_head(length, 2 * HEAD_DIM), f32(heads, length, 2 * HEAD_DIM)),
            (by_head(HEAD_DIM, 2 * HEAD_DIM), f32(heads, HEAD_DIM, 2 * HEAD_DIM)),
        ],
        [pltpu.VMEM((RIM + length, HEAD_DIM), jnp.float32)],
        heads * 2 * length**3 * 30,
        args,
    )


def mixer_finish(mix, state, gain, token, per_step):
    heads, length, _ = mix.shape
    flat, whole, by_head = mixer_specs(length, heads, per_step)
    return mixer_call(
        functools.partial(mixer_finish_kernel, per_step),
        heads,
        per_step,
        [
            by_head(length, 2 * HEAD_DIM),
            by_head(HEAD_DIM, HEAD_DIM),
            whole(1, HEAD_DIM),
            pl.BlockSpec(memory_space=pl.ANY),
        ],
        [
            (flat(length), f32(length, heads * HEAD_DIM)),
            (flat(length), b16(length, heads * HEAD_DIM)),
        ],
        [],
        heads * 2 * length**3,
        (mix, state, gain, token),
    )


def mixer_back_local(d_head, mixed, gain, q, k, wy, token, per_step):
    heads, length, _ = wy.shape
    flat, whole, by_head = mixer_specs(length, heads, per_step)
    return mixer_call(
        functools.partial(mixer_back_local_kernel, per_step),
        heads,
        per_step,
        [flat(length)] * 2
        + [whole(1, HEAD_DIM)]
        + [flat(length)] * 2
        + [by_head(length, 2 * HEAD_DIM), pl.BlockSpec(memory_space=pl.ANY)],
        [
            (by_head(length, HEAD_DIM), f32(heads, length, HEAD_DIM)),
            (by_head(length, HEAD_DIM), f32(heads, length, HEAD_DIM)),
            (by_head(HEAD_DIM, HEAD_DIM), f32(heads, HEAD_DIM, HEAD_DIM)),
            (whole(8, HEAD_DIM), f32(8, HEAD_DIM)),
        ],
        [],
        heads * 2 * length**3 * 5,
        (d_head, mixed, gain, q, k, wy, token),
    )


def mixer_back(pres, rims, convs, logit, live, q, k, v, wy, inv, state, d_mixed, d_fresh, d_state, per_step):
    length, channels = pres[0].shape
    heads = channels // HEAD_DIM
    taps = convs[0].shape[0]
    flat, whole, by_head = mixer_specs(length, heads, per_step)
    three = pl.BlockSpec((3, 8, per_step * HEAD_DIM), lambda h: (0, 0, h))
    return mixer_call(
        functools.partial(mixer_back_kernel, per_step, taps),
        heads,
        per_step,
        [flat(length)] * 3
        + [flat(RIM)] * 3
        + [flat(taps)] * 3
        + [whole(length, heads), whole(length, 1)]
        + [flat(length)] * 3
        + [
            by_head(length, 2 * HEAD_DIM),
            by_head(length, length),
            by_head(HEAD_DIM, HEAD_DIM),
            by_head(length, HEAD_DIM),
            by_head(length, HEAD_DIM),
            by_head(HEAD_DIM, HEAD_DIM),
        ],
        [(flat(length), b16(length, channels))] * 3
        + [
            (three, f32(3, 8, channels)),
            (three, f32(3, 8, channels)),
            (
                pl.BlockSpec((3, taps, per_step * HEAD_DIM), lambda h: (0, 0, h)),
                f32(3, taps, channels),
            ),
            (whole(length, heads), f32(length, heads)),
        ],
        [
            pltpu.VMEM((RIM + length, HEAD_DIM), jnp.float32),
            pltpu.VMEM((16 + length, HEAD_DIM), jnp.float32),
        ],
        heads * 2 * length**3 * 20,
        (*pres, *rims, *convs, logit, live, q, k, v, wy, inv, state, d_mixed, d_fresh, d_state),
    )


def feed_kernel(x_ref, d_ref, gate_w, up_w, down_w, feed_out, d_x_out, turned_out, feed_sum, d_x_sum):
    step = pl.program_id(0)
    x = x_ref[...]
    d_out = d_ref[...]
    gate = dot_low(x, gate_w[...])
    up = dot_low(x, up_w[...])
    d_hidden = dot_low(d_out, down_w[...], (1, 1))
    sig = jax.nn.sigmoid(gate)
    hidden = (gate * sig * up).astype(jnp.bfloat16)
    d_gate = (d_hidden * up * sig * (1.0 + gate * (1.0 - sig))).astype(jnp.bfloat16)
    d_up = (d_hidden * gate * sig).astype(jnp.bfloat16)
    for place, part in enumerate((hidden, d_gate, d_up)):
        turned_out[place] = part.T
    feed = dot_low(hidden, down_w[...])
    d_x = dot_low(d_gate, gate_w[...], (1, 1)) + dot_low(d_up, up_w[...], (1, 1))

    @pl.when(step == 0)
    def _():
        feed_sum[...] = feed
        d_x_sum[...] = d_x

    @pl.when(step > 0)
    def _():
        feed_sum[...] += feed
        d_x_sum[...] += d_x

    @pl.when(step == pl.num_programs(0) - 1)
    def _():
        feed_out[...] = feed_sum[...].astype(jnp.bfloat16)
        d_x_out[...] = d_x_sum[...].astype(jnp.bfloat16)


def feed_forward(x, d_out, gate_weight, up_weight, down_weight):
    length, width = x.shape
    units = gate_weight.shape[1]
    tile = 256 if units % 256 == 0 else units
    whole = pl.BlockSpec((length, width), lambda f: (0, 0))
    column = pl.BlockSpec((width, tile), lambda f: (0, f))
    return pl.pallas_call(
        feed_kernel,
        grid=(units // tile,),
        in_specs=[whole, whole, column, column, pl.BlockSpec((tile, width), lambda f: (f, 0))],
        out_specs=[whole, whole, pl.BlockSpec((3, tile, length), lambda f: (0, f, 0))],
        out_shape=[b16(length, width), b16(length, width), b16(3, units, length)],
        scratch_shapes=[pltpu.VMEM((length, width), jnp.float32)] * 2,
        compiler_params=pltpu.CompilerParams(vmem_limit_bytes=40 * 1024 * 1024),
        cost_estimate=pl.CostEstimate(
            flops=12 * length * width * units,
            bytes_accessed=6 * width * units,
            transcendentals=length * units,
        ),
    )(x, d_out, gate_weight, up_weight, down_weight)


MESH = pl.DeviceIdType.MESH


def partner(own, by):
    other = own
    bit = 1
    while bit <= by:
        if by & bit:
            other = other + bit - 2 * bit * ((own // bit) % 2)
        bit *= 2
    return other


def place(name, index):
    return {name: index}


def meet(devices):
    barrier = pltpu.get_barrier_semaphore()
    for device in devices:
        pl.semaphore_signal(barrier, inc=1, device_id=device, device_id_type=MESH)
    pl.semaphore_wait(barrier, len(devices))


def exchange_kernel(ways, kinds, *refs):
    count = len(kinds)
    sources, outs = refs[:count], refs[-4 - count : -4]
    sends, receives, hand_sends, hand_receives = refs[-4:]
    own = lax.axis_index("dp")
    core = lax.axis_index("head")
    peers = [partner(own, by) for by in range(1, ways)]
    other_core = place("head", 1 - core)
    shared = any(kind[0] == "halves" for kind in kinds)
    meet([place("dp", peer) for peer in peers] + ([other_core] if shared else []))
    copies, halves = [], []
    for index, (kind, source, out) in enumerate(zip(kinds, sources, outs)):
        for by in range(1, ways):
            peer = peers[by - 1]
            if kind[0] == "rows":
                src = source.at[kind[1] : kind[2], peer]
                dst = out.at[by - 1]
            elif kind[0] == "columns":
                width = source.shape[1] // ways
                src = source.at[:, pl.ds(pl.multiple_of(peer * width, width), width)]
                dst = out.at[by - 1]
            else:
                width = source.shape[1] // 2
                mine = pl.ds(pl.multiple_of(core * width, width), width)
                src = source.at[:, mine]
                dst = out.at[by - 1, :, mine]
            copy = pltpu.make_async_remote_copy(
                src_ref=src,
                dst_ref=dst,
                send_sem=sends.at[index * (ways - 1) + by - 1],
                recv_sem=receives.at[index * (ways - 1) + by - 1],
                device_id=place("dp", peer),
                device_id_type=MESH,
            )
            copy.start()
            copies.append(copy)
            if kind[0] == "halves":
                halves.append((index, by, copy, dst))
    handed = []
    for index, by, copy, dst in halves:
        copy.wait_recv()
        hand = pltpu.make_async_remote_copy(
            src_ref=dst,
            dst_ref=dst,
            send_sem=hand_sends.at[index * (ways - 1) + by - 1],
            recv_sem=hand_receives.at[index * (ways - 1) + by - 1],
            device_id=other_core,
            device_id_type=MESH,
        )
        hand.start()
        handed.append(hand)
    first_hops = [copy for _, _, copy, _ in halves]
    for copy in copies:
        copy.wait_send()
        if not any(copy is first for first in first_hops):
            copy.wait_recv()
    for hand in handed:
        hand.wait()


def plane_exchange(sources, kinds, tokens, number):
    ways = lax.axis_size("dp")
    shapes = []
    for source, kind in zip(sources, kinds):
        if kind[0] == "rows":
            shape = (ways - 1, kind[2] - kind[1]) + source.shape[2:]
        elif kind[0] == "columns":
            shape = (ways - 1, source.shape[0], source.shape[1] // ways)
        else:
            shape = (ways - 1,) + source.shape
        shapes.append(b16(*shape))
    anywhere = pl.BlockSpec(memory_space=pl.ANY)
    sems = pltpu.SemaphoreType.DMA((len(sources) * (ways - 1),))
    return pl.pallas_call(
        functools.partial(exchange_kernel, ways, kinds),
        out_shape=shapes,
        in_specs=[anywhere] * (len(sources) + len(tokens)),
        out_specs=[anywhere] * len(sources),
        scratch_shapes=[sems] * 4,
        compiler_params=pltpu.CompilerParams(collective_id=number, has_side_effects=True),
        cost_estimate=pl.CostEstimate(
            flops=0, bytes_accessed=40 * sum(s.size for s in shapes), transcendentals=0
        ),
    )(*sources, *tokens)


def chain_kernel(spans, reverse, ends, shifts, out, arriving, leaving, sends, receives):
    position = lax.axis_index("seq")
    heads = out.shape[0]
    step = -1 if reverse else 1
    first, last = (spans - 1, 0) if reverse else (0, spans - 1)
    meet([place("seq", (position + spans - 1) % spans), place("seq", (position + 1) % spans)])

    def copy_of(head):
        return pltpu.make_async_remote_copy(
            src_ref=leaving.at[head],
            dst_ref=arriving.at[head],
            send_sem=sends.at[head],
            recv_sem=receives.at[head],
            device_id=place("seq", position + step),
            device_id_type=MESH,
        )

    for head in range(heads):

        @pl.when(position == first)
        def _():
            out[head] = jnp.zeros_like(out[head])
            leaving[head] = shifts[head].astype(jnp.bfloat16)

        @pl.when(position != first)
        def _():
            copy_of(head).wait_recv()
            out[head] = arriving[head]

            @pl.when(position != last)
            def _():
                dims = (0, 0) if reverse else (1, 0)
                moved = dot_left(ends[head, :, :HEAD_DIM], arriving[head], dims)
                leaving[head] = (moved + shifts[head]).astype(jnp.bfloat16)

        @pl.when(position != last)
        def _():
            copy_of(head).start()

    @pl.when(position != last)
    def _():
        for head in range(heads):
            copy_of(head).wait_send()


def chained_states(ends, shifts, reverse, number):
    heads = ends.shape[0]
    state = (heads, HEAD_DIM, HEAD_DIM)
    inside = pl.BlockSpec(memory_space=pltpu.VMEM)
    return pl.pallas_call(
        functools.partial(chain_kernel, lax.axis_size("seq"), reverse),
        out_shape=b16(*state),
        in_specs=[inside] * 2,
        out_specs=inside,
        scratch_shapes=[
            pltpu.VMEM(state, jnp.bfloat16),
            pltpu.VMEM(state, jnp.bfloat16),
            pltpu.SemaphoreType.DMA((heads,)),
            pltpu.SemaphoreType.DMA((heads,)),
        ],
        compiler_params=pltpu.CompilerParams(collective_id=number, has_side_effects=True),
        cost_estimate=pl.CostEstimate(
            flops=0, bytes_accessed=40 * heads * HEAD_DIM * HEAD_DIM * 16, transcendentals=0
        ),
    )(ends, shifts)


def pieces_kernel(slots, ways, turned, at, *refs):
    lefts = refs[:slots]
    rights = refs[slots : slots + slots * ways]
    out, left_all, right_all = refs[slots + slots * ways + 1 :]
    length = rights[0].shape[0]
    rows = rights[0].shape[1]

    @pl.when(pl.program_id(0) == 0)
    def _():
        for slot in range(slots):
            span = slice(slot * length, (slot + 1) * length)
            block = lefts[slot][...]
            block = block.reshape((-1,) + block.shape[-2:])
            count = left_all.shape[0] // block.shape[0]
            for part in range(block.shape[0]):
                left_all[part * count : (part + 1) * count, span] = (
                    block[part] if turned else block[part].T
                )

    for slot in range(slots):
        for way in range(ways):
            right = rights[slot * ways + way][...]
            right_all[
                slot * length : (slot + 1) * length, way * rows : (way + 1) * rows
            ] = right.reshape(right.shape[-2:])
    out[0] = dot_low(left_all[...], right_all[...]).astype(jnp.bfloat16)


def span_pieces(lefts, count, rights, length, width, spans, turned, token):
    slots = len(lefts)
    ways = lax.axis_size("dp")
    rows = width // (ways * spans)

    def left_block(block, at_place):
        return pl.BlockSpec(block, lambda s, at: at_place(at[0]))

    def right_block(block, at_place, way):
        return pl.BlockSpec(
            block + (rows,), lambda s, at: tuple(at_place(at[0])) + (way * spans + s,)
        )

    return pl.pallas_call(
        functools.partial(pieces_kernel, slots, ways, turned),
        grid_spec=pltpu.PrefetchScalarGridSpec(
            num_scalar_prefetch=1,
            grid=(spans,),
            in_specs=[left_block(block, where) for _, block, where in lefts]
            + [right_block(block, where, way) for _, block, where in rights for way in range(ways)]
            + [pl.BlockSpec(memory_space=pl.ANY)],
            out_specs=pl.BlockSpec((1, count, ways * rows), lambda s, at: (s, 0, 0)),
            scratch_shapes=[
                pltpu.VMEM((count, slots * length), jnp.bfloat16),
                pltpu.VMEM((slots * length, ways * rows), jnp.bfloat16),
            ],
        ),
        out_shape=b16(spans, count, ways * rows),
        compiler_params=pltpu.CompilerParams(vmem_limit_bytes=32 * 1024 * 1024),
        cost_estimate=pl.CostEstimate(
            flops=2 * count * width * slots * length,
            bytes_accessed=4 * slots * length * width,
            transcendentals=0,
        ),
    )(
        lax.axis_index("dp")[None],
        *[array for array, _, _ in lefts],
        *[array for array, _, _ in rights for _ in range(ways)],
        token,
    )


def shards(
    tokens_in,
    lengths,
    first_gain,
    query_weight,
    key_weight,
    value_weight,
    beta_weight,
    query_conv,
    key_conv,
    value_conv,
    mixer_gain,
    output_weight,
    second_gain,
    gate_weight,
    up_weight,
    down_weight,
    upstream,
):
    num_rows, local_len, local_width = tokens_in.shape
    full_width = query_weight.shape[0]
    channels = query_weight.shape[1]
    local_heads = beta_weight.shape[1]
    groups = lax.axis_size("head")
    ways = lax.axis_size("dp")
    spans = lax.axis_size("seq")
    positions = lax.axis_index("seq") * local_len + jnp.arange(local_len, dtype=jnp.int32)
    live_mask = (positions[None, :] < lengths[:, None]).astype(jnp.float32)
    masked_up = upstream * live_mask[..., None].astype(jnp.bfloat16)
    gains = jnp.stack([first_gain, second_gain] + [first_gain] * 14)
    everything = gather_head(jnp.concatenate([tokens_in[0], masked_up[0], gains], 0), 1)
    gathered = everything[None, :local_len]
    upstream_full = everything[None, local_len : 2 * local_len]
    gain_one = everything[2 * local_len].astype(jnp.float32)
    gain_two = everything[2 * local_len + 1].astype(jnp.float32)
    stream_full = gathered.astype(jnp.float32)
    scale_one = inverse_rms(stream_full)
    normed_one = (stream_full * scale_one * gain_one).astype(jnp.bfloat16)

    def scattered(pieces):
        return lax.psum_scatter(pieces, "seq", scatter_dimension=0, tiled=False)

    def to_owner(piece):
        c = piece.shape[0]
        blocks = piece.reshape(c, ways, -1).transpose(1, 0, 2)
        return jnp.stack(in_order(exchanged(blocks, "dp"), "dp"), 0)

    if groups == 2:
        half_up = lax.all_gather(masked_up[0], "dp", axis=0, tiled=True)
        half_one = lax.all_gather(own_half(normed_one[0], local_width), "dp", axis=0, tiled=True)
        tokens_up = gather_head(half_up, 1)
        tokens_one = gather_head(half_one, 1)
    else:
        tokens_up = jnp.stack(spread(upstream_full[0], "dp")[1:])
        tokens_one = jnp.stack(spread(normed_one[0], "dp")[1:])
    per_step = 2 if local_heads % 2 == 0 else 1
    pres = [
        jnp.dot(normed_one[0], weight, preferred_element_type=jnp.float32).astype(jnp.bfloat16)
        for weight in (query_weight, key_weight, value_weight)
    ]
    beta_logit = jnp.dot(normed_one[0], beta_weight, preferred_element_type=jnp.float32)
    rims = passed_along(jnp.stack([pre[local_len - RIM :, :] for pre in pres]), "seq", 1)
    rims = [rims[0], rims[1], rims[2]]
    convs = [query_conv, key_conv, value_conv]
    live_col = live_mask[0][:, None]
    query, key, value, wy, inverse, mix, ends = mixer_local(
        pres, rims, convs, beta_logit, live_col, per_step
    )
    fused = groups == 2
    if fused:
        entering = chained_states(ends, ends[:, :, HEAD_DIM:], False, 1)
    else:
        entering = chain_state(ends[:, :, :HEAD_DIM], ends[:, :, HEAD_DIM:], False)
    head_gain = mixer_gain.astype(jnp.float32)[None, :]
    mixed, head_out = mixer_finish(
        mix, entering, head_gain, half_up if fused else entering, per_step
    )
    head_out = head_out[None]
    mixer_part = jnp.dot(head_out, output_weight, preferred_element_type=jnp.float32)
    stream_mid = stream_full + sum_head(mixer_part)
    scale_two = inverse_rms(stream_mid)
    normed_two = (stream_mid * scale_two * gain_two).astype(jnp.bfloat16)
    feed_part, d_two_part, turned = feed_forward(
        normed_two[0], upstream_full[0], gate_weight, up_weight, down_weight
    )
    layer_out = own_half(stream_mid + sum_head(feed_part[None]), local_width).astype(jnp.bfloat16)
    units = turned.shape[1] // ways
    turned = turned.reshape(3, ways, units, local_len)

    def piece(lefts, count, rights, is_turned, token):
        return scattered(
            span_pieces(
                lefts, count, rights, local_len, full_width, spans, is_turned, token
            )
        )

    def slots_of(own, others):
        return [(own, (local_len,), lambda at: (0,))] + [
            (others, (1, local_len), lambda at, by=by: (by, 0)) for by in range(ways - 1)
        ]

    def by_position(array):
        return [(array, (local_len,), lambda at, by=by: (at ^ by,)) for by in range(ways)]

    def feed_slots(which, others, index):
        own = [(turned, (1, 1, units, local_len), lambda at: (which, at, 0, 0))]
        return own + [
            (others, (1, 1, units, local_len), lambda at, by=by: (by, index, 0, 0))
            for by in range(ways - 1)
        ]

    normed_full = normed_two[0]
    if fused:
        (hidden_others,) = plane_exchange([turned], [("rows", 0, 1)], [half_one], 2)
        down_raw = span_pieces(
            feed_slots(0, hidden_others, 0), units, by_position(tokens_up),
            local_len, full_width, spans, True, feed_part,
        )
        d_others, two_others = plane_exchange(
            [turned, normed_full], [("rows", 1, 3), ("halves",)], [down_raw], 3
        )
    else:
        hidden_others = jnp.stack(exchanged(turned[:1].transpose(1, 0, 2, 3), "dp")[1:])
        down_raw = span_pieces(
            feed_slots(0, hidden_others, 0), units, slots_of(upstream_full[0], tokens_up),
            local_len, full_width, spans, True, feed_part,
        )
        d_others = jnp.stack(exchanged(turned[1:].transpose(1, 0, 2, 3), "dp")[1:])
        two_others = jnp.stack(spread(normed_full, "dp")[1:])
    down_piece = scattered(down_raw)
    two_slots = slots_of(normed_full, two_others)
    gate_piece = piece(feed_slots(1, d_others, 0), units, two_slots, True, down_piece)
    up_raw = span_pieces(
        feed_slots(2, d_others, 1), units, two_slots,
        local_len, full_width, spans, True, feed_part,
    )
    up_piece = scattered(up_raw)
    d_two = sum_head(d_two_part[None])
    d_stream = (
        upstream_full.astype(jnp.float32)
        + scale_two * gain_two * d_two
        - stream_mid
        * scale_two
        * scale_two
        * scale_two
        * (jnp.sum(d_two * gain_two * stream_mid, axis=-1, keepdims=True) / full_width)
    )
    grad_second = own_half(jnp.sum(d_two * stream_mid * scale_two, axis=(0, 1)), local_width)
    residual_full = d_stream.astype(jnp.bfloat16)
    d_head_out = jnp.einsum(
        "rsd,cd->rsc", residual_full, output_weight, preferred_element_type=jnp.float32
    )
    d_mixed, d_fresh, d_ends, grad_gain_part = mixer_back_local(
        d_head_out[0], mixed, head_gain, query, key, wy, up_raw, per_step
    )
    grad_gain_part = grad_gain_part[0]
    if fused:
        leaving = chained_states(ends, d_ends, True, 4)
    else:
        leaving = chain_state(jnp.swapaxes(ends[:, :, :HEAD_DIM], 1, 2), d_ends, True)
    *d_pres, tails, d_rims, grad_kernels, d_beta_logit = mixer_back(
        pres, rims, convs, beta_logit, live_col, query, key, value, wy, inverse,
        entering, d_mixed, d_fresh, leaving, per_step,
    )
    share_width = channels // ways
    residual = residual_full[0]
    if fused:
        out_others, res_others = plane_exchange(
            [head_out[0], residual], [("columns",), ("halves",)], [gate_piece], 5
        )
    else:
        out_others = jnp.stack(
            exchanged(head_out[0].reshape(local_len, ways, -1).transpose(1, 0, 2), "dp")[1:]
        )
        res_others = jnp.stack(spread(residual, "dp")[1:])

    def column_slots(own, others):
        if fused:
            first = [(own, (local_len, share_width), lambda at: (0, at))]
        else:
            mine = lax.dynamic_slice_in_dim(
                own, lax.axis_index("dp") * share_width, share_width, 1
            )
            first = [(mine, (local_len, share_width), lambda at: (0, 0))]
        return first + [
            (others, (1, local_len, share_width), lambda at, by=by: (by, 0, 0))
            for by in range(ways - 1)
        ]

    out_raw = span_pieces(
        column_slots(head_out[0], out_others), share_width, slots_of(residual, res_others),
        local_len, full_width, spans, False, d_rims,
    )
    out_piece = scattered(out_raw)
    tails = (tails + passed_along(d_rims, "seq", -1)).astype(jnp.bfloat16)
    d_pre_query, d_pre_key, d_pre_value = [
        jnp.concatenate([part[: local_len - 8], tail], 0)[None] for part, tail in zip(d_pres, tails)
    ]
    d_logit_low = d_beta_logit.astype(jnp.bfloat16)[None]
    d_normed_one = (
        jnp.einsum("rsc,dc->rsd", d_pre_query, query_weight, preferred_element_type=jnp.float32)
        + jnp.einsum("rsc,dc->rsd", d_pre_key, key_weight, preferred_element_type=jnp.float32)
        + jnp.einsum("rsc,dc->rsd", d_pre_value, value_weight, preferred_element_type=jnp.float32)
        + jnp.einsum("rsh,dh->rsd", d_logit_low, beta_weight, preferred_element_type=jnp.float32)
    )
    mix_sources = [d_pre_query[0], d_pre_key[0], d_pre_value[0]]
    if fused:
        mix_others = plane_exchange(mix_sources, [("columns",)] * 3, [up_piece, out_raw], 6)
        one_slots = by_position(tokens_one)
    else:
        mix_others = [
            jnp.stack(exchanged(part.reshape(local_len, ways, -1).transpose(1, 0, 2), "dp")[1:])
            for part in mix_sources
        ]
        one_slots = slots_of(normed_one[0], tokens_one)
    mix_raw = jnp.concatenate(
        [
            span_pieces(
                column_slots(own, others), share_width, one_slots,
                local_len, full_width, spans, False, d_rims,
            )
            for own, others in zip(mix_sources, mix_others)
        ],
        1,
    )
    mix_piece = scattered(mix_raw)
    grad_beta_part = jnp.einsum(
        "rsd,rsh->dh", normed_one, d_logit_low, preferred_element_type=jnp.float32
    )
    d_one = sum_head(d_normed_one)
    grad_tokens = own_half(
        d_stream
        + scale_one * gain_one * d_one
        - stream_full
        * scale_one
        * scale_one
        * scale_one
        * (jnp.sum(d_one * gain_one * stream_full, axis=-1, keepdims=True) / full_width),
        local_width,
    )
    grad_first = own_half(jnp.sum(d_one * stream_full * scale_one, axis=(0, 1)), local_width)
    small = [grad_first, grad_second, grad_kernels.reshape(-1), grad_beta_part.reshape(-1)]
    total = sum_doubling(jnp.concatenate(small + [grad_gain_part]), ("dp", "seq"))
    gain_total = sum_doubling(total[-HEAD_DIM:], ("head",))
    grad_first = total[:local_width]
    grad_second = total[local_width : 2 * local_width]
    kernel_end = 2 * local_width + grad_kernels.size
    kernel_sum = total[2 * local_width : kernel_end].reshape(grad_kernels.shape)
    share = lax.axis_index("dp") * spans + lax.axis_index("seq")
    rows = full_width // (ways * spans)
    grad_beta = lax.dynamic_slice_in_dim(
        total[kernel_end:-HEAD_DIM].reshape(full_width, local_heads), share * rows, rows, 0
    )
    feed = to_owner(jnp.concatenate([down_piece, gate_piece, up_piece], 0)).astype(jnp.float32)
    down, gate, up = [
        feed[:, place * units : (place + 1) * units].reshape(-1, rows) for place in range(3)
    ]
    out = to_owner(out_piece).reshape(-1, rows).astype(jnp.float32)
    mix = to_owner(mix_piece).astype(jnp.float32)
    third = mix.shape[1] // 3
    return (
        layer_out,
        grad_tokens,
        grad_first,
        mix[:, :third].reshape(-1, rows).T,
        mix[:, third : 2 * third].reshape(-1, rows).T,
        mix[:, 2 * third :].reshape(-1, rows).T,
        grad_beta,
        kernel_sum[0],
        kernel_sum[1],
        kernel_sum[2],
        gain_total,
        out,
        grad_second,
        gate.T,
        up.T,
        down,
    )


def solution(mesh):
    placed = (
        P("dp", "seq", "head"),
        P("dp"),
        P("head"),
        P(None, "head"),
        P(None, "head"),
        P(None, "head"),
        P(None, "head"),
        P(None, "head"),
        P(None, "head"),
        P(None, "head"),
        P(),
        P("head", None),
        P("head"),
        P(None, "head"),
        P(None, "head"),
        P("head", None),
        P("dp", "seq", "head"),
    )
    return jax.shard_map(
        shards,
        mesh=mesh,
        in_specs=placed,
        out_specs=(
            P("dp", "seq", "head"),
            P("dp", "seq", "head"),
            P("head"),
            P(("dp", "seq"), "head"),
            P(("dp", "seq"), "head"),
            P(("dp", "seq"), "head"),
            P(("dp", "seq"), "head"),
            P(None, "head"),
            P(None, "head"),
            P(None, "head"),
            P(),
            P("head", ("dp", "seq")),
            P("head"),
            P(("dp", "seq"), "head"),
            P(("dp", "seq"), "head"),
            P("head", ("dp", "seq")),
        ),
        check_vma=False,
    )
```

```python
import functools

import jax
import jax.numpy as jnp
from jax import lax
from jax.experimental import pallas as pl
from jax.experimental.pallas import tpu as pltpu
from jax.sharding import PartitionSpec as P

HEAD_DIM = 128


HIGH = lax.Precision.HIGHEST
EPSILON = 1e-05
UNIT_EPSILON = 1e-06
VMEM = 56 * 1024 * 1024
SHORT = pl.CostEstimate(flops=0, bytes_accessed=0, transcendentals=0)


def passed_along(value, axis, by):
    peers = lax.axis_size(axis)
    pairs = [(i, i + by) for i in range(peers) if 0 <= i + by < peers]
    return lax.ppermute(value, axis, pairs)


def swap_pairs(axis, by):
    peers = lax.axis_size(axis)
    return [(i, i ^ by) for i in range(peers)]


def exchanged(values, axis):
    peers = lax.axis_size(axis)
    own = lax.axis_index(axis)
    parts = [lax.dynamic_index_in_dim(values, own, 0, keepdims=False)]
    for by in range(1, peers):
        out = lax.dynamic_index_in_dim(values, own ^ by, 0, keepdims=False)
        parts.append(lax.ppermute(out, axis, swap_pairs(axis, by)))
    return parts


def spread(value, axis):
    peers = lax.axis_size(axis)
    return [value] + [
        lax.ppermute(value, axis, swap_pairs(axis, by)) for by in range(1, peers)
    ]


def in_order(parts, axis):
    stacked = jnp.stack(parts, 0)
    own = lax.axis_index(axis)
    return [
        lax.dynamic_index_in_dim(stacked, own ^ k, 0, keepdims=False) for k in range(len(parts))
    ]


def gather_head(value, axis):
    if lax.axis_size("head") == 2:
        other = lax.ppermute(value, "head", [(0, 1), (1, 0)])
        first = lax.axis_index("head") == 0
        return jnp.concatenate(
            [jnp.where(first, value, other), jnp.where(first, other, value)], axis
        )
    return lax.all_gather(value, "head", axis=axis, tiled=True)


def sum_head(value):
    low = value.astype(jnp.bfloat16)
    if lax.axis_size("head") == 2:
        other = lax.ppermute(low, "head", [(0, 1), (1, 0)])
        return low.astype(jnp.float32) + other.astype(jnp.float32)
    return lax.psum(low, "head").astype(jnp.float32)


def sum_doubling(value, axes):
    for axis in axes:
        by = 1
        while by < lax.axis_size(axis):
            value = value + lax.ppermute(value, axis, swap_pairs(axis, by))
            by *= 2
    return value


def own_half(value, width):
    return lax.dynamic_slice_in_dim(value, lax.axis_index("head") * width, width, value.ndim - 1)


def chain_state(maps, shifts, reverse):
    peers = lax.axis_size("seq")
    by = -1 if reverse else 1
    states = [passed_along(shifts.astype(jnp.bfloat16), "seq", by)]
    for step in range(peers - 2):
        out = (
            jnp.einsum("hij,hjk->hik", maps, states[-1].astype(jnp.float32), precision=HIGH)
            + shifts
        )
        states.append(passed_along(out.astype(jnp.bfloat16), "seq", by))
    return states[-1]


def inverse_rms(values):
    return lax.rsqrt(jnp.mean(values * values, axis=-1, keepdims=True) + EPSILON)


MESH = pl.DeviceIdType.MESH


def partner(own, by):
    other = own
    bit = 1
    while bit <= by:
        if by & bit:
            other = other + bit - 2 * bit * ((own // bit) % 2)
        bit *= 2
    return other


def place(name, index):
    return {name: index}


def meet(devices):
    barrier = pltpu.get_barrier_semaphore()
    for device in devices:
        pl.semaphore_signal(barrier, inc=1, device_id=device, device_id_type=MESH)
    pl.semaphore_wait(barrier, len(devices))


class Halves:
    def __init__(self, ways, source, out, sends, receives, hand_sends, hand_receives):
        own = lax.axis_index("dp")
        core = lax.axis_index("head")
        width = source.shape[1] // 2
        mine = pl.ds(pl.multiple_of(core * width, width), width)
        self.peers = [place("dp", partner(own, by)) for by in range(1, ways)]
        self.other = place("head", 1 - core)
        self.first = [
            pltpu.make_async_remote_copy(
                src_ref=source.at[:, mine],
                dst_ref=out.at[slot, :, mine],
                send_sem=sends.at[slot],
                recv_sem=receives.at[slot],
                device_id=peer,
                device_id_type=MESH,
            )
            for slot, peer in enumerate(self.peers)
        ]
        self.second = [
            pltpu.make_async_remote_copy(
                src_ref=out.at[slot, :, mine],
                dst_ref=out.at[slot, :, mine],
                send_sem=hand_sends.at[slot],
                recv_sem=hand_receives.at[slot],
                device_id=self.other,
                device_id_type=MESH,
            )
            for slot in range(ways - 1)
        ]

    def devices(self):
        return self.peers + [self.other]

    def start(self):
        for copy in self.first:
            copy.start()

    def hand_on(self):
        for copy, hand in zip(self.first, self.second):
            copy.wait_recv()
            hand.start()

    def finish(self):
        for copy, hand in zip(self.first, self.second):
            copy.wait_send()
            hand.wait()


def column_copies(ways, source, out, sends, receives):
    own = lax.axis_index("dp")
    width = source.shape[1] // ways
    copies = []
    for by in range(1, ways):
        peer = partner(own, by)
        copies.append(
            pltpu.make_async_remote_copy(
                src_ref=source.at[:, pl.ds(pl.multiple_of(peer * width, width), width)],
                dst_ref=out.at[by - 1],
                send_sem=sends.at[by - 1],
                recv_sem=receives.at[by - 1],
                device_id=place("dp", peer),
                device_id_type=MESH,
            )
        )
    return copies


def exchange_kernel(ways, kinds, *refs):
    count = len(kinds)
    sources, outs = refs[:count], refs[-6 - count : -6]
    sends, receives = refs[-6:-4]
    own = lax.axis_index("dp")
    shared = kinds[-1][0] == "halves"
    peers = [partner(own, by) for by in range(1, ways)]
    halves = Halves(ways, sources[-1], outs[-1], *refs[-4:]) if shared else None
    meet(halves.devices() if shared else [place("dp", peer) for peer in peers])
    if shared:
        halves.start()
    copies = []
    for index, (kind, source, out) in enumerate(zip(kinds, sources, outs)):
        if kind[0] == "halves":
            continue
        for by in range(1, ways):
            peer = peers[by - 1]
            if kind[0] == "rows":
                src = source.at[kind[1] : kind[2], peer]
            else:
                width = source.shape[1] // ways
                src = source.at[:, pl.ds(pl.multiple_of(peer * width, width), width)]
            copy = pltpu.make_async_remote_copy(
                src_ref=src,
                dst_ref=out.at[by - 1],
                send_sem=sends.at[index * (ways - 1) + by - 1],
                recv_sem=receives.at[index * (ways - 1) + by - 1],
                device_id=place("dp", peer),
                device_id_type=MESH,
            )
            copy.start()
            copies.append(copy)
    if shared:
        halves.hand_on()
    for copy in copies:
        copy.wait()
    if shared:
        halves.finish()


def plane_exchange(sources, kinds, tokens, number):
    ways = lax.axis_size("dp")
    shapes = []
    for source, kind in zip(sources, kinds):
        if kind[0] == "rows":
            shape = (ways - 1, kind[2] - kind[1]) + source.shape[2:]
        elif kind[0] == "columns":
            shape = (ways - 1, source.shape[0], source.shape[1] // ways)
        else:
            shape = (ways - 1,) + source.shape
        shapes.append(b16(*shape))
    anywhere = pl.BlockSpec(memory_space=pl.ANY)
    sems = pltpu.SemaphoreType.DMA((len(sources) * (ways - 1),))
    hand_sems = pltpu.SemaphoreType.DMA((ways - 1,))
    return pl.pallas_call(
        functools.partial(exchange_kernel, ways, kinds),
        out_shape=shapes,
        in_specs=[anywhere] * (len(sources) + len(tokens)),
        out_specs=[anywhere] * len(sources),
        scratch_shapes=[sems] * 2 + [hand_sems] * 4,
        compiler_params=pltpu.CompilerParams(
            collective_id=number, has_side_effects=True, vmem_limit_bytes=VMEM
        ),
        cost_estimate=SHORT,
    )(*sources, *tokens)


def halves(a):
    top = a.astype(jnp.bfloat16)
    return top, (a - top.astype(jnp.float32)).astype(jnp.bfloat16)


def dot_low(a, b, dims=(1, 0)):
    return lax.dot_general(
        a, b, (((dims[0],), (dims[1],)), ((), ())), preferred_element_type=jnp.float32
    )


def dot_left(a, b, dims=(1, 0)):
    top, rest = halves(a)
    return dot_low(top, b, dims) + dot_low(rest, b, dims)


def dot_right(a, b, dims=(1, 0)):
    top, rest = halves(b)
    return dot_low(a, top, dims) + dot_low(a, rest, dims)


def dot_both(a, b, dims=(1, 0)):
    a_top, a_rest = halves(a)
    b_top, b_rest = halves(b)
    return dot_low(a_top, b_top, dims) + (
        dot_low(a_top, b_rest, dims) + dot_low(a_rest, b_top, dims)
    )


def grid_marks(size):
    row = lax.broadcasted_iota(jnp.int32, (size, size), 0)
    col = lax.broadcasted_iota(jnp.int32, (size, size), 1)
    return row, col


def unit_lower_inverses(tiles):
    size = tiles[0].shape[0]
    row, col = grid_marks(size)
    unit = (row == col).astype(jnp.float32)
    base = 8
    near = (row // base == col // base) & (row > col)
    cores = [jnp.where(near, tile, 0.0) for tile in tiles]
    squares = [dot_both(core, core) for core in cores]
    fourths = [dot_both(square, square) for square in squares]
    found = [dot_both(unit - core, unit + square) for core, square in zip(cores, squares)]
    found = [dot_both(part, unit + fourth) for part, fourth in zip(found, fourths)]
    while base < size:
        wide = 2 * base
        near = (row // wide == col // wide) & (row // base > col // base)
        links = [jnp.where(near, tile, 0.0) for tile in tiles]
        steps = [dot_both(part, link) for part, link in zip(found, links)]
        found = [part - dot_both(step, part) for part, step in zip(found, steps)]
        base = wide
    return found


def lower_inverses(systems, tile):
    size = systems[0].shape[0]
    if size <= tile:
        return unit_lower_inverses(systems)
    half = size // 2
    diagonals = [s[:half, :half] for s in systems] + [s[half:, half:] for s in systems]
    found = lower_inverses(diagonals, tile)
    firsts, seconds = found[: len(systems)], found[len(systems) :]
    steps = [dot_both(second, s[half:, :half]) for second, s in zip(seconds, systems)]
    corners = [-dot_both(step, first) for step, first in zip(steps, firsts)]
    empty = jnp.zeros((half, half), jnp.float32)
    return [
        jnp.concatenate(
            [jnp.concatenate([first, empty], 1), jnp.concatenate([corner, second], 1)], 0
        )
        for first, corner, second in zip(firsts, corners, seconds)
    ]


RIM = 16


def conv_sum(ext, pre, rim, weights, taps, length):
    ext[:RIM, :] = rim.astype(jnp.float32)
    ext[RIM : RIM + length, :] = pre.astype(jnp.float32)
    first = RIM - taps + 1
    summed = weights[0:1, :] * ext[first : first + length, :]
    for tap in range(1, taps):
        summed = summed + weights[tap : tap + 1, :] * ext[first + tap : first + tap + length, :]
    return summed


def head_columns(refs, index):
    span = slice(index * HEAD_DIM, (index + 1) * HEAD_DIM)
    return [ref[:, span] for ref in refs]


def unit_scale(rows):
    return lax.rsqrt(jnp.sum(rows * rows, axis=-1, keepdims=True) + UNIT_EPSILON)


def column_of(values, index):
    lane = lax.broadcasted_iota(jnp.int32, values.shape, 1)
    return jnp.sum(jnp.where(lane == index, values, 0.0), axis=-1, keepdims=True)


def row_of(values, index):
    place = lax.broadcasted_iota(jnp.int32, values.shape, 0)
    return jnp.sum(jnp.where(place == index, values, 0.0), axis=0, keepdims=True)


def local_part(pres, rims, weights, logit, logit_t, live, live_t, ext, first, taps):
    length = live.shape[0]
    row, col = grid_marks(length)
    heads = range(pres[0].shape[1] // HEAD_DIM)
    queries, keys, values, systems, beta_rows = [], [], [], [], []
    for i in heads:
        span = slice(i * HEAD_DIM, (i + 1) * HEAD_DIM)
        active = []
        for pre, rim, weight in zip(pres, rims, weights):
            summed = conv_sum(
                ext, pre[:, span], rim[:, span], weight[:, span].astype(jnp.float32), taps, length
            )
            active.append(summed * jax.nn.sigmoid(summed))
        q, k, v = active
        q = (q * unit_scale(q)).astype(jnp.bfloat16)
        k = (k * unit_scale(k) * live).astype(jnp.bfloat16)
        v = v.astype(jnp.bfloat16)
        beta = jax.nn.sigmoid(column_of(logit, first + i)) * live
        beta_rows.append(jax.nn.sigmoid(row_of(logit_t, first + i)) * live_t)
        gram = dot_low(k, k, (1, 1))
        systems.append(jnp.where(row > col, beta * gram, 0.0))
        queries.append(q)
        keys.append(k)
        values.append(v)
    inverses = lower_inverses(systems, 128)
    wys = [
        dot_left(inverse * beta_row, jnp.concatenate([k, v], 1))
        for inverse, beta_row, k, v in zip(inverses, beta_rows, keys, values)
    ]
    wide = (HEAD_DIM, 2 * HEAD_DIM)
    place = lax.broadcasted_iota(jnp.int32, wide, 1)
    unit = (lax.broadcasted_iota(jnp.int32, wide, 0) == place).astype(jnp.float32)
    found = []
    for i in heads:
        ends = dot_right(keys[i], wys[i], (0, 0))
        ends = unit + jnp.where(place < HEAD_DIM, -ends, ends)
        scores = jnp.where(row >= col, dot_low(queries[i], keys[i], (1, 1)), 0.0)
        seen = dot_both(scores, wys[i])
        mix = jnp.concatenate(
            [queries[i].astype(jnp.float32) - seen[:, :HEAD_DIM], seen[:, HEAD_DIM:]], 1
        )
        found.append((queries[i], keys[i], values[i], wys[i], inverses[i], mix, ends))
    return found


def finish_part(mix, state, gain):
    mixed = mix[:, HEAD_DIM:] + dot_left(mix[:, :HEAD_DIM], state)
    scale = lax.rsqrt(jnp.mean(mixed * mixed, axis=-1, keepdims=True) + EPSILON)
    return mixed, (mixed * scale * gain).astype(jnp.bfloat16)


def back_local_part(d_out, mixed, gain, q, k, wy):
    row, col = grid_marks(q.shape[0])
    scale = lax.rsqrt(jnp.mean(mixed * mixed, axis=-1, keepdims=True) + EPSILON)
    weighted = gain * d_out
    inner = jnp.sum(weighted * mixed, axis=-1, keepdims=True)
    d_mixed = scale * weighted - mixed * (scale * scale * scale * inner / HEAD_DIM)
    gain_row = jnp.sum(d_out * mixed * scale, axis=0, keepdims=True)
    scores_t = jnp.where(col >= row, dot_low(k, q, (1, 1)), 0.0)
    d_fresh = dot_both(scores_t, d_mixed)
    d_end = dot_right(q, d_mixed, (0, 0)) - dot_both(wy[:, :HEAD_DIM], d_fresh, (0, 0))
    return d_mixed, d_fresh, d_end, gain_row


def back_part(q, k, v, wy, inverse, entering, leaving, d_mixed, d_fresh, logit, live):
    row, col = grid_marks(q.shape[0])
    d_fresh = d_fresh + dot_low(k, leaving)
    fresh = wy[:, HEAD_DIM:] - dot_left(wy[:, :HEAD_DIM], entering)
    d_scores = jnp.where(row >= col, dot_both(d_mixed, fresh, (1, 1)), 0.0)
    d_q = dot_left(d_mixed, entering, (1, 1)) + dot_left(d_scores, k)
    d_k = dot_left(d_scores, q, (0, 0)) + dot_left(fresh, leaving, (1, 1))
    d_wy = jnp.concatenate([-dot_left(d_fresh, entering, (1, 1)), d_fresh], 1)
    d_rhs = dot_both(inverse, d_wy, (0, 0))
    edges = jnp.where(row > col, -dot_both(d_rhs, wy, (1, 1)), 0.0)
    sig = jax.nn.sigmoid(logit)
    beta = sig * live
    both = jnp.concatenate([k, v], 1).astype(jnp.float32)
    gram = dot_low(k, k, (1, 1))
    d_beta = jnp.sum(d_rhs * both, axis=-1, keepdims=True) + jnp.sum(
        edges * gram, axis=-1, keepdims=True
    )
    scaled = beta * edges
    d_k = d_k + beta * d_rhs[:, :HEAD_DIM] + dot_left(scaled, k) + dot_left(scaled, k, (0, 0))
    d_v = beta * d_rhs[:, HEAD_DIM:]
    d_logit = d_beta * live * sig * (1.0 - sig)
    return d_q, d_k * live, d_v, d_logit


def back_conv_part(part, pre, rim, weight, grad, taps, ext, ext_back):
    length = pre.shape[0]
    weight = weight.astype(jnp.float32)
    summed = conv_sum(ext, pre, rim, weight, taps, length)
    gate = jax.nn.sigmoid(summed)
    if part < 2:
        active = summed * gate
        scale = unit_scale(active)
        inner = jnp.sum(active * grad, axis=-1, keepdims=True)
        grad = scale * grad - active * (scale * scale * scale * inner)
    d_conv = grad * gate * (1.0 + summed * (1.0 - gate))
    first = RIM - taps + 1
    rows = [
        jnp.sum(d_conv * ext[first + tap : first + tap + length, :], axis=0, keepdims=True)
        for tap in range(taps)
    ]
    ext_back[:8, :] = jnp.zeros((8, HEAD_DIM), jnp.float32)
    ext_back[8 : 8 + length, :] = d_conv
    ext_back[8 + length :, :] = jnp.zeros((8, HEAD_DIM), jnp.float32)
    own = jnp.zeros((length, HEAD_DIM), jnp.float32)
    before = jnp.zeros((8, HEAD_DIM), jnp.float32)
    for tap in range(taps):
        shift = taps - 1 - tap
        own = own + weight[tap : tap + 1, :] * ext_back[8 + shift : 8 + shift + length, :]
        before = before + weight[tap : tap + 1, :] * ext_back[shift : shift + 8, :]
    return own, before, jnp.concatenate(rows, 0)


def mixer_local_kernel(per_step, taps, *refs):
    pres, rims, weights = refs[:3], refs[3:6], refs[6:9]
    logit, logit_t, live, live_t = refs[9:13]
    q_out, k_out, v_out, wy_out, inv_out, mix_out, end_out, ext = refs[13:]
    found = local_part(
        pres, rims, weights, logit[...], logit_t[...], live[...], live_t[...], ext,
        pl.program_id(0) * per_step, taps,
    )
    for i, (q, k, v, wy, inverse, mix, ends) in enumerate(found):
        span = slice(i * HEAD_DIM, (i + 1) * HEAD_DIM)
        q_out[:, span] = q
        k_out[:, span] = k
        v_out[:, span] = v
        wy_out[i] = wy
        inv_out[i] = inverse
        mix_out[i] = mix
        end_out[i] = ends


def mixer_finish_kernel(per_step, mix, state, gain, mixed_out, head_out):
    for i in range(per_step):
        span = slice(i * HEAD_DIM, (i + 1) * HEAD_DIM)
        mixed_out[:, span], head_out[:, span] = finish_part(mix[i], state[i], gain[...])


def mixer_back_local_kernel(
    per_step, d_head, mixed_ref, gain_ref, q_ref, k_ref, wy,
    d_mixed_out, d_fresh_out, end_out, gain_out,
):
    gain_total = jnp.zeros((1, HEAD_DIM), jnp.float32)
    for i in range(per_step):
        d_out, mixed, q, k = head_columns((d_head, mixed_ref, q_ref, k_ref), i)
        d_mixed_out[i], d_fresh_out[i], end_out[i], gain_row = back_local_part(
            d_out, mixed, gain_ref[...], q, k, wy[i]
        )
        gain_total += gain_row

    @pl.when(pl.program_id(0) == 0)
    def _():
        gain_out[...] = jnp.zeros_like(gain_out)

    gain_out[...] += jnp.broadcast_to(gain_total, gain_out.shape)


def mixer_back_kernel(per_step, taps, *refs):
    pre_refs, rim_refs, weight_refs, (logit, live) = refs[:3], refs[3:6], refs[6:9], refs[9:11]
    (q_ref, k_ref, v_ref, wy, inv, state, d_mixed_ref, d_fresh_ref, d_state) = refs[11:20]
    d_q_out, d_k_out, d_v_out, tail_out, rim_out, conv_out, d_logit_out, ext, ext_back = refs[20:]
    length = live.shape[0]
    step = pl.program_id(0)

    @pl.when(step == 0)
    def _():
        d_logit_out[...] = jnp.zeros_like(d_logit_out)

    for i in range(per_step):
        q, k, v = head_columns((q_ref, k_ref, v_ref), i)
        *grads, d_logit = back_part(
            q, k, v, wy[i], inv[i], state[i], d_state[i], d_mixed_ref[i], d_fresh_ref[i],
            column_of(logit[...], step * per_step + i), live[...],
        )
        lane = lax.broadcasted_iota(jnp.int32, d_logit_out.shape, 1)
        d_logit_out[...] += jnp.where(lane == step * per_step + i, d_logit, 0.0)
        span = slice(i * HEAD_DIM, (i + 1) * HEAD_DIM)
        outs = (d_q_out, d_k_out, d_v_out)
        for part in range(3):
            own, before, rows = back_conv_part(
                part, pre_refs[part][:, span], rim_refs[part][:, span],
                weight_refs[part][:, span], grads[part], taps, ext, ext_back,
            )
            conv_out[part, :, span] = rows
            outs[part][:, span] = own.astype(jnp.bfloat16)
            tail_out[part, :, span] = own[length - 8 :, :]
            rim_out[part, :, span] = before


def mixer_specs(length, heads, per_step):
    width = per_step * HEAD_DIM

    def flat(rows):
        return pl.BlockSpec((rows, width), lambda h: (0, h))

    def whole(*shape):
        return pl.BlockSpec(shape, lambda h: (0,) * len(shape))

    def by_head(*shape):
        return pl.BlockSpec((per_step,) + shape, lambda h: (h,) + (0,) * len(shape))

    return flat, whole, by_head


def mixer_call(kernel, heads, per_step, ins, outs, scratch, flops, args):
    moved = sum(a.size * a.dtype.itemsize for a in args)
    return pl.pallas_call(
        kernel,
        grid=(heads // per_step,),
        in_specs=ins,
        out_specs=[spec for spec, _ in outs],
        out_shape=[shape for _, shape in outs],
        scratch_shapes=scratch,
        compiler_params=pltpu.CompilerParams(vmem_limit_bytes=VMEM),
        cost_estimate=SHORT,
    )(*args)


def f32(*shape):
    return jax.ShapeDtypeStruct(shape, jnp.float32)


def b16(*shape):
    return jax.ShapeDtypeStruct(shape, jnp.bfloat16)


def mixer_local(pres, rims, convs, logit, live, per_step):
    length, channels = pres[0].shape
    heads = channels // HEAD_DIM
    taps = convs[0].shape[0]
    flat, whole, by_head = mixer_specs(length, heads, per_step)
    args = (*pres, *rims, *convs, logit, logit.T, live, live.T)
    return mixer_call(
        functools.partial(mixer_local_kernel, per_step, taps),
        heads,
        per_step,
        [flat(length)] * 3
        + [flat(RIM)] * 3
        + [flat(taps)] * 3
        + [whole(length, heads), whole(heads, length), whole(length, 1), whole(1, length)],
        [(flat(length), b16(length, channels))] * 3
        + [
            (by_head(length, 2 * HEAD_DIM), f32(heads, length, 2 * HEAD_DIM)),
            (by_head(length, length), f32(heads, length, length)),
            (by_head(length, 2 * HEAD_DIM), f32(heads, length, 2 * HEAD_DIM)),
            (by_head(HEAD_DIM, 2 * HEAD_DIM), f32(heads, HEAD_DIM, 2 * HEAD_DIM)),
        ],
        [pltpu.VMEM((RIM + length, HEAD_DIM), jnp.float32)],
        heads * 2 * length**3 * 30,
        args,
    )


def mixer_finish(mix, state, gain, per_step):
    heads, length, _ = mix.shape
    flat, whole, by_head = mixer_specs(length, heads, per_step)
    return mixer_call(
        functools.partial(mixer_finish_kernel, per_step),
        heads,
        per_step,
        [by_head(length, 2 * HEAD_DIM), by_head(HEAD_DIM, HEAD_DIM), whole(1, HEAD_DIM)],
        [
            (flat(length), f32(length, heads * HEAD_DIM)),
            (flat(length), b16(length, heads * HEAD_DIM)),
        ],
        [],
        heads * 2 * length**3,
        (mix, state, gain),
    )


def mixer_back_local(d_head, mixed, gain, q, k, wy, per_step):
    heads, length, _ = wy.shape
    flat, whole, by_head = mixer_specs(length, heads, per_step)
    return mixer_call(
        functools.partial(mixer_back_local_kernel, per_step),
        heads,
        per_step,
        [flat(length)] * 2 + [whole(1, HEAD_DIM)] + [flat(length)] * 2 + [by_head(length, 2 * HEAD_DIM)],
        [
            (by_head(length, HEAD_DIM), f32(heads, length, HEAD_DIM)),
            (by_head(length, HEAD_DIM), f32(heads, length, HEAD_DIM)),
            (by_head(HEAD_DIM, HEAD_DIM), f32(heads, HEAD_DIM, HEAD_DIM)),
            (whole(8, HEAD_DIM), f32(8, HEAD_DIM)),
        ],
        [],
        heads * 2 * length**3 * 5,
        (d_head, mixed, gain, q, k, wy),
    )


def mixer_back(pres, rims, convs, logit, live, q, k, v, wy, inv, state, d_mixed, d_fresh, d_state, per_step):
    length, channels = pres[0].shape
    heads = channels // HEAD_DIM
    taps = convs[0].shape[0]
    flat, whole, by_head = mixer_specs(length, heads, per_step)
    three = pl.BlockSpec((3, 8, per_step * HEAD_DIM), lambda h: (0, 0, h))
    return mixer_call(
        functools.partial(mixer_back_kernel, per_step, taps),
        heads,
        per_step,
        [flat(length)] * 3
        + [flat(RIM)] * 3
        + [flat(taps)] * 3
        + [whole(length, heads), whole(length, 1)]
        + [flat(length)] * 3
        + [
            by_head(length, 2 * HEAD_DIM),
            by_head(length, length),
            by_head(HEAD_DIM, HEAD_DIM),
            by_head(length, HEAD_DIM),
            by_head(length, HEAD_DIM),
            by_head(HEAD_DIM, HEAD_DIM),
        ],
        [(flat(length), b16(length, channels))] * 3
        + [
            (three, f32(3, 8, channels)),
            (three, f32(3, 8, channels)),
            (
                pl.BlockSpec((3, taps, per_step * HEAD_DIM), lambda h: (0, 0, h)),
                f32(3, taps, channels),
            ),
            (whole(length, heads), f32(length, heads)),
        ],
        [
            pltpu.VMEM((RIM + length, HEAD_DIM), jnp.float32),
            pltpu.VMEM((16 + length, HEAD_DIM), jnp.float32),
        ],
        heads * 2 * length**3 * 20,
        (*pres, *rims, *convs, logit, live, q, k, v, wy, inv, state, d_mixed, d_fresh, d_state),
    )


def mixer_forward_kernel(per_step, taps, spans, *refs):
    pres, weights = refs[:3], refs[3:6]
    logit, logit_t, live, live_t, gain = refs[6:11]
    sources = refs[11:14]
    q_out, k_out, v_out, wy_out, inv_out, end_out, mixed_out, head_out, state_out, rim_out = refs[
        14:24
    ]
    ext, mix_all, rims, arriving, leaving, sends, receives, rim_sends, rim_receives = refs[24:]
    step = pl.program_id(0)
    position = lax.axis_index("seq")
    pairs = arriving.shape[0]
    length = live.shape[0]
    width = per_step * HEAD_DIM
    last = spans - 1
    after = place("seq", position + 1)

    def rim_copy(part):
        return pltpu.make_async_remote_copy(
            src_ref=sources[part].at[length - RIM :, :],
            dst_ref=rims.at[part],
            send_sem=rim_sends.at[part],
            recv_sem=rim_receives.at[part],
            device_id=after,
            device_id_type=MESH,
        )

    def state_copy(pair):
        return pltpu.make_async_remote_copy(
            src_ref=leaving.at[pair],
            dst_ref=arriving.at[pair],
            send_sem=sends.at[pair],
            recv_sem=receives.at[pair],
            device_id=after,
            device_id_type=MESH,
        )

    @pl.when(step == 0)
    def _():
        meet([place("seq", (position + last) % spans), place("seq", (position + 1) % spans)])

        @pl.when(position != last)
        def _():
            for part in range(3):
                rim_copy(part).start()

        @pl.when(position == 0)
        def _():
            rims[...] = jnp.zeros_like(rims)
            arriving[...] = jnp.zeros_like(arriving)

        @pl.when(position != 0)
        def _():
            for part in range(3):
                rim_copy(part).wait_recv()

        rim_out[...] = rims[...]

    @pl.when(step < pairs)
    def _():
        here = pl.ds(pl.multiple_of(step * width, width), width)
        found = local_part(
            pres, [rims[part, :, here] for part in range(3)], weights, logit[...], logit_t[...],
            live[...], live_t[...], ext, step * per_step, taps,
        )
        for i, (q, k, v, wy, inverse, mix, ends) in enumerate(found):
            span = slice(i * HEAD_DIM, (i + 1) * HEAD_DIM)
            q_out[:, span] = q
            k_out[:, span] = k
            v_out[:, span] = v
            wy_out[i] = wy
            inv_out[i] = inverse
            mix_all[step * per_step + i] = mix
            end_out[step * per_step + i] = ends

    pair = step - position

    @pl.when((pair >= 0) & (pair < pairs))
    def _():
        @pl.when(position != 0)
        def _():
            state_copy(pair).wait_recv()

        for i in range(per_step):
            ends = end_out[pair * per_step + i]
            moved = dot_left(ends[:, :HEAD_DIM], arriving[pair, i])
            leaving[pair, i] = (moved + ends[:, HEAD_DIM:]).astype(jnp.bfloat16)

        @pl.when(position != last)
        def _():
            state_copy(pair).start()

        for i in range(per_step):
            here = pl.ds(pl.multiple_of(pair * width + i * HEAD_DIM, HEAD_DIM), HEAD_DIM)
            state = arriving[pair, i]
            state_out[pair * per_step + i] = state
            mixed, head = finish_part(mix_all[pair * per_step + i], state, gain[...])
            mixed_out[:, here] = mixed
            head_out[:, here] = head

    @pl.when((step == pl.num_programs(0) - 1) & (position != last))
    def _():
        for part in range(3):
            rim_copy(part).wait_send()
        for index in range(pairs):
            state_copy(index).wait_send()


def mixer_forward(pres, convs, logit, live, gain, per_step, spans, number):
    length, channels = pres[0].shape
    heads = channels // HEAD_DIM
    pairs = heads // per_step
    taps = convs[0].shape[0]
    width = per_step * HEAD_DIM
    wide = (heads, length, 2 * HEAD_DIM)
    states = (heads, HEAD_DIM, HEAD_DIM)

    def at(step):
        return jnp.minimum(step, pairs - 1)

    def flat(rows):
        return pl.BlockSpec((rows, width), lambda s: (0, at(s)))

    def by_head(*shape):
        return pl.BlockSpec((per_step,) + shape, lambda s: (at(s),) + (0,) * len(shape))

    def whole(*shape):
        return pl.BlockSpec(shape, lambda s: (0,) * len(shape))

    anywhere = pl.BlockSpec(memory_space=pl.ANY)
    return pl.pallas_call(
        functools.partial(mixer_forward_kernel, per_step, taps, spans),
        grid=(pairs + spans - 1,),
        in_specs=[flat(length)] * 3
        + [flat(taps)] * 3
        + [whole(length, heads), whole(heads, length), whole(length, 1), whole(1, length)]
        + [whole(1, HEAD_DIM)]
        + [anywhere] * 3,
        out_specs=[flat(length)] * 3
        + [
            by_head(length, 2 * HEAD_DIM),
            by_head(length, length),
            whole(heads, HEAD_DIM, 2 * HEAD_DIM),
            whole(length, channels),
            whole(length, channels),
            whole(*states),
            whole(3, RIM, channels),
        ],
        out_shape=[b16(length, channels)] * 3
        + [
            f32(*wide),
            f32(heads, length, length),
            f32(heads, HEAD_DIM, 2 * HEAD_DIM),
            f32(length, channels),
            b16(length, channels),
            b16(*states),
            b16(3, RIM, channels),
        ],
        scratch_shapes=[
            pltpu.VMEM((RIM + length, HEAD_DIM), jnp.float32),
            pltpu.VMEM(wide, jnp.float32),
            pltpu.VMEM((3, RIM, channels), jnp.bfloat16),
            pltpu.VMEM((pairs, per_step, HEAD_DIM, HEAD_DIM), jnp.bfloat16),
            pltpu.VMEM((pairs, per_step, HEAD_DIM, HEAD_DIM), jnp.bfloat16),
            pltpu.SemaphoreType.DMA((pairs,)),
            pltpu.SemaphoreType.DMA((pairs,)),
            pltpu.SemaphoreType.DMA((3,)),
            pltpu.SemaphoreType.DMA((3,)),
        ],
        compiler_params=pltpu.CompilerParams(
            collective_id=number, has_side_effects=True, vmem_limit_bytes=VMEM
        ),
        cost_estimate=SHORT,
    )(*pres, *convs, logit, logit.T, live, live.T, gain, *pres)


def mixer_backward_kernel(per_step, taps, spans, ways, tokens, *refs):
    d_head, mixed_ref, q_one, k_one, wy_one, gain = refs[:6]
    pres, weights = refs[6:9], refs[9:12]
    q_ref, k_ref, v_ref, wy, inv = refs[12:17]
    logit, live, state, ends, rims = refs[17:22]
    head_source, residual, normed = refs[22 + tokens : 25 + tokens]
    d_q_out, d_k_out, d_v_out, conv_out, d_logit_out, gain_out = refs[25 + tokens : 31 + tokens]
    head_others, res_others, one_others = refs[31 + tokens : 34 + tokens]
    (
        d_mixed_all, d_fresh_all, d_end_all, arriving, sending, tails, rim_out, rim_in,
        ext, ext_back, sends, receives, rim_sends, rim_receives,
    ) = refs[34 + tokens : 48 + tokens]
    col_sends, col_receives, *half_sems = refs[48 + tokens :]
    halves = Halves(ways, residual, res_others, *half_sems[:4])
    later = Halves(ways, normed, one_others, *half_sems[4:])
    columns = column_copies(ways, head_source, head_others, col_sends, col_receives)
    step = pl.program_id(0)
    position = lax.axis_index("seq")
    pairs = arriving.shape[0]
    length = live.shape[0]
    last = spans - 1
    before_here = place("seq", position - 1)

    def state_copy(pair):
        return pltpu.make_async_remote_copy(
            src_ref=sending.at[pair],
            dst_ref=arriving.at[pair],
            send_sem=sends.at[pair],
            recv_sem=receives.at[pair],
            device_id=before_here,
            device_id_type=MESH,
        )

    def rim_copy():
        return pltpu.make_async_remote_copy(
            src_ref=rim_out,
            dst_ref=rim_in,
            send_sem=rim_sends.at[0],
            recv_sem=rim_receives.at[0],
            device_id=before_here,
            device_id_type=MESH,
        )

    @pl.when(step == 0)
    def _():
        meet(
            [place("seq", (position + last) % spans), place("seq", (position + 1) % spans)]
            + halves.devices()
        )
        halves.start()
        for copy in columns:
            copy.start()
        later.start()
        d_logit_out[...] = jnp.zeros_like(d_logit_out)
        gain_out[...] = jnp.zeros_like(gain_out)

        @pl.when(position == last)
        def _():
            arriving[...] = jnp.zeros_like(arriving)
            rim_in[...] = jnp.zeros_like(rim_in)

    @pl.when(step < pairs)
    def _():
        for i in range(per_step):
            d_out, mixed, q, k = head_columns((d_head, mixed_ref, q_one, k_one), i)
            d_mixed, d_fresh, d_end, gain_row = back_local_part(
                d_out, mixed, gain[...], q, k, wy_one[i]
            )
            d_mixed_all[step * per_step + i] = d_mixed
            d_fresh_all[step * per_step + i] = d_fresh
            d_end_all[step * per_step + i] = d_end
            gain_out[...] += jnp.broadcast_to(gain_row, gain_out.shape)

    pair = step - (last - position)

    @pl.when((pair >= 0) & (pair < pairs))
    def _():
        @pl.when(position != last)
        def _():
            state_copy(pair).wait_recv()

        for i in range(per_step):
            head = pair * per_step + i
            moved = dot_left(ends[head, :, :HEAD_DIM], arriving[pair, i], (0, 0))
            sending[pair, i] = (moved + d_end_all[head]).astype(jnp.bfloat16)

        @pl.when(position != 0)
        def _():
            state_copy(pair).start()

    ready = step - last

    @pl.when(ready >= 0)
    def _():
        outs = (d_q_out, d_k_out, d_v_out)
        for i in range(per_step):
            head = ready * per_step + i
            here = pl.ds(pl.multiple_of(head * HEAD_DIM, HEAD_DIM), HEAD_DIM)
            q, k, v = head_columns((q_ref, k_ref, v_ref), i)
            *grads, d_logit = back_part(
                q, k, v, wy[i], inv[i], state[head], arriving[ready, i],
                d_mixed_all[head], d_fresh_all[head], column_of(logit[...], head), live[...],
            )
            lane = lax.broadcasted_iota(jnp.int32, d_logit_out.shape, 1)
            d_logit_out[...] += jnp.where(lane == head, d_logit, 0.0)
            span = slice(i * HEAD_DIM, (i + 1) * HEAD_DIM)
            for part in range(3):
                own, before, rows = back_conv_part(
                    part, pres[part][:, span], rims[part, :, here],
                    weights[part][:, span], grads[part], taps, ext, ext_back,
                )
                conv_out[part, :, here] = rows
                outs[part][:, here] = own.astype(jnp.bfloat16)
                tails[part, :, here] = own[length - 16 :, :]
                rim_out[part, :, here] = before

    @pl.when(step == pl.num_programs(0) - 1)
    def _():
        @pl.when(position != 0)
        def _():
            rim_copy().start()

        halves.hand_on()
        later.hand_on()

        @pl.when(position != last)
        def _():
            rim_copy().wait_recv()

        for part, out in enumerate((d_q_out, d_k_out, d_v_out)):
            joined = tails[part] + jnp.concatenate(
                [jnp.zeros_like(rim_in[part]), rim_in[part]], 0
            )
            out[length - 16 :, :] = joined.astype(jnp.bfloat16)

        @pl.when(position != 0)
        def _():
            rim_copy().wait_send()
            for index in range(pairs):
                state_copy(index).wait_send()

        for copy in columns:
            copy.wait()
        halves.finish()
        later.finish()


def mixer_backward(
    d_head, mixed, gain, pres, rims, convs, logit, live, q, k, v, wy, inv, state, ends, tokens,
    head_out, residual, normed, per_step, spans, ways, number,
):
    length, channels = pres[0].shape
    heads = channels // HEAD_DIM
    pairs = heads // per_step
    taps = convs[0].shape[0]
    width = per_step * HEAD_DIM
    lag = spans - 1

    def early(step):
        return jnp.minimum(step, pairs - 1)

    def late(step):
        return jnp.maximum(step - lag, 0)

    def flat(rows, at):
        return pl.BlockSpec((rows, width), lambda s: (0, at(s)))

    def by_head(at, *shape):
        return pl.BlockSpec((per_step,) + shape, lambda s: (at(s),) + (0,) * len(shape))

    def whole(*shape):
        return pl.BlockSpec(shape, lambda s: (0,) * len(shape))

    wide = (length, 2 * HEAD_DIM)
    states = (pairs, per_step, HEAD_DIM, HEAD_DIM)
    return pl.pallas_call(
        functools.partial(mixer_backward_kernel, per_step, taps, spans, ways, len(tokens)),
        grid=(pairs + lag,),
        in_specs=[flat(length, early)] * 4
        + [by_head(early, *wide), whole(1, HEAD_DIM)]
        + [flat(length, late)] * 3
        + [flat(taps, late)] * 3
        + [flat(length, late)] * 3
        + [by_head(late, *wide), by_head(late, length, length)]
        + [whole(length, heads), whole(length, 1), whole(heads, HEAD_DIM, HEAD_DIM)]
        + [whole(heads, HEAD_DIM, 2 * HEAD_DIM), whole(3, RIM, channels)]
        + [pl.BlockSpec(memory_space=pl.ANY)] * (len(tokens) + 3),
        out_specs=[whole(length, channels)] * 3
        + [whole(3, taps, channels), whole(length, heads), whole(8, HEAD_DIM)]
        + [pl.BlockSpec(memory_space=pl.ANY)] * 3,
        out_shape=[b16(length, channels)] * 3
        + [f32(3, taps, channels), f32(length, heads), f32(8, HEAD_DIM)]
        + [b16(ways - 1, length, channels // ways)]
        + [b16(ways - 1, *residual.shape)] * 2,
        scratch_shapes=[
            pltpu.VMEM((heads, length, HEAD_DIM), jnp.float32),
            pltpu.VMEM((heads, length, HEAD_DIM), jnp.float32),
            pltpu.VMEM((heads, HEAD_DIM, HEAD_DIM), jnp.float32),
            pltpu.VMEM(states, jnp.bfloat16),
            pltpu.VMEM(states, jnp.bfloat16),
            pltpu.VMEM((3, 16, channels), jnp.float32),
            pltpu.VMEM((3, 8, channels), jnp.float32),
            pltpu.VMEM((3, 8, channels), jnp.float32),
            pltpu.VMEM((RIM + length, HEAD_DIM), jnp.float32),
            pltpu.VMEM((16 + length, HEAD_DIM), jnp.float32),
            pltpu.SemaphoreType.DMA((pairs,)),
            pltpu.SemaphoreType.DMA((pairs,)),
            pltpu.SemaphoreType.DMA((1,)),
            pltpu.SemaphoreType.DMA((1,)),
        ]
        + [pltpu.SemaphoreType.DMA((ways - 1,))] * 10,
        compiler_params=pltpu.CompilerParams(
            collective_id=number, has_side_effects=True, vmem_limit_bytes=VMEM
        ),
        cost_estimate=SHORT,
    )(
        d_head, mixed, q, k, wy, gain, *pres, *convs, q, k, v, wy, inv, logit, live, state, ends,
        rims, *tokens, head_out, residual, normed,
    )


def feed_kernel(
    x_ref, d_ref, gate_w, up_w, down_w, token, feed_out, d_x_out, turned_out, feed_sum, d_x_sum
):
    step = pl.program_id(0)
    x = x_ref[...]
    d_out = d_ref[...]
    gate = dot_low(x, gate_w[...])
    up = dot_low(x, up_w[...])
    d_hidden = dot_low(d_out, down_w[...], (1, 1))
    sig = jax.nn.sigmoid(gate)
    hidden = (gate * sig * up).astype(jnp.bfloat16)
    d_gate = (d_hidden * up * sig * (1.0 + gate * (1.0 - sig))).astype(jnp.bfloat16)
    d_up = (d_hidden * gate * sig).astype(jnp.bfloat16)
    for place, part in enumerate((hidden, d_gate, d_up)):
        turned_out[place] = part.T
    feed = dot_low(hidden, down_w[...])
    d_x = dot_low(d_gate, gate_w[...], (1, 1)) + dot_low(d_up, up_w[...], (1, 1))

    @pl.when(step == 0)
    def _():
        feed_sum[...] = feed
        d_x_sum[...] = d_x

    @pl.when(step > 0)
    def _():
        feed_sum[...] += feed
        d_x_sum[...] += d_x

    @pl.when(step == pl.num_programs(0) - 1)
    def _():
        feed_out[...] = feed_sum[...].astype(jnp.bfloat16)
        d_x_out[...] = d_x_sum[...].astype(jnp.bfloat16)


def feed_forward(x, d_out, gate_weight, up_weight, down_weight, token):
    length, width = x.shape
    units = gate_weight.shape[1]
    tile = 256 if units % 256 == 0 else units
    whole = pl.BlockSpec((length, width), lambda f: (0, 0))
    column = pl.BlockSpec((width, tile), lambda f: (0, f))
    return pl.pallas_call(
        feed_kernel,
        grid=(units // tile,),
        in_specs=[whole, whole, column, column]
        + [pl.BlockSpec((tile, width), lambda f: (f, 0)), pl.BlockSpec(memory_space=pl.ANY)],
        out_specs=[whole, whole, pl.BlockSpec((3, tile, length), lambda f: (0, f, 0))],
        out_shape=[b16(length, width), b16(length, width), b16(3, units, length)],
        scratch_shapes=[pltpu.VMEM((length, width), jnp.float32)] * 2,
        compiler_params=pltpu.CompilerParams(vmem_limit_bytes=VMEM),
        cost_estimate=SHORT,
    )(x, d_out, gate_weight, up_weight, down_weight, token)


def back_projection_kernel(ways, *refs):
    sources, d_logit, weights, beta_w = refs[:3], refs[3], refs[4:7], refs[7]
    shared, out, others = refs[8:11], refs[11], refs[12:15]
    sends, receives = refs[15:18], refs[18:21]
    step = pl.program_id(0)
    copies = [
        copy
        for part in range(3)
        for copy in column_copies(ways, shared[part], others[part], sends[part], receives[part])
    ]

    @pl.when(step == 0)
    def _():
        own = lax.axis_index("dp")
        meet([place("dp", partner(own, by)) for by in range(1, ways)])
        for copy in copies:
            copy.start()

    total = dot_low(d_logit[...], beta_w[...], (1, 1))
    for source, weight in zip(sources, weights):
        total = total + dot_low(source[...], weight[...], (1, 1))
    out[...] = total.astype(jnp.bfloat16)

    @pl.when(step == pl.num_programs(0) - 1)
    def _():
        for copy in copies:
            copy.wait()


def back_projection(sources, d_logit, weights, beta_weight, ways, number):
    length, channels = sources[0].shape
    width, heads = beta_weight.shape
    tile = width // 4
    anywhere = pl.BlockSpec(memory_space=pl.ANY)
    return pl.pallas_call(
        functools.partial(back_projection_kernel, ways),
        grid=(width // tile,),
        in_specs=[pl.BlockSpec((length, channels), lambda n: (0, 0))] * 3
        + [pl.BlockSpec((length, heads), lambda n: (0, 0))]
        + [pl.BlockSpec((tile, channels), lambda n: (n, 0))] * 3
        + [pl.BlockSpec((tile, heads), lambda n: (n, 0))]
        + [anywhere] * 3,
        out_specs=[pl.BlockSpec((length, tile), lambda n: (0, n))] + [anywhere] * 3,
        out_shape=[b16(length, width)] + [b16(ways - 1, length, channels // ways)] * 3,
        scratch_shapes=[pltpu.SemaphoreType.DMA((ways - 1,))] * 6,
        compiler_params=pltpu.CompilerParams(
            collective_id=number, has_side_effects=True, vmem_limit_bytes=VMEM
        ),
        cost_estimate=SHORT,
    )(*sources, d_logit, *weights, beta_weight, *sources)


def pieces_kernel(groups, slots, ways, turned, at, *refs):
    lefts = refs[: groups * slots]
    rights = refs[groups * slots : (groups + ways) * slots]
    out, left_all, right_all = refs[-3:]
    length = rights[0].shape[-2]
    rows = rights[0].shape[-1]
    count = left_all.shape[0] // groups

    @pl.when(pl.program_id(0) == 0)
    def _():
        for group in range(groups):
            for slot in range(slots):
                block = lefts[group * slots + slot][...]
                block = block.reshape(block.shape[-2:])
                left_all[
                    group * count : (group + 1) * count, slot * length : (slot + 1) * length
                ] = block if turned else block.T

    for slot in range(slots):
        for way in range(ways):
            right = rights[slot * ways + way][...]
            right_all[
                slot * length : (slot + 1) * length, way * rows : (way + 1) * rows
            ] = right.reshape(right.shape[-2:])
    out[0] = dot_low(left_all[...], right_all[...]).astype(jnp.bfloat16)


def span_pieces(lefts, count, rights, length, width, spans, turned, tokens=()):
    groups = len(lefts)
    lefts = [left for group in lefts for left in group]
    slots = len(rights)
    ways = lax.axis_size("dp")
    rows = width // (ways * spans)

    def left_block(block, at_place):
        return pl.BlockSpec(block, lambda s, at: at_place(at[0]))

    def right_block(block, at_place, way):
        return pl.BlockSpec(
            block + (rows,), lambda s, at: tuple(at_place(at[0])) + (way * spans + s,)
        )

    return pl.pallas_call(
        functools.partial(pieces_kernel, groups, slots, ways, turned),
        grid_spec=pltpu.PrefetchScalarGridSpec(
            num_scalar_prefetch=1,
            grid=(spans,),
            in_specs=[left_block(block, where) for _, block, where in lefts]
            + [right_block(block, where, way) for _, block, where in rights for way in range(ways)]
            + [pl.BlockSpec(memory_space=pl.ANY)] * len(tokens),
            out_specs=pl.BlockSpec((1, count, ways * rows), lambda s, at: (s, 0, 0)),
            scratch_shapes=[
                pltpu.VMEM((count, slots * length), jnp.bfloat16),
                pltpu.VMEM((slots * length, ways * rows), jnp.bfloat16),
            ],
        ),
        out_shape=b16(spans, count, ways * rows),
        compiler_params=pltpu.CompilerParams(vmem_limit_bytes=VMEM),
        cost_estimate=SHORT,
    )(
        lax.axis_index("dp")[None],
        *[array for array, _, _ in lefts],
        *[array for array, _, _ in rights for _ in range(ways)],
        *tokens,
    )


def widen_kernel(count, turned, *refs):
    for index in range(count):
        whole = refs[index][...].astype(jnp.float32)
        refs[count + index][...] = whole.T if turned[index] else whole


def widened(arrays, turned):
    inside = pl.BlockSpec(memory_space=pltpu.VMEM)
    shapes = [
        f32(*(array.shape[::-1] if turn else array.shape)) for array, turn in zip(arrays, turned)
    ]
    return pl.pallas_call(
        functools.partial(widen_kernel, len(arrays), turned),
        out_shape=shapes,
        in_specs=[inside] * len(arrays),
        out_specs=[inside] * len(arrays),
        compiler_params=pltpu.CompilerParams(vmem_limit_bytes=VMEM),
        cost_estimate=SHORT,
    )(*arrays)


def doublings(size):
    return [1 << bit for bit in range(size.bit_length() - 1)]


def finish_kernel(spans, ways, fed, *refs):
    out_raw, mix_raw, small = refs[:3]
    pieces, refs = refs[3 : 3 + fed], refs[3 + fed :]
    stages, small_out, refs = refs[: 4 + fed], refs[4 + fed], refs[5 + fed :]
    received, handed, totals, *refs = refs
    sends, receives, owner_sends, owner_receives, own_sems = refs[:5]
    small_in, small_sent, small_sends, small_receives = refs[5:]
    own = lax.axis_index("dp")
    position = lax.axis_index("seq")
    last = spans - 1
    rounds = spans - 1
    count = out_raw.shape[1]
    groups = 1 + mix_raw.shape[1] // count
    rows = stages[0].shape[1]
    peers = [partner(own, by) for by in range(1, ways)]

    def raw_at(group, shard):
        if group == 0:
            return out_raw.at[shard]
        return mix_raw.at[shard, (group - 1) * count : group * count, :]

    def line_copy(way, turn, group, src):
        step = 1 if way == 0 else -1
        slot = (way * rounds + turn) * groups + group
        return pltpu.make_async_remote_copy(
            src_ref=src,
            dst_ref=received.at[way, turn, group],
            send_sem=sends.at[slot],
            recv_sem=receives.at[slot],
            device_id=place("seq", position + step),
            device_id_type=MESH,
        )

    def owner_copies(index, source):
        high = source.shape[0]
        stage = stages[index]
        mine = stage.at[pl.ds(pl.multiple_of(own * high, high), high), :]
        copies = []
        for by, peer in enumerate(peers):
            copies.append(
                pltpu.make_async_remote_copy(
                    src_ref=source.at[:, pl.ds(pl.multiple_of(peer * rows, rows), rows)],
                    dst_ref=mine,
                    send_sem=owner_sends.at[index * (ways - 1) + by],
                    recv_sem=owner_receives.at[index * (ways - 1) + by],
                    device_id=place("dp", peer),
                    device_id_type=MESH,
                )
            )
        here = pltpu.make_async_copy(
            source.at[:, pl.ds(pl.multiple_of(own * rows, rows), rows)], mine, own_sems.at[index]
        )
        return copies + [here]

    partners = [place("dp", partner(own, by)) for by in doublings(ways)]
    partners += [place("seq", partner(position, by)) for by in doublings(spans)]
    partners += [place("head", 1 - lax.axis_index("head"))]

    def small_copy(turn):
        high = 8 if turn == len(partners) - 1 else small.shape[0]
        return pltpu.make_async_remote_copy(
            src_ref=small_sent.at[turn, :high, :],
            dst_ref=small_in.at[turn, :high, :],
            send_sem=small_sends.at[turn],
            recv_sem=small_receives.at[turn],
            device_id=partners[turn],
            device_id_type=MESH,
        )

    def small_turn(turn):
        if turn == 0:
            small_sent[0] = small[...]
        else:
            small_copy(turn - 1).wait_recv()
            if turn < len(partners):
                small_sent[turn] = small_sent[turn - 1] + small_in[turn - 1]
            else:
                small_out[...] = small_sent[turn - 1]
                small_out[:8, :] = small_sent[turn - 1, :8, :] + small_in[turn - 1, :8, :]
        if turn < len(partners):
            small_copy(turn).start()

    meet(
        [place("seq", (position + last) % spans), place("seq", (position + 1) % spans)]
        + [place("seq", partner(position, by)) for by in doublings(spans)[1:]]
        + [place("dp", peer) for peer in peers]
        + partners[-1:]
    )
    small_turn(0)
    along = (position, last - position)

    def source_send(way, index):
        turn, group = index // groups, index % groups
        shard = last - turn if way == 0 else turn
        if index >= 2:
            line_copy(way, (index - 2) // groups, (index - 2) % groups, totals.at[0]).wait_send()
        line_copy(way, turn, group, raw_at(group, shard)).start()

    for way in range(2):

        @pl.when(along[way] == 0)
        def _():
            for index in range(2):
                source_send(way, index)

    fed_copies = [owner_copies(index, piece) for index, piece in enumerate(pieces)]
    for copies in fed_copies:
        for copy in copies:
            copy.start()

    for way in range(2):

        @pl.when(along[way] == 0)
        def _():
            for index in range(2, groups + 2):
                source_send(way, index)

    for turn in range(1, rounds):
        for group in range(groups):
            for way in range(2):
                if turn * groups + group + 2 < rounds * groups:

                    @pl.when(along[way] == 0)
                    def _():
                        source_send(way, turn * groups + group + 2)

                shard = last - turn + position if way == 0 else turn - along[1]

                @pl.when((along[way] >= 1) & (along[way] <= turn))
                def _():
                    line_copy(way, turn - 1, group, handed.at[way, turn - 1, group]).wait_recv()
                    term = raw_at(group, shard)[...].astype(jnp.float32)
                    term = term + received[way, turn - 1, group].astype(jnp.float32)
                    handed[way, turn - 1, group] = term.astype(jnp.bfloat16)
                    line_copy(way, turn, group, handed.at[way, turn - 1, group]).start()

        small_turn(turn)

    for turn in range(rounds, len(partners) + 1):
        small_turn(turn)

    for group in range(groups):
        for way in range(2):

            @pl.when(along[way] >= 1)
            def _():
                line_copy(way, rounds - 1, group, totals.at[group]).wait_recv()

        total = raw_at(group, position)[...].astype(jnp.float32)
        for way in range(2):
            arrived = received[way, rounds - 1, group].astype(jnp.float32)
            total = total + jnp.where(along[way] >= 1, arrived, 0.0)
        totals[group] = total.astype(jnp.bfloat16)
        for copy in owner_copies(fed + group, totals.at[group]):
            copy.start()

    sources = list(pieces) + [totals.at[group] for group in range(groups)]
    for index, source in enumerate(sources):
        for copy in owner_copies(index, source):
            copy.wait()

    for turn in range(rounds):
        for way in range(2):

            @pl.when((along[way] >= 1) & (along[way] <= turn))
            def _():
                for group in range(groups):
                    line_copy(way, turn, group, totals.at[group]).wait_send()

    for way in range(2):

        @pl.when(along[way] == 0)
        def _():
            for group in range(groups - 2, groups):
                line_copy(way, rounds - 1, group, totals.at[group]).wait_send()

    for turn in range(len(partners)):
        small_copy(turn).wait_send()


def finished_gradients(out_raw, mix_raw, pieces, small, number):
    spans, ways = lax.axis_size("seq"), lax.axis_size("dp")
    _, count, wide = out_raw.shape
    groups = 1 + mix_raw.shape[1] // count
    rows = wide // ways
    fed = len(pieces)
    highs = [ways * piece.shape[0] for piece in pieces] + [ways * count] * groups
    inside = pl.BlockSpec(memory_space=pltpu.VMEM)
    shapes = [b16(high, rows) for high in highs]
    lines = (2, spans - 1, groups, count, wide)
    turns = len(doublings(ways)) + len(doublings(spans)) + 1
    return pl.pallas_call(
        functools.partial(finish_kernel, spans, ways, fed),
        out_shape=shapes + [f32(*small.shape)],
        in_specs=[inside] * 3 + [pl.BlockSpec(memory_space=pl.ANY)] * fed,
        out_specs=[inside] * (len(shapes) + 1),
        scratch_shapes=[
            pltpu.VMEM(lines, jnp.bfloat16),
            pltpu.VMEM((2, spans - 2, groups, count, wide), jnp.bfloat16),
            pltpu.VMEM((groups, count, wide), jnp.bfloat16),
        ]
        + [pltpu.SemaphoreType.DMA((2 * (spans - 1) * groups,))] * 2
        + [pltpu.SemaphoreType.DMA((len(highs) * (ways - 1),))] * 2
        + [pltpu.SemaphoreType.DMA((len(highs),))]
        + [pltpu.VMEM((turns,) + small.shape, jnp.float32)] * 2
        + [pltpu.SemaphoreType.DMA((turns,))] * 2,
        compiler_params=pltpu.CompilerParams(
            collective_id=number, has_side_effects=True, vmem_limit_bytes=VMEM
        ),
        cost_estimate=SHORT,
    )(out_raw, mix_raw, small, *pieces)


def shards(
    tokens_in,
    lengths,
    first_gain,
    query_weight,
    key_weight,
    value_weight,
    beta_weight,
    query_conv,
    key_conv,
    value_conv,
    mixer_gain,
    output_weight,
    second_gain,
    gate_weight,
    up_weight,
    down_weight,
    upstream,
):
    num_rows, local_len, local_width = tokens_in.shape
    full_width = query_weight.shape[0]
    channels = query_weight.shape[1]
    local_heads = beta_weight.shape[1]
    groups = lax.axis_size("head")
    ways = lax.axis_size("dp")
    spans = lax.axis_size("seq")
    positions = lax.axis_index("seq") * local_len + jnp.arange(local_len, dtype=jnp.int32)
    live_mask = (positions[None, :] < lengths[:, None]).astype(jnp.float32)
    masked_up = upstream * live_mask[..., None].astype(jnp.bfloat16)
    gains = jnp.stack([first_gain, second_gain] + [first_gain] * 14)
    everything = gather_head(jnp.concatenate([tokens_in[0], masked_up[0], gains], 0), 1)
    gathered = everything[None, :local_len]
    upstream_full = everything[None, local_len : 2 * local_len]
    gain_one = everything[2 * local_len].astype(jnp.float32)
    gain_two = everything[2 * local_len + 1].astype(jnp.float32)
    stream_full = gathered.astype(jnp.float32)
    scale_one = inverse_rms(stream_full)
    normed_one = (stream_full * scale_one * gain_one).astype(jnp.bfloat16)

    def scattered(pieces):
        return lax.psum_scatter(pieces, "seq", scatter_dimension=0, tiled=False)

    def to_owner(piece):
        c = piece.shape[0]
        blocks = piece.reshape(c, ways, -1).transpose(1, 0, 2)
        return jnp.stack(in_order(exchanged(blocks, "dp"), "dp"), 0)

    fused = groups == 2
    if fused:
        half_up = lax.all_gather(masked_up[0], "dp", axis=0, tiled=True)
        tokens_up = gather_head(half_up, 1)
    else:
        tokens_up = jnp.stack(spread(upstream_full[0], "dp")[1:])
    per_step = 2 if local_heads % 2 == 0 else 1
    pres = [
        jnp.dot(normed_one[0], weight, preferred_element_type=jnp.float32).astype(jnp.bfloat16)
        for weight in (query_weight, key_weight, value_weight)
    ]
    beta_logit = jnp.dot(normed_one[0], beta_weight, preferred_element_type=jnp.float32)
    convs = [query_conv, key_conv, value_conv]
    live_col = live_mask[0][:, None]
    head_gain = mixer_gain.astype(jnp.float32)[None, :]
    if fused:
        (
            query, key, value, wy, inverse, ends, mixed, head_out, entering, rims,
        ) = mixer_forward(pres, convs, beta_logit, live_col, head_gain, per_step, spans, 1)
    else:
        rims = passed_along(jnp.stack([pre[local_len - RIM :, :] for pre in pres]), "seq", 1)
        rims = [rims[0], rims[1], rims[2]]
        query, key, value, wy, inverse, mix, ends = mixer_local(
            pres, rims, convs, beta_logit, live_col, per_step
        )
        entering = chain_state(ends[:, :, :HEAD_DIM], ends[:, :, HEAD_DIM:], False)
        mixed, head_out = mixer_finish(mix, entering, head_gain, per_step)
    head_out = head_out[None]
    mixer_part = jnp.dot(head_out, output_weight, preferred_element_type=jnp.float32)
    stream_mid = stream_full + sum_head(mixer_part)
    scale_two = inverse_rms(stream_mid)
    normed_two = (stream_mid * scale_two * gain_two).astype(jnp.bfloat16)
    if fused:
        half_two = lax.all_gather(
            own_half(normed_two[0], local_width), "dp", axis=0, tiled=True
        )
    feed_part, d_two_part, turned = feed_forward(
        normed_two[0], upstream_full[0], gate_weight, up_weight, down_weight,
        half_up if fused else normed_two,
    )
    layer_out = own_half(stream_mid + sum_head(feed_part[None]), local_width).astype(jnp.bfloat16)
    units = turned.shape[1] // ways
    turned = turned.reshape(3, ways, units, local_len)

    def raw_piece(lefts, count, rights, is_turned, tokens=()):
        return span_pieces(
            lefts, count, rights, local_len, full_width, spans, is_turned, tokens
        )

    def slots_of(own, others):
        return [(own, (local_len,), lambda at: (0,))] + [
            (others, (1, local_len), lambda at, by=by: (by, 0)) for by in range(ways - 1)
        ]

    def by_position(array):
        return [(array, (local_len,), lambda at, by=by: (at ^ by,)) for by in range(ways)]

    def feed_slots(which, others, index):
        own = [(turned, (1, 1, units, local_len), lambda at: (which, at, 0, 0))]
        return own + [
            (others, (1, 1, units, local_len), lambda at, by=by: (by, index, 0, 0))
            for by in range(ways - 1)
        ]

    normed_full = normed_two[0]
    if fused:
        (hidden_others,) = plane_exchange([turned], [("rows", 0, 1)], [], 2)
        down_raw = raw_piece(
            [feed_slots(0, hidden_others, 0)], units, by_position(tokens_up), True
        )
        (d_others,) = plane_exchange([turned], [("rows", 1, 3)], [down_raw], 3)
        two_slots = by_position(gather_head(half_two, 1))
    else:
        hidden_others = jnp.stack(exchanged(turned[:1].transpose(1, 0, 2, 3), "dp")[1:])
        down_raw = raw_piece(
            [feed_slots(0, hidden_others, 0)], units, slots_of(upstream_full[0], tokens_up), True
        )
        d_others = jnp.stack(exchanged(turned[1:].transpose(1, 0, 2, 3), "dp")[1:])
        two_slots = slots_of(normed_full, jnp.stack(spread(normed_full, "dp")[1:]))
    down_piece = scattered(down_raw)
    gate_raw = raw_piece([feed_slots(1, d_others, 0)], units, two_slots, True)
    gate_piece = scattered(gate_raw)
    up_raw = raw_piece([feed_slots(2, d_others, 1)], units, two_slots, True, [gate_raw])
    up_piece = scattered(up_raw)
    d_two = sum_head(d_two_part[None])
    d_stream = (
        upstream_full.astype(jnp.float32)
        + scale_two * gain_two * d_two
        - stream_mid
        * scale_two
        * scale_two
        * scale_two
        * (jnp.sum(d_two * gain_two * stream_mid, axis=-1, keepdims=True) / full_width)
    )
    grad_second = own_half(jnp.sum(d_two * stream_mid * scale_two, axis=(0, 1)), local_width)
    residual_full = d_stream.astype(jnp.bfloat16)
    d_head_out = jnp.einsum(
        "rsd,cd->rsc", residual_full, output_weight, preferred_element_type=jnp.float32
    )
    if fused:
        (
            *mix_sources, grad_kernels, d_beta_logit, grad_gain_part, out_others, res_others,
            one_others,
        ) = mixer_backward(
            d_head_out[0], mixed, head_gain, pres, rims, convs, beta_logit, live_col,
            query, key, value, wy, inverse, entering, ends, [up_raw, down_piece],
            head_out[0], residual_full[0], normed_one[0], per_step, spans, ways, 4,
        )
    else:
        d_mixed, d_fresh, d_ends, grad_gain_part = mixer_back_local(
            d_head_out[0], mixed, head_gain, query, key, wy, per_step
        )
        leaving = chain_state(jnp.swapaxes(ends[:, :, :HEAD_DIM], 1, 2), d_ends, True)
        *d_pres, tails, d_rims, grad_kernels, d_beta_logit = mixer_back(
            pres, rims, convs, beta_logit, live_col, query, key, value, wy, inverse,
            entering, d_mixed, d_fresh, leaving, per_step,
        )
        tails = (tails + passed_along(d_rims, "seq", -1)).astype(jnp.bfloat16)
        mix_sources = [
            jnp.concatenate([part[: local_len - 8], tail], 0) for part, tail in zip(d_pres, tails)
        ]
    grad_gain_part = grad_gain_part[0]
    share_width = channels // ways
    residual = residual_full[0]
    if fused:
        d_one_part, *mix_others = back_projection(
            mix_sources, d_beta_logit.astype(jnp.bfloat16),
            [query_weight, key_weight, value_weight], beta_weight, ways, 5,
        )
    else:
        *mix_others, out_others = [
            jnp.stack(exchanged(part.reshape(local_len, ways, -1).transpose(1, 0, 2), "dp")[1:])
            for part in mix_sources + [head_out[0]]
        ]
        res_others = jnp.stack(spread(residual, "dp")[1:])

    def column_slots(own, others):
        if fused:
            first = [(own, (local_len, share_width), lambda at: (0, at))]
        else:
            mine = lax.dynamic_slice_in_dim(
                own, lax.axis_index("dp") * share_width, share_width, 1
            )
            first = [(mine, (local_len, share_width), lambda at: (0, 0))]
        return first + [
            (others, (1, local_len, share_width), lambda at, by=by: (by, 0, 0))
            for by in range(ways - 1)
        ]

    if fused:
        one_slots = slots_of(normed_one[0], one_others)
    else:
        one_slots = slots_of(normed_one[0], jnp.stack(spread(normed_one[0], "dp")[1:]))
    out_raw = raw_piece(
        [column_slots(head_out[0], out_others)], share_width, slots_of(residual, res_others), False,
        [gate_piece],
    )
    mix_raw = raw_piece(
        [column_slots(own, others) for own, others in zip(mix_sources, mix_others)],
        3 * share_width, one_slots, False, [out_raw],
    )
    d_logit_low = d_beta_logit.astype(jnp.bfloat16)
    if not fused:
        d_one_part = jnp.dot(d_logit_low, beta_weight.T, preferred_element_type=jnp.float32)
        for part, weight in zip(mix_sources, (query_weight, key_weight, value_weight)):
            d_one_part = d_one_part + jnp.dot(
                part, weight.T, preferred_element_type=jnp.float32
            )
    grad_beta_part = lax.dot_general(
        d_logit_low, normed_one[0], (((0,), (0,)), ((), ())), preferred_element_type=jnp.float32
    )
    d_one = sum_head(d_one_part[None])
    grad_tokens = own_half(
        d_stream
        + scale_one * gain_one * d_one
        - stream_full
        * scale_one
        * scale_one
        * scale_one
        * (jnp.sum(d_one * gain_one * stream_full, axis=-1, keepdims=True) / full_width),
        local_width,
    )
    grad_first = own_half(jnp.sum(d_one * stream_full * scale_one, axis=(0, 1)), local_width)
    lane = 128
    sizes = [HEAD_DIM, local_width, local_width, grad_kernels.size, grad_beta_part.size]
    parts = [grad_gain_part, grad_first, grad_second, grad_kernels, grad_beta_part]
    shares = [
        jnp.pad(part.reshape(-1, lane), ((0, -(size // lane) % 8), (0, 0)))
        for part, size in zip(parts, sizes)
    ]
    small = jnp.concatenate(shares, 0)
    if fused:
        *finished, small = finished_gradients(
            out_raw, mix_raw, [down_piece, gate_piece, up_piece], small, 6
        )
        down, gate, up, out, *mix = widened(
            finished, [False, True, True, False, True, True, True]
        )
        gain_total = small[0]
    else:
        small = sum_doubling(small, ("dp", "seq"))
        gain_total = sum_doubling(small[0], ("head",))
    starts = [0]
    for part in shares:
        starts.append(starts[-1] + part.shape[0])
    totals = [
        small[start : start + size // lane].reshape(part.shape)
        for start, size, part in zip(starts, sizes, parts)
    ]
    grad_first, grad_second, kernel_sum, beta_sum = totals[1:]
    share = lax.axis_index("dp") * spans + lax.axis_index("seq")
    rows = full_width // (ways * spans)
    grad_beta = lax.dynamic_slice_in_dim(beta_sum, share * rows, rows, 1).T
    if not fused:
        feed = to_owner(jnp.concatenate([down_piece, gate_piece, up_piece], 0))
        down, gate, up = [
            feed[:, place * units : (place + 1) * units].reshape(-1, rows).astype(jnp.float32)
            for place in range(3)
        ]
        gate, up = gate.T, up.T
        out = to_owner(scattered(out_raw)).reshape(-1, rows).astype(jnp.float32)
        mix = to_owner(scattered(mix_raw)).astype(jnp.float32)
        third = mix.shape[1] // 3
        mix = [mix[:, i * third : (i + 1) * third].reshape(-1, rows).T for i in range(3)]
    return (
        layer_out,
        grad_tokens,
        grad_first,
        mix[0],
        mix[1],
        mix[2],
        grad_beta,
        kernel_sum[0],
        kernel_sum[1],
        kernel_sum[2],
        gain_total,
        out,
        grad_second,
        gate,
        up,
        down,
    )


def solution(mesh):
    placed = (
        P("dp", "seq", "head"),
        P("dp"),
        P("head"),
        P(None, "head"),
        P(None, "head"),
        P(None, "head"),
        P(None, "head"),
        P(None, "head"),
        P(None, "head"),
        P(None, "head"),
        P(),
        P("head", None),
        P("head"),
        P(None, "head"),
        P(None, "head"),
        P("head", None),
        P("dp", "seq", "head"),
    )
    return jax.shard_map(
        shards,
        mesh=mesh,
        in_specs=placed,
        out_specs=(
            P("dp", "seq", "head"),
            P("dp", "seq", "head"),
            P("head"),
            P(("dp", "seq"), "head"),
            P(("dp", "seq"), "head"),
            P(("dp", "seq"), "head"),
            P(("dp", "seq"), "head"),
            P(None, "head"),
            P(None, "head"),
            P(None, "head"),
            P(),
            P("head", ("dp", "seq")),
            P("head"),
            P(("dp", "seq"), "head"),
            P(("dp", "seq"), "head"),
            P("head", ("dp", "seq")),
        ),
        check_vma=False,
    )
```

```python
import functools

import jax
import jax.numpy as jnp
from jax import lax
from jax.experimental import pallas as pl
from jax.experimental.pallas import tpu as pltpu
from jax.sharding import PartitionSpec as P

HEAD_DIM = 128


HIGH = lax.Precision.HIGHEST
EPSILON = 1e-05
UNIT_EPSILON = 1e-06
VMEM = 56 * 1024 * 1024
SHORT = pl.CostEstimate(flops=0, bytes_accessed=0, transcendentals=0)


def passed_along(value, axis, by):
    peers = lax.axis_size(axis)
    pairs = [(i, i + by) for i in range(peers) if 0 <= i + by < peers]
    return lax.ppermute(value, axis, pairs)


def swap_pairs(axis, by):
    peers = lax.axis_size(axis)
    return [(i, i ^ by) for i in range(peers)]


def exchanged(values, axis):
    peers = lax.axis_size(axis)
    own = lax.axis_index(axis)
    parts = [lax.dynamic_index_in_dim(values, own, 0, keepdims=False)]
    for by in range(1, peers):
        out = lax.dynamic_index_in_dim(values, own ^ by, 0, keepdims=False)
        parts.append(lax.ppermute(out, axis, swap_pairs(axis, by)))
    return parts


def spread(value, axis):
    peers = lax.axis_size(axis)
    return [value] + [
        lax.ppermute(value, axis, swap_pairs(axis, by)) for by in range(1, peers)
    ]


def in_order(parts, axis):
    stacked = jnp.stack(parts, 0)
    own = lax.axis_index(axis)
    return [
        lax.dynamic_index_in_dim(stacked, own ^ k, 0, keepdims=False) for k in range(len(parts))
    ]


def gather_head(value, axis):
    if lax.axis_size("head") == 2:
        other = lax.ppermute(value, "head", [(0, 1), (1, 0)])
        first = lax.axis_index("head") == 0
        return jnp.concatenate(
            [jnp.where(first, value, other), jnp.where(first, other, value)], axis
        )
    return lax.all_gather(value, "head", axis=axis, tiled=True)


def swapped(value):
    return lax.ppermute(value, "head", [(0, 1), (1, 0)])


def sum_head(value):
    low = value.astype(jnp.bfloat16)
    if lax.axis_size("head") == 2:
        other = lax.ppermute(low, "head", [(0, 1), (1, 0)])
        return low.astype(jnp.float32) + other.astype(jnp.float32)
    return lax.psum(low, "head").astype(jnp.float32)


def sum_doubling(value, axes):
    for axis in axes:
        by = 1
        while by < lax.axis_size(axis):
            value = value + lax.ppermute(value, axis, swap_pairs(axis, by))
            by *= 2
    return value


def own_half(value, width):
    return lax.dynamic_slice_in_dim(value, lax.axis_index("head") * width, width, value.ndim - 1)


def chain_state(maps, shifts, reverse):
    peers = lax.axis_size("seq")
    by = -1 if reverse else 1
    states = [passed_along(shifts.astype(jnp.bfloat16), "seq", by)]
    for step in range(peers - 2):
        out = (
            jnp.einsum("hij,hjk->hik", maps, states[-1].astype(jnp.float32), precision=HIGH)
            + shifts
        )
        states.append(passed_along(out.astype(jnp.bfloat16), "seq", by))
    return states[-1]


def inverse_rms(values):
    return lax.rsqrt(jnp.mean(values * values, axis=-1, keepdims=True) + EPSILON)


MESH = pl.DeviceIdType.MESH


def partner(own, by):
    other = own
    bit = 1
    while bit <= by:
        if by & bit:
            other = other + bit - 2 * bit * ((own // bit) % 2)
        bit *= 2
    return other


def place(name, index):
    return {name: index}


def meet(devices):
    barrier = pltpu.get_barrier_semaphore()
    for device in devices:
        pl.semaphore_signal(barrier, inc=1, device_id=device, device_id_type=MESH)
    pl.semaphore_wait(barrier, len(devices))


class Halves:
    def __init__(self, ways, source, out, sends, receives, hand_sends, hand_receives):
        own = lax.axis_index("dp")
        core = lax.axis_index("head")
        width = source.shape[1] // 2
        mine = pl.ds(pl.multiple_of(core * width, width), width)
        self.peers = [place("dp", partner(own, by)) for by in range(1, ways)]
        self.other = place("head", 1 - core)
        self.first = [
            pltpu.make_async_remote_copy(
                src_ref=source.at[:, mine],
                dst_ref=out.at[slot, :, mine],
                send_sem=sends.at[slot],
                recv_sem=receives.at[slot],
                device_id=peer,
                device_id_type=MESH,
            )
            for slot, peer in enumerate(self.peers)
        ]
        self.second = [
            pltpu.make_async_remote_copy(
                src_ref=out.at[slot, :, mine],
                dst_ref=out.at[slot, :, mine],
                send_sem=hand_sends.at[slot],
                recv_sem=hand_receives.at[slot],
                device_id=self.other,
                device_id_type=MESH,
            )
            for slot in range(ways - 1)
        ]

    def devices(self):
        return self.peers + [self.other]

    def start(self):
        for copy in self.first:
            copy.start()

    def hand_on(self):
        for copy, hand in zip(self.first, self.second):
            copy.wait_recv()
            hand.start()

    def finish(self):
        for copy, hand in zip(self.first, self.second):
            copy.wait_send()
            hand.wait()


def column_copies(ways, source, out, sends, receives):
    own = lax.axis_index("dp")
    width = source.shape[1] // ways
    copies = []
    for by in range(1, ways):
        peer = partner(own, by)
        copies.append(
            pltpu.make_async_remote_copy(
                src_ref=source.at[:, pl.ds(pl.multiple_of(peer * width, width), width)],
                dst_ref=out.at[by - 1],
                send_sem=sends.at[by - 1],
                recv_sem=receives.at[by - 1],
                device_id=place("dp", peer),
                device_id_type=MESH,
            )
        )
    return copies


def halves(a):
    top = a.astype(jnp.bfloat16)
    return top, (a - top.astype(jnp.float32)).astype(jnp.bfloat16)


def dot_low(a, b, dims=(1, 0)):
    return lax.dot_general(
        a, b, (((dims[0],), (dims[1],)), ((), ())), preferred_element_type=jnp.float32
    )


def dot_left(a, b, dims=(1, 0)):
    top, rest = halves(a)
    return dot_low(top, b, dims) + dot_low(rest, b, dims)


def dot_right(a, b, dims=(1, 0)):
    top, rest = halves(b)
    return dot_low(a, top, dims) + dot_low(a, rest, dims)


def dot_both(a, b, dims=(1, 0)):
    a_top, a_rest = halves(a)
    b_top, b_rest = halves(b)
    return dot_low(a_top, b_top, dims) + (
        dot_low(a_top, b_rest, dims) + dot_low(a_rest, b_top, dims)
    )


def grid_marks(size):
    row = lax.broadcasted_iota(jnp.int32, (size, size), 0)
    col = lax.broadcasted_iota(jnp.int32, (size, size), 1)
    return row, col


def unit_lower_inverses(tiles):
    size = tiles[0].shape[0]
    row, col = grid_marks(size)
    unit = (row == col).astype(jnp.float32)
    base = 8
    near = (row // base == col // base) & (row > col)
    cores = [jnp.where(near, tile, 0.0) for tile in tiles]
    squares = [dot_both(core, core) for core in cores]
    fourths = [dot_both(square, square) for square in squares]
    found = [dot_both(unit - core, unit + square) for core, square in zip(cores, squares)]
    found = [dot_both(part, unit + fourth) for part, fourth in zip(found, fourths)]
    while base < size:
        wide = 2 * base
        near = (row // wide == col // wide) & (row // base > col // base)
        links = [jnp.where(near, tile, 0.0) for tile in tiles]
        steps = [dot_both(part, link) for part, link in zip(found, links)]
        found = [part - dot_both(step, part) for part, step in zip(found, steps)]
        base = wide
    return found


def lower_inverses(systems, tile):
    size = systems[0].shape[0]
    if size <= tile:
        return unit_lower_inverses(systems)
    half = size // 2
    diagonals = [s[:half, :half] for s in systems] + [s[half:, half:] for s in systems]
    found = lower_inverses(diagonals, tile)
    firsts, seconds = found[: len(systems)], found[len(systems) :]
    steps = [dot_both(second, s[half:, :half]) for second, s in zip(seconds, systems)]
    corners = [-dot_both(step, first) for step, first in zip(steps, firsts)]
    empty = jnp.zeros((half, half), jnp.float32)
    return [
        jnp.concatenate(
            [jnp.concatenate([first, empty], 1), jnp.concatenate([corner, second], 1)], 0
        )
        for first, corner, second in zip(firsts, corners, seconds)
    ]


RIM = 16


def conv_sum(ext, pre, rim, weights, taps, length):
    ext[:RIM, :] = rim.astype(jnp.float32)
    ext[RIM : RIM + length, :] = pre.astype(jnp.float32)
    first = RIM - taps + 1
    summed = weights[0:1, :] * ext[first : first + length, :]
    for tap in range(1, taps):
        summed = summed + weights[tap : tap + 1, :] * ext[first + tap : first + tap + length, :]
    return summed


def head_columns(refs, index):
    span = slice(index * HEAD_DIM, (index + 1) * HEAD_DIM)
    return [ref[:, span] for ref in refs]


def unit_scale(rows):
    return lax.rsqrt(jnp.sum(rows * rows, axis=-1, keepdims=True) + UNIT_EPSILON)


def column_of(values, index):
    lane = lax.broadcasted_iota(jnp.int32, values.shape, 1)
    return jnp.sum(jnp.where(lane == index, values, 0.0), axis=-1, keepdims=True)


def row_of(values, index):
    place = lax.broadcasted_iota(jnp.int32, values.shape, 0)
    return jnp.sum(jnp.where(place == index, values, 0.0), axis=0, keepdims=True)


def local_part(pres, rims, weights, logit, logit_t, live, live_t, ext, first, taps):
    length = live.shape[0]
    row, col = grid_marks(length)
    heads = range(pres[0].shape[1] // HEAD_DIM)
    queries, keys, values, systems, beta_rows = [], [], [], [], []
    for i in heads:
        span = slice(i * HEAD_DIM, (i + 1) * HEAD_DIM)
        active = []
        for pre, rim, weight in zip(pres, rims, weights):
            summed = conv_sum(
                ext, pre[:, span], rim[:, span], weight[:, span].astype(jnp.float32), taps, length
            )
            active.append(summed * jax.nn.sigmoid(summed))
        q, k, v = active
        q = (q * unit_scale(q)).astype(jnp.bfloat16)
        k = (k * unit_scale(k) * live).astype(jnp.bfloat16)
        v = v.astype(jnp.bfloat16)
        beta = jax.nn.sigmoid(column_of(logit, first + i)) * live
        beta_rows.append(jax.nn.sigmoid(row_of(logit_t, first + i)) * live_t)
        gram = dot_low(k, k, (1, 1))
        systems.append(jnp.where(row > col, beta * gram, 0.0))
        queries.append(q)
        keys.append(k)
        values.append(v)
    inverses = lower_inverses(systems, 128)
    wys = [
        dot_left(inverse * beta_row, jnp.concatenate([k, v], 1))
        for inverse, beta_row, k, v in zip(inverses, beta_rows, keys, values)
    ]
    wide = (HEAD_DIM, 2 * HEAD_DIM)
    place = lax.broadcasted_iota(jnp.int32, wide, 1)
    unit = (lax.broadcasted_iota(jnp.int32, wide, 0) == place).astype(jnp.float32)
    found = []
    for i in heads:
        ends = dot_right(keys[i], wys[i], (0, 0))
        ends = unit + jnp.where(place < HEAD_DIM, -ends, ends)
        scores = jnp.where(row >= col, dot_low(queries[i], keys[i], (1, 1)), 0.0)
        seen = dot_both(scores, wys[i])
        mix = jnp.concatenate(
            [queries[i].astype(jnp.float32) - seen[:, :HEAD_DIM], seen[:, HEAD_DIM:]], 1
        )
        found.append((queries[i], keys[i], values[i], wys[i], inverses[i], mix, ends))
    return found


def finish_part(mix, state, gain):
    mixed = mix[:, HEAD_DIM:] + dot_left(mix[:, :HEAD_DIM], state)
    scale = lax.rsqrt(jnp.mean(mixed * mixed, axis=-1, keepdims=True) + EPSILON)
    return mixed, (mixed * scale * gain).astype(jnp.bfloat16)


def back_local_part(d_out, mixed, gain, q, k, wy):
    row, col = grid_marks(q.shape[0])
    scale = lax.rsqrt(jnp.mean(mixed * mixed, axis=-1, keepdims=True) + EPSILON)
    weighted = gain * d_out
    inner = jnp.sum(weighted * mixed, axis=-1, keepdims=True)
    d_mixed = scale * weighted - mixed * (scale * scale * scale * inner / HEAD_DIM)
    gain_row = jnp.sum(d_out * mixed * scale, axis=0, keepdims=True)
    scores_t = jnp.where(col >= row, dot_low(k, q, (1, 1)), 0.0)
    d_fresh = dot_both(scores_t, d_mixed)
    d_end = dot_right(q, d_mixed, (0, 0)) - dot_both(wy[:, :HEAD_DIM], d_fresh, (0, 0))
    return d_mixed, d_fresh, d_end, gain_row


def back_part(q, k, v, wy, inverse, entering, leaving, d_mixed, d_fresh, logit, live):
    row, col = grid_marks(q.shape[0])
    d_fresh = d_fresh + dot_low(k, leaving)
    fresh = wy[:, HEAD_DIM:] - dot_left(wy[:, :HEAD_DIM], entering)
    d_scores = jnp.where(row >= col, dot_both(d_mixed, fresh, (1, 1)), 0.0)
    d_q = dot_left(d_mixed, entering, (1, 1)) + dot_left(d_scores, k)
    d_k = dot_left(d_scores, q, (0, 0)) + dot_left(fresh, leaving, (1, 1))
    d_wy = jnp.concatenate([-dot_left(d_fresh, entering, (1, 1)), d_fresh], 1)
    d_rhs = dot_both(inverse, d_wy, (0, 0))
    edges = jnp.where(row > col, -dot_both(d_rhs, wy, (1, 1)), 0.0)
    sig = jax.nn.sigmoid(logit)
    beta = sig * live
    both = jnp.concatenate([k, v], 1).astype(jnp.float32)
    gram = dot_low(k, k, (1, 1))
    d_beta = jnp.sum(d_rhs * both, axis=-1, keepdims=True) + jnp.sum(
        edges * gram, axis=-1, keepdims=True
    )
    scaled = beta * edges
    d_k = d_k + beta * d_rhs[:, :HEAD_DIM] + dot_left(scaled, k) + dot_left(scaled, k, (0, 0))
    d_v = beta * d_rhs[:, HEAD_DIM:]
    d_logit = d_beta * live * sig * (1.0 - sig)
    return d_q, d_k * live, d_v, d_logit


def back_conv_part(part, pre, rim, weight, grad, taps, ext, ext_back):
    length = pre.shape[0]
    weight = weight.astype(jnp.float32)
    summed = conv_sum(ext, pre, rim, weight, taps, length)
    gate = jax.nn.sigmoid(summed)
    if part < 2:
        active = summed * gate
        scale = unit_scale(active)
        inner = jnp.sum(active * grad, axis=-1, keepdims=True)
        grad = scale * grad - active * (scale * scale * scale * inner)
    d_conv = grad * gate * (1.0 + summed * (1.0 - gate))
    first = RIM - taps + 1
    rows = [
        jnp.sum(d_conv * ext[first + tap : first + tap + length, :], axis=0, keepdims=True)
        for tap in range(taps)
    ]
    ext_back[:8, :] = jnp.zeros((8, HEAD_DIM), jnp.float32)
    ext_back[8 : 8 + length, :] = d_conv
    ext_back[8 + length :, :] = jnp.zeros((8, HEAD_DIM), jnp.float32)
    own = jnp.zeros((length, HEAD_DIM), jnp.float32)
    before = jnp.zeros((8, HEAD_DIM), jnp.float32)
    for tap in range(taps):
        shift = taps - 1 - tap
        own = own + weight[tap : tap + 1, :] * ext_back[8 + shift : 8 + shift + length, :]
        before = before + weight[tap : tap + 1, :] * ext_back[shift : shift + 8, :]
    return own, before, jnp.concatenate(rows, 0)


def mixer_local_kernel(per_step, taps, *refs):
    pres, rims, weights = refs[:3], refs[3:6], refs[6:9]
    logit, logit_t, live, live_t = refs[9:13]
    q_out, k_out, v_out, wy_out, inv_out, mix_out, end_out, ext = refs[13:]
    found = local_part(
        pres, rims, weights, logit[...], logit_t[...], live[...], live_t[...], ext,
        pl.program_id(0) * per_step, taps,
    )
    for i, (q, k, v, wy, inverse, mix, ends) in enumerate(found):
        span = slice(i * HEAD_DIM, (i + 1) * HEAD_DIM)
        q_out[:, span] = q
        k_out[:, span] = k
        v_out[:, span] = v
        wy_out[i] = wy
        inv_out[i] = inverse
        mix_out[i] = mix
        end_out[i] = ends


def mixer_finish_kernel(per_step, mix, state, gain, mixed_out, head_out):
    for i in range(per_step):
        span = slice(i * HEAD_DIM, (i + 1) * HEAD_DIM)
        mixed_out[:, span], head_out[:, span] = finish_part(mix[i], state[i], gain[...])


def mixer_back_local_kernel(
    per_step, d_head, mixed_ref, gain_ref, q_ref, k_ref, wy,
    d_mixed_out, d_fresh_out, end_out, gain_out,
):
    gain_total = jnp.zeros((1, HEAD_DIM), jnp.float32)
    for i in range(per_step):
        d_out, mixed, q, k = head_columns((d_head, mixed_ref, q_ref, k_ref), i)
        d_mixed_out[i], d_fresh_out[i], end_out[i], gain_row = back_local_part(
            d_out, mixed, gain_ref[...], q, k, wy[i]
        )
        gain_total += gain_row

    @pl.when(pl.program_id(0) == 0)
    def _():
        gain_out[...] = jnp.zeros_like(gain_out)

    gain_out[...] += jnp.broadcast_to(gain_total, gain_out.shape)


def mixer_back_kernel(per_step, taps, *refs):
    pre_refs, rim_refs, weight_refs, (logit, live) = refs[:3], refs[3:6], refs[6:9], refs[9:11]
    (q_ref, k_ref, v_ref, wy, inv, state, d_mixed_ref, d_fresh_ref, d_state) = refs[11:20]
    d_q_out, d_k_out, d_v_out, tail_out, rim_out, conv_out, d_logit_out, ext, ext_back = refs[20:]
    length = live.shape[0]
    step = pl.program_id(0)

    @pl.when(step == 0)
    def _():
        d_logit_out[...] = jnp.zeros_like(d_logit_out)

    for i in range(per_step):
        q, k, v = head_columns((q_ref, k_ref, v_ref), i)
        *grads, d_logit = back_part(
            q, k, v, wy[i], inv[i], state[i], d_state[i], d_mixed_ref[i], d_fresh_ref[i],
            column_of(logit[...], step * per_step + i), live[...],
        )
        lane = lax.broadcasted_iota(jnp.int32, d_logit_out.shape, 1)
        d_logit_out[...] += jnp.where(lane == step * per_step + i, d_logit, 0.0)
        span = slice(i * HEAD_DIM, (i + 1) * HEAD_DIM)
        outs = (d_q_out, d_k_out, d_v_out)
        for part in range(3):
            own, before, rows = back_conv_part(
                part, pre_refs[part][:, span], rim_refs[part][:, span],
                weight_refs[part][:, span], grads[part], taps, ext, ext_back,
            )
            conv_out[part, :, span] = rows
            outs[part][:, span] = own.astype(jnp.bfloat16)
            tail_out[part, :, span] = own[length - 8 :, :]
            rim_out[part, :, span] = before


def mixer_specs(length, heads, per_step):
    width = per_step * HEAD_DIM

    def flat(rows):
        return pl.BlockSpec((rows, width), lambda h: (0, h))

    def whole(*shape):
        return pl.BlockSpec(shape, lambda h: (0,) * len(shape))

    def by_head(*shape):
        return pl.BlockSpec((per_step,) + shape, lambda h: (h,) + (0,) * len(shape))

    return flat, whole, by_head


def mixer_call(kernel, heads, per_step, ins, outs, scratch, flops, args):
    moved = sum(a.size * a.dtype.itemsize for a in args)
    return pl.pallas_call(
        kernel,
        grid=(heads // per_step,),
        in_specs=ins,
        out_specs=[spec for spec, _ in outs],
        out_shape=[shape for _, shape in outs],
        scratch_shapes=scratch,
        compiler_params=pltpu.CompilerParams(vmem_limit_bytes=VMEM),
        cost_estimate=SHORT,
    )(*args)


def f32(*shape):
    return jax.ShapeDtypeStruct(shape, jnp.float32)


def b16(*shape):
    return jax.ShapeDtypeStruct(shape, jnp.bfloat16)


def mixer_local(pres, rims, convs, logit, live, per_step):
    length, channels = pres[0].shape
    heads = channels // HEAD_DIM
    taps = convs[0].shape[0]
    flat, whole, by_head = mixer_specs(length, heads, per_step)
    args = (*pres, *rims, *convs, logit, logit.T, live, live.T)
    return mixer_call(
        functools.partial(mixer_local_kernel, per_step, taps),
        heads,
        per_step,
        [flat(length)] * 3
        + [flat(RIM)] * 3
        + [flat(taps)] * 3
        + [whole(length, heads), whole(heads, length), whole(length, 1), whole(1, length)],
        [(flat(length), b16(length, channels))] * 3
        + [
            (by_head(length, 2 * HEAD_DIM), f32(heads, length, 2 * HEAD_DIM)),
            (by_head(length, length), f32(heads, length, length)),
            (by_head(length, 2 * HEAD_DIM), f32(heads, length, 2 * HEAD_DIM)),
            (by_head(HEAD_DIM, 2 * HEAD_DIM), f32(heads, HEAD_DIM, 2 * HEAD_DIM)),
        ],
        [pltpu.VMEM((RIM + length, HEAD_DIM), jnp.float32)],
        heads * 2 * length**3 * 30,
        args,
    )


def mixer_finish(mix, state, gain, per_step):
    heads, length, _ = mix.shape
    flat, whole, by_head = mixer_specs(length, heads, per_step)
    return mixer_call(
        functools.partial(mixer_finish_kernel, per_step),
        heads,
        per_step,
        [by_head(length, 2 * HEAD_DIM), by_head(HEAD_DIM, HEAD_DIM), whole(1, HEAD_DIM)],
        [
            (flat(length), f32(length, heads * HEAD_DIM)),
            (flat(length), b16(length, heads * HEAD_DIM)),
        ],
        [],
        heads * 2 * length**3,
        (mix, state, gain),
    )


def mixer_back_local(d_head, mixed, gain, q, k, wy, per_step):
    heads, length, _ = wy.shape
    flat, whole, by_head = mixer_specs(length, heads, per_step)
    return mixer_call(
        functools.partial(mixer_back_local_kernel, per_step),
        heads,
        per_step,
        [flat(length)] * 2 + [whole(1, HEAD_DIM)] + [flat(length)] * 2 + [by_head(length, 2 * HEAD_DIM)],
        [
            (by_head(length, HEAD_DIM), f32(heads, length, HEAD_DIM)),
            (by_head(length, HEAD_DIM), f32(heads, length, HEAD_DIM)),
            (by_head(HEAD_DIM, HEAD_DIM), f32(heads, HEAD_DIM, HEAD_DIM)),
            (whole(8, HEAD_DIM), f32(8, HEAD_DIM)),
        ],
        [],
        heads * 2 * length**3 * 5,
        (d_head, mixed, gain, q, k, wy),
    )


def mixer_back(pres, rims, convs, logit, live, q, k, v, wy, inv, state, d_mixed, d_fresh, d_state, per_step):
    length, channels = pres[0].shape
    heads = channels // HEAD_DIM
    taps = convs[0].shape[0]
    flat, whole, by_head = mixer_specs(length, heads, per_step)
    three = pl.BlockSpec((3, 8, per_step * HEAD_DIM), lambda h: (0, 0, h))
    return mixer_call(
        functools.partial(mixer_back_kernel, per_step, taps),
        heads,
        per_step,
        [flat(length)] * 3
        + [flat(RIM)] * 3
        + [flat(taps)] * 3
        + [whole(length, heads), whole(length, 1)]
        + [flat(length)] * 3
        + [
            by_head(length, 2 * HEAD_DIM),
            by_head(length, length),
            by_head(HEAD_DIM, HEAD_DIM),
            by_head(length, HEAD_DIM),
            by_head(length, HEAD_DIM),
            by_head(HEAD_DIM, HEAD_DIM),
        ],
        [(flat(length), b16(length, channels))] * 3
        + [
            (three, f32(3, 8, channels)),
            (three, f32(3, 8, channels)),
            (
                pl.BlockSpec((3, taps, per_step * HEAD_DIM), lambda h: (0, 0, h)),
                f32(3, taps, channels),
            ),
            (whole(length, heads), f32(length, heads)),
        ],
        [
            pltpu.VMEM((RIM + length, HEAD_DIM), jnp.float32),
            pltpu.VMEM((16 + length, HEAD_DIM), jnp.float32),
        ],
        heads * 2 * length**3 * 20,
        (*pres, *rims, *convs, logit, live, q, k, v, wy, inv, state, d_mixed, d_fresh, d_state),
    )


def mixer_forward_kernel(per_step, taps, spans, *refs):
    pres, weights = refs[:3], refs[3:6]
    logit, logit_t, live, live_t, gain = refs[6:11]
    sources = refs[11:14]
    q_out, k_out, v_out, wy_out, inv_out, end_out, mixed_out, head_out, state_out, rim_out = refs[
        14:24
    ]
    ext, mix_all, rims, arriving, leaving, sends, receives, rim_sends, rim_receives = refs[24:]
    step = pl.program_id(0)
    position = lax.axis_index("seq")
    pairs = arriving.shape[0]
    length = live.shape[0]
    width = per_step * HEAD_DIM
    last = spans - 1
    after = place("seq", position + 1)

    def rim_copy(part):
        return pltpu.make_async_remote_copy(
            src_ref=sources[part].at[length - RIM :, :],
            dst_ref=rims.at[part],
            send_sem=rim_sends.at[part],
            recv_sem=rim_receives.at[part],
            device_id=after,
            device_id_type=MESH,
        )

    def state_copy(pair):
        return pltpu.make_async_remote_copy(
            src_ref=leaving.at[pair],
            dst_ref=arriving.at[pair],
            send_sem=sends.at[pair],
            recv_sem=receives.at[pair],
            device_id=after,
            device_id_type=MESH,
        )

    @pl.when(step == 0)
    def _():
        meet([place("seq", (position + last) % spans), place("seq", (position + 1) % spans)])

        @pl.when(position != last)
        def _():
            for part in range(3):
                rim_copy(part).start()

        @pl.when(position == 0)
        def _():
            rims[...] = jnp.zeros_like(rims)
            arriving[...] = jnp.zeros_like(arriving)

        @pl.when(position != 0)
        def _():
            for part in range(3):
                rim_copy(part).wait_recv()

        rim_out[...] = rims[...]

    @pl.when(step < pairs)
    def _():
        here = pl.ds(pl.multiple_of(step * width, width), width)
        found = local_part(
            pres, [rims[part, :, here] for part in range(3)], weights, logit[...], logit_t[...],
            live[...], live_t[...], ext, step * per_step, taps,
        )
        for i, (q, k, v, wy, inverse, mix, ends) in enumerate(found):
            span = slice(i * HEAD_DIM, (i + 1) * HEAD_DIM)
            q_out[:, span] = q
            k_out[:, span] = k
            v_out[:, span] = v
            wy_out[i] = wy
            inv_out[i] = inverse
            mix_all[step * per_step + i] = mix
            end_out[step * per_step + i] = ends

    pair = step - position

    @pl.when((pair >= 0) & (pair < pairs))
    def _():
        @pl.when(position != 0)
        def _():
            state_copy(pair).wait_recv()

        for i in range(per_step):
            ends = end_out[pair * per_step + i]
            moved = dot_left(ends[:, :HEAD_DIM], arriving[pair, i])
            leaving[pair, i] = (moved + ends[:, HEAD_DIM:]).astype(jnp.bfloat16)

        @pl.when(position != last)
        def _():
            state_copy(pair).start()

        for i in range(per_step):
            here = pl.ds(pl.multiple_of(pair * width + i * HEAD_DIM, HEAD_DIM), HEAD_DIM)
            state = arriving[pair, i]
            state_out[pair * per_step + i] = state
            mixed, head = finish_part(mix_all[pair * per_step + i], state, gain[...])
            mixed_out[:, here] = mixed
            head_out[:, here] = head

    @pl.when((step == pl.num_programs(0) - 1) & (position != last))
    def _():
        for part in range(3):
            rim_copy(part).wait_send()
        for index in range(pairs):
            state_copy(index).wait_send()


def mixer_forward(pres, convs, logit, logit_t, live, gain, per_step, spans, number):
    length, channels = pres[0].shape
    heads = channels // HEAD_DIM
    pairs = heads // per_step
    taps = convs[0].shape[0]
    width = per_step * HEAD_DIM
    wide = (heads, length, 2 * HEAD_DIM)
    states = (heads, HEAD_DIM, HEAD_DIM)

    def at(step):
        return jnp.minimum(step, pairs - 1)

    def flat(rows):
        return pl.BlockSpec((rows, width), lambda s: (0, at(s)))

    def by_head(*shape):
        return pl.BlockSpec((per_step,) + shape, lambda s: (at(s),) + (0,) * len(shape))

    def whole(*shape):
        return pl.BlockSpec(shape, lambda s: (0,) * len(shape))

    anywhere = pl.BlockSpec(memory_space=pl.ANY)
    return pl.pallas_call(
        functools.partial(mixer_forward_kernel, per_step, taps, spans),
        grid=(pairs + spans - 1,),
        in_specs=[flat(length)] * 3
        + [flat(taps)] * 3
        + [whole(length, heads), whole(heads, length), whole(length, 1), whole(1, length)]
        + [whole(1, HEAD_DIM)]
        + [anywhere] * 3,
        out_specs=[flat(length)] * 3
        + [
            by_head(length, 2 * HEAD_DIM),
            by_head(length, length),
            whole(heads, HEAD_DIM, 2 * HEAD_DIM),
            whole(length, channels),
            whole(length, channels),
            whole(*states),
            whole(3, RIM, channels),
        ],
        out_shape=[b16(length, channels)] * 3
        + [
            f32(*wide),
            f32(heads, length, length),
            f32(heads, HEAD_DIM, 2 * HEAD_DIM),
            f32(length, channels),
            b16(length, channels),
            b16(*states),
            b16(3, RIM, channels),
        ],
        scratch_shapes=[
            pltpu.VMEM((RIM + length, HEAD_DIM), jnp.float32),
            pltpu.VMEM(wide, jnp.float32),
            pltpu.VMEM((3, RIM, channels), jnp.bfloat16),
            pltpu.VMEM((pairs, per_step, HEAD_DIM, HEAD_DIM), jnp.bfloat16),
            pltpu.VMEM((pairs, per_step, HEAD_DIM, HEAD_DIM), jnp.bfloat16),
            pltpu.SemaphoreType.DMA((pairs,)),
            pltpu.SemaphoreType.DMA((pairs,)),
            pltpu.SemaphoreType.DMA((3,)),
            pltpu.SemaphoreType.DMA((3,)),
        ],
        compiler_params=pltpu.CompilerParams(
            collective_id=number, has_side_effects=True, vmem_limit_bytes=VMEM
        ),
        cost_estimate=SHORT,
    )(*pres, *convs, logit, logit_t, live, live.T, gain, *pres)


def mixer_backward_kernel(per_step, taps, spans, ways, tokens, *refs):
    d_head, mixed_ref, q_one, k_one, wy_one, gain = refs[:6]
    pres, weights = refs[6:9], refs[9:12]
    q_ref, k_ref, v_ref, wy, inv = refs[12:17]
    logit, live, state, ends, rims = refs[17:22]
    head_source, residual, up_source = refs[22 + tokens : 25 + tokens]
    d_q_out, d_k_out, d_v_out, conv_out, d_logit_out, gain_out = refs[25 + tokens : 31 + tokens]
    head_others, res_others, up_others = refs[31 + tokens : 34 + tokens]
    (
        d_mixed_all, d_fresh_all, d_end_all, arriving, sending, tails, rim_out, rim_in,
        ext, ext_back, sends, receives, rim_sends, rim_receives,
    ) = refs[34 + tokens : 48 + tokens]
    col_sends, col_receives, up_sends, up_receives, *half_sems = refs[48 + tokens :]
    halves = Halves(ways, residual, res_others, *half_sems)
    columns = row_copies(ways, (2, 3), up_source, up_others, up_sends, up_receives)
    columns += column_copies(ways, head_source, head_others, col_sends, col_receives)
    step = pl.program_id(0)
    position = lax.axis_index("seq")
    pairs = arriving.shape[0]
    length = live.shape[0]
    last = spans - 1
    before_here = place("seq", position - 1)

    def state_copy(pair):
        return pltpu.make_async_remote_copy(
            src_ref=sending.at[pair],
            dst_ref=arriving.at[pair],
            send_sem=sends.at[pair],
            recv_sem=receives.at[pair],
            device_id=before_here,
            device_id_type=MESH,
        )

    def rim_copy():
        return pltpu.make_async_remote_copy(
            src_ref=rim_out,
            dst_ref=rim_in,
            send_sem=rim_sends.at[0],
            recv_sem=rim_receives.at[0],
            device_id=before_here,
            device_id_type=MESH,
        )

    @pl.when(step == 0)
    def _():
        meet(
            [place("seq", (position + last) % spans), place("seq", (position + 1) % spans)]
            + halves.devices()
        )
        for copy in columns:
            copy.start()
        halves.start()
        d_logit_out[...] = jnp.zeros_like(d_logit_out)
        gain_out[...] = jnp.zeros_like(gain_out)

        @pl.when(position == last)
        def _():
            arriving[...] = jnp.zeros_like(arriving)
            rim_in[...] = jnp.zeros_like(rim_in)

    @pl.when(step < pairs)
    def _():
        for i in range(per_step):
            d_out, mixed, q, k = head_columns((d_head, mixed_ref, q_one, k_one), i)
            d_mixed, d_fresh, d_end, gain_row = back_local_part(
                d_out, mixed, gain[...], q, k, wy_one[i]
            )
            d_mixed_all[step * per_step + i] = d_mixed
            d_fresh_all[step * per_step + i] = d_fresh
            d_end_all[step * per_step + i] = d_end
            gain_out[...] += jnp.broadcast_to(gain_row, gain_out.shape)

    pair = step - (last - position)

    @pl.when((pair >= 0) & (pair < pairs))
    def _():
        @pl.when(position != last)
        def _():
            state_copy(pair).wait_recv()

        for i in range(per_step):
            head = pair * per_step + i
            moved = dot_left(ends[head, :, :HEAD_DIM], arriving[pair, i], (0, 0))
            sending[pair, i] = (moved + d_end_all[head]).astype(jnp.bfloat16)

        @pl.when(position != 0)
        def _():
            state_copy(pair).start()

    ready = step - last

    @pl.when(ready >= 0)
    def _():
        outs = (d_q_out, d_k_out, d_v_out)
        for i in range(per_step):
            head = ready * per_step + i
            here = pl.ds(pl.multiple_of(head * HEAD_DIM, HEAD_DIM), HEAD_DIM)
            q, k, v = head_columns((q_ref, k_ref, v_ref), i)
            *grads, d_logit = back_part(
                q, k, v, wy[i], inv[i], state[head], arriving[ready, i],
                d_mixed_all[head], d_fresh_all[head], column_of(logit[...], head), live[...],
            )
            lane = lax.broadcasted_iota(jnp.int32, d_logit_out.shape, 1)
            d_logit_out[...] += jnp.where(lane == head, d_logit, 0.0)
            span = slice(i * HEAD_DIM, (i + 1) * HEAD_DIM)
            for part in range(3):
                own, before, rows = back_conv_part(
                    part, pres[part][:, span], rims[part, :, here],
                    weights[part][:, span], grads[part], taps, ext, ext_back,
                )
                conv_out[part, :, here] = rows
                outs[part][:, here] = own.astype(jnp.bfloat16)
                tails[part, :, here] = own[length - 16 :, :]
                rim_out[part, :, here] = before

    @pl.when(step == pl.num_programs(0) - 1)
    def _():
        @pl.when(position != 0)
        def _():
            rim_copy().start()

        halves.hand_on()

        @pl.when(position != last)
        def _():
            rim_copy().wait_recv()

        for part, out in enumerate((d_q_out, d_k_out, d_v_out)):
            joined = tails[part] + jnp.concatenate(
                [jnp.zeros_like(rim_in[part]), rim_in[part]], 0
            )
            out[length - 16 :, :] = joined.astype(jnp.bfloat16)

        @pl.when(position != 0)
        def _():
            rim_copy().wait_send()
            for index in range(pairs):
                state_copy(index).wait_send()

        for copy in columns:
            copy.wait()
        halves.finish()


def mixer_backward(
    d_head, mixed, gain, pres, rims, convs, logit, live, q, k, v, wy, inv, state, ends, tokens,
    head_out, residual, turned, per_step, spans, ways, number,
):
    length, channels = pres[0].shape
    heads = channels // HEAD_DIM
    pairs = heads // per_step
    taps = convs[0].shape[0]
    width = per_step * HEAD_DIM
    lag = spans - 1

    def early(step):
        return jnp.minimum(step, pairs - 1)

    def late(step):
        return jnp.maximum(step - lag, 0)

    def flat(rows, at):
        return pl.BlockSpec((rows, width), lambda s: (0, at(s)))

    def by_head(at, *shape):
        return pl.BlockSpec((per_step,) + shape, lambda s: (at(s),) + (0,) * len(shape))

    def whole(*shape):
        return pl.BlockSpec(shape, lambda s: (0,) * len(shape))

    wide = (length, 2 * HEAD_DIM)
    states = (pairs, per_step, HEAD_DIM, HEAD_DIM)
    return pl.pallas_call(
        functools.partial(mixer_backward_kernel, per_step, taps, spans, ways, len(tokens)),
        grid=(pairs + lag,),
        in_specs=[flat(length, early)] * 4
        + [by_head(early, *wide), whole(1, HEAD_DIM)]
        + [flat(length, late)] * 3
        + [flat(taps, late)] * 3
        + [flat(length, late)] * 3
        + [by_head(late, *wide), by_head(late, length, length)]
        + [whole(length, heads), whole(length, 1), whole(heads, HEAD_DIM, HEAD_DIM)]
        + [whole(heads, HEAD_DIM, 2 * HEAD_DIM), whole(3, RIM, channels)]
        + [pl.BlockSpec(memory_space=pl.ANY)] * (len(tokens) + 3),
        out_specs=[whole(length, channels)] * 3
        + [whole(3, taps, channels), whole(length, heads), whole(8, HEAD_DIM)]
        + [pl.BlockSpec(memory_space=pl.ANY)] * 3,
        out_shape=[b16(length, channels)] * 3
        + [f32(3, taps, channels), f32(length, heads), f32(8, HEAD_DIM)]
        + [b16(ways - 1, length, channels // ways)]
        + [b16(ways - 1, *residual.shape), b16(ways - 1, 1, *turned.shape[2:])],
        scratch_shapes=[
            pltpu.VMEM((heads, length, HEAD_DIM), jnp.float32),
            pltpu.VMEM((heads, length, HEAD_DIM), jnp.float32),
            pltpu.VMEM((heads, HEAD_DIM, HEAD_DIM), jnp.float32),
            pltpu.VMEM(states, jnp.bfloat16),
            pltpu.VMEM(states, jnp.bfloat16),
            pltpu.VMEM((3, 16, channels), jnp.float32),
            pltpu.VMEM((3, 8, channels), jnp.float32),
            pltpu.VMEM((3, 8, channels), jnp.float32),
            pltpu.VMEM((RIM + length, HEAD_DIM), jnp.float32),
            pltpu.VMEM((16 + length, HEAD_DIM), jnp.float32),
            pltpu.SemaphoreType.DMA((pairs,)),
            pltpu.SemaphoreType.DMA((pairs,)),
            pltpu.SemaphoreType.DMA((1,)),
            pltpu.SemaphoreType.DMA((1,)),
        ]
        + [pltpu.SemaphoreType.DMA((ways - 1,))] * 8,
        compiler_params=pltpu.CompilerParams(
            collective_id=number, has_side_effects=True, vmem_limit_bytes=VMEM
        ),
        cost_estimate=SHORT,
    )(
        d_head, mixed, q, k, wy, gain, *pres, *convs, q, k, v, wy, inv, logit, live, state, ends,
        rims, *tokens, head_out, residual, turned,
    )


def feed_kernel(
    x_ref, d_ref, gate_w, up_w, down_w, token, feed_out, d_x_out, turned_out, feed_sum, d_x_sum
):
    step = pl.program_id(0)
    x = x_ref[...]
    d_out = d_ref[...]
    gate = dot_low(x, gate_w[...])
    up = dot_low(x, up_w[...])
    d_hidden = dot_low(d_out, down_w[...], (1, 1))
    sig = jax.nn.sigmoid(gate)
    hidden = (gate * sig * up).astype(jnp.bfloat16)
    d_gate = (d_hidden * up * sig * (1.0 + gate * (1.0 - sig))).astype(jnp.bfloat16)
    d_up = (d_hidden * gate * sig).astype(jnp.bfloat16)
    for place, part in enumerate((hidden, d_gate, d_up)):
        turned_out[place] = part.T
    feed = dot_low(hidden, down_w[...])
    d_x = dot_low(d_gate, gate_w[...], (1, 1)) + dot_low(d_up, up_w[...], (1, 1))

    @pl.when(step == 0)
    def _():
        feed_sum[...] = feed
        d_x_sum[...] = d_x

    @pl.when(step > 0)
    def _():
        feed_sum[...] += feed
        d_x_sum[...] += d_x

    @pl.when(step == pl.num_programs(0) - 1)
    def _():
        feed_out[...] = feed_sum[...].astype(jnp.bfloat16)
        d_x_out[...] = d_x_sum[...].astype(jnp.bfloat16)


def feed_forward(x, d_out, gate_weight, up_weight, down_weight, token):
    length, width = x.shape
    units = gate_weight.shape[1]
    tile = 256 if units % 256 == 0 else units
    whole = pl.BlockSpec((length, width), lambda f: (0, 0))
    column = pl.BlockSpec((width, tile), lambda f: (0, f))
    return pl.pallas_call(
        feed_kernel,
        grid=(units // tile,),
        in_specs=[whole, whole, column, column]
        + [pl.BlockSpec((tile, width), lambda f: (f, 0)), pl.BlockSpec(memory_space=pl.ANY)],
        out_specs=[whole, whole, pl.BlockSpec((3, tile, length), lambda f: (0, f, 0))],
        out_shape=[b16(length, width), b16(length, width), b16(3, units, length)],
        scratch_shapes=[pltpu.VMEM((length, width), jnp.float32)] * 2,
        compiler_params=pltpu.CompilerParams(vmem_limit_bytes=VMEM),
        cost_estimate=SHORT,
    )(x, d_out, gate_weight, up_weight, down_weight, token)


def back_projection_kernel(ways, *refs):
    sources, d_logit, weights, beta_w = refs[:3], refs[3], refs[4:7], refs[7]
    shared, out, others = refs[8:11], refs[-10], refs[-9:-6]
    sends, receives = refs[-6:-3], refs[-3:]
    step = pl.program_id(0)
    copies = [
        copy
        for part in range(3)
        for copy in column_copies(ways, shared[part], others[part], sends[part], receives[part])
    ]

    @pl.when(step == 0)
    def _():
        own = lax.axis_index("dp")
        meet([place("dp", partner(own, by)) for by in range(1, ways)])
        for copy in copies:
            copy.start()

    total = dot_low(d_logit[...], beta_w[...], (1, 1))
    for source, weight in zip(sources, weights):
        total = total + dot_low(source[...], weight[...], (1, 1))
    out[...] = total.astype(jnp.bfloat16)

    @pl.when(step == pl.num_programs(0) - 1)
    def _():
        for copy in copies:
            copy.wait()


def back_projection(sources, d_logit, weights, beta_weight, ways, tokens, number):
    length, channels = sources[0].shape
    width, heads = beta_weight.shape
    tile = width // 4
    anywhere = pl.BlockSpec(memory_space=pl.ANY)
    return pl.pallas_call(
        functools.partial(back_projection_kernel, ways),
        grid=(width // tile,),
        in_specs=[pl.BlockSpec((length, channels), lambda n: (0, 0))] * 3
        + [pl.BlockSpec((length, heads), lambda n: (0, 0))]
        + [pl.BlockSpec((tile, channels), lambda n: (n, 0))] * 3
        + [pl.BlockSpec((tile, heads), lambda n: (n, 0))]
        + [anywhere] * (3 + len(tokens)),
        out_specs=[pl.BlockSpec((length, tile), lambda n: (0, n))] + [anywhere] * 3,
        out_shape=[b16(length, width)] + [b16(ways - 1, length, channels // ways)] * 3,
        scratch_shapes=[pltpu.SemaphoreType.DMA((ways - 1,))] * 6,
        compiler_params=pltpu.CompilerParams(
            collective_id=number, has_side_effects=True, vmem_limit_bytes=VMEM
        ),
        cost_estimate=SHORT,
    )(*sources, d_logit, *weights, beta_weight, *sources, *tokens)


def project_kernel(tokens, both_gains, q_w, k_w, v_w, beta_w, *refs):
    q_out, k_out, v_out, logit_out, logit_t_out, stream_out, normed_out, half_out, gains_out = refs[
        :9
    ]
    arriving, gains, gains_in, sends, receives = refs[9:]
    step = pl.program_id(0)
    half = tokens.shape[1]

    @pl.when(step == 0)
    def _():
        core = lax.axis_index("head")
        other = place("head", 1 - core)
        mine = pl.ds(pl.multiple_of(core * half, half), half)
        theirs = pl.ds(pl.multiple_of((1 - core) * half, half), half)
        row = lax.broadcasted_iota(jnp.int32, gains.shape, 0)
        both = both_gains[...].astype(jnp.float32)
        gains[...] = jnp.where(row == 0, both[0:1], both[1:2]).astype(jnp.bfloat16)
        meet([other])
        copies = [
            pltpu.make_async_remote_copy(
                src_ref=source, dst_ref=target, send_sem=sends.at[index],
                recv_sem=receives.at[index], device_id=other, device_id_type=MESH,
            )
            for index, (source, target) in enumerate(((tokens, arriving), (gains, gains_in)))
        ]
        for copy in copies:
            copy.start()
        stream_out[:, mine] = tokens[...]
        gains_out[:, mine] = gains[...]
        for copy in copies:
            copy.wait()
        stream_out[:, theirs] = arriving[...]
        gains_out[:, theirs] = gains_in[...]
        stream = stream_out[...].astype(jnp.float32)
        scale = lax.rsqrt(jnp.mean(stream * stream, axis=-1, keepdims=True) + EPSILON)
        gain = gains_out[...].astype(jnp.float32)[0:1]
        normed_out[...] = (stream * scale * gain).astype(jnp.bfloat16)
        half_out[...] = normed_out[:, mine]
        logit_out[...] = dot_low(normed_out[...], beta_w[...], (1, 1))
        logit_t_out[...] = dot_low(beta_w[...], normed_out[...], (1, 1))

    for part, (weight, out) in enumerate(((q_w, q_out), (k_w, k_out), (v_w, v_out))):

        @pl.when(step // 2 == part)
        def _():
            out[...] = dot_low(normed_out[...], weight[...]).astype(jnp.bfloat16)


def projected(tokens, first_gain, second_gain, weights, beta_weight, number):
    length, half = tokens.shape
    width, channels = weights[0].shape
    heads = beta_weight.shape[1]
    tile = channels // 2

    def whole(*shape):
        return pl.BlockSpec(shape, lambda s: (0,) * len(shape))

    def tiles(rows, part):
        return pl.BlockSpec((rows, tile), lambda s: (0, jnp.clip(s - 2 * part, 0, 1)))

    return pl.pallas_call(
        project_kernel,
        grid=(6,),
        in_specs=[whole(length, half), whole(2, half)]
        + [tiles(width, part) for part in range(3)]
        + [whole(heads, width)],
        out_specs=[tiles(length, part) for part in range(3)]
        + [whole(length, heads), whole(heads, length), whole(length, width)]
        + [whole(length, width), whole(length, half), whole(16, width)],
        out_shape=[b16(length, channels)] * 3
        + [f32(length, heads), f32(heads, length), b16(length, width)]
        + [b16(length, width), b16(length, half), b16(16, width)],
        scratch_shapes=[
            pltpu.VMEM((length, half), jnp.bfloat16),
            pltpu.VMEM((16, half), jnp.bfloat16),
            pltpu.VMEM((16, half), jnp.bfloat16),
            pltpu.SemaphoreType.DMA((2,)),
            pltpu.SemaphoreType.DMA((2,)),
        ],
        compiler_params=pltpu.CompilerParams(
            collective_id=number, has_side_effects=True, vmem_limit_bytes=VMEM
        ),
        cost_estimate=SHORT,
    )(tokens, jnp.stack([first_gain, second_gain]), *weights, beta_weight.T)


def units_kernel(
    head_ref, out_w, stream_ref, gains, d_ref, live, gate_w, up_w, down_w, token,
    turned_out, d_gate_out, d_up_out, hidden_out, stream_out, normed_out,
    part_low, arriving, sends, receives,
):
    @pl.when(pl.program_id(0) == 0)
    def _():
        other = place("head", 1 - lax.axis_index("head"))
        meet([other])
        pieces = part_low.shape[0]
        width = part_low.shape[2]
        copies = []
        for piece in range(pieces):
            span = slice(piece * width, (piece + 1) * width)
            part_low[piece] = dot_low(head_ref[...], out_w[:, span]).astype(jnp.bfloat16)
            copy = pltpu.make_async_remote_copy(
                src_ref=part_low.at[piece], dst_ref=arriving.at[piece],
                send_sem=sends.at[piece], recv_sem=receives.at[piece],
                device_id=other, device_id_type=MESH,
            )
            copy.start()
            copies.append(copy)
        squares = 0.0
        for piece, copy in enumerate(copies):
            span = slice(piece * width, (piece + 1) * width)
            copy.wait()
            both = part_low[piece].astype(jnp.float32) + arriving[piece].astype(jnp.float32)
            stream = stream_ref[:, span].astype(jnp.float32) + both
            stream_out[:, span] = stream
            squares = squares + jnp.sum(stream * stream, axis=-1, keepdims=True)
        scale = lax.rsqrt(squares / (pieces * width) + EPSILON)
        gain = gains[...].astype(jnp.float32)[1:2]
        normed_out[...] = (stream_out[...] * scale * gain).astype(jnp.bfloat16)

    x = normed_out[...]
    gate = dot_low(x, gate_w[...])
    up = dot_low(x, up_w[...])
    d_hidden = dot_low(d_ref[...], down_w[...], (1, 1))
    sig = jax.nn.sigmoid(gate)
    hidden = (gate * sig * up).astype(jnp.bfloat16)
    d_gate = (d_hidden * up * sig * (1.0 + gate * (1.0 - sig))).astype(jnp.bfloat16)
    d_up = (d_hidden * gate * sig).astype(jnp.bfloat16)
    for index, (part, out) in enumerate(
        ((hidden, hidden_out), (d_gate, d_gate_out), (d_up, d_up_out))
    ):
        out[...] = part
        if index == 0:
            part = (part.astype(jnp.float32) * live[...]).astype(jnp.bfloat16)
        turned_out[index] = part.T


def hidden_units(
    head_out, out_weight, stream, gains, d_out, live, gate_weight, up_weight, down_weight, token,
    number,
):
    length, width = stream.shape
    channels = head_out.shape[1]
    units = gate_weight.shape[1]
    tile = 256
    whole = pl.BlockSpec((length, width), lambda f: (0, 0))
    column = pl.BlockSpec((width, tile), lambda f: (0, f))
    flat = pl.BlockSpec((length, tile), lambda f: (0, f))
    return pl.pallas_call(
        units_kernel,
        grid=(units // tile,),
        in_specs=[
            pl.BlockSpec((length, channels), lambda f: (0, 0)),
            pl.BlockSpec((channels, width), lambda f: (0, 0)),
            whole,
            pl.BlockSpec((16, width), lambda f: (0, 0)),
            whole,
            pl.BlockSpec((length, 1), lambda f: (0, 0)),
            column,
            column,
        ]
        + [pl.BlockSpec((tile, width), lambda f: (f, 0)), pl.BlockSpec(memory_space=pl.ANY)],
        out_specs=[pl.BlockSpec((3, tile, length), lambda f: (0, f, 0))] + [flat] * 3 + [whole] * 2,
        out_shape=[b16(3, units, length)]
        + [b16(length, units)] * 3
        + [f32(length, width), b16(length, width)],
        scratch_shapes=[pltpu.VMEM((4, length, width // 4), jnp.bfloat16)] * 2
        + [pltpu.SemaphoreType.DMA((4,))] * 2,
        compiler_params=pltpu.CompilerParams(
            collective_id=number, has_side_effects=True, vmem_limit_bytes=VMEM
        ),
        cost_estimate=SHORT,
    )(
        head_out, out_weight, stream, gains, d_out, live, gate_weight, up_weight, down_weight,
        token,
    )


def row_copies(ways, entries, source, out, sends, receives):
    own = lax.axis_index("dp")
    copies = []
    for by in range(1, ways):
        peer = partner(own, by)
        copies.append(
            pltpu.make_async_remote_copy(
                src_ref=source.at[entries[0] : entries[1], peer],
                dst_ref=out.at[by - 1],
                send_sem=sends.at[by - 1],
                recv_sem=receives.at[by - 1],
                device_id=place("dp", peer),
                device_id_type=MESH,
            )
        )
    return copies


def rows_kernel(ways, entries, source, *refs):
    out, sends, receives = refs[-3:]
    own = lax.axis_index("dp")
    meet([place("dp", partner(own, by)) for by in range(1, ways)])
    copies = row_copies(ways, entries, source, out, sends, receives)
    for copy in copies:
        copy.start()
    for copy in copies:
        copy.wait()


def exchanged_rows(source, entries, tokens, number):
    ways = lax.axis_size("dp")
    anywhere = pl.BlockSpec(memory_space=pl.ANY)
    return pl.pallas_call(
        functools.partial(rows_kernel, ways, entries),
        out_shape=b16(ways - 1, entries[1] - entries[0], *source.shape[2:]),
        in_specs=[anywhere] * (1 + len(tokens)),
        out_specs=anywhere,
        scratch_shapes=[pltpu.SemaphoreType.DMA((ways - 1,))] * 2,
        compiler_params=pltpu.CompilerParams(
            collective_id=number, has_side_effects=True, vmem_limit_bytes=VMEM
        ),
        cost_estimate=SHORT,
    )(source, *tokens)


def feed_back_kernel(ways, entries, *refs):
    d_gate, d_up, hidden, gate_w, up_w, down_w, source, normed = refs[:8]
    d_x_out, feed_out, others, normed_others, sends, receives, *half_sems = refs[-10:]
    halves = Halves(ways, normed, normed_others, *half_sems)
    copies = row_copies(ways, entries, source, others, sends, receives)

    @pl.when(pl.program_id(0) == 0)
    def _():
        meet(halves.devices())
        halves.start()
        for copy in copies:
            copy.start()

    d_x = dot_low(d_gate[...], gate_w[...], (1, 1)) + dot_low(d_up[...], up_w[...], (1, 1))
    d_x_out[...] = d_x.astype(jnp.bfloat16)
    feed_out[...] = dot_low(hidden[...], down_w[...]).astype(jnp.bfloat16)

    @pl.when(pl.program_id(0) == pl.num_programs(0) - 1)
    def _():
        halves.hand_on()
        for copy in copies:
            copy.wait()
        halves.finish()


def feed_back(d_gate, d_up, hidden, weights, source, entries, normed, tokens, number):
    ways = lax.axis_size("dp")
    length, units = hidden.shape
    width = normed.shape[1]
    tile = width // 8
    anywhere = pl.BlockSpec(memory_space=pl.ANY)
    whole = pl.BlockSpec((length, units), lambda n: (0, 0))
    row = pl.BlockSpec((tile, units), lambda n: (n, 0))
    out = pl.BlockSpec((length, tile), lambda n: (0, n))
    return pl.pallas_call(
        functools.partial(feed_back_kernel, ways, entries),
        grid=(8,),
        in_specs=[whole] * 3
        + [row, row, pl.BlockSpec((units, tile), lambda n: (0, n))]
        + [anywhere] * (2 + len(tokens)),
        out_specs=[out, out, anywhere, anywhere],
        out_shape=[b16(length, width)] * 2
        + [
            b16(ways - 1, entries[1] - entries[0], *source.shape[2:]),
            b16(ways - 1, length, width),
        ],
        scratch_shapes=[pltpu.SemaphoreType.DMA((ways - 1,))] * 6,
        compiler_params=pltpu.CompilerParams(
            collective_id=number, has_side_effects=True, vmem_limit_bytes=VMEM
        ),
        cost_estimate=SHORT,
    )(d_gate, d_up, hidden, *weights, source, normed, *tokens)


def pieces_kernel(groups, slots, ways, turned, at, *refs):
    lefts = refs[: groups * slots]
    rights = refs[groups * slots : (groups + ways) * slots]
    out, left_all, right_all = refs[-3:]
    length = rights[0].shape[-2]
    rows = rights[0].shape[-1]
    count = left_all.shape[0] // groups

    @pl.when(pl.program_id(0) == 0)
    def _():
        for group in range(groups):
            for slot in range(slots):
                block = lefts[group * slots + slot][...]
                block = block.reshape(block.shape[-2:])
                left_all[
                    group * count : (group + 1) * count, slot * length : (slot + 1) * length
                ] = block if turned else block.T

    for slot in range(slots):
        for way in range(ways):
            right = rights[slot * ways + way][...]
            right_all[
                slot * length : (slot + 1) * length, way * rows : (way + 1) * rows
            ] = right.reshape(right.shape[-2:])
    out[0] = dot_low(left_all[...], right_all[...]).astype(jnp.bfloat16)


def span_pieces(lefts, count, rights, length, width, spans, turned, tokens=()):
    groups = len(lefts)
    lefts = [left for group in lefts for left in group]
    slots = len(rights)
    ways = lax.axis_size("dp")
    rows = width // (ways * spans)

    def left_block(block, at_place):
        return pl.BlockSpec(block, lambda s, at: at_place(at[0]))

    def right_block(block, at_place, column):
        return pl.BlockSpec(
            block + (rows,), lambda s, at: tuple(at_place(at[0])) + (column(s),)
        )

    rights = [right for slot in rights for right in slot]

    return pl.pallas_call(
        functools.partial(pieces_kernel, groups, slots, ways, turned),
        grid_spec=pltpu.PrefetchScalarGridSpec(
            num_scalar_prefetch=1,
            grid=(spans,),
            in_specs=[left_block(block, where) for _, block, where in lefts]
            + [right_block(block, where, column) for _, block, where, column in rights]
            + [pl.BlockSpec(memory_space=pl.ANY)] * len(tokens),
            out_specs=pl.BlockSpec((1, count, ways * rows), lambda s, at: (s, 0, 0)),
            scratch_shapes=[
                pltpu.VMEM((count, slots * length), jnp.bfloat16),
                pltpu.VMEM((slots * length, ways * rows), jnp.bfloat16),
            ],
        ),
        out_shape=b16(spans, count, ways * rows),
        compiler_params=pltpu.CompilerParams(vmem_limit_bytes=VMEM),
        cost_estimate=SHORT,
    )(
        lax.axis_index("dp")[None],
        *[array for array, _, _ in lefts],
        *[array for array, _, _, _ in rights],
        *tokens,
    )


def widen_kernel(count, turned, starts, share_of, *refs):
    small = refs[count]
    outs = refs[count + 1 :]
    for index in range(count):
        whole = refs[index][...].astype(jnp.float32)
        outs[index][...] = whole.T if turned[index] else whole
    gain, first, second, taps, beta = outs[count], *outs[count + 1 : count + 3], outs[count + 3 : -1], outs[-1]
    gain[...] = small[starts[0] : starts[0] + 1, :]
    first[...] = small[starts[1] : starts[1] + first.shape[0], :]
    second[...] = small[starts[2] : starts[2] + second.shape[0], :]
    row = starts[3]
    for out in taps:
        high, wide = out.shape
        for tap in range(high):
            for lane in range(wide // 128):
                out[tap : tap + 1, lane * 128 : (lane + 1) * 128] = small[row : row + 1, :]
                row += 1
    heads = beta.shape[1]
    width = share_of[1] // 128
    share = lax.axis_index("dp") * share_of[0] + lax.axis_index("seq")
    rows = [small[pl.ds(starts[4] + head * width + share, 1), :] for head in range(heads)]
    beta[...] = jnp.concatenate(rows, 0).T


def widened(arrays, turned, small, starts, channels, taps, heads, width):
    inside = pl.BlockSpec(memory_space=pltpu.VMEM)
    shapes = [
        f32(*(array.shape[::-1] if turn else array.shape)) for array, turn in zip(arrays, turned)
    ]
    shapes += [f32(1, 128), f32(width // 256, 128), f32(width // 256, 128)]
    shapes += [f32(taps, channels)] * 3 + [f32(128, heads)]
    return pl.pallas_call(
        functools.partial(
            widen_kernel, len(arrays), turned, starts, (lax.axis_size("seq"), width)
        ),
        out_shape=shapes,
        in_specs=[inside] * (len(arrays) + 1),
        out_specs=[inside] * len(shapes),
        compiler_params=pltpu.CompilerParams(vmem_limit_bytes=VMEM),
        cost_estimate=SHORT,
    )(*arrays, small)


def doublings(size):
    return [1 << bit for bit in range(size.bit_length() - 1)]


def finish_kernel(spans, ways, fed, *refs):
    out_raw, mix_raw, small = refs[:3]
    pieces, refs = refs[3 : 3 + fed], refs[3 + fed :]
    stages, small_out, refs = refs[: 4 + fed], refs[4 + fed], refs[5 + fed :]
    received, handed, totals, *refs = refs
    sends, receives, owner_sends, owner_receives, own_sems = refs[:5]
    small_in, small_sent, small_sends, small_receives = refs[5:]
    own = lax.axis_index("dp")
    core = lax.axis_index("head")
    position = lax.axis_index("seq")
    last = spans - 1
    rounds = spans - 1
    count = out_raw.shape[1]
    groups = 1 + mix_raw.shape[1] // count
    rows = stages[0].shape[1]
    peers = [partner(own, by) for by in range(1, ways)]

    def raw_at(group, shard):
        if group == 0:
            return out_raw.at[shard]
        return mix_raw.at[shard, (group - 1) * count : group * count, :]

    def line_copy(way, turn, group, src):
        step = 1 if way == 0 else -1
        slot = (way * rounds + turn) * groups + group
        return pltpu.make_async_remote_copy(
            src_ref=src,
            dst_ref=received.at[way, turn, group],
            send_sem=sends.at[slot],
            recv_sem=receives.at[slot],
            device_id=place("seq", position + step),
            device_id_type=MESH,
        )

    def owner_copies(index, source):
        high = source.shape[0]
        turn = core * (ways // 2) if index == 0 or index > fed else 0

        def block_of(peer):
            start = ((peer + turn) % ways) * rows
            return source.at[:, pl.ds(pl.multiple_of(start, rows), rows)]

        stage = stages[index]
        mine = stage.at[pl.ds(pl.multiple_of(own * high, high), high), :]
        copies = []
        for by, peer in enumerate(peers):
            copies.append(
                pltpu.make_async_remote_copy(
                    src_ref=block_of(peer),
                    dst_ref=mine,
                    send_sem=owner_sends.at[index * (ways - 1) + by],
                    recv_sem=owner_receives.at[index * (ways - 1) + by],
                    device_id=place("dp", peer),
                    device_id_type=MESH,
                )
            )
        here = pltpu.make_async_copy(block_of(own), mine, own_sems.at[index])
        return copies + [here]

    partners = [place("dp", partner(own, by)) for by in doublings(ways)]
    partners += [place("seq", partner(position, by)) for by in doublings(spans)]
    partners += [place("head", 1 - lax.axis_index("head"))]

    def small_copy(turn):
        high = 8 if turn == len(partners) - 1 else small.shape[0]
        return pltpu.make_async_remote_copy(
            src_ref=small_sent.at[turn, :high, :],
            dst_ref=small_in.at[turn, :high, :],
            send_sem=small_sends.at[turn],
            recv_sem=small_receives.at[turn],
            device_id=partners[turn],
            device_id_type=MESH,
        )

    def small_turn(turn):
        if turn == 0:
            small_sent[0] = small[...]
        else:
            small_copy(turn - 1).wait_recv()
            if turn < len(partners):
                small_sent[turn] = small_sent[turn - 1] + small_in[turn - 1]
            else:
                small_out[...] = small_sent[turn - 1]
                small_out[:8, :] = small_sent[turn - 1, :8, :] + small_in[turn - 1, :8, :]
        if turn < len(partners):
            small_copy(turn).start()

    meet(
        [place("seq", (position + last) % spans), place("seq", (position + 1) % spans)]
        + [place("seq", partner(position, by)) for by in doublings(spans)[1:]]
        + [place("dp", peer) for peer in peers]
        + partners[-1:]
    )
    small_turn(0)
    along = (position, last - position)

    def source_send(way, index):
        turn, group = index // groups, index % groups
        shard = last - turn if way == 0 else turn
        if index >= 2:
            line_copy(way, (index - 2) // groups, (index - 2) % groups, totals.at[0]).wait_send()
        line_copy(way, turn, group, raw_at(group, shard)).start()

    for way in range(2):

        @pl.when(along[way] == 0)
        def _():
            for index in range(2):
                source_send(way, index)

    fed_copies = [owner_copies(index, piece) for index, piece in enumerate(pieces)]
    for copies in fed_copies:
        for copy in copies:
            copy.start()

    for way in range(2):

        @pl.when(along[way] == 0)
        def _():
            for index in range(2, groups + 2):
                source_send(way, index)

    at_end = (position == 0) | (position == last)

    def finish(group):
        for way in range(2):

            @pl.when(along[way] >= 1)
            def _():
                line_copy(way, rounds - 1, group, totals.at[group]).wait_recv()

        total = raw_at(group, position)[...].astype(jnp.float32)
        for way in range(2):
            arrived = received[way, rounds - 1, group].astype(jnp.float32)
            total = total + jnp.where(along[way] >= 1, arrived, 0.0)
        totals[group] = total.astype(jnp.bfloat16)
        for copy in owner_copies(fed + group, totals.at[group]):
            copy.start()

    for turn in range(1, rounds):
        for group in range(groups):
            for way in range(2):
                if turn * groups + group + 2 < rounds * groups:

                    @pl.when(along[way] == 0)
                    def _():
                        source_send(way, turn * groups + group + 2)

                shard = last - turn + position if way == 0 else turn - along[1]

                @pl.when((along[way] >= 1) & (along[way] <= turn))
                def _():
                    line_copy(way, turn - 1, group, handed.at[way, turn - 1, group]).wait_recv()
                    term = raw_at(group, shard)[...].astype(jnp.float32)
                    term = term + received[way, turn - 1, group].astype(jnp.float32)
                    handed[way, turn - 1, group] = term.astype(jnp.bfloat16)
                    line_copy(way, turn, group, handed.at[way, turn - 1, group]).start()

            if turn == rounds - 1:

                @pl.when(at_end)
                def _():
                    finish(group)

        small_turn(turn)

    for turn in range(rounds, len(partners) + 1):
        small_turn(turn)

    @pl.when(jnp.logical_not(at_end))
    def _():
        for group in range(groups):
            finish(group)

    sources = list(pieces) + [totals.at[group] for group in range(groups)]
    for index, source in enumerate(sources):
        for copy in owner_copies(index, source):
            copy.wait()

    for turn in range(rounds):
        for way in range(2):

            @pl.when((along[way] >= 1) & (along[way] <= turn))
            def _():
                for group in range(groups):
                    line_copy(way, turn, group, totals.at[group]).wait_send()

    for way in range(2):

        @pl.when(along[way] == 0)
        def _():
            for group in range(groups - 2, groups):
                line_copy(way, rounds - 1, group, totals.at[group]).wait_send()

    for turn in range(len(partners)):
        small_copy(turn).wait_send()


def finished_gradients(out_raw, mix_raw, pieces, small, number):
    spans, ways = lax.axis_size("seq"), lax.axis_size("dp")
    _, count, wide = out_raw.shape
    groups = 1 + mix_raw.shape[1] // count
    rows = wide // ways
    fed = len(pieces)
    highs = [ways * piece.shape[0] for piece in pieces] + [ways * count] * groups
    inside = pl.BlockSpec(memory_space=pltpu.VMEM)
    shapes = [b16(high, rows) for high in highs]
    lines = (2, spans - 1, groups, count, wide)
    turns = len(doublings(ways)) + len(doublings(spans)) + 1
    return pl.pallas_call(
        functools.partial(finish_kernel, spans, ways, fed),
        out_shape=shapes + [f32(*small.shape)],
        in_specs=[inside] * 3 + [pl.BlockSpec(memory_space=pl.ANY)] * fed,
        out_specs=[inside] * (len(shapes) + 1),
        scratch_shapes=[
            pltpu.VMEM(lines, jnp.bfloat16),
            pltpu.VMEM((2, spans - 2, groups, count, wide), jnp.bfloat16),
            pltpu.VMEM((groups, count, wide), jnp.bfloat16),
        ]
        + [pltpu.SemaphoreType.DMA((2 * (spans - 1) * groups,))] * 2
        + [pltpu.SemaphoreType.DMA((len(highs) * (ways - 1),))] * 2
        + [pltpu.SemaphoreType.DMA((len(highs),))]
        + [pltpu.VMEM((turns,) + small.shape, jnp.float32)] * 2
        + [pltpu.SemaphoreType.DMA((turns,))] * 2,
        compiler_params=pltpu.CompilerParams(
            collective_id=number, has_side_effects=True, vmem_limit_bytes=VMEM
        ),
        cost_estimate=SHORT,
    )(out_raw, mix_raw, small, *pieces)


def shards(
    tokens_in,
    lengths,
    first_gain,
    query_weight,
    key_weight,
    value_weight,
    beta_weight,
    query_conv,
    key_conv,
    value_conv,
    mixer_gain,
    output_weight,
    second_gain,
    gate_weight,
    up_weight,
    down_weight,
    upstream,
):
    num_rows, local_len, local_width = tokens_in.shape
    full_width = query_weight.shape[0]
    channels = query_weight.shape[1]
    local_heads = beta_weight.shape[1]
    groups = lax.axis_size("head")
    ways = lax.axis_size("dp")
    spans = lax.axis_size("seq")
    positions = lax.axis_index("seq") * local_len + jnp.arange(local_len, dtype=jnp.int32)
    live_mask = (positions[None, :] < lengths[:, None]).astype(jnp.float32)
    live_low = live_mask[..., None].astype(jnp.bfloat16)
    fused = groups == 2
    weights = [query_weight, key_weight, value_weight]
    if fused:
        *pres, beta_logit, logit_turned, gathered, normed_one, normed_half, gains = projected(
            tokens_in[0], first_gain, second_gain, weights, beta_weight, 7
        )
        upstream_full = gather_head(upstream, 2) * live_low
        half_up = lax.all_gather(upstream[0], "dp", axis=0, tiled=True)
        half_one = lax.all_gather(normed_half, "dp", axis=0, tiled=True)
    else:
        gains = jnp.stack([first_gain, second_gain] + [first_gain] * 14)
        masked_up = upstream[0] * live_low[0]
        everything = gather_head(jnp.concatenate([tokens_in[0], masked_up, gains], 0), 1)
        gathered = everything[:local_len]
        upstream_full = everything[None, local_len : 2 * local_len]
        gains = everything[2 * local_len :]
        scale_one = inverse_rms(gathered.astype(jnp.float32))
        normed_one = (
            gathered.astype(jnp.float32) * scale_one * gains[0].astype(jnp.float32)
        ).astype(jnp.bfloat16)
        pres = [
            jnp.dot(normed_one, weight, preferred_element_type=jnp.float32).astype(jnp.bfloat16)
            for weight in weights
        ]
        beta_logit = jnp.dot(normed_one, beta_weight, preferred_element_type=jnp.float32)
        tokens_up = jnp.stack(spread(upstream_full[0], "dp")[1:])

    def scattered(pieces):
        return lax.psum_scatter(pieces, "seq", scatter_dimension=0, tiled=False)

    def to_owner(piece):
        c = piece.shape[0]
        blocks = piece.reshape(c, ways, -1).transpose(1, 0, 2)
        return jnp.stack(in_order(exchanged(blocks, "dp"), "dp"), 0)

    per_step = 2 if local_heads % 2 == 0 else 1
    gain_one, gain_two = gains[0].astype(jnp.float32), gains[1].astype(jnp.float32)
    stream_full = gathered[None].astype(jnp.float32)
    scale_one = inverse_rms(stream_full)
    normed_one = normed_one[None]
    convs = [query_conv, key_conv, value_conv]
    live_col = live_mask[0][:, None]
    head_gain = mixer_gain.astype(jnp.float32)[None, :]
    if fused:
        (
            query, key, value, wy, inverse, ends, mixed, head_out, entering, rims,
        ) = mixer_forward(
            pres, convs, beta_logit, logit_turned, live_col, head_gain, per_step, spans, 1
        )
    else:
        rims = passed_along(jnp.stack([pre[local_len - RIM :, :] for pre in pres]), "seq", 1)
        rims = [rims[0], rims[1], rims[2]]
        query, key, value, wy, inverse, mix, ends = mixer_local(
            pres, rims, convs, beta_logit, live_col, per_step
        )
        entering = chain_state(ends[:, :, :HEAD_DIM], ends[:, :, HEAD_DIM:], False)
        mixed, head_out = mixer_finish(mix, entering, head_gain, per_step)
    head_out = head_out[None]
    if fused:
        turned, d_gate, d_up, hidden, stream_mid, normed_two = hidden_units(
            head_out[0], output_weight, gathered, gains, upstream_full[0], live_col,
            gate_weight, up_weight, down_weight, half_up, 8,
        )
        half_up, hidden = lax.optimization_barrier((half_up, hidden))
        stream_mid, normed_two = stream_mid[None], normed_two[None]
    else:
        mixer_part = jnp.dot(head_out, output_weight, preferred_element_type=jnp.float32)
        stream_mid = stream_full + sum_head(mixer_part)
        normed_two = (stream_mid * inverse_rms(stream_mid) * gain_two).astype(jnp.bfloat16)
        feed_part, d_two_part, turned = feed_forward(
            normed_two[0], upstream_full[0], gate_weight, up_weight, down_weight, normed_two
        )
    scale_two = inverse_rms(stream_mid)
    units = turned.shape[1] // ways
    turned = turned.reshape(3, ways, units, local_len)

    def raw_piece(lefts, count, rights, is_turned, tokens=()):
        return span_pieces(
            lefts, count, rights, local_len, full_width, spans, is_turned, tokens
        )

    def slots_of(own, others):
        slots = [(own, (local_len,), lambda at: (0,))] + [
            (others, (1, local_len), lambda at, by=by: (by, 0)) for by in range(ways - 1)
        ]
        return [
            [slot + ((lambda s, way=way: way * spans + s),) for way in range(ways)]
            for slot in slots
        ]

    def halves_of(same, other):
        half = ways // 2
        return [
            [
                (
                    same if way < half else other,
                    (local_len,),
                    lambda at, by=by: (at ^ by,),
                    lambda s, way=way: (way % half) * spans + s,
                )
                for way in range(ways)
            ]
            for by in range(ways)
        ]

    def feed_slots(which, others, index):
        own = [(turned, (1, 1, units, local_len), lambda at: (which, at, 0, 0))]
        return own + [
            (others, (1, 1, units, local_len), lambda at, by=by: (by, index, 0, 0))
            for by in range(ways - 1)
        ]

    normed_full = normed_two[0]
    if fused:
        hidden_others = exchanged_rows(turned, (0, 1), [half_one], 2)
        down_raw = raw_piece(
            [feed_slots(0, hidden_others, 0)], units, halves_of(half_up, swapped(half_up)), True
        )
        d_two_part, feed_part, d_others, two_others = feed_back(
            d_gate, d_up, hidden, [gate_weight, up_weight, down_weight], turned, (1, 2),
            normed_full, [down_raw], 3,
        )
        two_slots = slots_of(normed_full, two_others)
    else:
        hidden_others = jnp.stack(exchanged(turned[:1].transpose(1, 0, 2, 3), "dp")[1:])
        down_raw = raw_piece(
            [feed_slots(0, hidden_others, 0)], units, slots_of(upstream_full[0], tokens_up), True
        )
        d_others = jnp.stack(exchanged(turned[1:].transpose(1, 0, 2, 3), "dp")[1:])
        two_slots = slots_of(normed_full, jnp.stack(spread(normed_full, "dp")[1:]))
    down_piece = scattered(down_raw)
    gate_raw = raw_piece([feed_slots(1, d_others, 0)], units, two_slots, True)
    gate_piece = scattered(gate_raw)
    layer_out = own_half(stream_mid + sum_head(feed_part[None]), local_width).astype(jnp.bfloat16)
    d_two = sum_head(d_two_part[None])
    d_stream = (
        upstream_full.astype(jnp.float32)
        + scale_two * gain_two * d_two
        - stream_mid
        * scale_two
        * scale_two
        * scale_two
        * (jnp.sum(d_two * gain_two * stream_mid, axis=-1, keepdims=True) / full_width)
    )
    grad_second = own_half(jnp.sum(d_two * stream_mid * scale_two, axis=(0, 1)), local_width)
    residual_full = d_stream.astype(jnp.bfloat16)
    d_head_out = jnp.einsum(
        "rsd,cd->rsc", residual_full, output_weight, preferred_element_type=jnp.float32
    )
    if fused:
        (
            *mix_sources, grad_kernels, d_beta_logit, grad_gain_part, out_others, res_others,
            up_others,
        ) = mixer_backward(
            d_head_out[0], mixed, head_gain, pres, rims, convs, beta_logit, live_col,
            query, key, value, wy, inverse, entering, ends, [gate_raw, down_piece],
            head_out[0], residual_full[0], turned, per_step, spans, ways, 4,
        )
    else:
        d_mixed, d_fresh, d_ends, grad_gain_part = mixer_back_local(
            d_head_out[0], mixed, head_gain, query, key, wy, per_step
        )
        leaving = chain_state(jnp.swapaxes(ends[:, :, :HEAD_DIM], 1, 2), d_ends, True)
        *d_pres, tails, d_rims, grad_kernels, d_beta_logit = mixer_back(
            pres, rims, convs, beta_logit, live_col, query, key, value, wy, inverse,
            entering, d_mixed, d_fresh, leaving, per_step,
        )
        tails = (tails + passed_along(d_rims, "seq", -1)).astype(jnp.bfloat16)
        mix_sources = [
            jnp.concatenate([part[: local_len - 8], tail], 0) for part, tail in zip(d_pres, tails)
        ]
    grad_gain_part = grad_gain_part[0]
    if fused:
        up_raw = raw_piece([feed_slots(2, up_others, 0)], units, two_slots, True)
    else:
        up_raw = raw_piece([feed_slots(2, d_others, 1)], units, two_slots, True)
    up_piece = scattered(up_raw)
    share_width = channels // ways
    residual = residual_full[0]
    if fused:
        d_one_part, *mix_others = back_projection(
            mix_sources, d_beta_logit.astype(jnp.bfloat16),
            weights, beta_weight, ways, [up_raw], 5,
        )
    else:
        *mix_others, out_others = [
            jnp.stack(exchanged(part.reshape(local_len, ways, -1).transpose(1, 0, 2), "dp")[1:])
            for part in mix_sources + [head_out[0]]
        ]
        res_others = jnp.stack(spread(residual, "dp")[1:])

    def column_slots(own, others):
        if fused:
            first = [(own, (local_len, share_width), lambda at: (0, at))]
        else:
            mine = lax.dynamic_slice_in_dim(
                own, lax.axis_index("dp") * share_width, share_width, 1
            )
            first = [(mine, (local_len, share_width), lambda at: (0, 0))]
        return first + [
            (others, (1, local_len, share_width), lambda at, by=by: (by, 0, 0))
            for by in range(ways - 1)
        ]

    if fused:
        one_slots = halves_of(half_one, swapped(half_one))
    else:
        one_slots = slots_of(normed_one[0], jnp.stack(spread(normed_one[0], "dp")[1:]))
    out_raw = raw_piece(
        [column_slots(head_out[0], out_others)], share_width, slots_of(residual, res_others), False,
        [gate_piece],
    )
    mix_raw = raw_piece(
        [column_slots(own, others) for own, others in zip(mix_sources, mix_others)],
        3 * share_width, one_slots, False, [out_raw],
    )
    d_logit_low = d_beta_logit.astype(jnp.bfloat16)
    if not fused:
        d_one_part = jnp.dot(d_logit_low, beta_weight.T, preferred_element_type=jnp.float32)
        for part, weight in zip(mix_sources, (query_weight, key_weight, value_weight)):
            d_one_part = d_one_part + jnp.dot(
                part, weight.T, preferred_element_type=jnp.float32
            )
    grad_beta_part = lax.dot_general(
        d_logit_low, normed_one[0], (((0,), (0,)), ((), ())), preferred_element_type=jnp.float32
    )
    d_one = sum_head(d_one_part[None])
    grad_tokens = own_half(
        d_stream
        + scale_one * gain_one * d_one
        - stream_full
        * scale_one
        * scale_one
        * scale_one
        * (jnp.sum(d_one * gain_one * stream_full, axis=-1, keepdims=True) / full_width),
        local_width,
    )
    grad_first = own_half(jnp.sum(d_one * stream_full * scale_one, axis=(0, 1)), local_width)
    lane = 128
    sizes = [HEAD_DIM, local_width, local_width, grad_kernels.size, grad_beta_part.size]
    parts = [grad_gain_part, grad_first, grad_second, grad_kernels, grad_beta_part]
    shares = [
        jnp.pad(part.reshape(-1, lane), ((0, -(size // lane) % 8), (0, 0)))
        for part, size in zip(parts, sizes)
    ]
    small = jnp.concatenate(shares, 0)
    starts = [0]
    for part in shares:
        starts.append(starts[-1] + part.shape[0])
    share = lax.axis_index("dp") * spans + lax.axis_index("seq")
    rows = full_width // (ways * spans)
    if fused:
        *finished, small = finished_gradients(
            out_raw, mix_raw, [down_piece, gate_piece, up_piece], small, 6
        )
        results = widened(
            finished, [False, True, True, False, True, True, True],
            small, starts, channels, query_conv.shape[0], local_heads, full_width,
        )
        down, gate, up, out, *mix = results[:7]
        gain_total, grad_first, grad_second = [part.reshape(-1) for part in results[7:10]]
        kernel_sum, grad_beta = results[10:13], results[13]
    else:
        small = sum_doubling(small, ("dp", "seq"))
        gain_total = sum_doubling(small[0], ("head",))
        totals = [
            small[start : start + size // lane].reshape(part.shape)
            for start, size, part in zip(starts, sizes, parts)
        ]
        grad_first, grad_second, kernel_sum, beta_sum = totals[1:]
        grad_beta = lax.dynamic_slice_in_dim(beta_sum, share * rows, rows, 1).T
        feed = to_owner(jnp.concatenate([down_piece, gate_piece, up_piece], 0))
        down, gate, up = [
            feed[:, place * units : (place + 1) * units].reshape(-1, rows).astype(jnp.float32)
            for place in range(3)
        ]
        gate, up = gate.T, up.T
        out = to_owner(scattered(out_raw)).reshape(-1, rows).astype(jnp.float32)
        mix = to_owner(scattered(mix_raw)).astype(jnp.float32)
        third = mix.shape[1] // 3
        mix = [mix[:, i * third : (i + 1) * third].reshape(-1, rows).T for i in range(3)]
    return (
        layer_out,
        grad_tokens,
        grad_first,
        mix[0],
        mix[1],
        mix[2],
        grad_beta,
        kernel_sum[0],
        kernel_sum[1],
        kernel_sum[2],
        gain_total,
        out,
        grad_second,
        gate,
        up,
        down,
    )


def solution(mesh):
    placed = (
        P("dp", "seq", "head"),
        P("dp"),
        P("head"),
        P(None, "head"),
        P(None, "head"),
        P(None, "head"),
        P(None, "head"),
        P(None, "head"),
        P(None, "head"),
        P(None, "head"),
        P(),
        P("head", None),
        P("head"),
        P(None, "head"),
        P(None, "head"),
        P("head", None),
        P("dp", "seq", "head"),
    )
    return jax.shard_map(
        shards,
        mesh=mesh,
        in_specs=placed,
        out_specs=(
            P("dp", "seq", "head"),
            P("dp", "seq", "head"),
            P("head"),
            P(("dp", "seq"), "head"),
            P(("dp", "seq"), "head"),
            P(("dp", "seq"), "head"),
            P(("dp", "seq"), "head"),
            P(None, "head"),
            P(None, "head"),
            P(None, "head"),
            P(),
            P("head", ("dp", "seq")),
            P("head"),
            P(("dp", "seq"), "head"),
            P(("dp", "seq"), "head"),
            P("head", ("dp", "seq")),
        ),
        check_vma=False,
    )
```

```python
import functools

import jax
import jax.numpy as jnp
from jax import lax
from jax.experimental import pallas as pl
from jax.experimental.pallas import tpu as pltpu
from jax.sharding import PartitionSpec as P

HEAD_DIM = 128


HIGH = lax.Precision.HIGHEST
EPSILON = 1e-05
UNIT_EPSILON = 1e-06
VMEM = 56 * 1024 * 1024
SHORT = pl.CostEstimate(flops=0, bytes_accessed=0, transcendentals=0)


def passed_along(value, axis, by):
    peers = lax.axis_size(axis)
    pairs = [(i, i + by) for i in range(peers) if 0 <= i + by < peers]
    return lax.ppermute(value, axis, pairs)


def swap_pairs(axis, by):
    peers = lax.axis_size(axis)
    return [(i, i ^ by) for i in range(peers)]


def exchanged(values, axis):
    peers = lax.axis_size(axis)
    own = lax.axis_index(axis)
    parts = [lax.dynamic_index_in_dim(values, own, 0, keepdims=False)]
    for by in range(1, peers):
        out = lax.dynamic_index_in_dim(values, own ^ by, 0, keepdims=False)
        parts.append(lax.ppermute(out, axis, swap_pairs(axis, by)))
    return parts


def spread(value, axis):
    peers = lax.axis_size(axis)
    return [value] + [
        lax.ppermute(value, axis, swap_pairs(axis, by)) for by in range(1, peers)
    ]


def in_order(parts, axis):
    stacked = jnp.stack(parts, 0)
    own = lax.axis_index(axis)
    return [
        lax.dynamic_index_in_dim(stacked, own ^ k, 0, keepdims=False) for k in range(len(parts))
    ]


def gather_head(value, axis):
    if lax.axis_size("head") == 2:
        other = lax.ppermute(value, "head", [(0, 1), (1, 0)])
        first = lax.axis_index("head") == 0
        return jnp.concatenate(
            [jnp.where(first, value, other), jnp.where(first, other, value)], axis
        )
    return lax.all_gather(value, "head", axis=axis, tiled=True)


def swapped(value):
    return lax.ppermute(value, "head", [(0, 1), (1, 0)])


def sum_head(value):
    low = value.astype(jnp.bfloat16)
    if lax.axis_size("head") == 2:
        other = lax.ppermute(low, "head", [(0, 1), (1, 0)])
        return low.astype(jnp.float32) + other.astype(jnp.float32)
    return lax.psum(low, "head").astype(jnp.float32)


def sum_doubling(value, axes):
    for axis in axes:
        by = 1
        while by < lax.axis_size(axis):
            value = value + lax.ppermute(value, axis, swap_pairs(axis, by))
            by *= 2
    return value


def own_half(value, width):
    return lax.dynamic_slice_in_dim(value, lax.axis_index("head") * width, width, value.ndim - 1)


def chain_state(maps, shifts, reverse):
    peers = lax.axis_size("seq")
    by = -1 if reverse else 1
    states = [passed_along(shifts.astype(jnp.bfloat16), "seq", by)]
    for step in range(peers - 2):
        out = (
            jnp.einsum("hij,hjk->hik", maps, states[-1].astype(jnp.float32), precision=HIGH)
            + shifts
        )
        states.append(passed_along(out.astype(jnp.bfloat16), "seq", by))
    return states[-1]


def inverse_rms(values):
    return lax.rsqrt(jnp.mean(values * values, axis=-1, keepdims=True) + EPSILON)


MESH = pl.DeviceIdType.MESH


def partner(own, by):
    other = own
    bit = 1
    while bit <= by:
        if by & bit:
            other = other + bit - 2 * bit * ((own // bit) % 2)
        bit *= 2
    return other


def place(name, index):
    return {name: index}


def meet(devices):
    barrier = pltpu.get_barrier_semaphore()
    for device in devices:
        pl.semaphore_signal(barrier, inc=1, device_id=device, device_id_type=MESH)
    pl.semaphore_wait(barrier, len(devices))


class Halves:
    def __init__(
        self, ways, source, out, sends, receives, hand_sends, hand_receives, distances=None
    ):
        own = lax.axis_index("dp")
        core = lax.axis_index("head")
        width = source.shape[1] // 2
        mine = pl.ds(pl.multiple_of(core * width, width), width)
        distances = distances or list(range(1, ways))
        self.peers = [place("dp", partner(own, by)) for by in distances]
        self.other = place("head", 1 - core)
        self.first = [
            pltpu.make_async_remote_copy(
                src_ref=source.at[:, mine],
                dst_ref=out.at[slot, :, mine],
                send_sem=sends.at[slot],
                recv_sem=receives.at[slot],
                device_id=peer,
                device_id_type=MESH,
            )
            for slot, peer in enumerate(self.peers)
        ]
        self.second = [
            pltpu.make_async_remote_copy(
                src_ref=out.at[slot, :, mine],
                dst_ref=out.at[slot, :, mine],
                send_sem=hand_sends.at[slot],
                recv_sem=hand_receives.at[slot],
                device_id=self.other,
                device_id_type=MESH,
            )
            for slot in range(len(distances))
        ]

    def devices(self):
        return self.peers + [self.other]

    def start(self):
        for copy in self.first:
            copy.start()

    def hand_on(self):
        for copy, hand in zip(self.first, self.second):
            copy.wait_recv()
            hand.start()

    def finish(self):
        for copy, hand in zip(self.first, self.second):
            copy.wait_send()
            hand.wait()


def column_copies(ways, source, out, sends, receives):
    own = lax.axis_index("dp")
    width = source.shape[1] // ways
    copies = []
    for by in range(1, ways):
        peer = partner(own, by)
        copies.append(
            pltpu.make_async_remote_copy(
                src_ref=source.at[:, pl.ds(pl.multiple_of(peer * width, width), width)],
                dst_ref=out.at[by - 1],
                send_sem=sends.at[by - 1],
                recv_sem=receives.at[by - 1],
                device_id=place("dp", peer),
                device_id_type=MESH,
            )
        )
    return copies


def halves(a):
    top = a.astype(jnp.bfloat16)
    return top, (a - top.astype(jnp.float32)).astype(jnp.bfloat16)


def dot_low(a, b, dims=(1, 0)):
    return lax.dot_general(
        a, b, (((dims[0],), (dims[1],)), ((), ())), preferred_element_type=jnp.float32
    )


def dot_left(a, b, dims=(1, 0)):
    top, rest = halves(a)
    return dot_low(top, b, dims) + dot_low(rest, b, dims)


def dot_right(a, b, dims=(1, 0)):
    top, rest = halves(b)
    return dot_low(a, top, dims) + dot_low(a, rest, dims)


def dot_both(a, b, dims=(1, 0)):
    a_top, a_rest = halves(a)
    b_top, b_rest = halves(b)
    return dot_low(a_top, b_top, dims) + (
        dot_low(a_top, b_rest, dims) + dot_low(a_rest, b_top, dims)
    )


def grid_marks(size):
    row = lax.broadcasted_iota(jnp.int32, (size, size), 0)
    col = lax.broadcasted_iota(jnp.int32, (size, size), 1)
    return row, col


def unit_lower_inverses(tiles):
    size = tiles[0].shape[0]
    row, col = grid_marks(size)
    unit = (row == col).astype(jnp.float32)
    base = 8
    near = (row // base == col // base) & (row > col)
    cores = [jnp.where(near, tile, 0.0) for tile in tiles]
    squares = [dot_both(core, core) for core in cores]
    fourths = [dot_both(square, square) for square in squares]
    found = [dot_both(unit - core, unit + square) for core, square in zip(cores, squares)]
    found = [dot_both(part, unit + fourth) for part, fourth in zip(found, fourths)]
    while base < size:
        wide = 2 * base
        near = (row // wide == col // wide) & (row // base > col // base)
        links = [jnp.where(near, tile, 0.0) for tile in tiles]
        steps = [dot_both(part, link) for part, link in zip(found, links)]
        found = [part - dot_both(step, part) for part, step in zip(found, steps)]
        base = wide
    return found


def lower_inverses(systems, tile):
    size = systems[0].shape[0]
    if size <= tile:
        return unit_lower_inverses(systems)
    half = size // 2
    diagonals = [s[:half, :half] for s in systems] + [s[half:, half:] for s in systems]
    found = lower_inverses(diagonals, tile)
    firsts, seconds = found[: len(systems)], found[len(systems) :]
    steps = [dot_both(second, s[half:, :half]) for second, s in zip(seconds, systems)]
    corners = [-dot_both(step, first) for step, first in zip(steps, firsts)]
    empty = jnp.zeros((half, half), jnp.float32)
    return [
        jnp.concatenate(
            [jnp.concatenate([first, empty], 1), jnp.concatenate([corner, second], 1)], 0
        )
        for first, corner, second in zip(firsts, corners, seconds)
    ]


RIM = 16


def conv_sum(ext, pre, rim, weights, taps, length):
    ext[:RIM, :] = rim.astype(jnp.float32)
    ext[RIM : RIM + length, :] = pre.astype(jnp.float32)
    first = RIM - taps + 1
    summed = weights[0:1, :] * ext[first : first + length, :]
    for tap in range(1, taps):
        summed = summed + weights[tap : tap + 1, :] * ext[first + tap : first + tap + length, :]
    return summed


def head_columns(refs, index):
    span = slice(index * HEAD_DIM, (index + 1) * HEAD_DIM)
    return [ref[:, span] for ref in refs]


def unit_scale(rows):
    return lax.rsqrt(jnp.sum(rows * rows, axis=-1, keepdims=True) + UNIT_EPSILON)


def column_of(values, index):
    lane = lax.broadcasted_iota(jnp.int32, values.shape, 1)
    return jnp.sum(jnp.where(lane == index, values, 0.0), axis=-1, keepdims=True)


def row_of(values, index):
    place = lax.broadcasted_iota(jnp.int32, values.shape, 0)
    return jnp.sum(jnp.where(place == index, values, 0.0), axis=0, keepdims=True)


def local_part(pres, rims, weights, logit, logit_t, live, live_t, ext, first, taps):
    length = live.shape[0]
    row, col = grid_marks(length)
    heads = range(pres[0].shape[1] // HEAD_DIM)
    queries, keys, values, systems, beta_rows = [], [], [], [], []
    for i in heads:
        span = slice(i * HEAD_DIM, (i + 1) * HEAD_DIM)
        active = []
        for pre, rim, weight in zip(pres, rims, weights):
            summed = conv_sum(
                ext, pre[:, span], rim[:, span], weight[:, span].astype(jnp.float32), taps, length
            )
            active.append(summed * jax.nn.sigmoid(summed))
        q, k, v = active
        q = (q * unit_scale(q)).astype(jnp.bfloat16)
        k = (k * unit_scale(k) * live).astype(jnp.bfloat16)
        v = v.astype(jnp.bfloat16)
        beta = jax.nn.sigmoid(column_of(logit, first + i)) * live
        beta_rows.append(jax.nn.sigmoid(row_of(logit_t, first + i)) * live_t)
        gram = dot_low(k, k, (1, 1))
        systems.append(jnp.where(row > col, beta * gram, 0.0))
        queries.append(q)
        keys.append(k)
        values.append(v)
    inverses = lower_inverses(systems, 128)
    wys = [
        dot_left(inverse * beta_row, jnp.concatenate([k, v], 1))
        for inverse, beta_row, k, v in zip(inverses, beta_rows, keys, values)
    ]
    wide = (HEAD_DIM, 2 * HEAD_DIM)
    place = lax.broadcasted_iota(jnp.int32, wide, 1)
    unit = (lax.broadcasted_iota(jnp.int32, wide, 0) == place).astype(jnp.float32)
    found = []
    for i in heads:
        ends = dot_right(keys[i], wys[i], (0, 0))
        ends = unit + jnp.where(place < HEAD_DIM, -ends, ends)
        scores = jnp.where(row >= col, dot_low(queries[i], keys[i], (1, 1)), 0.0)
        seen = dot_both(scores, wys[i])
        mix = jnp.concatenate(
            [queries[i].astype(jnp.float32) - seen[:, :HEAD_DIM], seen[:, HEAD_DIM:]], 1
        )
        found.append((queries[i], keys[i], values[i], wys[i], inverses[i], mix, ends))
    return found


def finish_part(mix, state, gain):
    mixed = mix[:, HEAD_DIM:] + dot_left(mix[:, :HEAD_DIM], state)
    scale = lax.rsqrt(jnp.mean(mixed * mixed, axis=-1, keepdims=True) + EPSILON)
    return mixed, (mixed * scale * gain).astype(jnp.bfloat16)


def back_local_part(d_out, mixed, gain, q, k, wy):
    row, col = grid_marks(q.shape[0])
    scale = lax.rsqrt(jnp.mean(mixed * mixed, axis=-1, keepdims=True) + EPSILON)
    weighted = gain * d_out
    inner = jnp.sum(weighted * mixed, axis=-1, keepdims=True)
    d_mixed = scale * weighted - mixed * (scale * scale * scale * inner / HEAD_DIM)
    gain_row = jnp.sum(d_out * mixed * scale, axis=0, keepdims=True)
    scores_t = jnp.where(col >= row, dot_low(k, q, (1, 1)), 0.0)
    d_fresh = dot_both(scores_t, d_mixed)
    d_end = dot_right(q, d_mixed, (0, 0)) - dot_both(wy[:, :HEAD_DIM], d_fresh, (0, 0))
    return d_mixed, d_fresh, d_end, gain_row


def back_part(q, k, v, wy, inverse, entering, leaving, d_mixed, d_fresh, logit, live):
    row, col = grid_marks(q.shape[0])
    d_fresh = d_fresh + dot_low(k, leaving)
    fresh = wy[:, HEAD_DIM:] - dot_left(wy[:, :HEAD_DIM], entering)
    d_scores = jnp.where(row >= col, dot_both(d_mixed, fresh, (1, 1)), 0.0)
    d_q = dot_left(d_mixed, entering, (1, 1)) + dot_left(d_scores, k)
    d_k = dot_left(d_scores, q, (0, 0)) + dot_left(fresh, leaving, (1, 1))
    d_wy = jnp.concatenate([-dot_left(d_fresh, entering, (1, 1)), d_fresh], 1)
    d_rhs = dot_both(inverse, d_wy, (0, 0))
    edges = jnp.where(row > col, -dot_both(d_rhs, wy, (1, 1)), 0.0)
    sig = jax.nn.sigmoid(logit)
    beta = sig * live
    both = jnp.concatenate([k, v], 1).astype(jnp.float32)
    gram = dot_low(k, k, (1, 1))
    d_beta = jnp.sum(d_rhs * both, axis=-1, keepdims=True) + jnp.sum(
        edges * gram, axis=-1, keepdims=True
    )
    scaled = beta * edges
    d_k = d_k + beta * d_rhs[:, :HEAD_DIM] + dot_left(scaled, k) + dot_left(scaled, k, (0, 0))
    d_v = beta * d_rhs[:, HEAD_DIM:]
    d_logit = d_beta * live * sig * (1.0 - sig)
    return d_q, d_k * live, d_v, d_logit


def back_conv_part(part, pre, rim, weight, grad, taps, ext, ext_back):
    length = pre.shape[0]
    weight = weight.astype(jnp.float32)
    summed = conv_sum(ext, pre, rim, weight, taps, length)
    gate = jax.nn.sigmoid(summed)
    if part < 2:
        active = summed * gate
        scale = unit_scale(active)
        inner = jnp.sum(active * grad, axis=-1, keepdims=True)
        grad = scale * grad - active * (scale * scale * scale * inner)
    d_conv = grad * gate * (1.0 + summed * (1.0 - gate))
    first = RIM - taps + 1
    rows = [
        jnp.sum(d_conv * ext[first + tap : first + tap + length, :], axis=0, keepdims=True)
        for tap in range(taps)
    ]
    ext_back[:8, :] = jnp.zeros((8, HEAD_DIM), jnp.float32)
    ext_back[8 : 8 + length, :] = d_conv
    ext_back[8 + length :, :] = jnp.zeros((8, HEAD_DIM), jnp.float32)
    own = jnp.zeros((length, HEAD_DIM), jnp.float32)
    before = jnp.zeros((8, HEAD_DIM), jnp.float32)
    for tap in range(taps):
        shift = taps - 1 - tap
        own = own + weight[tap : tap + 1, :] * ext_back[8 + shift : 8 + shift + length, :]
        before = before + weight[tap : tap + 1, :] * ext_back[shift : shift + 8, :]
    return own, before, jnp.concatenate(rows, 0)


def mixer_local_kernel(per_step, taps, *refs):
    pres, rims, weights = refs[:3], refs[3:6], refs[6:9]
    logit, logit_t, live, live_t = refs[9:13]
    q_out, k_out, v_out, wy_out, inv_out, mix_out, end_out, ext = refs[13:]
    found = local_part(
        pres, rims, weights, logit[...], logit_t[...], live[...], live_t[...], ext,
        pl.program_id(0) * per_step, taps,
    )
    for i, (q, k, v, wy, inverse, mix, ends) in enumerate(found):
        span = slice(i * HEAD_DIM, (i + 1) * HEAD_DIM)
        q_out[:, span] = q
        k_out[:, span] = k
        v_out[:, span] = v
        wy_out[i] = wy
        inv_out[i] = inverse
        mix_out[i] = mix
        end_out[i] = ends


def mixer_finish_kernel(per_step, mix, state, gain, mixed_out, head_out):
    for i in range(per_step):
        span = slice(i * HEAD_DIM, (i + 1) * HEAD_DIM)
        mixed_out[:, span], head_out[:, span] = finish_part(mix[i], state[i], gain[...])


def mixer_back_local_kernel(
    per_step, d_head, mixed_ref, gain_ref, q_ref, k_ref, wy,
    d_mixed_out, d_fresh_out, end_out, gain_out,
):
    gain_total = jnp.zeros((1, HEAD_DIM), jnp.float32)
    for i in range(per_step):
        d_out, mixed, q, k = head_columns((d_head, mixed_ref, q_ref, k_ref), i)
        d_mixed_out[i], d_fresh_out[i], end_out[i], gain_row = back_local_part(
            d_out, mixed, gain_ref[...], q, k, wy[i]
        )
        gain_total += gain_row

    @pl.when(pl.program_id(0) == 0)
    def _():
        gain_out[...] = jnp.zeros_like(gain_out)

    gain_out[...] += jnp.broadcast_to(gain_total, gain_out.shape)


def mixer_back_kernel(per_step, taps, *refs):
    pre_refs, rim_refs, weight_refs, (logit, live) = refs[:3], refs[3:6], refs[6:9], refs[9:11]
    (q_ref, k_ref, v_ref, wy, inv, state, d_mixed_ref, d_fresh_ref, d_state) = refs[11:20]
    d_q_out, d_k_out, d_v_out, tail_out, rim_out, conv_out, d_logit_out, ext, ext_back = refs[20:]
    length = live.shape[0]
    step = pl.program_id(0)

    @pl.when(step == 0)
    def _():
        d_logit_out[...] = jnp.zeros_like(d_logit_out)

    for i in range(per_step):
        q, k, v = head_columns((q_ref, k_ref, v_ref), i)
        *grads, d_logit = back_part(
            q, k, v, wy[i], inv[i], state[i], d_state[i], d_mixed_ref[i], d_fresh_ref[i],
            column_of(logit[...], step * per_step + i), live[...],
        )
        lane = lax.broadcasted_iota(jnp.int32, d_logit_out.shape, 1)
        d_logit_out[...] += jnp.where(lane == step * per_step + i, d_logit, 0.0)
        span = slice(i * HEAD_DIM, (i + 1) * HEAD_DIM)
        outs = (d_q_out, d_k_out, d_v_out)
        for part in range(3):
            own, before, rows = back_conv_part(
                part, pre_refs[part][:, span], rim_refs[part][:, span],
                weight_refs[part][:, span], grads[part], taps, ext, ext_back,
            )
            conv_out[part, :, span] = rows
            outs[part][:, span] = own.astype(jnp.bfloat16)
            tail_out[part, :, span] = own[length - 8 :, :]
            rim_out[part, :, span] = before


def mixer_specs(length, heads, per_step):
    width = per_step * HEAD_DIM

    def flat(rows):
        return pl.BlockSpec((rows, width), lambda h: (0, h))

    def whole(*shape):
        return pl.BlockSpec(shape, lambda h: (0,) * len(shape))

    def by_head(*shape):
        return pl.BlockSpec((per_step,) + shape, lambda h: (h,) + (0,) * len(shape))

    return flat, whole, by_head


def mixer_call(kernel, heads, per_step, ins, outs, scratch, flops, args):
    moved = sum(a.size * a.dtype.itemsize for a in args)
    return pl.pallas_call(
        kernel,
        grid=(heads // per_step,),
        in_specs=ins,
        out_specs=[spec for spec, _ in outs],
        out_shape=[shape for _, shape in outs],
        scratch_shapes=scratch,
        compiler_params=pltpu.CompilerParams(vmem_limit_bytes=VMEM),
        cost_estimate=SHORT,
    )(*args)


def f32(*shape):
    return jax.ShapeDtypeStruct(shape, jnp.float32)


def b16(*shape):
    return jax.ShapeDtypeStruct(shape, jnp.bfloat16)


def mixer_local(pres, rims, convs, logit, live, per_step):
    length, channels = pres[0].shape
    heads = channels // HEAD_DIM
    taps = convs[0].shape[0]
    flat, whole, by_head = mixer_specs(length, heads, per_step)
    args = (*pres, *rims, *convs, logit, logit.T, live, live.T)
    return mixer_call(
        functools.partial(mixer_local_kernel, per_step, taps),
        heads,
        per_step,
        [flat(length)] * 3
        + [flat(RIM)] * 3
        + [flat(taps)] * 3
        + [whole(length, heads), whole(heads, length), whole(length, 1), whole(1, length)],
        [(flat(length), b16(length, channels))] * 3
        + [
            (by_head(length, 2 * HEAD_DIM), f32(heads, length, 2 * HEAD_DIM)),
            (by_head(length, length), f32(heads, length, length)),
            (by_head(length, 2 * HEAD_DIM), f32(heads, length, 2 * HEAD_DIM)),
            (by_head(HEAD_DIM, 2 * HEAD_DIM), f32(heads, HEAD_DIM, 2 * HEAD_DIM)),
        ],
        [pltpu.VMEM((RIM + length, HEAD_DIM), jnp.float32)],
        heads * 2 * length**3 * 30,
        args,
    )


def mixer_finish(mix, state, gain, per_step):
    heads, length, _ = mix.shape
    flat, whole, by_head = mixer_specs(length, heads, per_step)
    return mixer_call(
        functools.partial(mixer_finish_kernel, per_step),
        heads,
        per_step,
        [by_head(length, 2 * HEAD_DIM), by_head(HEAD_DIM, HEAD_DIM), whole(1, HEAD_DIM)],
        [
            (flat(length), f32(length, heads * HEAD_DIM)),
            (flat(length), b16(length, heads * HEAD_DIM)),
        ],
        [],
        heads * 2 * length**3,
        (mix, state, gain),
    )


def mixer_back_local(d_head, mixed, gain, q, k, wy, per_step):
    heads, length, _ = wy.shape
    flat, whole, by_head = mixer_specs(length, heads, per_step)
    return mixer_call(
        functools.partial(mixer_back_local_kernel, per_step),
        heads,
        per_step,
        [flat(length)] * 2 + [whole(1, HEAD_DIM)] + [flat(length)] * 2 + [by_head(length, 2 * HEAD_DIM)],
        [
            (by_head(length, HEAD_DIM), f32(heads, length, HEAD_DIM)),
            (by_head(length, HEAD_DIM), f32(heads, length, HEAD_DIM)),
            (by_head(HEAD_DIM, HEAD_DIM), f32(heads, HEAD_DIM, HEAD_DIM)),
            (whole(8, HEAD_DIM), f32(8, HEAD_DIM)),
        ],
        [],
        heads * 2 * length**3 * 5,
        (d_head, mixed, gain, q, k, wy),
    )


def mixer_back(pres, rims, convs, logit, live, q, k, v, wy, inv, state, d_mixed, d_fresh, d_state, per_step):
    length, channels = pres[0].shape
    heads = channels // HEAD_DIM
    taps = convs[0].shape[0]
    flat, whole, by_head = mixer_specs(length, heads, per_step)
    three = pl.BlockSpec((3, 8, per_step * HEAD_DIM), lambda h: (0, 0, h))
    return mixer_call(
        functools.partial(mixer_back_kernel, per_step, taps),
        heads,
        per_step,
        [flat(length)] * 3
        + [flat(RIM)] * 3
        + [flat(taps)] * 3
        + [whole(length, heads), whole(length, 1)]
        + [flat(length)] * 3
        + [
            by_head(length, 2 * HEAD_DIM),
            by_head(length, length),
            by_head(HEAD_DIM, HEAD_DIM),
            by_head(length, HEAD_DIM),
            by_head(length, HEAD_DIM),
            by_head(HEAD_DIM, HEAD_DIM),
        ],
        [(flat(length), b16(length, channels))] * 3
        + [
            (three, f32(3, 8, channels)),
            (three, f32(3, 8, channels)),
            (
                pl.BlockSpec((3, taps, per_step * HEAD_DIM), lambda h: (0, 0, h)),
                f32(3, taps, channels),
            ),
            (whole(length, heads), f32(length, heads)),
        ],
        [
            pltpu.VMEM((RIM + length, HEAD_DIM), jnp.float32),
            pltpu.VMEM((16 + length, HEAD_DIM), jnp.float32),
        ],
        heads * 2 * length**3 * 20,
        (*pres, *rims, *convs, logit, live, q, k, v, wy, inv, state, d_mixed, d_fresh, d_state),
    )


def mixer_forward_kernel(per_step, taps, spans, ways, *refs):
    pres, weights = refs[:3], refs[3:6]
    logit, logit_t, live, live_t, gain = refs[6:11]
    sources, normed = refs[11:14], refs[14]
    q_out, k_out, v_out, wy_out, inv_out, end_out, mixed_out, head_out, state_out, rim_out = refs[
        15:25
    ]
    normed_others = refs[25]
    ext, mix_all, rims, arriving, leaving, sends, receives, rim_sends, rim_receives = refs[26:35]
    halves = Halves(ways, normed, normed_others, *refs[35:], distances=list(range(1, ways - 1)))
    step = pl.program_id(0)
    position = lax.axis_index("seq")
    pairs = arriving.shape[0]
    length = live.shape[0]
    width = per_step * HEAD_DIM
    last = spans - 1
    after = place("seq", position + 1)

    def rim_copy(part):
        return pltpu.make_async_remote_copy(
            src_ref=sources[part].at[length - RIM :, :],
            dst_ref=rims.at[part],
            send_sem=rim_sends.at[part],
            recv_sem=rim_receives.at[part],
            device_id=after,
            device_id_type=MESH,
        )

    def state_copy(pair, i):
        return pltpu.make_async_remote_copy(
            src_ref=leaving.at[pair, i],
            dst_ref=arriving.at[pair, i],
            send_sem=sends.at[pair * per_step + i],
            recv_sem=receives.at[pair * per_step + i],
            device_id=after,
            device_id_type=MESH,
        )

    @pl.when(step == 0)
    def _():
        meet(
            [place("seq", (position + last) % spans), place("seq", (position + 1) % spans)]
            + halves.devices()
        )

        @pl.when(position != last)
        def _():
            for part in range(3):
                rim_copy(part).start()

        halves.start()

        @pl.when(position == 0)
        def _():
            rims[...] = jnp.zeros_like(rims)
            arriving[...] = jnp.zeros_like(arriving)

        @pl.when(position != 0)
        def _():
            for part in range(3):
                rim_copy(part).wait_recv()

        rim_out[...] = rims[...]

    @pl.when(step < pairs)
    def _():
        here = pl.ds(pl.multiple_of(step * width, width), width)
        found = local_part(
            pres, [rims[part, :, here] for part in range(3)], weights, logit[...], logit_t[...],
            live[...], live_t[...], ext, step * per_step, taps,
        )
        for i, (q, k, v, wy, inverse, mix, ends) in enumerate(found):
            span = slice(i * HEAD_DIM, (i + 1) * HEAD_DIM)
            q_out[:, span] = q
            k_out[:, span] = k
            v_out[:, span] = v
            wy_out[i] = wy
            inv_out[i] = inverse
            mix_all[step * per_step + i] = mix
            end_out[step * per_step + i] = ends

    pair = step - position

    @pl.when((pair >= 0) & (pair < pairs))
    def _():
        for i in range(per_step):

            @pl.when(position != 0)
            def _():
                state_copy(pair, i).wait_recv()

            ends = end_out[pair * per_step + i]
            moved = dot_left(ends[:, :HEAD_DIM], arriving[pair, i])
            leaving[pair, i] = (moved + ends[:, HEAD_DIM:]).astype(jnp.bfloat16)

            @pl.when(position != last)
            def _():
                state_copy(pair, i).start()

        for i in range(per_step):
            here = pl.ds(pl.multiple_of(pair * width + i * HEAD_DIM, HEAD_DIM), HEAD_DIM)
            state = arriving[pair, i]
            state_out[pair * per_step + i] = state
            mixed, head = finish_part(mix_all[pair * per_step + i], state, gain[...])
            mixed_out[:, here] = mixed
            head_out[:, here] = head

    @pl.when(step == pairs)
    def _():
        halves.hand_on()

    @pl.when(step == pl.num_programs(0) - 1)
    def _():
        @pl.when(position != last)
        def _():
            for part in range(3):
                rim_copy(part).wait_send()
            for index in range(pairs):
                for i in range(per_step):
                    state_copy(index, i).wait_send()

        halves.finish()


def mixer_forward(pres, convs, logit, logit_t, live, gain, normed, per_step, spans, ways, number):
    length, channels = pres[0].shape
    heads = channels // HEAD_DIM
    pairs = heads // per_step
    taps = convs[0].shape[0]
    width = per_step * HEAD_DIM
    wide = (heads, length, 2 * HEAD_DIM)
    states = (heads, HEAD_DIM, HEAD_DIM)

    def at(step):
        return jnp.minimum(step, pairs - 1)

    def flat(rows):
        return pl.BlockSpec((rows, width), lambda s: (0, at(s)))

    def by_head(*shape):
        return pl.BlockSpec((per_step,) + shape, lambda s: (at(s),) + (0,) * len(shape))

    def whole(*shape):
        return pl.BlockSpec(shape, lambda s: (0,) * len(shape))

    anywhere = pl.BlockSpec(memory_space=pl.ANY)
    return pl.pallas_call(
        functools.partial(mixer_forward_kernel, per_step, taps, spans, ways),
        grid=(pairs + spans - 1,),
        in_specs=[flat(length)] * 3
        + [flat(taps)] * 3
        + [whole(length, heads), whole(heads, length), whole(length, 1), whole(1, length)]
        + [whole(1, HEAD_DIM)]
        + [anywhere] * 4,
        out_specs=[flat(length)] * 3
        + [
            by_head(length, 2 * HEAD_DIM),
            by_head(length, length),
            whole(heads, HEAD_DIM, 2 * HEAD_DIM),
            whole(length, channels),
            whole(length, channels),
            whole(*states),
            whole(3, RIM, channels),
            anywhere,
        ],
        out_shape=[b16(length, channels)] * 3
        + [
            f32(*wide),
            f32(heads, length, length),
            f32(heads, HEAD_DIM, 2 * HEAD_DIM),
            f32(length, channels),
            b16(length, channels),
            b16(*states),
            b16(3, RIM, channels),
            b16(ways - 2, *normed.shape),
        ],
        scratch_shapes=[
            pltpu.VMEM((RIM + length, HEAD_DIM), jnp.float32),
            pltpu.VMEM(wide, jnp.float32),
            pltpu.VMEM((3, RIM, channels), jnp.bfloat16),
            pltpu.VMEM((pairs, per_step, HEAD_DIM, HEAD_DIM), jnp.bfloat16),
            pltpu.VMEM((pairs, per_step, HEAD_DIM, HEAD_DIM), jnp.bfloat16),
            pltpu.SemaphoreType.DMA((heads,)),
            pltpu.SemaphoreType.DMA((heads,)),
            pltpu.SemaphoreType.DMA((3,)),
            pltpu.SemaphoreType.DMA((3,)),
        ]
        + [pltpu.SemaphoreType.DMA((ways - 2,))] * 4,
        compiler_params=pltpu.CompilerParams(
            collective_id=number, has_side_effects=True, vmem_limit_bytes=VMEM
        ),
        cost_estimate=SHORT,
    )(*pres, *convs, logit, logit_t, live, live.T, gain, *pres, normed)


def mixer_backward_kernel(per_step, taps, spans, ways, tokens, *refs):
    d_head, mixed_ref, q_one, k_one, wy_one, gain = refs[:6]
    pres, weights = refs[6:9], refs[9:12]
    q_ref, k_ref, v_ref, wy, inv = refs[12:17]
    logit, live, state, ends, rims = refs[17:22]
    head_source, residual, up_source = refs[22 + tokens : 25 + tokens]
    d_q_out, d_k_out, d_v_out, conv_out, d_logit_out, gain_out = refs[25 + tokens : 31 + tokens]
    head_others, res_others, up_others = refs[31 + tokens : 34 + tokens]
    (
        d_mixed_all, d_fresh_all, d_end_all, arriving, sending, tails, rim_out, rim_in,
        ext, ext_back, sends, receives, rim_sends, rim_receives,
    ) = refs[34 + tokens : 48 + tokens]
    col_sends, col_receives, up_sends, up_receives, *half_sems = refs[48 + tokens :]
    halves = Halves(ways, residual, res_others, *half_sems)
    columns = row_copies(ways, (1, 2), up_source, up_others, up_sends, up_receives)
    columns += column_copies(ways, head_source, head_others, col_sends, col_receives)
    step = pl.program_id(0)
    position = lax.axis_index("seq")
    pairs = arriving.shape[0]
    length = live.shape[0]
    last = spans - 1
    before_here = place("seq", position - 1)

    def state_copy(pair):
        return pltpu.make_async_remote_copy(
            src_ref=sending.at[pair],
            dst_ref=arriving.at[pair],
            send_sem=sends.at[pair],
            recv_sem=receives.at[pair],
            device_id=before_here,
            device_id_type=MESH,
        )

    def rim_copy():
        return pltpu.make_async_remote_copy(
            src_ref=rim_out,
            dst_ref=rim_in,
            send_sem=rim_sends.at[0],
            recv_sem=rim_receives.at[0],
            device_id=before_here,
            device_id_type=MESH,
        )

    @pl.when(step == 0)
    def _():
        meet(
            [place("seq", (position + last) % spans), place("seq", (position + 1) % spans)]
            + halves.devices()
        )
        for copy in columns:
            copy.start()
        halves.start()
        d_logit_out[...] = jnp.zeros_like(d_logit_out)
        gain_out[...] = jnp.zeros_like(gain_out)

        @pl.when(position == last)
        def _():
            arriving[...] = jnp.zeros_like(arriving)
            rim_in[...] = jnp.zeros_like(rim_in)

    @pl.when(step < pairs)
    def _():
        for i in range(per_step):
            d_out, mixed, q, k = head_columns((d_head, mixed_ref, q_one, k_one), i)
            d_mixed, d_fresh, d_end, gain_row = back_local_part(
                d_out, mixed, gain[...], q, k, wy_one[i]
            )
            d_mixed_all[step * per_step + i] = d_mixed
            d_fresh_all[step * per_step + i] = d_fresh
            d_end_all[step * per_step + i] = d_end
            gain_out[...] += jnp.broadcast_to(gain_row, gain_out.shape)

    pair = step - (last - position)

    @pl.when((pair >= 0) & (pair < pairs))
    def _():
        @pl.when(position != last)
        def _():
            state_copy(pair).wait_recv()

        for i in range(per_step):
            head = pair * per_step + i
            moved = dot_left(ends[head, :, :HEAD_DIM], arriving[pair, i], (0, 0))
            sending[pair, i] = (moved + d_end_all[head]).astype(jnp.bfloat16)

        @pl.when(position != 0)
        def _():
            state_copy(pair).start()

    ready = step - last

    @pl.when(ready >= 0)
    def _():
        outs = (d_q_out, d_k_out, d_v_out)
        for i in range(per_step):
            head = ready * per_step + i
            here = pl.ds(pl.multiple_of(head * HEAD_DIM, HEAD_DIM), HEAD_DIM)
            q, k, v = head_columns((q_ref, k_ref, v_ref), i)
            *grads, d_logit = back_part(
                q, k, v, wy[i], inv[i], state[head], arriving[ready, i],
                d_mixed_all[head], d_fresh_all[head], column_of(logit[...], head), live[...],
            )
            lane = lax.broadcasted_iota(jnp.int32, d_logit_out.shape, 1)
            d_logit_out[...] += jnp.where(lane == head, d_logit, 0.0)
            span = slice(i * HEAD_DIM, (i + 1) * HEAD_DIM)
            for part in range(3):
                own, before, rows = back_conv_part(
                    part, pres[part][:, span], rims[part, :, here],
                    weights[part][:, span], grads[part], taps, ext, ext_back,
                )
                conv_out[part, :, here] = rows
                outs[part][:, here] = own.astype(jnp.bfloat16)
                tails[part, :, here] = own[length - 16 :, :]
                rim_out[part, :, here] = before

    @pl.when(step == pl.num_programs(0) - 1)
    def _():
        @pl.when(position != 0)
        def _():
            rim_copy().start()

        halves.hand_on()

        @pl.when(position != last)
        def _():
            rim_copy().wait_recv()

        for part, out in enumerate((d_q_out, d_k_out, d_v_out)):
            joined = tails[part] + jnp.concatenate(
                [jnp.zeros_like(rim_in[part]), rim_in[part]], 0
            )
            out[length - 16 :, :] = joined.astype(jnp.bfloat16)

        @pl.when(position != 0)
        def _():
            rim_copy().wait_send()
            for index in range(pairs):
                state_copy(index).wait_send()

        for copy in columns:
            copy.wait()
        halves.finish()


def mixer_backward(
    d_head, mixed, gain, pres, rims, convs, logit, live, q, k, v, wy, inv, state, ends, tokens,
    head_out, residual, turned, per_step, spans, ways, number,
):
    length, channels = pres[0].shape
    heads = channels // HEAD_DIM
    pairs = heads // per_step
    taps = convs[0].shape[0]
    width = per_step * HEAD_DIM
    lag = spans - 1

    def early(step):
        return jnp.minimum(step, pairs - 1)

    def late(step):
        return jnp.maximum(step - lag, 0)

    def flat(rows, at):
        return pl.BlockSpec((rows, width), lambda s: (0, at(s)))

    def by_head(at, *shape):
        return pl.BlockSpec((per_step,) + shape, lambda s: (at(s),) + (0,) * len(shape))

    def whole(*shape):
        return pl.BlockSpec(shape, lambda s: (0,) * len(shape))

    wide = (length, 2 * HEAD_DIM)
    states = (pairs, per_step, HEAD_DIM, HEAD_DIM)
    return pl.pallas_call(
        functools.partial(mixer_backward_kernel, per_step, taps, spans, ways, len(tokens)),
        grid=(pairs + lag,),
        in_specs=[flat(length, early)] * 4
        + [by_head(early, *wide), whole(1, HEAD_DIM)]
        + [flat(length, late)] * 3
        + [flat(taps, late)] * 3
        + [flat(length, late)] * 3
        + [by_head(late, *wide), by_head(late, length, length)]
        + [whole(length, heads), whole(length, 1), whole(heads, HEAD_DIM, HEAD_DIM)]
        + [whole(heads, HEAD_DIM, 2 * HEAD_DIM), whole(3, RIM, channels)]
        + [pl.BlockSpec(memory_space=pl.ANY)] * (len(tokens) + 3),
        out_specs=[whole(length, channels)] * 3
        + [whole(3, taps, channels), whole(length, heads), whole(8, HEAD_DIM)]
        + [pl.BlockSpec(memory_space=pl.ANY)] * 3,
        out_shape=[b16(length, channels)] * 3
        + [f32(3, taps, channels), f32(length, heads), f32(8, HEAD_DIM)]
        + [b16(ways - 1, length, channels // ways)]
        + [b16(ways - 1, *residual.shape), b16(ways - 1, 1, *turned.shape[2:])],
        scratch_shapes=[
            pltpu.VMEM((heads, length, HEAD_DIM), jnp.float32),
            pltpu.VMEM((heads, length, HEAD_DIM), jnp.float32),
            pltpu.VMEM((heads, HEAD_DIM, HEAD_DIM), jnp.float32),
            pltpu.VMEM(states, jnp.bfloat16),
            pltpu.VMEM(states, jnp.bfloat16),
            pltpu.VMEM((3, 16, channels), jnp.float32),
            pltpu.VMEM((3, 8, channels), jnp.float32),
            pltpu.VMEM((3, 8, channels), jnp.float32),
            pltpu.VMEM((RIM + length, HEAD_DIM), jnp.float32),
            pltpu.VMEM((16 + length, HEAD_DIM), jnp.float32),
            pltpu.SemaphoreType.DMA((pairs,)),
            pltpu.SemaphoreType.DMA((pairs,)),
            pltpu.SemaphoreType.DMA((1,)),
            pltpu.SemaphoreType.DMA((1,)),
        ]
        + [pltpu.SemaphoreType.DMA((ways - 1,))] * 8,
        compiler_params=pltpu.CompilerParams(
            collective_id=number, has_side_effects=True, vmem_limit_bytes=VMEM
        ),
        cost_estimate=SHORT,
    )(
        d_head, mixed, q, k, wy, gain, *pres, *convs, q, k, v, wy, inv, logit, live, state, ends,
        rims, *tokens, head_out, residual, turned,
    )


def feed_kernel(
    x_ref, d_ref, gate_w, up_w, down_w, token, feed_out, d_x_out, turned_out, feed_sum, d_x_sum
):
    step = pl.program_id(0)
    x = x_ref[...]
    d_out = d_ref[...]
    gate = dot_low(x, gate_w[...])
    up = dot_low(x, up_w[...])
    d_hidden = dot_low(d_out, down_w[...], (1, 1))
    sig = jax.nn.sigmoid(gate)
    hidden = (gate * sig * up).astype(jnp.bfloat16)
    d_gate = (d_hidden * up * sig * (1.0 + gate * (1.0 - sig))).astype(jnp.bfloat16)
    d_up = (d_hidden * gate * sig).astype(jnp.bfloat16)
    for place, part in enumerate((hidden, d_gate, d_up)):
        turned_out[place] = part.T
    feed = dot_low(hidden, down_w[...])
    d_x = dot_low(d_gate, gate_w[...], (1, 1)) + dot_low(d_up, up_w[...], (1, 1))

    @pl.when(step == 0)
    def _():
        feed_sum[...] = feed
        d_x_sum[...] = d_x

    @pl.when(step > 0)
    def _():
        feed_sum[...] += feed
        d_x_sum[...] += d_x

    @pl.when(step == pl.num_programs(0) - 1)
    def _():
        feed_out[...] = feed_sum[...].astype(jnp.bfloat16)
        d_x_out[...] = d_x_sum[...].astype(jnp.bfloat16)


def feed_forward(x, d_out, gate_weight, up_weight, down_weight, token):
    length, width = x.shape
    units = gate_weight.shape[1]
    tile = 256 if units % 256 == 0 else units
    whole = pl.BlockSpec((length, width), lambda f: (0, 0))
    column = pl.BlockSpec((width, tile), lambda f: (0, f))
    return pl.pallas_call(
        feed_kernel,
        grid=(units // tile,),
        in_specs=[whole, whole, column, column]
        + [pl.BlockSpec((tile, width), lambda f: (f, 0)), pl.BlockSpec(memory_space=pl.ANY)],
        out_specs=[whole, whole, pl.BlockSpec((3, tile, length), lambda f: (0, f, 0))],
        out_shape=[b16(length, width), b16(length, width), b16(3, units, length)],
        scratch_shapes=[pltpu.VMEM((length, width), jnp.float32)] * 2,
        compiler_params=pltpu.CompilerParams(vmem_limit_bytes=VMEM),
        cost_estimate=SHORT,
    )(x, d_out, gate_weight, up_weight, down_weight, token)


def back_projection_kernel(ways, *refs):
    sources, d_logit, weights, beta_w = refs[:3], refs[3], refs[4:7], refs[7]
    shared, normed = refs[8:11], refs[11]
    out, others, normed_far = refs[-15], refs[-14:-11], refs[-11]
    sends, receives = refs[-10:-7], refs[-7:-4]
    far = Halves(ways, normed, normed_far, *refs[-4:], distances=[ways - 1])
    step = pl.program_id(0)
    copies = [
        copy
        for part in range(3)
        for copy in column_copies(ways, shared[part], others[part], sends[part], receives[part])
    ]

    @pl.when(step == 0)
    def _():
        own = lax.axis_index("dp")
        meet([place("dp", partner(own, by)) for by in range(1, ways)] + [far.other])
        for copy in copies:
            copy.start()
        far.start()

    total = dot_low(d_logit[...].astype(jnp.bfloat16), beta_w[...])
    for source, weight in zip(sources, weights):
        total = total + dot_low(source[...], weight[...], (1, 1))
    out[...] = total.astype(jnp.bfloat16)

    @pl.when(step == pl.num_programs(0) - 1)
    def _():
        far.hand_on()
        for copy in copies:
            copy.wait()
        far.finish()


def back_projection(sources, d_logit, weights, beta_weight, normed, ways, tokens, number):
    length, channels = sources[0].shape
    width, heads = beta_weight.shape
    tile = width // 4
    anywhere = pl.BlockSpec(memory_space=pl.ANY)
    return pl.pallas_call(
        functools.partial(back_projection_kernel, ways),
        grid=(width // tile,),
        in_specs=[pl.BlockSpec((length, channels), lambda n: (0, 0))] * 3
        + [pl.BlockSpec((length, heads), lambda n: (0, 0))]
        + [pl.BlockSpec((tile, channels), lambda n: (n, 0))] * 3
        + [pl.BlockSpec((heads, tile), lambda n: (0, n))]
        + [anywhere] * (4 + len(tokens)),
        out_specs=[pl.BlockSpec((length, tile), lambda n: (0, n))] + [anywhere] * 4,
        out_shape=[b16(length, width)]
        + [b16(ways - 1, length, channels // ways)] * 3
        + [b16(1, *normed.shape)],
        scratch_shapes=[pltpu.SemaphoreType.DMA((ways - 1,))] * 6
        + [pltpu.SemaphoreType.DMA((1,))] * 4,
        compiler_params=pltpu.CompilerParams(
            collective_id=number, has_side_effects=True, vmem_limit_bytes=VMEM
        ),
        cost_estimate=SHORT,
    )(*sources, d_logit, *weights, beta_weight.T, *sources, normed, *tokens)


def project_kernel(tokens, first_gain, second_gain, q_w, k_w, v_w, beta_w, *refs):
    q_out, k_out, v_out, logit_out, logit_t_out, stream_out, normed_out, gains_out = refs[:8]
    arriving, gains, gains_in, sends, receives = refs[8:]
    step = pl.program_id(0)
    half = tokens.shape[1]

    @pl.when(step == 0)
    def _():
        core = lax.axis_index("head")
        other = place("head", 1 - core)
        mine = pl.ds(pl.multiple_of(core * half, half), half)
        theirs = pl.ds(pl.multiple_of((1 - core) * half, half), half)
        row = lax.broadcasted_iota(jnp.int32, gains.shape, 0)
        first, second = [
            jnp.concatenate(
                [part[...].astype(jnp.float32)[i : i + 1] for i in range(part.shape[0])], 1
            )
            for part in (first_gain, second_gain)
        ]
        gains[...] = jnp.where(row == 0, first, second).astype(jnp.bfloat16)
        meet([other])
        copies = [
            pltpu.make_async_remote_copy(
                src_ref=source, dst_ref=target, send_sem=sends.at[index],
                recv_sem=receives.at[index], device_id=other, device_id_type=MESH,
            )
            for index, (source, target) in enumerate(((tokens, arriving), (gains, gains_in)))
        ]
        for copy in copies:
            copy.start()
        stream_out[:, mine] = tokens[...]
        gains_out[:, mine] = gains[...]
        for copy in copies:
            copy.wait()
        stream_out[:, theirs] = arriving[...]
        gains_out[:, theirs] = gains_in[...]
        stream = stream_out[...].astype(jnp.float32)
        scale = lax.rsqrt(jnp.mean(stream * stream, axis=-1, keepdims=True) + EPSILON)
        gain = gains_out[...].astype(jnp.float32)[0:1]
        normed_out[...] = (stream * scale * gain).astype(jnp.bfloat16)
        logit_out[...] = dot_low(normed_out[...], beta_w[...], (1, 1))
        logit_t_out[...] = dot_low(beta_w[...], normed_out[...], (1, 1))

    for part, (weight, out) in enumerate(((q_w, q_out), (k_w, k_out), (v_w, v_out))):

        @pl.when(step // 2 == part)
        def _():
            out[...] = dot_low(normed_out[...], weight[...]).astype(jnp.bfloat16)


def projected(tokens, first_gain, second_gain, weights, beta_weight, number):
    length, half = tokens.shape
    width, channels = weights[0].shape
    heads = beta_weight.shape[1]
    tile = channels // 2

    def whole(*shape):
        return pl.BlockSpec(shape, lambda s: (0,) * len(shape))

    def tiles(rows, part):
        return pl.BlockSpec((rows, tile), lambda s: (0, jnp.clip(s - 2 * part, 0, 1)))

    return pl.pallas_call(
        project_kernel,
        grid=(6,),
        in_specs=[whole(length, half)] + [whole(half // 128, 128)] * 2
        + [tiles(width, part) for part in range(3)]
        + [whole(heads, width)],
        out_specs=[tiles(length, part) for part in range(3)]
        + [whole(length, heads), whole(heads, length), whole(length, width)]
        + [whole(length, width), whole(16, width)],
        out_shape=[b16(length, channels)] * 3
        + [f32(length, heads), f32(heads, length), b16(length, width)]
        + [b16(length, width), b16(16, width)],
        scratch_shapes=[
            pltpu.VMEM((length, half), jnp.bfloat16),
            pltpu.VMEM((16, half), jnp.bfloat16),
            pltpu.VMEM((16, half), jnp.bfloat16),
            pltpu.SemaphoreType.DMA((2,)),
            pltpu.SemaphoreType.DMA((2,)),
        ],
        compiler_params=pltpu.CompilerParams(
            collective_id=number, has_side_effects=True, vmem_limit_bytes=VMEM
        ),
        cost_estimate=SHORT,
    )(
        tokens, first_gain.reshape(-1, 128), second_gain.reshape(-1, 128), *weights, beta_weight.T
    )


def units_kernel(
    ways, steps, head_ref, out_w, stream_ref, gains, d_own, d_other, live, gate_w, up_w, down_w,
    token,
    turned_out, d_gate_out, d_up_out, hidden_out, stream_out, normed_out, own_out, others,
    part_low, arriving, turned_hidden, d_ref, sends, receives, hidden_sends, hidden_receives,
):
    own = lax.axis_index("dp")
    tile = hidden_out.shape[1]
    part_rows = tile // ways

    def hidden_copy(step, by):
        peer = partner(own, by)
        start = pl.multiple_of(step * tile + peer * part_rows, part_rows)
        return pltpu.make_async_remote_copy(
            src_ref=turned_hidden.at[pl.ds(start, part_rows), :],
            dst_ref=others.at[
                by - 1, pl.ds(pl.multiple_of(step * part_rows, part_rows), part_rows), :
            ],
            send_sem=hidden_sends.at[(by - 1) * steps + step],
            recv_sem=hidden_receives.at[(by - 1) * steps + step],
            device_id=place("dp", peer),
            device_id_type=MESH,
        )

    @pl.when(pl.program_id(0) == 0)
    def _():
        other = place("head", 1 - lax.axis_index("head"))
        meet([other] + [place("dp", partner(own, by)) for by in range(1, ways)])
        pieces = part_low.shape[0]
        width = part_low.shape[2]
        copies = []
        for piece in range(pieces):
            span = slice(piece * width, (piece + 1) * width)
            part_low[piece] = dot_low(head_ref[...], out_w[:, span]).astype(jnp.bfloat16)
            copy = pltpu.make_async_remote_copy(
                src_ref=part_low.at[piece], dst_ref=arriving.at[piece],
                send_sem=sends.at[piece], recv_sem=receives.at[piece],
                device_id=other, device_id_type=MESH,
            )
            copy.start()
            copies.append(copy)
        core = lax.axis_index("head")
        half = d_own.shape[1]
        for place_of, part in ((core, d_own), (1 - core, d_other)):
            masked = part[...].astype(jnp.float32) * live[...]
            here = pl.ds(pl.multiple_of(place_of * half, half), half)
            d_ref[:, here] = masked.astype(jnp.bfloat16)
        squares = 0.0
        for piece, copy in enumerate(copies):
            span = slice(piece * width, (piece + 1) * width)
            copy.wait()
            both = part_low[piece].astype(jnp.float32) + arriving[piece].astype(jnp.float32)
            stream = stream_ref[:, span].astype(jnp.float32) + both
            stream_out[:, span] = stream
            squares = squares + jnp.sum(stream * stream, axis=-1, keepdims=True)
        scale = lax.rsqrt(squares / (pieces * width) + EPSILON)
        gain = gains[...].astype(jnp.float32)[1:2]
        normed_out[...] = (stream_out[...] * scale * gain).astype(jnp.bfloat16)

    x = normed_out[...]
    gate = dot_low(x, gate_w[...])
    up = dot_low(x, up_w[...])
    d_hidden = dot_low(d_ref[...], down_w[...], (1, 1))
    sig = jax.nn.sigmoid(gate)
    hidden = (gate * sig * up).astype(jnp.bfloat16)
    d_gate = (d_hidden * up * sig * (1.0 + gate * (1.0 - sig))).astype(jnp.bfloat16)
    d_up = (d_hidden * gate * sig).astype(jnp.bfloat16)
    for index, (part, out) in enumerate(
        ((hidden, hidden_out), (d_gate, d_gate_out), (d_up, d_up_out))
    ):
        out[...] = part
        if index > 0:
            turned_out[index - 1] = part.T
    step = pl.program_id(0)
    live_hidden = (hidden.astype(jnp.float32) * live[...]).astype(jnp.bfloat16)
    turned_hidden[pl.ds(pl.multiple_of(step * tile, tile), tile), :] = live_hidden.T
    for by in range(1, ways):
        hidden_copy(step, by).start()
    own_out[pl.ds(pl.multiple_of(step * part_rows, part_rows), part_rows), :] = turned_hidden[
        pl.ds(pl.multiple_of(step * tile + own * part_rows, part_rows), part_rows), :
    ]

    @pl.when(step == steps - 1)
    def _():
        for index in range(steps):
            for by in range(1, ways):
                hidden_copy(index, by).wait()


def hidden_units(
    head_out, out_weight, stream, gains, d_own, d_other, live, gate_weight, up_weight,
    down_weight, token, number,
):
    ways = lax.axis_size("dp")
    length, width = stream.shape
    channels = head_out.shape[1]
    units = gate_weight.shape[1]
    tile = 256
    whole = pl.BlockSpec((length, width), lambda f: (0, 0))
    column = pl.BlockSpec((width, tile), lambda f: (0, f))
    flat = pl.BlockSpec((length, tile), lambda f: (0, f))
    chunk = units // ways
    return pl.pallas_call(
        functools.partial(units_kernel, ways, units // tile),
        grid=(units // tile,),
        in_specs=[
            pl.BlockSpec((length, channels), lambda f: (0, 0)),
            pl.BlockSpec((channels, width), lambda f: (0, 0)),
            whole,
            pl.BlockSpec((16, width), lambda f: (0, 0)),
            pl.BlockSpec((length, width // 2), lambda f: (0, 0)),
            pl.BlockSpec((length, width // 2), lambda f: (0, 0)),
            pl.BlockSpec((length, 1), lambda f: (0, 0)),
            column,
            column,
        ]
        + [pl.BlockSpec((tile, width), lambda f: (f, 0)), pl.BlockSpec(memory_space=pl.ANY)],
        out_specs=[pl.BlockSpec((2, tile, length), lambda f: (0, f, 0))]
        + [flat] * 3
        + [whole] * 2
        + [pl.BlockSpec((chunk, length), lambda f: (0, 0)), pl.BlockSpec(memory_space=pl.ANY)],
        out_shape=[b16(2, units, length)]
        + [b16(length, units)] * 3
        + [f32(length, width), b16(length, width)]
        + [b16(chunk, length), b16(ways - 1, chunk, length)],
        scratch_shapes=[pltpu.VMEM((4, length, width // 4), jnp.bfloat16)] * 2
        + [pltpu.VMEM((units, length), jnp.bfloat16), pltpu.VMEM((length, width), jnp.bfloat16)]
        + [pltpu.SemaphoreType.DMA((4,))] * 2
        + [pltpu.SemaphoreType.DMA(((ways - 1) * (units // tile),))] * 2,
        compiler_params=pltpu.CompilerParams(
            collective_id=number, has_side_effects=True, vmem_limit_bytes=VMEM
        ),
        cost_estimate=SHORT,
    )(
        head_out, out_weight, stream, gains, d_own, d_other, live, gate_weight, up_weight,
        down_weight, token,
    )


def row_copies(ways, entries, source, out, sends, receives):
    own = lax.axis_index("dp")
    copies = []
    for by in range(1, ways):
        peer = partner(own, by)
        copies.append(
            pltpu.make_async_remote_copy(
                src_ref=source.at[entries[0] : entries[1], peer],
                dst_ref=out.at[by - 1],
                send_sem=sends.at[by - 1],
                recv_sem=receives.at[by - 1],
                device_id=place("dp", peer),
                device_id_type=MESH,
            )
        )
    return copies


def feed_back_kernel(ways, entries, *refs):
    d_gate, d_up, hidden, gate_w, up_w, down_w = refs[:6]
    up_own, up_other, live, gains, source, normed, stream_in, out_w_in = refs[6:14]
    feed_out, d_stream_out, low_out, d_head_out, second_out, others, normed_others = refs[-20:-13]
    d_x, arriving, masked, stream_ref, out_w = refs[-13:-8]
    swap_sems, load_sems = refs[-8:-6]
    sends, receives = refs[-6:-4]
    halves = Halves(ways, normed, normed_others, *refs[-4:])
    copies = row_copies(ways, entries, source, others, sends, receives)
    step = pl.program_id(0)
    tile = feed_out.shape[1]
    width = d_x.shape[1]
    loads = [
        pltpu.make_async_copy(stream_in, stream_ref, load_sems.at[0]),
        pltpu.make_async_copy(out_w_in, out_w, load_sems.at[1]),
    ]

    @pl.when(step == 0)
    def _():
        meet(halves.devices())
        halves.start()
        for copy in copies + loads:
            copy.start()

    d_tile = dot_low(d_gate[...], gate_w[...], (1, 1)) + dot_low(d_up[...], up_w[...], (1, 1))
    d_x[:, pl.ds(pl.multiple_of(step * tile, tile), tile)] = d_tile.astype(jnp.bfloat16)
    feed_out[...] = dot_low(hidden[...], down_w[...]).astype(jnp.bfloat16)

    @pl.when(step == pl.num_programs(0) - 1)
    def _():
        swap = pltpu.make_async_remote_copy(
            src_ref=d_x, dst_ref=arriving, send_sem=swap_sems.at[0], recv_sem=swap_sems.at[1],
            device_id=halves.other, device_id_type=MESH,
        )
        swap.start()
        core = lax.axis_index("head")
        half = up_own.shape[1]
        for place_of, part in ((core, up_own), (1 - core, up_other)):
            here = pl.ds(pl.multiple_of(place_of * half, half), half)
            masked[:, here] = (part[...].astype(jnp.float32) * live[...]).astype(jnp.bfloat16)
        for copy in loads:
            copy.wait()
        swap.wait()
        d_two = d_x[...].astype(jnp.float32) + arriving[...].astype(jnp.float32)
        stream = stream_ref[...]
        scale = lax.rsqrt(jnp.mean(stream * stream, axis=-1, keepdims=True) + EPSILON)
        weighted = gains[...].astype(jnp.float32)[1:2] * d_two
        inner = jnp.sum(weighted * stream, axis=-1, keepdims=True)
        d_stream = (
            masked[...].astype(jnp.float32)
            + scale * weighted
            - stream * (scale * scale * scale * inner / width)
        )
        second_out[...] = jnp.sum(d_two * stream * scale, axis=0, keepdims=True)
        d_stream_out[...] = d_stream
        low_out[...] = d_stream.astype(jnp.bfloat16)
        d_head_out[...] = dot_low(low_out[...], out_w[...], (1, 1))
        halves.hand_on()
        for copy in copies:
            copy.wait()
        halves.finish()


def feed_back(
    d_gate, d_up, hidden, weights, up_own, up_other, live, gains, source, entries, normed, stream,
    out_weight, tokens, number,
):
    ways = lax.axis_size("dp")
    length, units = hidden.shape
    width = normed.shape[1]
    channels = out_weight.shape[0]
    tile = width // 8
    anywhere = pl.BlockSpec(memory_space=pl.ANY)
    row = pl.BlockSpec((tile, units), lambda n: (n, 0))
    out = pl.BlockSpec((length, tile), lambda n: (0, n))

    def whole(*shape):
        return pl.BlockSpec(shape, lambda n: (0,) * len(shape))

    return pl.pallas_call(
        functools.partial(feed_back_kernel, ways, entries),
        grid=(8,),
        in_specs=[whole(length, units)] * 3
        + [row, row, pl.BlockSpec((units, tile), lambda n: (0, n))]
        + [whole(length, width // 2)] * 2
        + [whole(length, 1), whole(16, width)]
        + [anywhere] * (4 + len(tokens)),
        out_specs=[out, whole(length, width), whole(length, width), whole(length, channels)]
        + [whole(1, width), anywhere, anywhere],
        out_shape=[
            b16(length, width), f32(length, width), b16(length, width), f32(length, channels),
            f32(1, width),
            b16(ways - 1, entries[1] - entries[0], *source.shape[2:]),
            b16(ways - 1, length, width),
        ],
        scratch_shapes=[pltpu.VMEM((length, width), jnp.bfloat16)] * 3
        + [pltpu.VMEM((length, width), jnp.float32), pltpu.VMEM(out_weight.shape, jnp.bfloat16)]
        + [pltpu.SemaphoreType.DMA((2,))] * 2
        + [pltpu.SemaphoreType.DMA((ways - 1,))] * 6,
        compiler_params=pltpu.CompilerParams(
            collective_id=number, has_side_effects=True, vmem_limit_bytes=VMEM
        ),
        cost_estimate=SHORT,
    )(
        d_gate, d_up, hidden, *weights, up_own, up_other, live, gains, source, normed, stream,
        out_weight, *tokens,
    )


def pieces_kernel(groups, slots, ways, turned, at, *refs):
    lefts = refs[: groups * slots]
    rights = refs[groups * slots : (groups + ways) * slots]
    out, left_all, right_all = refs[-3:]
    length = rights[0].shape[-2]
    rows = rights[0].shape[-1]
    count = left_all.shape[0] // groups

    @pl.when(pl.program_id(0) == 0)
    def _():
        for group in range(groups):
            for slot in range(slots):
                block = lefts[group * slots + slot][...]
                block = block.reshape(block.shape[-2:])
                left_all[
                    group * count : (group + 1) * count, slot * length : (slot + 1) * length
                ] = block if turned else block.T

    for slot in range(slots):
        for way in range(ways):
            right = rights[slot * ways + way][...]
            right_all[
                slot * length : (slot + 1) * length, way * rows : (way + 1) * rows
            ] = right.reshape(right.shape[-2:])
    out[0] = dot_low(left_all[...], right_all[...]).astype(jnp.bfloat16)


def span_pieces(lefts, count, rights, length, width, spans, turned, tokens=()):
    groups = len(lefts)
    lefts = [left for group in lefts for left in group]
    slots = len(rights)
    ways = lax.axis_size("dp")
    rows = width // (ways * spans)

    def left_block(block, at_place):
        return pl.BlockSpec(block, lambda s, at: at_place(at[0]))

    def right_block(block, at_place, column):
        return pl.BlockSpec(
            block + (rows,), lambda s, at: tuple(at_place(at[0])) + (column(s),)
        )

    rights = [right for slot in rights for right in slot]

    return pl.pallas_call(
        functools.partial(pieces_kernel, groups, slots, ways, turned),
        grid_spec=pltpu.PrefetchScalarGridSpec(
            num_scalar_prefetch=1,
            grid=(spans,),
            in_specs=[left_block(block, where) for _, block, where in lefts]
            + [right_block(block, where, column) for _, block, where, column in rights]
            + [pl.BlockSpec(memory_space=pl.ANY)] * len(tokens),
            out_specs=pl.BlockSpec((1, count, ways * rows), lambda s, at: (s, 0, 0)),
            scratch_shapes=[
                pltpu.VMEM((count, slots * length), jnp.bfloat16),
                pltpu.VMEM((slots * length, ways * rows), jnp.bfloat16),
            ],
        ),
        out_shape=b16(spans, count, ways * rows),
        compiler_params=pltpu.CompilerParams(vmem_limit_bytes=VMEM),
        cost_estimate=SHORT,
    )(
        lax.axis_index("dp")[None],
        *[array for array, _, _ in lefts],
        *[array for array, _, _, _ in rights],
        *tokens,
    )


def widen_kernel(count, turned, starts, share_of, ways, *refs):
    small = refs[count]
    outs = refs[count + 1 :]
    chunk = refs[0].shape[0] // ways
    part = 256 // ways
    for way in range(ways):
        for tile in range(chunk // part):
            start = way * chunk + tile * part
            to = tile * 256 + way * part
            outs[0][to : to + part, :] = refs[0][start : start + part, :].astype(jnp.float32)
    for index in range(1, count):
        whole = refs[index][...].astype(jnp.float32)
        outs[index][...] = whole.T if turned[index] else whole
    gain, first, second, taps, beta = outs[count], *outs[count + 1 : count + 3], outs[count + 3 : -1], outs[-1]
    gain[...] = small[starts[0] : starts[0] + 1, :]
    first[...] = small[starts[1] : starts[1] + first.shape[0], :]
    second[...] = small[starts[2] : starts[2] + second.shape[0], :]
    row = starts[3]
    for out in taps:
        high, wide = out.shape
        for tap in range(high):
            for lane in range(wide // 128):
                out[tap : tap + 1, lane * 128 : (lane + 1) * 128] = small[row : row + 1, :]
                row += 1
    heads = beta.shape[0]
    width = share_of[1] // 128
    share = lax.axis_index("dp") * share_of[0] + lax.axis_index("seq")
    rows = [small[pl.ds(starts[4] + head * width + share, 1), :] for head in range(heads)]
    beta[...] = jnp.concatenate(rows, 0)


def widened(arrays, turned, small, starts, channels, taps, heads, width):
    inside = pl.BlockSpec(memory_space=pltpu.VMEM)
    shapes = [
        f32(*(array.shape[::-1] if turn else array.shape)) for array, turn in zip(arrays, turned)
    ]
    shapes += [f32(1, 128), f32(width // 256, 128), f32(width // 256, 128)]
    shapes += [f32(taps, channels)] * 3 + [f32(heads, 128)]
    return pl.pallas_call(
        functools.partial(
            widen_kernel, len(arrays), turned, starts, (lax.axis_size("seq"), width),
            lax.axis_size("dp"),
        ),
        out_shape=shapes,
        in_specs=[inside] * (len(arrays) + 1),
        out_specs=[inside] * len(shapes),
        compiler_params=pltpu.CompilerParams(vmem_limit_bytes=VMEM),
        cost_estimate=SHORT,
    )(*arrays, small)


def doublings(size):
    return [1 << bit for bit in range(size.bit_length() - 1)]


def finish_kernel(spans, ways, fed, split, *refs):
    out_raw, mix_raw, small = refs[:3]
    pieces, refs = refs[3 : 3 + fed], refs[3 + fed :]
    stages, small_out, refs = refs[: 4 + fed], refs[4 + fed], refs[5 + fed :]
    received, handed, totals, *refs = refs
    sends, receives, owner_sends, owner_receives, own_sems = refs[:5]
    small_in, small_sent, small_sends, small_receives = refs[5:]
    own = lax.axis_index("dp")
    core = lax.axis_index("head")
    position = lax.axis_index("seq")
    last = spans - 1
    rounds = spans - 1
    whole = out_raw.shape[1]
    count = whole // split
    groups = split + mix_raw.shape[1] // count
    rows = stages[0].shape[1]
    peers = [partner(own, by) for by in range(1, ways)]

    def raw_at(group, shard):
        if group < split:
            return out_raw.at[shard, group * count : (group + 1) * count, :]
        return mix_raw.at[shard, (group - split) * count : (group - split + 1) * count, :]

    def line_copy(way, turn, group, src):
        step = 1 if way == 0 else -1
        slot = (way * rounds + turn) * groups + group
        return pltpu.make_async_remote_copy(
            src_ref=src,
            dst_ref=received.at[way, turn, group],
            send_sem=sends.at[slot],
            recv_sem=receives.at[slot],
            device_id=place("seq", position + step),
            device_id_type=MESH,
        )

    def owner_copies(index, source):
        high = source.shape[0]
        turn = core * (ways // 2) if index == 0 else 0

        def block_of(peer):
            start = ((peer + turn) % ways) * rows
            return source.at[:, pl.ds(pl.multiple_of(start, rows), rows)]

        if index < fed:
            stage, start = stages[index], own * high
        else:
            stage = stages[fed + (index - fed) // split]
            start = own * whole + (index - fed) % split * high
        mine = stage.at[pl.ds(pl.multiple_of(start, high), high), :]
        copies = []
        for by, peer in enumerate(peers):
            copies.append(
                pltpu.make_async_remote_copy(
                    src_ref=block_of(peer),
                    dst_ref=mine,
                    send_sem=owner_sends.at[index * (ways - 1) + by],
                    recv_sem=owner_receives.at[index * (ways - 1) + by],
                    device_id=place("dp", peer),
                    device_id_type=MESH,
                )
            )
        here = pltpu.make_async_copy(block_of(own), mine, own_sems.at[index])
        return copies + [here]

    partners = [place("dp", partner(own, by)) for by in doublings(ways)]
    partners += [place("seq", partner(position, by)) for by in doublings(spans)]
    partners += [place("head", 1 - lax.axis_index("head"))]

    def small_copy(turn):
        high = 8 if turn == len(partners) - 1 else small.shape[0]
        return pltpu.make_async_remote_copy(
            src_ref=small_sent.at[turn, :high, :],
            dst_ref=small_in.at[turn, :high, :],
            send_sem=small_sends.at[turn],
            recv_sem=small_receives.at[turn],
            device_id=partners[turn],
            device_id_type=MESH,
        )

    def small_turn(turn):
        if turn == 0:
            small_sent[0] = small[...]
        else:
            small_copy(turn - 1).wait_recv()
            if turn < len(partners):
                small_sent[turn] = small_sent[turn - 1] + small_in[turn - 1]
            else:
                small_out[...] = small_sent[turn - 1]
                small_out[:8, :] = small_sent[turn - 1, :8, :] + small_in[turn - 1, :8, :]
        if turn < len(partners):
            small_copy(turn).start()

    meet(
        [place("seq", (position + last) % spans), place("seq", (position + 1) % spans)]
        + [place("seq", partner(position, by)) for by in doublings(spans)[1:]]
        + [place("dp", peer) for peer in peers]
        + partners[-1:]
    )
    small_turn(0)
    along = (position, last - position)

    ahead = 6

    def source_send(way, index):
        turn, group = index // groups, index % groups
        shard = last - turn if way == 0 else turn
        if index >= ahead:
            before = index - ahead
            line_copy(way, before // groups, before % groups, totals.at[0]).wait_send()
        line_copy(way, turn, group, raw_at(group, shard)).start()

    for way in range(2):

        @pl.when(along[way] == 0)
        def _():
            for index in range(ahead):
                source_send(way, index)

    fed_copies = [owner_copies(index, piece) for index, piece in enumerate(pieces)]
    for copies in fed_copies:
        for copy in copies:
            copy.start()

    for way in range(2):

        @pl.when(along[way] == 0)
        def _():
            for index in range(ahead, groups + ahead):
                source_send(way, index)

    at_end = (position == 0) | (position == last)

    def finish(group):
        for way in range(2):

            @pl.when(along[way] >= 1)
            def _():
                line_copy(way, rounds - 1, group, totals.at[group]).wait_recv()

        total = raw_at(group, position)[...].astype(jnp.float32)
        for way in range(2):
            arrived = received[way, rounds - 1, group].astype(jnp.float32)
            total = total + jnp.where(along[way] >= 1, arrived, 0.0)
        totals[group] = total.astype(jnp.bfloat16)
        for copy in owner_copies(fed + group, totals.at[group]):
            copy.start()

    for turn in range(1, rounds):
        for group in range(groups):
            for way in range(2):
                if turn * groups + group + ahead < rounds * groups:

                    @pl.when(along[way] == 0)
                    def _():
                        source_send(way, turn * groups + group + ahead)

                shard = last - turn + position if way == 0 else turn - along[1]

                @pl.when((along[way] >= 1) & (along[way] <= turn))
                def _():
                    line_copy(way, turn - 1, group, handed.at[way, turn - 1, group]).wait_recv()
                    term = raw_at(group, shard)[...].astype(jnp.float32)
                    term = term + received[way, turn - 1, group].astype(jnp.float32)
                    handed[way, turn - 1, group] = term.astype(jnp.bfloat16)
                    line_copy(way, turn, group, handed.at[way, turn - 1, group]).start()

            if turn == rounds - 1:

                @pl.when(at_end)
                def _():
                    finish(group)

        small_turn(turn)

    later = list(range(rounds, len(partners) + 1))

    @pl.when(at_end)
    def _():
        for turn in later:
            small_turn(turn)

    @pl.when(jnp.logical_not(at_end))
    def _():
        done = 0
        for group in range(groups):
            finish(group)
            while done < len(later) and (group + 1) * len(later) >= (done + 1) * groups:
                small_turn(later[done])
                done += 1

    sources = list(pieces) + [totals.at[group] for group in range(groups)]
    for index, source in enumerate(sources):
        for copy in owner_copies(index, source):
            copy.wait()

    for turn in range(rounds):
        for way in range(2):

            @pl.when((along[way] >= 1) & (along[way] <= turn))
            def _():
                for group in range(groups):
                    line_copy(way, turn, group, totals.at[group]).wait_send()

    for way in range(2):

        @pl.when(along[way] == 0)
        def _():
            for group in range(groups - ahead, groups):
                line_copy(way, rounds - 1, group, totals.at[group]).wait_send()

    for turn in range(len(partners)):
        small_copy(turn).wait_send()


def finished_gradients(out_raw, mix_raw, pieces, small, number):
    spans, ways = lax.axis_size("seq"), lax.axis_size("dp")
    split = 2
    _, whole, wide = out_raw.shape
    count = whole // split
    grads = 1 + mix_raw.shape[1] // whole
    groups = grads * split
    rows = wide // ways
    fed = len(pieces)
    highs = [ways * piece.shape[0] for piece in pieces] + [ways * whole] * grads
    inside = pl.BlockSpec(memory_space=pltpu.VMEM)
    shapes = [b16(high, rows) for high in highs]
    lines = (2, spans - 1, groups, count, wide)
    turns = len(doublings(ways)) + len(doublings(spans)) + 1
    return pl.pallas_call(
        functools.partial(finish_kernel, spans, ways, fed, split),
        out_shape=shapes + [f32(*small.shape)],
        in_specs=[inside] * 3 + [pl.BlockSpec(memory_space=pl.ANY)] * fed,
        out_specs=[inside] * (len(shapes) + 1),
        scratch_shapes=[
            pltpu.VMEM(lines, jnp.bfloat16),
            pltpu.VMEM((2, spans - 2, groups, count, wide), jnp.bfloat16),
            pltpu.VMEM((groups, count, wide), jnp.bfloat16),
        ]
        + [pltpu.SemaphoreType.DMA((2 * (spans - 1) * groups,))] * 2
        + [pltpu.SemaphoreType.DMA(((fed + groups) * (ways - 1),))] * 2
        + [pltpu.SemaphoreType.DMA((fed + groups,))]
        + [pltpu.VMEM((turns,) + small.shape, jnp.float32)] * 2
        + [pltpu.SemaphoreType.DMA((turns,))] * 2,
        compiler_params=pltpu.CompilerParams(
            collective_id=number, has_side_effects=True, vmem_limit_bytes=VMEM
        ),
        cost_estimate=SHORT,
    )(out_raw, mix_raw, small, *pieces)


def shards(
    tokens_in,
    lengths,
    first_gain,
    query_weight,
    key_weight,
    value_weight,
    beta_weight,
    query_conv,
    key_conv,
    value_conv,
    mixer_gain,
    output_weight,
    second_gain,
    gate_weight,
    up_weight,
    down_weight,
    upstream,
):
    num_rows, local_len, local_width = tokens_in.shape
    full_width = query_weight.shape[0]
    channels = query_weight.shape[1]
    local_heads = beta_weight.shape[1]
    groups = lax.axis_size("head")
    ways = lax.axis_size("dp")
    spans = lax.axis_size("seq")
    positions = lax.axis_index("seq") * local_len + jnp.arange(local_len, dtype=jnp.int32)
    live_mask = (positions[None, :] < lengths[:, None]).astype(jnp.float32)
    live_low = live_mask[..., None].astype(jnp.bfloat16)
    fused = groups == 2
    weights = [query_weight, key_weight, value_weight]
    if fused:
        *pres, beta_logit, logit_turned, gathered, normed_one, gains = projected(
            tokens_in[0], first_gain, second_gain, weights, beta_weight, 7
        )
        upstream_other = swapped(upstream[0])
        upstream_other, beta_logit = lax.optimization_barrier((upstream_other, beta_logit))
        first = lax.axis_index("head") == 0
        upstream_full = live_low * jnp.concatenate(
            [
                jnp.where(first, upstream, upstream_other[None]),
                jnp.where(first, upstream_other[None], upstream),
            ],
            2,
        )
        half_up = lax.all_gather(upstream[0], "dp", axis=0, tiled=True)
    else:
        gains = jnp.stack([first_gain, second_gain] + [first_gain] * 14)
        masked_up = upstream[0] * live_low[0]
        everything = gather_head(jnp.concatenate([tokens_in[0], masked_up, gains], 0), 1)
        gathered = everything[:local_len]
        upstream_full = everything[None, local_len : 2 * local_len]
        gains = everything[2 * local_len :]
        scale_one = inverse_rms(gathered.astype(jnp.float32))
        normed_one = (
            gathered.astype(jnp.float32) * scale_one * gains[0].astype(jnp.float32)
        ).astype(jnp.bfloat16)
        pres = [
            jnp.dot(normed_one, weight, preferred_element_type=jnp.float32).astype(jnp.bfloat16)
            for weight in weights
        ]
        beta_logit = jnp.dot(normed_one, beta_weight, preferred_element_type=jnp.float32)
        tokens_up = jnp.stack(spread(upstream_full[0], "dp")[1:])

    def scattered(pieces):
        return lax.psum_scatter(pieces, "seq", scatter_dimension=0, tiled=False)

    def to_owner(piece):
        c = piece.shape[0]
        blocks = piece.reshape(c, ways, -1).transpose(1, 0, 2)
        return jnp.stack(in_order(exchanged(blocks, "dp"), "dp"), 0)

    per_step = 2 if local_heads % 2 == 0 else 1
    gain_one, gain_two = gains[0].astype(jnp.float32), gains[1].astype(jnp.float32)
    stream_full = gathered[None].astype(jnp.float32)
    scale_one = inverse_rms(stream_full)
    normed_one = normed_one[None]
    convs = [query_conv, key_conv, value_conv]
    live_col = live_mask[0][:, None]
    head_gain = mixer_gain.astype(jnp.float32)[None, :]
    if fused:
        (
            query, key, value, wy, inverse, ends, mixed, head_out, entering, rims, one_near,
        ) = mixer_forward(
            pres, convs, beta_logit, logit_turned, live_col, head_gain, normed_one[0],
            per_step, spans, ways, 1,
        )
        half_up, mixed = lax.optimization_barrier((half_up, mixed))
    else:
        rims = passed_along(jnp.stack([pre[local_len - RIM :, :] for pre in pres]), "seq", 1)
        rims = [rims[0], rims[1], rims[2]]
        query, key, value, wy, inverse, mix, ends = mixer_local(
            pres, rims, convs, beta_logit, live_col, per_step
        )
        entering = chain_state(ends[:, :, :HEAD_DIM], ends[:, :, HEAD_DIM:], False)
        mixed, head_out = mixer_finish(mix, entering, head_gain, per_step)
    head_out = head_out[None]
    if fused:
        (
            turned, d_gate, d_up, hidden, stream_mid, normed_two, own_hidden, hidden_others,
        ) = hidden_units(
            head_out[0], output_weight, gathered, gains, upstream[0], upstream_other, live_col,
            gate_weight, up_weight, down_weight, half_up, 8,
        )
        stream_mid, normed_two = stream_mid[None], normed_two[None]
    else:
        mixer_part = jnp.dot(head_out, output_weight, preferred_element_type=jnp.float32)
        stream_mid = stream_full + sum_head(mixer_part)
        normed_two = (stream_mid * inverse_rms(stream_mid) * gain_two).astype(jnp.bfloat16)
        feed_part, d_two_part, turned = feed_forward(
            normed_two[0], upstream_full[0], gate_weight, up_weight, down_weight, normed_two
        )
    scale_two = inverse_rms(stream_mid)
    units = turned.shape[1] // ways
    turned = turned.reshape(-1, ways, units, local_len)

    def raw_piece(lefts, count, rights, is_turned, tokens=()):
        return span_pieces(
            lefts, count, rights, local_len, full_width, spans, is_turned, tokens
        )

    def slots_of(own, others):
        slots = [(own, (local_len,), lambda at: (0,))] + [
            (others, (1, local_len), lambda at, by=by: (by, 0)) for by in range(ways - 1)
        ]
        return [
            [slot + ((lambda s, way=way: way * spans + s),) for way in range(ways)]
            for slot in slots
        ]

    def halves_of(same, other):
        half = ways // 2
        return [
            [
                (
                    same if way < half else other,
                    (local_len,),
                    lambda at, by=by: (at ^ by,),
                    lambda s, way=way: (way % half) * spans + s,
                )
                for way in range(ways)
            ]
            for by in range(ways)
        ]

    def feed_slots(which, others, index):
        own = [(turned, (1, 1, units, local_len), lambda at: (which, at, 0, 0))]
        return own + [
            (others, (1, 1, units, local_len), lambda at, by=by: (by, index, 0, 0))
            for by in range(ways - 1)
        ]

    normed_full = normed_two[0]
    if fused:
        hidden_slots = [(own_hidden, (units, local_len), lambda at: (0, 0))] + [
            (hidden_others, (1, units, local_len), lambda at, by=by: (by, 0, 0))
            for by in range(ways - 1)
        ]
        down_raw = raw_piece(
            [hidden_slots], units, halves_of(half_up, swapped(half_up)), True
        )
        feed_part, d_stream, residual, d_head_out, second_row, d_others, two_others = feed_back(
            d_gate, d_up, hidden, [gate_weight, up_weight, down_weight], upstream[0],
            upstream_other, live_col, gains, turned, (0, 1), normed_full, stream_mid[0],
            output_weight, [down_raw], 3,
        )
        d_stream, residual_full, d_head_out = d_stream[None], residual[None], d_head_out[None]
        grad_second = own_half(second_row[0], local_width)
        two_slots = slots_of(normed_full, two_others)
    else:
        hidden_others = jnp.stack(exchanged(turned[:1].transpose(1, 0, 2, 3), "dp")[1:])
        down_raw = raw_piece(
            [feed_slots(0, hidden_others, 0)], units, slots_of(upstream_full[0], tokens_up), True
        )
        d_others = jnp.stack(exchanged(turned[1:].transpose(1, 0, 2, 3), "dp")[1:])
        two_slots = slots_of(normed_full, jnp.stack(spread(normed_full, "dp")[1:]))
    down_piece = scattered(down_raw)
    first = turned.shape[0] - 2
    gate_raw = raw_piece([feed_slots(first, d_others, 0)], units, two_slots, True)
    gate_piece = scattered(gate_raw)
    layer_out = own_half(stream_mid + sum_head(feed_part[None]), local_width).astype(jnp.bfloat16)
    if not fused:
        d_two = sum_head(d_two_part[None])
        d_stream = (
            upstream_full.astype(jnp.float32)
            + scale_two * gain_two * d_two
            - stream_mid
            * scale_two
            * scale_two
            * scale_two
            * (jnp.sum(d_two * gain_two * stream_mid, axis=-1, keepdims=True) / full_width)
        )
        grad_second = own_half(jnp.sum(d_two * stream_mid * scale_two, axis=(0, 1)), local_width)
        residual_full = d_stream.astype(jnp.bfloat16)
        d_head_out = jnp.einsum(
            "rsd,cd->rsc", residual_full, output_weight, preferred_element_type=jnp.float32
        )
    if fused:
        (
            *mix_sources, grad_kernels, d_beta_logit, grad_gain_part, out_others, res_others,
            up_others,
        ) = mixer_backward(
            d_head_out[0], mixed, head_gain, pres, rims, convs, beta_logit, live_col,
            query, key, value, wy, inverse, entering, ends, [gate_raw, down_piece],
            head_out[0], residual_full[0], turned, per_step, spans, ways, 4,
        )
    else:
        d_mixed, d_fresh, d_ends, grad_gain_part = mixer_back_local(
            d_head_out[0], mixed, head_gain, query, key, wy, per_step
        )
        leaving = chain_state(jnp.swapaxes(ends[:, :, :HEAD_DIM], 1, 2), d_ends, True)
        *d_pres, tails, d_rims, grad_kernels, d_beta_logit = mixer_back(
            pres, rims, convs, beta_logit, live_col, query, key, value, wy, inverse,
            entering, d_mixed, d_fresh, leaving, per_step,
        )
        tails = (tails + passed_along(d_rims, "seq", -1)).astype(jnp.bfloat16)
        mix_sources = [
            jnp.concatenate([part[: local_len - 8], tail], 0) for part, tail in zip(d_pres, tails)
        ]
    grad_gain_part = grad_gain_part[0]
    if fused:
        up_raw = raw_piece([feed_slots(1, up_others, 0)], units, two_slots, True)
    else:
        up_raw = raw_piece([feed_slots(2, d_others, 1)], units, two_slots, True)
    up_piece = scattered(up_raw)
    share_width = channels // ways
    residual = residual_full[0]
    if fused:
        d_one_part, *mix_others, one_far = back_projection(
            mix_sources, d_beta_logit, weights, beta_weight, normed_one[0], ways, [up_raw], 5,
        )
    else:
        *mix_others, out_others = [
            jnp.stack(exchanged(part.reshape(local_len, ways, -1).transpose(1, 0, 2), "dp")[1:])
            for part in mix_sources + [head_out[0]]
        ]
        res_others = jnp.stack(spread(residual, "dp")[1:])

    def column_slots(own, others):
        if fused:
            first = [(own, (local_len, share_width), lambda at: (0, at))]
        else:
            mine = lax.dynamic_slice_in_dim(
                own, lax.axis_index("dp") * share_width, share_width, 1
            )
            first = [(mine, (local_len, share_width), lambda at: (0, 0))]
        return first + [
            (others, (1, local_len, share_width), lambda at, by=by: (by, 0, 0))
            for by in range(ways - 1)
        ]

    if fused:
        one_slots = slots_of(normed_one[0], one_near)[: ways - 1]
        one_slots += slots_of(normed_one[0], one_far)[1:2]
    else:
        one_slots = slots_of(normed_one[0], jnp.stack(spread(normed_one[0], "dp")[1:]))
    out_raw = raw_piece(
        [column_slots(head_out[0], out_others)], share_width, slots_of(residual, res_others), False,
        [gate_piece],
    )
    mix_raw = raw_piece(
        [column_slots(own, others) for own, others in zip(mix_sources, mix_others)],
        3 * share_width, one_slots, False, [out_raw],
    )
    d_logit_low = d_beta_logit.astype(jnp.bfloat16)
    if not fused:
        d_one_part = jnp.dot(d_logit_low, beta_weight.T, preferred_element_type=jnp.float32)
        for part, weight in zip(mix_sources, (query_weight, key_weight, value_weight)):
            d_one_part = d_one_part + jnp.dot(
                part, weight.T, preferred_element_type=jnp.float32
            )
    grad_beta_part = lax.dot_general(
        d_logit_low, normed_one[0], (((0,), (0,)), ((), ())), preferred_element_type=jnp.float32
    )
    d_one = sum_head(d_one_part[None])
    grad_tokens = own_half(
        d_stream
        + scale_one * gain_one * d_one
        - stream_full
        * scale_one
        * scale_one
        * scale_one
        * (jnp.sum(d_one * gain_one * stream_full, axis=-1, keepdims=True) / full_width),
        local_width,
    )
    grad_first = own_half(jnp.sum(d_one * stream_full * scale_one, axis=(0, 1)), local_width)
    lane = 128
    sizes = [HEAD_DIM, local_width, local_width, grad_kernels.size, grad_beta_part.size]
    parts = [grad_gain_part, grad_first, grad_second, grad_kernels, grad_beta_part]
    shares = [
        jnp.pad(part.reshape(-1, lane), ((0, -(size // lane) % 8), (0, 0)))
        for part, size in zip(parts, sizes)
    ]
    small = jnp.concatenate(shares, 0)
    starts = [0]
    for part in shares:
        starts.append(starts[-1] + part.shape[0])
    share = lax.axis_index("dp") * spans + lax.axis_index("seq")
    rows = full_width // (ways * spans)
    if fused:
        *finished, small = finished_gradients(
            out_raw, mix_raw, [down_piece, gate_piece, up_piece], small, 6
        )
        results = widened(
            finished, [False, True, True, False, True, True, True],
            small, starts, channels, query_conv.shape[0], local_heads, full_width,
        )
        down, gate, up, out, *mix = results[:7]
        gain_total, grad_first, grad_second = [part.reshape(-1) for part in results[7:10]]
        kernel_sum, grad_beta = results[10:13], results[13].T
    else:
        small = sum_doubling(small, ("dp", "seq"))
        gain_total = sum_doubling(small[0], ("head",))
        totals = [
            small[start : start + size // lane].reshape(part.shape)
            for start, size, part in zip(starts, sizes, parts)
        ]
        grad_first, grad_second, kernel_sum, beta_sum = totals[1:]
        grad_beta = lax.dynamic_slice_in_dim(beta_sum, share * rows, rows, 1).T
        feed = to_owner(jnp.concatenate([down_piece, gate_piece, up_piece], 0))
        down, gate, up = [
            feed[:, place * units : (place + 1) * units].reshape(-1, rows).astype(jnp.float32)
            for place in range(3)
        ]
        gate, up = gate.T, up.T
        out = to_owner(scattered(out_raw)).reshape(-1, rows).astype(jnp.float32)
        mix = to_owner(scattered(mix_raw)).astype(jnp.float32)
        third = mix.shape[1] // 3
        mix = [mix[:, i * third : (i + 1) * third].reshape(-1, rows).T for i in range(3)]
    return (
        layer_out,
        grad_tokens,
        grad_first,
        mix[0],
        mix[1],
        mix[2],
        grad_beta,
        kernel_sum[0],
        kernel_sum[1],
        kernel_sum[2],
        gain_total,
        out,
        grad_second,
        gate,
        up,
        down,
    )


def solution(mesh):
    placed = (
        P("dp", "seq", "head"),
        P("dp"),
        P("head"),
        P(None, "head"),
        P(None, "head"),
        P(None, "head"),
        P(None, "head"),
        P(None, "head"),
        P(None, "head"),
        P(None, "head"),
        P(),
        P("head", None),
        P("head"),
        P(None, "head"),
        P(None, "head"),
        P("head", None),
        P("dp", "seq", "head"),
    )
    return jax.shard_map(
        shards,
        mesh=mesh,
        in_specs=placed,
        out_specs=(
            P("dp", "seq", "head"),
            P("dp", "seq", "head"),
            P("head"),
            P(("dp", "seq"), "head"),
            P(("dp", "seq"), "head"),
            P(("dp", "seq"), "head"),
            P(("dp", "seq"), "head"),
            P(None, "head"),
            P(None, "head"),
            P(None, "head"),
            P(),
            P("head", ("dp", "seq")),
            P("head"),
            P(("dp", "seq"), "head"),
            P(("dp", "seq"), "head"),
            P("head", ("dp", "seq")),
        ),
        check_vma=False,
    )
```

```python
import functools

import jax
import jax.numpy as jnp
from jax import lax
from jax.experimental import pallas as pl
from jax.experimental.pallas import tpu as pltpu
from jax.sharding import PartitionSpec as P

HEAD_DIM = 128


HIGH = lax.Precision.HIGHEST
EPSILON = 1e-05
UNIT_EPSILON = 1e-06
VMEM = 56 * 1024 * 1024
SHORT = pl.CostEstimate(flops=0, bytes_accessed=0, transcendentals=0)


def passed_along(value, axis, by):
    peers = lax.axis_size(axis)
    pairs = [(i, i + by) for i in range(peers) if 0 <= i + by < peers]
    return lax.ppermute(value, axis, pairs)


def swap_pairs(axis, by):
    peers = lax.axis_size(axis)
    return [(i, i ^ by) for i in range(peers)]


def exchanged(values, axis):
    peers = lax.axis_size(axis)
    own = lax.axis_index(axis)
    parts = [lax.dynamic_index_in_dim(values, own, 0, keepdims=False)]
    for by in range(1, peers):
        out = lax.dynamic_index_in_dim(values, own ^ by, 0, keepdims=False)
        parts.append(lax.ppermute(out, axis, swap_pairs(axis, by)))
    return parts


def spread(value, axis):
    peers = lax.axis_size(axis)
    return [value] + [
        lax.ppermute(value, axis, swap_pairs(axis, by)) for by in range(1, peers)
    ]


def in_order(parts, axis):
    stacked = jnp.stack(parts, 0)
    own = lax.axis_index(axis)
    return [
        lax.dynamic_index_in_dim(stacked, own ^ k, 0, keepdims=False) for k in range(len(parts))
    ]


def gather_head(value, axis):
    if lax.axis_size("head") == 2:
        other = lax.ppermute(value, "head", [(0, 1), (1, 0)])
        first = lax.axis_index("head") == 0
        return jnp.concatenate(
            [jnp.where(first, value, other), jnp.where(first, other, value)], axis
        )
    return lax.all_gather(value, "head", axis=axis, tiled=True)


def swapped(value):
    return lax.ppermute(value, "head", [(0, 1), (1, 0)])


def sum_head(value):
    low = value.astype(jnp.bfloat16)
    if lax.axis_size("head") == 2:
        other = lax.ppermute(low, "head", [(0, 1), (1, 0)])
        return low.astype(jnp.float32) + other.astype(jnp.float32)
    return lax.psum(low, "head").astype(jnp.float32)


def sum_doubling(value, axes):
    for axis in axes:
        by = 1
        while by < lax.axis_size(axis):
            value = value + lax.ppermute(value, axis, swap_pairs(axis, by))
            by *= 2
    return value


def own_half(value, width):
    return lax.dynamic_slice_in_dim(value, lax.axis_index("head") * width, width, value.ndim - 1)


def chain_state(maps, shifts, reverse):
    peers = lax.axis_size("seq")
    by = -1 if reverse else 1
    states = [passed_along(shifts.astype(jnp.bfloat16), "seq", by)]
    for step in range(peers - 2):
        out = (
            jnp.einsum("hij,hjk->hik", maps, states[-1].astype(jnp.float32), precision=HIGH)
            + shifts
        )
        states.append(passed_along(out.astype(jnp.bfloat16), "seq", by))
    return states[-1]


def inverse_rms(values):
    return lax.rsqrt(jnp.mean(values * values, axis=-1, keepdims=True) + EPSILON)


MESH = pl.DeviceIdType.MESH


def partner(own, by):
    other = own
    bit = 1
    while bit <= by:
        if by & bit:
            other = other + bit - 2 * bit * ((own // bit) % 2)
        bit *= 2
    return other


def place(name, index):
    return {name: index}


def meet(devices):
    barrier = pltpu.get_barrier_semaphore()
    for device in devices:
        pl.semaphore_signal(barrier, inc=1, device_id=device, device_id_type=MESH)
    pl.semaphore_wait(barrier, len(devices))


class Halves:
    def __init__(
        self, ways, source, out, sends, receives, hand_sends, hand_receives, distances=None
    ):
        own = lax.axis_index("dp")
        core = lax.axis_index("head")
        width = source.shape[1] // 2
        mine = pl.ds(pl.multiple_of(core * width, width), width)
        distances = distances or list(range(1, ways))
        self.peers = [place("dp", partner(own, by)) for by in distances]
        self.other = place("head", 1 - core)
        self.first = [
            pltpu.make_async_remote_copy(
                src_ref=source.at[:, mine],
                dst_ref=out.at[slot, :, mine],
                send_sem=sends.at[slot],
                recv_sem=receives.at[slot],
                device_id=peer,
                device_id_type=MESH,
            )
            for slot, peer in enumerate(self.peers)
        ]
        self.second = [
            pltpu.make_async_remote_copy(
                src_ref=out.at[slot, :, mine],
                dst_ref=out.at[slot, :, mine],
                send_sem=hand_sends.at[slot],
                recv_sem=hand_receives.at[slot],
                device_id=self.other,
                device_id_type=MESH,
            )
            for slot in range(len(distances))
        ]

    def devices(self):
        return self.peers + [self.other]

    def start(self):
        for copy in self.first:
            copy.start()

    def hand_on(self):
        for copy, hand in zip(self.first, self.second):
            copy.wait_recv()
            hand.start()

    def finish(self):
        for copy, hand in zip(self.first, self.second):
            copy.wait_send()
            hand.wait()


def column_copies(ways, source, out, sends, receives):
    own = lax.axis_index("dp")
    width = source.shape[1] // ways
    copies = []
    for by in range(1, ways):
        peer = partner(own, by)
        copies.append(
            pltpu.make_async_remote_copy(
                src_ref=source.at[:, pl.ds(pl.multiple_of(peer * width, width), width)],
                dst_ref=out.at[by - 1],
                send_sem=sends.at[by - 1],
                recv_sem=receives.at[by - 1],
                device_id=place("dp", peer),
                device_id_type=MESH,
            )
        )
    return copies


def halves(a):
    top = a.astype(jnp.bfloat16)
    return top, (a - top.astype(jnp.float32)).astype(jnp.bfloat16)


def dot_low(a, b, dims=(1, 0)):
    return lax.dot_general(
        a, b, (((dims[0],), (dims[1],)), ((), ())), preferred_element_type=jnp.float32
    )


def dot_left(a, b, dims=(1, 0)):
    top, rest = halves(a)
    return dot_low(top, b, dims) + dot_low(rest, b, dims)


def dot_right(a, b, dims=(1, 0)):
    top, rest = halves(b)
    return dot_low(a, top, dims) + dot_low(a, rest, dims)


def dot_both(a, b, dims=(1, 0)):
    a_top, a_rest = halves(a)
    b_top, b_rest = halves(b)
    return dot_low(a_top, b_top, dims) + (
        dot_low(a_top, b_rest, dims) + dot_low(a_rest, b_top, dims)
    )


def grid_marks(size):
    row = lax.broadcasted_iota(jnp.int32, (size, size), 0)
    col = lax.broadcasted_iota(jnp.int32, (size, size), 1)
    return row, col


def unit_lower_inverses(tiles):
    size = tiles[0].shape[0]
    row, col = grid_marks(size)
    unit = (row == col).astype(jnp.float32)
    base = 8
    near = (row // base == col // base) & (row > col)
    cores = [jnp.where(near, tile, 0.0) for tile in tiles]
    squares = [dot_both(core, core) for core in cores]
    fourths = [dot_both(square, square) for square in squares]
    found = [dot_both(unit - core, unit + square) for core, square in zip(cores, squares)]
    found = [dot_both(part, unit + fourth) for part, fourth in zip(found, fourths)]
    while base < size:
        wide = 2 * base
        near = (row // wide == col // wide) & (row // base > col // base)
        links = [jnp.where(near, tile, 0.0) for tile in tiles]
        steps = [dot_both(part, link) for part, link in zip(found, links)]
        found = [part - dot_both(step, part) for part, step in zip(found, steps)]
        base = wide
    return found


def lower_inverses(systems, tile):
    size = systems[0].shape[0]
    if size <= tile:
        return unit_lower_inverses(systems)
    half = size // 2
    diagonals = [s[:half, :half] for s in systems] + [s[half:, half:] for s in systems]
    found = lower_inverses(diagonals, tile)
    firsts, seconds = found[: len(systems)], found[len(systems) :]
    steps = [dot_both(second, s[half:, :half]) for second, s in zip(seconds, systems)]
    corners = [-dot_both(step, first) for step, first in zip(steps, firsts)]
    empty = jnp.zeros((half, half), jnp.float32)
    return [
        jnp.concatenate(
            [jnp.concatenate([first, empty], 1), jnp.concatenate([corner, second], 1)], 0
        )
        for first, corner, second in zip(firsts, corners, seconds)
    ]


RIM = 16


def conv_sum(ext, pre, rim, weights, taps, length):
    ext[:RIM, :] = rim.astype(jnp.float32)
    ext[RIM : RIM + length, :] = pre.astype(jnp.float32)
    first = RIM - taps + 1
    summed = weights[0:1, :] * ext[first : first + length, :]
    for tap in range(1, taps):
        summed = summed + weights[tap : tap + 1, :] * ext[first + tap : first + tap + length, :]
    return summed


def head_columns(refs, index):
    span = slice(index * HEAD_DIM, (index + 1) * HEAD_DIM)
    return [ref[:, span] for ref in refs]


def unit_scale(rows):
    return lax.rsqrt(jnp.sum(rows * rows, axis=-1, keepdims=True) + UNIT_EPSILON)


def column_of(values, index):
    lane = lax.broadcasted_iota(jnp.int32, values.shape, 1)
    return jnp.sum(jnp.where(lane == index, values, 0.0), axis=-1, keepdims=True)


def row_of(values, index):
    place = lax.broadcasted_iota(jnp.int32, values.shape, 0)
    return jnp.sum(jnp.where(place == index, values, 0.0), axis=0, keepdims=True)


def local_part(pres, rims, weights, logit, logit_t, live, live_t, ext, first, taps):
    length = live.shape[0]
    row, col = grid_marks(length)
    heads = range(pres[0].shape[1] // HEAD_DIM)
    queries, keys, values, systems, beta_rows = [], [], [], [], []
    for i in heads:
        span = slice(i * HEAD_DIM, (i + 1) * HEAD_DIM)
        active = []
        for pre, rim, weight in zip(pres, rims, weights):
            summed = conv_sum(
                ext, pre[:, span], rim[:, span], weight[:, span].astype(jnp.float32), taps, length
            )
            active.append(summed * jax.nn.sigmoid(summed))
        q, k, v = active
        q = (q * unit_scale(q)).astype(jnp.bfloat16)
        k = (k * unit_scale(k) * live).astype(jnp.bfloat16)
        v = v.astype(jnp.bfloat16)
        beta = jax.nn.sigmoid(column_of(logit, first + i)) * live
        beta_rows.append(jax.nn.sigmoid(row_of(logit_t, first + i)) * live_t)
        gram = dot_low(k, k, (1, 1))
        systems.append(jnp.where(row > col, beta * gram, 0.0))
        queries.append(q)
        keys.append(k)
        values.append(v)
    inverses = lower_inverses(systems, 128)
    wys = [
        dot_left(inverse * beta_row, jnp.concatenate([k, v], 1))
        for inverse, beta_row, k, v in zip(inverses, beta_rows, keys, values)
    ]
    wide = (HEAD_DIM, 2 * HEAD_DIM)
    place = lax.broadcasted_iota(jnp.int32, wide, 1)
    unit = (lax.broadcasted_iota(jnp.int32, wide, 0) == place).astype(jnp.float32)
    found = []
    for i in heads:
        ends = dot_right(keys[i], wys[i], (0, 0))
        ends = unit + jnp.where(place < HEAD_DIM, -ends, ends)
        scores = jnp.where(row >= col, dot_low(queries[i], keys[i], (1, 1)), 0.0)
        seen = dot_both(scores, wys[i])
        mix = jnp.concatenate(
            [queries[i].astype(jnp.float32) - seen[:, :HEAD_DIM], seen[:, HEAD_DIM:]], 1
        )
        found.append((queries[i], keys[i], values[i], wys[i], inverses[i], mix, ends))
    return found


def finish_part(mix, state, gain):
    mixed = mix[:, HEAD_DIM:] + dot_left(mix[:, :HEAD_DIM], state)
    scale = lax.rsqrt(jnp.mean(mixed * mixed, axis=-1, keepdims=True) + EPSILON)
    return mixed, (mixed * scale * gain).astype(jnp.bfloat16)


def back_local_part(d_out, mixed, gain, q, k, wy):
    row, col = grid_marks(q.shape[0])
    scale = lax.rsqrt(jnp.mean(mixed * mixed, axis=-1, keepdims=True) + EPSILON)
    weighted = gain * d_out
    inner = jnp.sum(weighted * mixed, axis=-1, keepdims=True)
    d_mixed = scale * weighted - mixed * (scale * scale * scale * inner / HEAD_DIM)
    gain_row = jnp.sum(d_out * mixed * scale, axis=0, keepdims=True)
    scores_t = jnp.where(col >= row, dot_low(k, q, (1, 1)), 0.0)
    d_fresh = dot_both(scores_t, d_mixed)
    d_end = dot_right(q, d_mixed, (0, 0)) - dot_both(wy[:, :HEAD_DIM], d_fresh, (0, 0))
    return d_mixed, d_fresh, d_end, gain_row


def back_part(q, k, v, wy, inverse, entering, leaving, d_mixed, d_fresh, logit, live):
    row, col = grid_marks(q.shape[0])
    d_fresh = d_fresh + dot_low(k, leaving)
    fresh = wy[:, HEAD_DIM:] - dot_left(wy[:, :HEAD_DIM], entering)
    d_scores = jnp.where(row >= col, dot_both(d_mixed, fresh, (1, 1)), 0.0)
    d_q = dot_left(d_mixed, entering, (1, 1)) + dot_left(d_scores, k)
    d_k = dot_left(d_scores, q, (0, 0)) + dot_left(fresh, leaving, (1, 1))
    d_wy = jnp.concatenate([-dot_left(d_fresh, entering, (1, 1)), d_fresh], 1)
    d_rhs = dot_both(inverse, d_wy, (0, 0))
    edges = jnp.where(row > col, -dot_both(d_rhs, wy, (1, 1)), 0.0)
    sig = jax.nn.sigmoid(logit)
    beta = sig * live
    both = jnp.concatenate([k, v], 1).astype(jnp.float32)
    gram = dot_low(k, k, (1, 1))
    d_beta = jnp.sum(d_rhs * both, axis=-1, keepdims=True) + jnp.sum(
        edges * gram, axis=-1, keepdims=True
    )
    scaled = beta * edges
    d_k = d_k + beta * d_rhs[:, :HEAD_DIM] + dot_left(scaled, k) + dot_left(scaled, k, (0, 0))
    d_v = beta * d_rhs[:, HEAD_DIM:]
    d_logit = d_beta * live * sig * (1.0 - sig)
    return d_q, d_k * live, d_v, d_logit


def back_conv_part(part, pre, rim, weight, grad, taps, ext, ext_back):
    length = pre.shape[0]
    weight = weight.astype(jnp.float32)
    summed = conv_sum(ext, pre, rim, weight, taps, length)
    gate = jax.nn.sigmoid(summed)
    if part < 2:
        active = summed * gate
        scale = unit_scale(active)
        inner = jnp.sum(active * grad, axis=-1, keepdims=True)
        grad = scale * grad - active * (scale * scale * scale * inner)
    d_conv = grad * gate * (1.0 + summed * (1.0 - gate))
    first = RIM - taps + 1
    rows = [
        jnp.sum(d_conv * ext[first + tap : first + tap + length, :], axis=0, keepdims=True)
        for tap in range(taps)
    ]
    ext_back[:8, :] = jnp.zeros((8, HEAD_DIM), jnp.float32)
    ext_back[8 : 8 + length, :] = d_conv
    ext_back[8 + length :, :] = jnp.zeros((8, HEAD_DIM), jnp.float32)
    own = jnp.zeros((length, HEAD_DIM), jnp.float32)
    before = jnp.zeros((8, HEAD_DIM), jnp.float32)
    for tap in range(taps):
        shift = taps - 1 - tap
        own = own + weight[tap : tap + 1, :] * ext_back[8 + shift : 8 + shift + length, :]
        before = before + weight[tap : tap + 1, :] * ext_back[shift : shift + 8, :]
    return own, before, jnp.concatenate(rows, 0)


def mixer_local_kernel(per_step, taps, *refs):
    pres, rims, weights = refs[:3], refs[3:6], refs[6:9]
    logit, logit_t, live, live_t = refs[9:13]
    q_out, k_out, v_out, wy_out, inv_out, mix_out, end_out, ext = refs[13:]
    found = local_part(
        pres, rims, weights, logit[...], logit_t[...], live[...], live_t[...], ext,
        pl.program_id(0) * per_step, taps,
    )
    for i, (q, k, v, wy, inverse, mix, ends) in enumerate(found):
        span = slice(i * HEAD_DIM, (i + 1) * HEAD_DIM)
        q_out[:, span] = q
        k_out[:, span] = k
        v_out[:, span] = v
        wy_out[i] = wy
        inv_out[i] = inverse
        mix_out[i] = mix
        end_out[i] = ends


def mixer_finish_kernel(per_step, mix, state, gain, mixed_out, head_out):
    for i in range(per_step):
        span = slice(i * HEAD_DIM, (i + 1) * HEAD_DIM)
        mixed_out[:, span], head_out[:, span] = finish_part(mix[i], state[i], gain[...])


def mixer_back_local_kernel(
    per_step, d_head, mixed_ref, gain_ref, q_ref, k_ref, wy,
    d_mixed_out, d_fresh_out, end_out, gain_out,
):
    gain_total = jnp.zeros((1, HEAD_DIM), jnp.float32)
    for i in range(per_step):
        d_out, mixed, q, k = head_columns((d_head, mixed_ref, q_ref, k_ref), i)
        d_mixed_out[i], d_fresh_out[i], end_out[i], gain_row = back_local_part(
            d_out, mixed, gain_ref[...], q, k, wy[i]
        )
        gain_total += gain_row

    @pl.when(pl.program_id(0) == 0)
    def _():
        gain_out[...] = jnp.zeros_like(gain_out)

    gain_out[...] += jnp.broadcast_to(gain_total, gain_out.shape)


def mixer_back_kernel(per_step, taps, *refs):
    pre_refs, rim_refs, weight_refs, (logit, live) = refs[:3], refs[3:6], refs[6:9], refs[9:11]
    (q_ref, k_ref, v_ref, wy, inv, state, d_mixed_ref, d_fresh_ref, d_state) = refs[11:20]
    d_q_out, d_k_out, d_v_out, tail_out, rim_out, conv_out, d_logit_out, ext, ext_back = refs[20:]
    length = live.shape[0]
    step = pl.program_id(0)

    @pl.when(step == 0)
    def _():
        d_logit_out[...] = jnp.zeros_like(d_logit_out)

    for i in range(per_step):
        q, k, v = head_columns((q_ref, k_ref, v_ref), i)
        *grads, d_logit = back_part(
            q, k, v, wy[i], inv[i], state[i], d_state[i], d_mixed_ref[i], d_fresh_ref[i],
            column_of(logit[...], step * per_step + i), live[...],
        )
        lane = lax.broadcasted_iota(jnp.int32, d_logit_out.shape, 1)
        d_logit_out[...] += jnp.where(lane == step * per_step + i, d_logit, 0.0)
        span = slice(i * HEAD_DIM, (i + 1) * HEAD_DIM)
        outs = (d_q_out, d_k_out, d_v_out)
        for part in range(3):
            own, before, rows = back_conv_part(
                part, pre_refs[part][:, span], rim_refs[part][:, span],
                weight_refs[part][:, span], grads[part], taps, ext, ext_back,
            )
            conv_out[part, :, span] = rows
            outs[part][:, span] = own.astype(jnp.bfloat16)
            tail_out[part, :, span] = own[length - 8 :, :]
            rim_out[part, :, span] = before


def mixer_specs(length, heads, per_step):
    width = per_step * HEAD_DIM

    def flat(rows):
        return pl.BlockSpec((rows, width), lambda h: (0, h))

    def whole(*shape):
        return pl.BlockSpec(shape, lambda h: (0,) * len(shape))

    def by_head(*shape):
        return pl.BlockSpec((per_step,) + shape, lambda h: (h,) + (0,) * len(shape))

    return flat, whole, by_head


def mixer_call(kernel, heads, per_step, ins, outs, scratch, flops, args):
    moved = sum(a.size * a.dtype.itemsize for a in args)
    return pl.pallas_call(
        kernel,
        grid=(heads // per_step,),
        in_specs=ins,
        out_specs=[spec for spec, _ in outs],
        out_shape=[shape for _, shape in outs],
        scratch_shapes=scratch,
        compiler_params=pltpu.CompilerParams(vmem_limit_bytes=VMEM),
        cost_estimate=SHORT,
    )(*args)


def f32(*shape):
    return jax.ShapeDtypeStruct(shape, jnp.float32)


def b16(*shape):
    return jax.ShapeDtypeStruct(shape, jnp.bfloat16)


def mixer_local(pres, rims, convs, logit, live, per_step):
    length, channels = pres[0].shape
    heads = channels // HEAD_DIM
    taps = convs[0].shape[0]
    flat, whole, by_head = mixer_specs(length, heads, per_step)
    args = (*pres, *rims, *convs, logit, logit.T, live, live.T)
    return mixer_call(
        functools.partial(mixer_local_kernel, per_step, taps),
        heads,
        per_step,
        [flat(length)] * 3
        + [flat(RIM)] * 3
        + [flat(taps)] * 3
        + [whole(length, heads), whole(heads, length), whole(length, 1), whole(1, length)],
        [(flat(length), b16(length, channels))] * 3
        + [
            (by_head(length, 2 * HEAD_DIM), f32(heads, length, 2 * HEAD_DIM)),
            (by_head(length, length), f32(heads, length, length)),
            (by_head(length, 2 * HEAD_DIM), f32(heads, length, 2 * HEAD_DIM)),
            (by_head(HEAD_DIM, 2 * HEAD_DIM), f32(heads, HEAD_DIM, 2 * HEAD_DIM)),
        ],
        [pltpu.VMEM((RIM + length, HEAD_DIM), jnp.float32)],
        heads * 2 * length**3 * 30,
        args,
    )


def mixer_finish(mix, state, gain, per_step):
    heads, length, _ = mix.shape
    flat, whole, by_head = mixer_specs(length, heads, per_step)
    return mixer_call(
        functools.partial(mixer_finish_kernel, per_step),
        heads,
        per_step,
        [by_head(length, 2 * HEAD_DIM), by_head(HEAD_DIM, HEAD_DIM), whole(1, HEAD_DIM)],
        [
            (flat(length), f32(length, heads * HEAD_DIM)),
            (flat(length), b16(length, heads * HEAD_DIM)),
        ],
        [],
        heads * 2 * length**3,
        (mix, state, gain),
    )


def mixer_back_local(d_head, mixed, gain, q, k, wy, per_step):
    heads, length, _ = wy.shape
    flat, whole, by_head = mixer_specs(length, heads, per_step)
    return mixer_call(
        functools.partial(mixer_back_local_kernel, per_step),
        heads,
        per_step,
        [flat(length)] * 2 + [whole(1, HEAD_DIM)] + [flat(length)] * 2 + [by_head(length, 2 * HEAD_DIM)],
        [
            (by_head(length, HEAD_DIM), f32(heads, length, HEAD_DIM)),
            (by_head(length, HEAD_DIM), f32(heads, length, HEAD_DIM)),
            (by_head(HEAD_DIM, HEAD_DIM), f32(heads, HEAD_DIM, HEAD_DIM)),
            (whole(8, HEAD_DIM), f32(8, HEAD_DIM)),
        ],
        [],
        heads * 2 * length**3 * 5,
        (d_head, mixed, gain, q, k, wy),
    )


def mixer_back(pres, rims, convs, logit, live, q, k, v, wy, inv, state, d_mixed, d_fresh, d_state, per_step):
    length, channels = pres[0].shape
    heads = channels // HEAD_DIM
    taps = convs[0].shape[0]
    flat, whole, by_head = mixer_specs(length, heads, per_step)
    three = pl.BlockSpec((3, 8, per_step * HEAD_DIM), lambda h: (0, 0, h))
    return mixer_call(
        functools.partial(mixer_back_kernel, per_step, taps),
        heads,
        per_step,
        [flat(length)] * 3
        + [flat(RIM)] * 3
        + [flat(taps)] * 3
        + [whole(length, heads), whole(length, 1)]
        + [flat(length)] * 3
        + [
            by_head(length, 2 * HEAD_DIM),
            by_head(length, length),
            by_head(HEAD_DIM, HEAD_DIM),
            by_head(length, HEAD_DIM),
            by_head(length, HEAD_DIM),
            by_head(HEAD_DIM, HEAD_DIM),
        ],
        [(flat(length), b16(length, channels))] * 3
        + [
            (three, f32(3, 8, channels)),
            (three, f32(3, 8, channels)),
            (
                pl.BlockSpec((3, taps, per_step * HEAD_DIM), lambda h: (0, 0, h)),
                f32(3, taps, channels),
            ),
            (whole(length, heads), f32(length, heads)),
        ],
        [
            pltpu.VMEM((RIM + length, HEAD_DIM), jnp.float32),
            pltpu.VMEM((16 + length, HEAD_DIM), jnp.float32),
        ],
        heads * 2 * length**3 * 20,
        (*pres, *rims, *convs, logit, live, q, k, v, wy, inv, state, d_mixed, d_fresh, d_state),
    )


def mixer_forward_kernel(per_step, taps, spans, ways, *refs):
    pres, weights = refs[:3], refs[3:6]
    logit, logit_t, live, live_t, gain = refs[6:11]
    sources, normed = refs[11:14], refs[14]
    q_out, k_out, v_out, wy_out, inv_out, end_out, mixed_out, head_out, state_out, rim_out = refs[
        15:25
    ]
    normed_others = refs[25]
    ext, mix_all, rims, arriving, leaving, sends, receives, rim_sends, rim_receives = refs[26:35]
    halves = Halves(ways, normed, normed_others, *refs[35:], distances=list(range(1, ways - 1)))
    step = pl.program_id(0)
    position = lax.axis_index("seq")
    pairs = arriving.shape[0]
    length = live.shape[0]
    width = per_step * HEAD_DIM
    last = spans - 1
    after = place("seq", position + 1)

    def rim_copy(part):
        return pltpu.make_async_remote_copy(
            src_ref=sources[part].at[length - RIM :, :],
            dst_ref=rims.at[part],
            send_sem=rim_sends.at[part],
            recv_sem=rim_receives.at[part],
            device_id=after,
            device_id_type=MESH,
        )

    def state_copy(pair, i):
        return pltpu.make_async_remote_copy(
            src_ref=leaving.at[pair, i],
            dst_ref=arriving.at[pair, i],
            send_sem=sends.at[pair * per_step + i],
            recv_sem=receives.at[pair * per_step + i],
            device_id=after,
            device_id_type=MESH,
        )

    @pl.when(step == 0)
    def _():
        meet(
            [place("seq", (position + last) % spans), place("seq", (position + 1) % spans)]
            + halves.devices()
        )

        @pl.when(position != last)
        def _():
            for part in range(3):
                rim_copy(part).start()

        halves.start()

        @pl.when(position == 0)
        def _():
            rims[...] = jnp.zeros_like(rims)
            arriving[...] = jnp.zeros_like(arriving)

        @pl.when(position != 0)
        def _():
            for part in range(3):
                rim_copy(part).wait_recv()

        rim_out[...] = rims[...]

    @pl.when(step < pairs)
    def _():
        here = pl.ds(pl.multiple_of(step * width, width), width)
        found = local_part(
            pres, [rims[part, :, here] for part in range(3)], weights, logit[...], logit_t[...],
            live[...], live_t[...], ext, step * per_step, taps,
        )
        for i, (q, k, v, wy, inverse, mix, ends) in enumerate(found):
            span = slice(i * HEAD_DIM, (i + 1) * HEAD_DIM)
            q_out[:, span] = q
            k_out[:, span] = k
            v_out[:, span] = v
            wy_out[i] = wy
            inv_out[i] = inverse
            mix_all[step * per_step + i] = mix
            end_out[step * per_step + i] = ends

    pair = step - position

    @pl.when((pair >= 0) & (pair < pairs))
    def _():
        for i in range(per_step):

            @pl.when(position != 0)
            def _():
                state_copy(pair, i).wait_recv()

            ends = end_out[pair * per_step + i]
            moved = dot_left(ends[:, :HEAD_DIM], arriving[pair, i])
            leaving[pair, i] = (moved + ends[:, HEAD_DIM:]).astype(jnp.bfloat16)

            @pl.when(position != last)
            def _():
                state_copy(pair, i).start()

        for i in range(per_step):
            here = pl.ds(pl.multiple_of(pair * width + i * HEAD_DIM, HEAD_DIM), HEAD_DIM)
            state = arriving[pair, i]
            state_out[pair * per_step + i] = state
            mixed, head = finish_part(
                mix_all[pair * per_step + i], state, gain[...].astype(jnp.float32)
            )
            mixed_out[:, here] = mixed
            head_out[:, here] = head

    @pl.when(step == pairs)
    def _():
        halves.hand_on()

    @pl.when(step == pl.num_programs(0) - 1)
    def _():
        @pl.when(position != last)
        def _():
            for part in range(3):
                rim_copy(part).wait_send()
            for index in range(pairs):
                for i in range(per_step):
                    state_copy(index, i).wait_send()

        halves.finish()


def mixer_forward(
    pres, convs, logit, logit_t, live, live_t, gain, normed, per_step, spans, ways, number
):
    length, channels = pres[0].shape
    heads = channels // HEAD_DIM
    pairs = heads // per_step
    taps = convs[0].shape[0]
    width = per_step * HEAD_DIM
    wide = (heads, length, 2 * HEAD_DIM)
    states = (heads, HEAD_DIM, HEAD_DIM)

    def at(step):
        return jnp.minimum(step, pairs - 1)

    def flat(rows):
        return pl.BlockSpec((rows, width), lambda s: (0, at(s)))

    def by_head(*shape):
        return pl.BlockSpec((per_step,) + shape, lambda s: (at(s),) + (0,) * len(shape))

    def whole(*shape):
        return pl.BlockSpec(shape, lambda s: (0,) * len(shape))

    anywhere = pl.BlockSpec(memory_space=pl.ANY)
    return pl.pallas_call(
        functools.partial(mixer_forward_kernel, per_step, taps, spans, ways),
        grid=(pairs + spans - 1,),
        in_specs=[flat(length)] * 3
        + [flat(taps)] * 3
        + [whole(length, heads), whole(heads, length), whole(length, 1), whole(1, length)]
        + [whole(1, HEAD_DIM)]
        + [anywhere] * 4,
        out_specs=[flat(length)] * 3
        + [
            by_head(length, 2 * HEAD_DIM),
            by_head(length, length),
            whole(heads, HEAD_DIM, 2 * HEAD_DIM),
            whole(length, channels),
            whole(length, channels),
            whole(*states),
            whole(3, RIM, channels),
            anywhere,
        ],
        out_shape=[b16(length, channels)] * 3
        + [
            f32(*wide),
            f32(heads, length, length),
            f32(heads, HEAD_DIM, 2 * HEAD_DIM),
            f32(length, channels),
            b16(length, channels),
            b16(*states),
            b16(3, RIM, channels),
            b16(ways - 2, *normed.shape),
        ],
        scratch_shapes=[
            pltpu.VMEM((RIM + length, HEAD_DIM), jnp.float32),
            pltpu.VMEM(wide, jnp.float32),
            pltpu.VMEM((3, RIM, channels), jnp.bfloat16),
            pltpu.VMEM((pairs, per_step, HEAD_DIM, HEAD_DIM), jnp.bfloat16),
            pltpu.VMEM((pairs, per_step, HEAD_DIM, HEAD_DIM), jnp.bfloat16),
            pltpu.SemaphoreType.DMA((heads,)),
            pltpu.SemaphoreType.DMA((heads,)),
            pltpu.SemaphoreType.DMA((3,)),
            pltpu.SemaphoreType.DMA((3,)),
        ]
        + [pltpu.SemaphoreType.DMA((ways - 2,))] * 4,
        compiler_params=pltpu.CompilerParams(
            collective_id=number, has_side_effects=True, vmem_limit_bytes=VMEM
        ),
        cost_estimate=SHORT,
    )(*pres, *convs, logit, logit_t, live, live_t, gain, *pres, normed)


def mixer_backward_kernel(per_step, taps, spans, ways, tokens, *refs):
    d_head, mixed_ref, q_one, k_one, wy_one, gain = refs[:6]
    pres, weights = refs[6:9], refs[9:12]
    q_ref, k_ref, v_ref, wy, inv = refs[12:17]
    logit, live, state, ends, rims = refs[17:22]
    head_source, residual, up_source = refs[22 + tokens : 25 + tokens]
    d_q_out, d_k_out, d_v_out, conv_out, d_logit_out, gain_out = refs[25 + tokens : 31 + tokens]
    head_others, res_others, up_others = refs[31 + tokens : 34 + tokens]
    (
        d_mixed_all, d_fresh_all, d_end_all, arriving, sending, tails, rim_out, rim_in,
        ext, ext_back, sends, receives, rim_sends, rim_receives,
    ) = refs[34 + tokens : 48 + tokens]
    col_sends, col_receives, up_sends, up_receives, *half_sems = refs[48 + tokens :]
    halves = Halves(ways, residual, res_others, *half_sems)
    columns = row_copies(ways, (1, 2), up_source, up_others, up_sends, up_receives)
    columns += column_copies(ways, head_source, head_others, col_sends, col_receives)
    step = pl.program_id(0)
    position = lax.axis_index("seq")
    pairs = arriving.shape[0]
    length = live.shape[0]
    last = spans - 1
    before_here = place("seq", position - 1)

    def state_copy(pair):
        return pltpu.make_async_remote_copy(
            src_ref=sending.at[pair],
            dst_ref=arriving.at[pair],
            send_sem=sends.at[pair],
            recv_sem=receives.at[pair],
            device_id=before_here,
            device_id_type=MESH,
        )

    def rim_copy():
        return pltpu.make_async_remote_copy(
            src_ref=rim_out,
            dst_ref=rim_in,
            send_sem=rim_sends.at[0],
            recv_sem=rim_receives.at[0],
            device_id=before_here,
            device_id_type=MESH,
        )

    @pl.when(step == 0)
    def _():
        meet(
            [place("seq", (position + last) % spans), place("seq", (position + 1) % spans)]
            + halves.devices()
        )
        for copy in columns:
            copy.start()
        halves.start()
        d_logit_out[...] = jnp.zeros_like(d_logit_out)
        gain_out[...] = jnp.zeros_like(gain_out)

        @pl.when(position == last)
        def _():
            arriving[...] = jnp.zeros_like(arriving)
            rim_in[...] = jnp.zeros_like(rim_in)

    @pl.when(step < pairs)
    def _():
        for i in range(per_step):
            d_out, mixed, q, k = head_columns((d_head, mixed_ref, q_one, k_one), i)
            d_mixed, d_fresh, d_end, gain_row = back_local_part(
                d_out, mixed, gain[...].astype(jnp.float32), q, k, wy_one[i]
            )
            d_mixed_all[step * per_step + i] = d_mixed
            d_fresh_all[step * per_step + i] = d_fresh
            d_end_all[step * per_step + i] = d_end
            gain_out[...] += jnp.broadcast_to(gain_row, gain_out.shape)

    pair = step - (last - position)

    @pl.when((pair >= 0) & (pair < pairs))
    def _():
        @pl.when(position != last)
        def _():
            state_copy(pair).wait_recv()

        for i in range(per_step):
            head = pair * per_step + i
            moved = dot_left(ends[head, :, :HEAD_DIM], arriving[pair, i], (0, 0))
            sending[pair, i] = (moved + d_end_all[head]).astype(jnp.bfloat16)

        @pl.when(position != 0)
        def _():
            state_copy(pair).start()

    ready = step - last

    @pl.when(ready >= 0)
    def _():
        outs = (d_q_out, d_k_out, d_v_out)
        for i in range(per_step):
            head = ready * per_step + i
            here = pl.ds(pl.multiple_of(head * HEAD_DIM, HEAD_DIM), HEAD_DIM)
            q, k, v = head_columns((q_ref, k_ref, v_ref), i)
            *grads, d_logit = back_part(
                q, k, v, wy[i], inv[i], state[head], arriving[ready, i],
                d_mixed_all[head], d_fresh_all[head], column_of(logit[...], head), live[...],
            )
            lane = lax.broadcasted_iota(jnp.int32, d_logit_out.shape, 1)
            d_logit_out[...] += jnp.where(lane == head, d_logit, 0.0)
            span = slice(i * HEAD_DIM, (i + 1) * HEAD_DIM)
            for part in range(3):
                own, before, rows = back_conv_part(
                    part, pres[part][:, span], rims[part, :, here],
                    weights[part][:, span], grads[part], taps, ext, ext_back,
                )
                conv_out[part, :, here] = rows
                outs[part][:, here] = own.astype(jnp.bfloat16)
                tails[part, :, here] = own[length - 16 :, :]
                rim_out[part, :, here] = before

    @pl.when(step == pl.num_programs(0) - 1)
    def _():
        @pl.when(position != 0)
        def _():
            rim_copy().start()

        halves.hand_on()

        @pl.when(position != last)
        def _():
            rim_copy().wait_recv()

        for part, out in enumerate((d_q_out, d_k_out, d_v_out)):
            joined = tails[part] + jnp.concatenate(
                [jnp.zeros_like(rim_in[part]), rim_in[part]], 0
            )
            out[length - 16 :, :] = joined.astype(jnp.bfloat16)

        @pl.when(position != 0)
        def _():
            rim_copy().wait_send()
            for index in range(pairs):
                state_copy(index).wait_send()

        for copy in columns:
            copy.wait()
        halves.finish()


def mixer_backward(
    d_head, mixed, gain, pres, rims, convs, logit, live, q, k, v, wy, inv, state, ends, tokens,
    head_out, residual, turned, per_step, spans, ways, number,
):
    length, channels = pres[0].shape
    heads = channels // HEAD_DIM
    pairs = heads // per_step
    taps = convs[0].shape[0]
    width = per_step * HEAD_DIM
    lag = spans - 1

    def early(step):
        return jnp.minimum(step, pairs - 1)

    def late(step):
        return jnp.maximum(step - lag, 0)

    def flat(rows, at):
        return pl.BlockSpec((rows, width), lambda s: (0, at(s)))

    def by_head(at, *shape):
        return pl.BlockSpec((per_step,) + shape, lambda s: (at(s),) + (0,) * len(shape))

    def whole(*shape):
        return pl.BlockSpec(shape, lambda s: (0,) * len(shape))

    wide = (length, 2 * HEAD_DIM)
    states = (pairs, per_step, HEAD_DIM, HEAD_DIM)
    return pl.pallas_call(
        functools.partial(mixer_backward_kernel, per_step, taps, spans, ways, len(tokens)),
        grid=(pairs + lag,),
        in_specs=[flat(length, early)] * 4
        + [by_head(early, *wide), whole(1, HEAD_DIM)]
        + [flat(length, late)] * 3
        + [flat(taps, late)] * 3
        + [flat(length, late)] * 3
        + [by_head(late, *wide), by_head(late, length, length)]
        + [whole(length, heads), whole(length, 1), whole(heads, HEAD_DIM, HEAD_DIM)]
        + [whole(heads, HEAD_DIM, 2 * HEAD_DIM), whole(3, RIM, channels)]
        + [pl.BlockSpec(memory_space=pl.ANY)] * (len(tokens) + 3),
        out_specs=[whole(length, channels)] * 3
        + [whole(3, taps, channels), whole(length, heads), whole(8, HEAD_DIM)]
        + [pl.BlockSpec(memory_space=pl.ANY)] * 3,
        out_shape=[b16(length, channels)] * 3
        + [f32(3, taps, channels), f32(length, heads), f32(8, HEAD_DIM)]
        + [b16(ways - 1, length, channels // ways)]
        + [b16(ways - 1, *residual.shape), b16(ways - 1, 1, *turned.shape[2:])],
        scratch_shapes=[
            pltpu.VMEM((heads, length, HEAD_DIM), jnp.float32),
            pltpu.VMEM((heads, length, HEAD_DIM), jnp.float32),
            pltpu.VMEM((heads, HEAD_DIM, HEAD_DIM), jnp.float32),
            pltpu.VMEM(states, jnp.bfloat16),
            pltpu.VMEM(states, jnp.bfloat16),
            pltpu.VMEM((3, 16, channels), jnp.float32),
            pltpu.VMEM((3, 8, channels), jnp.float32),
            pltpu.VMEM((3, 8, channels), jnp.float32),
            pltpu.VMEM((RIM + length, HEAD_DIM), jnp.float32),
            pltpu.VMEM((16 + length, HEAD_DIM), jnp.float32),
            pltpu.SemaphoreType.DMA((pairs,)),
            pltpu.SemaphoreType.DMA((pairs,)),
            pltpu.SemaphoreType.DMA((1,)),
            pltpu.SemaphoreType.DMA((1,)),
        ]
        + [pltpu.SemaphoreType.DMA((ways - 1,))] * 8,
        compiler_params=pltpu.CompilerParams(
            collective_id=number, has_side_effects=True, vmem_limit_bytes=VMEM
        ),
        cost_estimate=SHORT,
    )(
        d_head, mixed, q, k, wy, gain, *pres, *convs, q, k, v, wy, inv, logit, live, state, ends,
        rims, *tokens, head_out, residual, turned,
    )


def feed_kernel(
    x_ref, d_ref, gate_w, up_w, down_w, token, feed_out, d_x_out, turned_out, feed_sum, d_x_sum
):
    step = pl.program_id(0)
    x = x_ref[...]
    d_out = d_ref[...]
    gate = dot_low(x, gate_w[...])
    up = dot_low(x, up_w[...])
    d_hidden = dot_low(d_out, down_w[...], (1, 1))
    sig = jax.nn.sigmoid(gate)
    hidden = (gate * sig * up).astype(jnp.bfloat16)
    d_gate = (d_hidden * up * sig * (1.0 + gate * (1.0 - sig))).astype(jnp.bfloat16)
    d_up = (d_hidden * gate * sig).astype(jnp.bfloat16)
    for place, part in enumerate((hidden, d_gate, d_up)):
        turned_out[place] = part.T
    feed = dot_low(hidden, down_w[...])
    d_x = dot_low(d_gate, gate_w[...], (1, 1)) + dot_low(d_up, up_w[...], (1, 1))

    @pl.when(step == 0)
    def _():
        feed_sum[...] = feed
        d_x_sum[...] = d_x

    @pl.when(step > 0)
    def _():
        feed_sum[...] += feed
        d_x_sum[...] += d_x

    @pl.when(step == pl.num_programs(0) - 1)
    def _():
        feed_out[...] = feed_sum[...].astype(jnp.bfloat16)
        d_x_out[...] = d_x_sum[...].astype(jnp.bfloat16)


def feed_forward(x, d_out, gate_weight, up_weight, down_weight, token):
    length, width = x.shape
    units = gate_weight.shape[1]
    tile = 256 if units % 256 == 0 else units
    whole = pl.BlockSpec((length, width), lambda f: (0, 0))
    column = pl.BlockSpec((width, tile), lambda f: (0, f))
    return pl.pallas_call(
        feed_kernel,
        grid=(units // tile,),
        in_specs=[whole, whole, column, column]
        + [pl.BlockSpec((tile, width), lambda f: (f, 0)), pl.BlockSpec(memory_space=pl.ANY)],
        out_specs=[whole, whole, pl.BlockSpec((3, tile, length), lambda f: (0, f, 0))],
        out_shape=[b16(length, width), b16(length, width), b16(3, units, length)],
        scratch_shapes=[pltpu.VMEM((length, width), jnp.float32)] * 2,
        compiler_params=pltpu.CompilerParams(vmem_limit_bytes=VMEM),
        cost_estimate=SHORT,
    )(x, d_out, gate_weight, up_weight, down_weight, token)


def back_projection_kernel(ways, *refs):
    sources, d_logit, weights, beta_w = refs[:3], refs[3], refs[4:7], refs[7]
    shared, normed = refs[8:11], refs[11]
    out, others, normed_far = refs[-15], refs[-14:-11], refs[-11]
    sends, receives = refs[-10:-7], refs[-7:-4]
    far = Halves(ways, normed, normed_far, *refs[-4:], distances=[ways - 1])
    step = pl.program_id(0)
    copies = [
        copy
        for part in range(3)
        for copy in column_copies(ways, shared[part], others[part], sends[part], receives[part])
    ]

    @pl.when(step == 0)
    def _():
        own = lax.axis_index("dp")
        meet([place("dp", partner(own, by)) for by in range(1, ways)] + [far.other])
        for copy in copies:
            copy.start()
        far.start()

    total = dot_low(d_logit[...].astype(jnp.bfloat16), beta_w[...])
    for source, weight in zip(sources, weights):
        total = total + dot_low(source[...], weight[...], (1, 1))
    out[...] = total.astype(jnp.bfloat16)

    @pl.when(step == pl.num_programs(0) - 1)
    def _():
        far.hand_on()
        for copy in copies:
            copy.wait()
        far.finish()


def back_projection(sources, d_logit, weights, beta_weight, normed, ways, tokens, number):
    length, channels = sources[0].shape
    width, heads = beta_weight.shape
    tile = width // 4
    anywhere = pl.BlockSpec(memory_space=pl.ANY)
    return pl.pallas_call(
        functools.partial(back_projection_kernel, ways),
        grid=(width // tile,),
        in_specs=[pl.BlockSpec((length, channels), lambda n: (0, 0))] * 3
        + [pl.BlockSpec((length, heads), lambda n: (0, 0))]
        + [pl.BlockSpec((tile, channels), lambda n: (n, 0))] * 3
        + [pl.BlockSpec((heads, tile), lambda n: (0, n))]
        + [anywhere] * (4 + len(tokens)),
        out_specs=[pl.BlockSpec((length, tile), lambda n: (0, n))] + [anywhere] * 4,
        out_shape=[b16(length, width)]
        + [b16(ways - 1, length, channels // ways)] * 3
        + [b16(1, *normed.shape)],
        scratch_shapes=[pltpu.SemaphoreType.DMA((ways - 1,))] * 6
        + [pltpu.SemaphoreType.DMA((1,))] * 4,
        compiler_params=pltpu.CompilerParams(
            collective_id=number, has_side_effects=True, vmem_limit_bytes=VMEM
        ),
        cost_estimate=SHORT,
    )(*sources, d_logit, *weights, beta_weight.T, *sources, normed, *tokens)


def project_kernel(lengths, tokens, first_gain, second_gain, q_w, k_w, v_w, beta_w, *refs):
    q_out, k_out, v_out, logit_out, logit_t_out, stream_out, normed_out, gains_out = refs[:8]
    live_out, live_t_out, arriving, gains, gains_in, sends, receives = refs[8:]
    step = pl.program_id(0)
    half = tokens.shape[1]

    @pl.when(step == 0)
    def _():
        core = lax.axis_index("head")
        other = place("head", 1 - core)
        mine = pl.ds(pl.multiple_of(core * half, half), half)
        theirs = pl.ds(pl.multiple_of((1 - core) * half, half), half)
        row = lax.broadcasted_iota(jnp.int32, gains.shape, 0)
        first, second = [
            jnp.concatenate(
                [part[...].astype(jnp.float32)[i : i + 1] for i in range(part.shape[0])], 1
            )
            for part in (first_gain, second_gain)
        ]
        gains[...] = jnp.where(row == 0, first, second).astype(jnp.bfloat16)
        meet([other])
        copies = [
            pltpu.make_async_remote_copy(
                src_ref=source, dst_ref=target, send_sem=sends.at[index],
                recv_sem=receives.at[index], device_id=other, device_id_type=MESH,
            )
            for index, (source, target) in enumerate(((tokens, arriving), (gains, gains_in)))
        ]
        for copy in copies:
            copy.start()
        left = lengths[0] - lax.axis_index("seq") * tokens.shape[0]
        for axis, out in ((0, live_out), (1, live_t_out)):
            index = lax.broadcasted_iota(jnp.int32, out.shape, axis)
            out[...] = jnp.where(index < left, 1.0, 0.0)
        stream_out[:, mine] = tokens[...]
        gains_out[:, mine] = gains[...]
        for copy in copies:
            copy.wait()
        stream_out[:, theirs] = arriving[...]
        gains_out[:, theirs] = gains_in[...]
        stream = stream_out[...].astype(jnp.float32)
        scale = lax.rsqrt(jnp.mean(stream * stream, axis=-1, keepdims=True) + EPSILON)
        gain = gains_out[...].astype(jnp.float32)[0:1]
        normed_out[...] = (stream * scale * gain).astype(jnp.bfloat16)
        logit_out[...] = dot_low(normed_out[...], beta_w[...], (1, 1))
        logit_t_out[...] = dot_low(beta_w[...], normed_out[...], (1, 1))

    for part, (weight, out) in enumerate(((q_w, q_out), (k_w, k_out), (v_w, v_out))):

        @pl.when(step // 2 == part)
        def _():
            out[...] = dot_low(normed_out[...], weight[...]).astype(jnp.bfloat16)


def projected(lengths, tokens, first_gain, second_gain, weights, beta_weight, number):
    length, half = tokens.shape
    width, channels = weights[0].shape
    heads = beta_weight.shape[1]
    tile = channels // 2

    def whole(*shape):
        return pl.BlockSpec(shape, lambda s: (0,) * len(shape))

    def tiles(rows, part):
        return pl.BlockSpec((rows, tile), lambda s: (0, jnp.clip(s - 2 * part, 0, 1)))

    return pl.pallas_call(
        project_kernel,
        grid=(6,),
        in_specs=[pl.BlockSpec(memory_space=pltpu.SMEM), whole(length, half)]
        + [whole(half // 128, 128)] * 2
        + [tiles(width, part) for part in range(3)]
        + [whole(heads, width)],
        out_specs=[tiles(length, part) for part in range(3)]
        + [whole(length, heads), whole(heads, length), whole(length, width)]
        + [whole(length, width), whole(16, width), whole(length, 1), whole(1, length)],
        out_shape=[b16(length, channels)] * 3
        + [f32(length, heads), f32(heads, length), b16(length, width)]
        + [b16(length, width), b16(16, width), f32(length, 1), f32(1, length)],
        scratch_shapes=[
            pltpu.VMEM((length, half), jnp.bfloat16),
            pltpu.VMEM((16, half), jnp.bfloat16),
            pltpu.VMEM((16, half), jnp.bfloat16),
            pltpu.SemaphoreType.DMA((2,)),
            pltpu.SemaphoreType.DMA((2,)),
        ],
        compiler_params=pltpu.CompilerParams(
            collective_id=number, has_side_effects=True, vmem_limit_bytes=VMEM
        ),
        cost_estimate=SHORT,
    )(
        lengths, tokens, first_gain.reshape(-1, 128), second_gain.reshape(-1, 128), *weights,
        beta_weight.T,
    )


def units_kernel(
    ways, steps, head_ref, out_w, stream_ref, gains, d_own, d_other, live, gate_w, up_w, down_w,
    plane, turned_out, d_gate_out, d_up_out, hidden_out, stream_out, normed_out, own_out, others,
    plane_out, part_low, arriving, turned_hidden, d_ref, sends, receives, hidden_sends,
    hidden_receives, plane_sems,
):
    plane_copy = pltpu.make_async_remote_copy(
        src_ref=plane, dst_ref=plane_out, send_sem=plane_sems.at[0], recv_sem=plane_sems.at[1],
        device_id=place("head", 1 - lax.axis_index("head")), device_id_type=MESH,
    )
    own = lax.axis_index("dp")
    tile = hidden_out.shape[1]
    part_rows = tile // ways

    def hidden_copy(step, by):
        peer = partner(own, by)
        start = pl.multiple_of(step * tile + peer * part_rows, part_rows)
        return pltpu.make_async_remote_copy(
            src_ref=turned_hidden.at[pl.ds(start, part_rows), :],
            dst_ref=others.at[
                by - 1, pl.ds(pl.multiple_of(step * part_rows, part_rows), part_rows), :
            ],
            send_sem=hidden_sends.at[(by - 1) * steps + step],
            recv_sem=hidden_receives.at[(by - 1) * steps + step],
            device_id=place("dp", peer),
            device_id_type=MESH,
        )

    @pl.when(pl.program_id(0) == 0)
    def _():
        other = place("head", 1 - lax.axis_index("head"))
        meet([other] + [place("dp", partner(own, by)) for by in range(1, ways)])
        pieces = part_low.shape[0]
        width = part_low.shape[2]
        copies = []
        for piece in range(pieces):
            span = slice(piece * width, (piece + 1) * width)
            part_low[piece] = dot_low(head_ref[...], out_w[:, span]).astype(jnp.bfloat16)
            copy = pltpu.make_async_remote_copy(
                src_ref=part_low.at[piece], dst_ref=arriving.at[piece],
                send_sem=sends.at[piece], recv_sem=receives.at[piece],
                device_id=other, device_id_type=MESH,
            )
            copy.start()
            copies.append(copy)
        core = lax.axis_index("head")
        half = d_own.shape[1]
        plane_copy.start()
        for place_of, part in ((core, d_own), (1 - core, d_other)):
            masked = part[...].astype(jnp.float32) * live[...]
            here = pl.ds(pl.multiple_of(place_of * half, half), half)
            d_ref[:, here] = masked.astype(jnp.bfloat16)
        squares = 0.0
        for piece, copy in enumerate(copies):
            span = slice(piece * width, (piece + 1) * width)
            copy.wait()
            both = part_low[piece].astype(jnp.float32) + arriving[piece].astype(jnp.float32)
            stream = stream_ref[:, span].astype(jnp.float32) + both
            stream_out[:, span] = stream
            squares = squares + jnp.sum(stream * stream, axis=-1, keepdims=True)
        scale = lax.rsqrt(squares / (pieces * width) + EPSILON)
        gain = gains[...].astype(jnp.float32)[1:2]
        normed_out[...] = (stream_out[...] * scale * gain).astype(jnp.bfloat16)

    x = normed_out[...]
    gate = dot_low(x, gate_w[...])
    up = dot_low(x, up_w[...])
    d_hidden = dot_low(d_ref[...], down_w[...], (1, 1))
    sig = jax.nn.sigmoid(gate)
    hidden = (gate * sig * up).astype(jnp.bfloat16)
    d_gate = (d_hidden * up * sig * (1.0 + gate * (1.0 - sig))).astype(jnp.bfloat16)
    d_up = (d_hidden * gate * sig).astype(jnp.bfloat16)
    for index, (part, out) in enumerate(
        ((hidden, hidden_out), (d_gate, d_gate_out), (d_up, d_up_out))
    ):
        out[...] = part
        if index > 0:
            turned_out[index - 1] = part.T
    step = pl.program_id(0)
    live_hidden = (hidden.astype(jnp.float32) * live[...]).astype(jnp.bfloat16)
    turned_hidden[pl.ds(pl.multiple_of(step * tile, tile), tile), :] = live_hidden.T
    for by in range(1, ways):
        hidden_copy(step, by).start()
    own_out[pl.ds(pl.multiple_of(step * part_rows, part_rows), part_rows), :] = turned_hidden[
        pl.ds(pl.multiple_of(step * tile + own * part_rows, part_rows), part_rows), :
    ]

    @pl.when(step == steps - 1)
    def _():
        for index in range(steps):
            for by in range(1, ways):
                hidden_copy(index, by).wait()
        plane_copy.wait()


def hidden_units(
    head_out, out_weight, stream, gains, d_own, d_other, live, gate_weight, up_weight,
    down_weight, plane, number,
):
    ways = lax.axis_size("dp")
    length, width = stream.shape
    channels = head_out.shape[1]
    units = gate_weight.shape[1]
    tile = 256
    whole = pl.BlockSpec((length, width), lambda f: (0, 0))
    column = pl.BlockSpec((width, tile), lambda f: (0, f))
    flat = pl.BlockSpec((length, tile), lambda f: (0, f))
    chunk = units // ways
    return pl.pallas_call(
        functools.partial(units_kernel, ways, units // tile),
        grid=(units // tile,),
        in_specs=[
            pl.BlockSpec((length, channels), lambda f: (0, 0)),
            pl.BlockSpec((channels, width), lambda f: (0, 0)),
            whole,
            pl.BlockSpec((16, width), lambda f: (0, 0)),
            pl.BlockSpec((length, width // 2), lambda f: (0, 0)),
            pl.BlockSpec((length, width // 2), lambda f: (0, 0)),
            pl.BlockSpec((length, 1), lambda f: (0, 0)),
            column,
            column,
        ]
        + [pl.BlockSpec((tile, width), lambda f: (f, 0)), pl.BlockSpec(memory_space=pl.ANY)],
        out_specs=[pl.BlockSpec((2, tile, length), lambda f: (0, f, 0))]
        + [flat] * 3
        + [whole] * 2
        + [pl.BlockSpec((chunk, length), lambda f: (0, 0))]
        + [pl.BlockSpec(memory_space=pl.ANY)] * 2,
        out_shape=[b16(2, units, length)]
        + [b16(length, units)] * 3
        + [f32(length, width), b16(length, width)]
        + [b16(chunk, length), b16(ways - 1, chunk, length), b16(*plane.shape)],
        scratch_shapes=[pltpu.VMEM((4, length, width // 4), jnp.bfloat16)] * 2
        + [pltpu.VMEM((units, length), jnp.bfloat16), pltpu.VMEM((length, width), jnp.bfloat16)]
        + [pltpu.SemaphoreType.DMA((4,))] * 2
        + [pltpu.SemaphoreType.DMA(((ways - 1) * (units // tile),))] * 2
        + [pltpu.SemaphoreType.DMA((2,))],
        compiler_params=pltpu.CompilerParams(
            collective_id=number, has_side_effects=True, vmem_limit_bytes=VMEM
        ),
        cost_estimate=SHORT,
    )(
        head_out, out_weight, stream, gains, d_own, d_other, live, gate_weight, up_weight,
        down_weight, plane,
    )


def row_copies(ways, entries, source, out, sends, receives):
    own = lax.axis_index("dp")
    copies = []
    for by in range(1, ways):
        peer = partner(own, by)
        copies.append(
            pltpu.make_async_remote_copy(
                src_ref=source.at[entries[0] : entries[1], peer],
                dst_ref=out.at[by - 1],
                send_sem=sends.at[by - 1],
                recv_sem=receives.at[by - 1],
                device_id=place("dp", peer),
                device_id_type=MESH,
            )
        )
    return copies


def feed_back_kernel(ways, entries, *refs):
    d_gate, d_up, hidden, gate_w, up_w, down_w = refs[:6]
    up_own, up_other, live, gains, source, normed, stream_in, out_w_in = refs[6:14]
    feed_out, d_stream_out, low_out, d_head_out, second_out, others, normed_others = refs[-20:-13]
    d_x, arriving, masked, stream_ref, out_w = refs[-13:-8]
    swap_sems, load_sems = refs[-8:-6]
    sends, receives = refs[-6:-4]
    halves = Halves(ways, normed, normed_others, *refs[-4:])
    copies = row_copies(ways, entries, source, others, sends, receives)
    step = pl.program_id(0)
    tile = feed_out.shape[1]
    width = d_x.shape[1]
    loads = [
        pltpu.make_async_copy(stream_in, stream_ref, load_sems.at[0]),
        pltpu.make_async_copy(out_w_in, out_w, load_sems.at[1]),
    ]

    @pl.when(step == 0)
    def _():
        meet(halves.devices())
        halves.start()
        for copy in copies + loads:
            copy.start()

    d_tile = dot_low(d_gate[...], gate_w[...], (1, 1)) + dot_low(d_up[...], up_w[...], (1, 1))
    d_x[:, pl.ds(pl.multiple_of(step * tile, tile), tile)] = d_tile.astype(jnp.bfloat16)
    feed_out[...] = dot_low(hidden[...], down_w[...]).astype(jnp.bfloat16)

    @pl.when(step == pl.num_programs(0) - 1)
    def _():
        swap = pltpu.make_async_remote_copy(
            src_ref=d_x, dst_ref=arriving, send_sem=swap_sems.at[0], recv_sem=swap_sems.at[1],
            device_id=halves.other, device_id_type=MESH,
        )
        swap.start()
        core = lax.axis_index("head")
        half = up_own.shape[1]
        for place_of, part in ((core, up_own), (1 - core, up_other)):
            here = pl.ds(pl.multiple_of(place_of * half, half), half)
            masked[:, here] = (part[...].astype(jnp.float32) * live[...]).astype(jnp.bfloat16)
        for copy in loads:
            copy.wait()
        swap.wait()
        d_two = d_x[...].astype(jnp.float32) + arriving[...].astype(jnp.float32)
        stream = stream_ref[...]
        scale = lax.rsqrt(jnp.mean(stream * stream, axis=-1, keepdims=True) + EPSILON)
        weighted = gains[...].astype(jnp.float32)[1:2] * d_two
        inner = jnp.sum(weighted * stream, axis=-1, keepdims=True)
        d_stream = (
            masked[...].astype(jnp.float32)
            + scale * weighted
            - stream * (scale * scale * scale * inner / width)
        )
        second_out[...] = jnp.sum(d_two * stream * scale, axis=0, keepdims=True)
        d_stream_out[...] = d_stream
        low_out[...] = d_stream.astype(jnp.bfloat16)
        d_head_out[...] = dot_low(low_out[...], out_w[...], (1, 1))
        halves.hand_on()
        for copy in copies:
            copy.wait()
        halves.finish()


def feed_back(
    d_gate, d_up, hidden, weights, up_own, up_other, live, gains, source, entries, normed, stream,
    out_weight, tokens, number,
):
    ways = lax.axis_size("dp")
    length, units = hidden.shape
    width = normed.shape[1]
    channels = out_weight.shape[0]
    tile = width // 8
    anywhere = pl.BlockSpec(memory_space=pl.ANY)
    row = pl.BlockSpec((tile, units), lambda n: (n, 0))
    out = pl.BlockSpec((length, tile), lambda n: (0, n))

    def whole(*shape):
        return pl.BlockSpec(shape, lambda n: (0,) * len(shape))

    return pl.pallas_call(
        functools.partial(feed_back_kernel, ways, entries),
        grid=(8,),
        in_specs=[whole(length, units)] * 3
        + [row, row, pl.BlockSpec((units, tile), lambda n: (0, n))]
        + [whole(length, width // 2)] * 2
        + [whole(length, 1), whole(16, width)]
        + [anywhere] * (4 + len(tokens)),
        out_specs=[out, whole(length, width), whole(length, width), whole(length, channels)]
        + [whole(1, width), anywhere, anywhere],
        out_shape=[
            b16(length, width), f32(length, width), b16(length, width), f32(length, channels),
            f32(1, width),
            b16(ways - 1, entries[1] - entries[0], *source.shape[2:]),
            b16(ways - 1, length, width),
        ],
        scratch_shapes=[pltpu.VMEM((length, width), jnp.bfloat16)] * 3
        + [pltpu.VMEM((length, width), jnp.float32), pltpu.VMEM(out_weight.shape, jnp.bfloat16)]
        + [pltpu.SemaphoreType.DMA((2,))] * 2
        + [pltpu.SemaphoreType.DMA((ways - 1,))] * 6,
        compiler_params=pltpu.CompilerParams(
            collective_id=number, has_side_effects=True, vmem_limit_bytes=VMEM
        ),
        cost_estimate=SHORT,
    )(
        d_gate, d_up, hidden, *weights, up_own, up_other, live, gains, source, normed, stream,
        out_weight, *tokens,
    )


def pieces_kernel(groups, slots, ways, turned, at, *refs):
    lefts = refs[: groups * slots]
    rights = refs[groups * slots : (groups + ways) * slots]
    out, left_all, right_all = refs[-3:]
    length = rights[0].shape[-2]
    rows = rights[0].shape[-1]
    count = left_all.shape[0] // groups

    @pl.when(pl.program_id(0) == 0)
    def _():
        for group in range(groups):
            for slot in range(slots):
                block = lefts[group * slots + slot][...]
                block = block.reshape(block.shape[-2:])
                left_all[
                    group * count : (group + 1) * count, slot * length : (slot + 1) * length
                ] = block if turned else block.T

    for slot in range(slots):
        for way in range(ways):
            right = rights[slot * ways + way][...]
            right_all[
                slot * length : (slot + 1) * length, way * rows : (way + 1) * rows
            ] = right.reshape(right.shape[-2:])
    out[0] = dot_low(left_all[...], right_all[...]).astype(jnp.bfloat16)


def span_pieces(lefts, count, rights, length, width, spans, turned, tokens=()):
    groups = len(lefts)
    lefts = [left for group in lefts for left in group]
    slots = len(rights)
    ways = lax.axis_size("dp")
    rows = width // (ways * spans)

    def left_block(block, at_place):
        return pl.BlockSpec(block, lambda s, at: at_place(at[0]))

    def right_block(block, at_place, column):
        return pl.BlockSpec(
            block + (rows,), lambda s, at: tuple(at_place(at[0])) + (column(s),)
        )

    rights = [right for slot in rights for right in slot]

    return pl.pallas_call(
        functools.partial(pieces_kernel, groups, slots, ways, turned),
        grid_spec=pltpu.PrefetchScalarGridSpec(
            num_scalar_prefetch=1,
            grid=(spans,),
            in_specs=[left_block(block, where) for _, block, where in lefts]
            + [right_block(block, where, column) for _, block, where, column in rights]
            + [pl.BlockSpec(memory_space=pl.ANY)] * len(tokens),
            out_specs=pl.BlockSpec((1, count, ways * rows), lambda s, at: (s, 0, 0)),
            scratch_shapes=[
                pltpu.VMEM((count, slots * length), jnp.bfloat16),
                pltpu.VMEM((slots * length, ways * rows), jnp.bfloat16),
            ],
        ),
        out_shape=b16(spans, count, ways * rows),
        compiler_params=pltpu.CompilerParams(vmem_limit_bytes=VMEM),
        cost_estimate=SHORT,
    )(
        lax.axis_index("dp")[None],
        *[array for array, _, _ in lefts],
        *[array for array, _, _, _ in rights],
        *tokens,
    )


def widen_kernel(count, turned, starts, share_of, ways, *refs):
    small = refs[count]
    outs = refs[count + 1 :]
    chunk = refs[0].shape[0] // ways
    part = 256 // ways
    for way in range(ways):
        for tile in range(chunk // part):
            start = way * chunk + tile * part
            to = tile * 256 + way * part
            outs[0][to : to + part, :] = refs[0][start : start + part, :].astype(jnp.float32)
    for index in range(1, count):
        whole = refs[index][...].astype(jnp.float32)
        outs[index][...] = whole.T if turned[index] else whole
    gain, first, second, taps, beta = outs[count], *outs[count + 1 : count + 3], outs[count + 3 : -1], outs[-1]
    gain[...] = small[starts[0] : starts[0] + 1, :]
    first[...] = small[starts[1] : starts[1] + first.shape[0], :]
    second[...] = small[starts[2] : starts[2] + second.shape[0], :]
    row = starts[3]
    for out in taps:
        high, wide = out.shape
        for tap in range(high):
            for lane in range(wide // 128):
                out[tap : tap + 1, lane * 128 : (lane + 1) * 128] = small[row : row + 1, :]
                row += 1
    heads = beta.shape[0]
    width = share_of[1] // 128
    share = lax.axis_index("dp") * share_of[0] + lax.axis_index("seq")
    rows = [small[pl.ds(starts[4] + head * width + share, 1), :] for head in range(heads)]
    beta[...] = jnp.concatenate(rows, 0)


def widened(arrays, turned, small, starts, channels, taps, heads, width):
    inside = pl.BlockSpec(memory_space=pltpu.VMEM)
    shapes = [
        f32(*(array.shape[::-1] if turn else array.shape)) for array, turn in zip(arrays, turned)
    ]
    shapes += [f32(1, 128), f32(width // 256, 128), f32(width // 256, 128)]
    shapes += [f32(taps, channels)] * 3 + [f32(heads, 128)]
    return pl.pallas_call(
        functools.partial(
            widen_kernel, len(arrays), turned, starts, (lax.axis_size("seq"), width),
            lax.axis_size("dp"),
        ),
        out_shape=shapes,
        in_specs=[inside] * (len(arrays) + 1),
        out_specs=[inside] * len(shapes),
        compiler_params=pltpu.CompilerParams(vmem_limit_bytes=VMEM),
        cost_estimate=SHORT,
    )(*arrays, small)


def doublings(size):
    return [1 << bit for bit in range(size.bit_length() - 1)]


def finish_kernel(spans, ways, fed, split, *refs):
    out_raw, mix_raw, small = refs[:3]
    pieces, refs = refs[3 : 3 + fed], refs[3 + fed :]
    stages, small_out, refs = refs[: 4 + fed], refs[4 + fed], refs[5 + fed :]
    received, handed, totals, *refs = refs
    sends, receives, owner_sends, owner_receives, own_sems = refs[:5]
    small_in, small_sent, small_sends, small_receives = refs[5:]
    own = lax.axis_index("dp")
    core = lax.axis_index("head")
    position = lax.axis_index("seq")
    last = spans - 1
    rounds = spans - 1
    whole = out_raw.shape[1]
    count = whole // split
    groups = split + mix_raw.shape[1] // count
    rows = stages[0].shape[1]
    peers = [partner(own, by) for by in range(1, ways)]

    def raw_at(group, shard):
        if group < split:
            return out_raw.at[shard, group * count : (group + 1) * count, :]
        return mix_raw.at[shard, (group - split) * count : (group - split + 1) * count, :]

    def line_copy(way, turn, group, src):
        step = 1 if way == 0 else -1
        slot = (way * rounds + turn) * groups + group
        return pltpu.make_async_remote_copy(
            src_ref=src,
            dst_ref=received.at[way, turn, group],
            send_sem=sends.at[slot],
            recv_sem=receives.at[slot],
            device_id=place("seq", position + step),
            device_id_type=MESH,
        )

    def owner_copies(index, source):
        high = source.shape[0]
        turn = core * (ways // 2) if index == 0 else 0

        def block_of(peer):
            start = ((peer + turn) % ways) * rows
            return source.at[:, pl.ds(pl.multiple_of(start, rows), rows)]

        if index < fed:
            stage, start = stages[index], own * high
        else:
            stage = stages[fed + (index - fed) // split]
            start = own * whole + (index - fed) % split * high
        mine = stage.at[pl.ds(pl.multiple_of(start, high), high), :]
        copies = []
        for by, peer in enumerate(peers):
            copies.append(
                pltpu.make_async_remote_copy(
                    src_ref=block_of(peer),
                    dst_ref=mine,
                    send_sem=owner_sends.at[index * (ways - 1) + by],
                    recv_sem=owner_receives.at[index * (ways - 1) + by],
                    device_id=place("dp", peer),
                    device_id_type=MESH,
                )
            )
        here = pltpu.make_async_copy(block_of(own), mine, own_sems.at[index])
        return copies + [here]

    partners = [place("dp", partner(own, by)) for by in doublings(ways)]
    partners += [place("seq", partner(position, by)) for by in doublings(spans)]
    partners += [place("head", 1 - lax.axis_index("head"))]

    def small_copy(turn):
        high = 8 if turn == len(partners) - 1 else small.shape[0]
        return pltpu.make_async_remote_copy(
            src_ref=small_sent.at[turn, :high, :],
            dst_ref=small_in.at[turn, :high, :],
            send_sem=small_sends.at[turn],
            recv_sem=small_receives.at[turn],
            device_id=partners[turn],
            device_id_type=MESH,
        )

    def small_turn(turn):
        if turn == 0:
            small_sent[0] = small[...]
        else:
            small_copy(turn - 1).wait_recv()
            if turn < len(partners):
                small_sent[turn] = small_sent[turn - 1] + small_in[turn - 1]
            else:
                small_out[...] = small_sent[turn - 1]
                small_out[:8, :] = small_sent[turn - 1, :8, :] + small_in[turn - 1, :8, :]
        if turn < len(partners):
            small_copy(turn).start()

    meet(
        [place("seq", (position + last) % spans), place("seq", (position + 1) % spans)]
        + [place("seq", partner(position, by)) for by in doublings(spans)[1:]]
        + [place("dp", peer) for peer in peers]
        + partners[-1:]
    )
    small_turn(0)
    along = (position, last - position)

    ahead = 6

    def source_send(way, index):
        turn, group = index // groups, index % groups
        shard = last - turn if way == 0 else turn
        if index >= ahead:
            before = index - ahead
            line_copy(way, before // groups, before % groups, totals.at[0]).wait_send()
        line_copy(way, turn, group, raw_at(group, shard)).start()

    for way in range(2):

        @pl.when(along[way] == 0)
        def _():
            for index in range(ahead):
                source_send(way, index)

    fed_copies = [owner_copies(index, piece) for index, piece in enumerate(pieces)]
    for copies in fed_copies:
        for copy in copies:
            copy.start()

    for way in range(2):

        @pl.when(along[way] == 0)
        def _():
            for index in range(ahead, groups + ahead):
                source_send(way, index)

    at_end = (position == 0) | (position == last)

    def finish(group):
        for way in range(2):

            @pl.when(along[way] >= 1)
            def _():
                line_copy(way, rounds - 1, group, totals.at[group]).wait_recv()

        total = raw_at(group, position)[...].astype(jnp.float32)
        for way in range(2):
            arrived = received[way, rounds - 1, group].astype(jnp.float32)
            total = total + jnp.where(along[way] >= 1, arrived, 0.0)
        totals[group] = total.astype(jnp.bfloat16)
        for copy in owner_copies(fed + group, totals.at[group]):
            copy.start()

    for turn in range(1, rounds):
        for group in range(groups):
            for way in range(2):
                if turn * groups + group + ahead < rounds * groups:

                    @pl.when(along[way] == 0)
                    def _():
                        source_send(way, turn * groups + group + ahead)

                shard = last - turn + position if way == 0 else turn - along[1]

                @pl.when((along[way] >= 1) & (along[way] <= turn))
                def _():
                    line_copy(way, turn - 1, group, handed.at[way, turn - 1, group]).wait_recv()
                    term = raw_at(group, shard)[...].astype(jnp.float32)
                    term = term + received[way, turn - 1, group].astype(jnp.float32)
                    handed[way, turn - 1, group] = term.astype(jnp.bfloat16)
                    line_copy(way, turn, group, handed.at[way, turn - 1, group]).start()

            if turn == rounds - 1:

                @pl.when(at_end)
                def _():
                    finish(group)

        small_turn(turn)

    later = list(range(rounds, len(partners) + 1))

    @pl.when(at_end)
    def _():
        for turn in later:
            small_turn(turn)

    @pl.when(jnp.logical_not(at_end))
    def _():
        done = 0
        for group in range(groups):
            finish(group)
            while done < len(later) and (group + 1) * len(later) >= (done + 1) * groups:
                small_turn(later[done])
                done += 1

    sources = list(pieces) + [totals.at[group] for group in range(groups)]
    for index, source in enumerate(sources):
        for copy in owner_copies(index, source):
            copy.wait()

    for turn in range(rounds):
        for way in range(2):

            @pl.when((along[way] >= 1) & (along[way] <= turn))
            def _():
                for group in range(groups):
                    line_copy(way, turn, group, totals.at[group]).wait_send()

    for way in range(2):

        @pl.when(along[way] == 0)
        def _():
            for group in range(groups - ahead, groups):
                line_copy(way, rounds - 1, group, totals.at[group]).wait_send()

    for turn in range(len(partners)):
        small_copy(turn).wait_send()


def finished_gradients(out_raw, mix_raw, pieces, small, number):
    spans, ways = lax.axis_size("seq"), lax.axis_size("dp")
    split = 2
    _, whole, wide = out_raw.shape
    count = whole // split
    grads = 1 + mix_raw.shape[1] // whole
    groups = grads * split
    rows = wide // ways
    fed = len(pieces)
    highs = [ways * piece.shape[0] for piece in pieces] + [ways * whole] * grads
    inside = pl.BlockSpec(memory_space=pltpu.VMEM)
    shapes = [b16(high, rows) for high in highs]
    lines = (2, spans - 1, groups, count, wide)
    turns = len(doublings(ways)) + len(doublings(spans)) + 1
    return pl.pallas_call(
        functools.partial(finish_kernel, spans, ways, fed, split),
        out_shape=shapes + [f32(*small.shape)],
        in_specs=[inside] * 3 + [pl.BlockSpec(memory_space=pl.ANY)] * fed,
        out_specs=[inside] * (len(shapes) + 1),
        scratch_shapes=[
            pltpu.VMEM(lines, jnp.bfloat16),
            pltpu.VMEM((2, spans - 2, groups, count, wide), jnp.bfloat16),
            pltpu.VMEM((groups, count, wide), jnp.bfloat16),
        ]
        + [pltpu.SemaphoreType.DMA((2 * (spans - 1) * groups,))] * 2
        + [pltpu.SemaphoreType.DMA(((fed + groups) * (ways - 1),))] * 2
        + [pltpu.SemaphoreType.DMA((fed + groups,))]
        + [pltpu.VMEM((turns,) + small.shape, jnp.float32)] * 2
        + [pltpu.SemaphoreType.DMA((turns,))] * 2,
        compiler_params=pltpu.CompilerParams(
            collective_id=number, has_side_effects=True, vmem_limit_bytes=VMEM
        ),
        cost_estimate=SHORT,
    )(out_raw, mix_raw, small, *pieces)


def shards(
    tokens_in,
    lengths,
    first_gain,
    query_weight,
    key_weight,
    value_weight,
    beta_weight,
    query_conv,
    key_conv,
    value_conv,
    mixer_gain,
    output_weight,
    second_gain,
    gate_weight,
    up_weight,
    down_weight,
    upstream,
):
    num_rows, local_len, local_width = tokens_in.shape
    full_width = query_weight.shape[0]
    channels = query_weight.shape[1]
    local_heads = beta_weight.shape[1]
    groups = lax.axis_size("head")
    ways = lax.axis_size("dp")
    spans = lax.axis_size("seq")
    positions = lax.axis_index("seq") * local_len + jnp.arange(local_len, dtype=jnp.int32)
    live_mask = (positions[None, :] < lengths[:, None]).astype(jnp.float32)
    live_low = live_mask[..., None].astype(jnp.bfloat16)
    fused = groups == 2
    weights = [query_weight, key_weight, value_weight]
    if fused:
        (
            *pres, beta_logit, logit_turned, gathered, normed_one, gains, live_col, live_row,
        ) = projected(
            lengths, tokens_in[0], first_gain, second_gain, weights, beta_weight, 7
        )
        upstream_other = swapped(upstream[0])
        upstream_other, beta_logit = lax.optimization_barrier((upstream_other, beta_logit))
        first = lax.axis_index("head") == 0
        upstream_full = live_low * jnp.concatenate(
            [
                jnp.where(first, upstream, upstream_other[None]),
                jnp.where(first, upstream_other[None], upstream),
            ],
            2,
        )
        half_up = lax.all_gather(upstream[0], "dp", axis=0, tiled=True)
    else:
        gains = jnp.stack([first_gain, second_gain] + [first_gain] * 14)
        masked_up = upstream[0] * live_low[0]
        everything = gather_head(jnp.concatenate([tokens_in[0], masked_up, gains], 0), 1)
        gathered = everything[:local_len]
        upstream_full = everything[None, local_len : 2 * local_len]
        gains = everything[2 * local_len :]
        scale_one = inverse_rms(gathered.astype(jnp.float32))
        normed_one = (
            gathered.astype(jnp.float32) * scale_one * gains[0].astype(jnp.float32)
        ).astype(jnp.bfloat16)
        pres = [
            jnp.dot(normed_one, weight, preferred_element_type=jnp.float32).astype(jnp.bfloat16)
            for weight in weights
        ]
        beta_logit = jnp.dot(normed_one, beta_weight, preferred_element_type=jnp.float32)
        tokens_up = jnp.stack(spread(upstream_full[0], "dp")[1:])

    def scattered(pieces):
        return lax.psum_scatter(pieces, "seq", scatter_dimension=0, tiled=False)

    def to_owner(piece):
        c = piece.shape[0]
        blocks = piece.reshape(c, ways, -1).transpose(1, 0, 2)
        return jnp.stack(in_order(exchanged(blocks, "dp"), "dp"), 0)

    per_step = 2 if local_heads % 2 == 0 else 1
    gain_one, gain_two = gains[0].astype(jnp.float32), gains[1].astype(jnp.float32)
    stream_full = gathered[None].astype(jnp.float32)
    scale_one = inverse_rms(stream_full)
    normed_one = normed_one[None]
    convs = [query_conv, key_conv, value_conv]
    if not fused:
        live_col = live_mask[0][:, None]
    head_gain = mixer_gain[None, :] if fused else mixer_gain.astype(jnp.float32)[None, :]
    if fused:
        (
            query, key, value, wy, inverse, ends, mixed, head_out, entering, rims, one_near,
        ) = mixer_forward(
            pres, convs, beta_logit, logit_turned, live_col, live_row, head_gain, normed_one[0],
            per_step, spans, ways, 1,
        )
    else:
        rims = passed_along(jnp.stack([pre[local_len - RIM :, :] for pre in pres]), "seq", 1)
        rims = [rims[0], rims[1], rims[2]]
        query, key, value, wy, inverse, mix, ends = mixer_local(
            pres, rims, convs, beta_logit, live_col, per_step
        )
        entering = chain_state(ends[:, :, :HEAD_DIM], ends[:, :, HEAD_DIM:], False)
        mixed, head_out = mixer_finish(mix, entering, head_gain, per_step)
    head_out = head_out[None]
    if fused:
        (
            turned, d_gate, d_up, hidden, stream_mid, normed_two, own_hidden, hidden_others,
            other_up,
        ) = hidden_units(
            head_out[0], output_weight, gathered, gains, upstream[0], upstream_other, live_col,
            gate_weight, up_weight, down_weight, half_up, 8,
        )
        stream_mid, normed_two = stream_mid[None], normed_two[None]
    else:
        mixer_part = jnp.dot(head_out, output_weight, preferred_element_type=jnp.float32)
        stream_mid = stream_full + sum_head(mixer_part)
        normed_two = (stream_mid * inverse_rms(stream_mid) * gain_two).astype(jnp.bfloat16)
        feed_part, d_two_part, turned = feed_forward(
            normed_two[0], upstream_full[0], gate_weight, up_weight, down_weight, normed_two
        )
    scale_two = inverse_rms(stream_mid)
    units = turned.shape[1] // ways
    turned = turned.reshape(-1, ways, units, local_len)

    def raw_piece(lefts, count, rights, is_turned, tokens=()):
        return span_pieces(
            lefts, count, rights, local_len, full_width, spans, is_turned, tokens
        )

    def slots_of(own, others):
        slots = [(own, (local_len,), lambda at: (0,))] + [
            (others, (1, local_len), lambda at, by=by: (by, 0)) for by in range(ways - 1)
        ]
        return [
            [slot + ((lambda s, way=way: way * spans + s),) for way in range(ways)]
            for slot in slots
        ]

    def halves_of(same, other):
        half = ways // 2
        return [
            [
                (
                    same if way < half else other,
                    (local_len,),
                    lambda at, by=by: (at ^ by,),
                    lambda s, way=way: (way % half) * spans + s,
                )
                for way in range(ways)
            ]
            for by in range(ways)
        ]

    def feed_slots(which, others, index):
        own = [(turned, (1, 1, units, local_len), lambda at: (which, at, 0, 0))]
        return own + [
            (others, (1, 1, units, local_len), lambda at, by=by: (by, index, 0, 0))
            for by in range(ways - 1)
        ]

    normed_full = normed_two[0]
    if fused:
        hidden_slots = [(own_hidden, (units, local_len), lambda at: (0, 0))] + [
            (hidden_others, (1, units, local_len), lambda at, by=by: (by, 0, 0))
            for by in range(ways - 1)
        ]
        down_raw = raw_piece(
            [hidden_slots], units, halves_of(half_up, other_up), True
        )
        feed_part, d_stream, residual, d_head_out, second_row, d_others, two_others = feed_back(
            d_gate, d_up, hidden, [gate_weight, up_weight, down_weight], upstream[0],
            upstream_other, live_col, gains, turned, (0, 1), normed_full, stream_mid[0],
            output_weight, [down_raw], 3,
        )
        d_stream, residual_full, d_head_out = d_stream[None], residual[None], d_head_out[None]
        grad_second = own_half(second_row[0], local_width)
        two_slots = slots_of(normed_full, two_others)
    else:
        hidden_others = jnp.stack(exchanged(turned[:1].transpose(1, 0, 2, 3), "dp")[1:])
        down_raw = raw_piece(
            [feed_slots(0, hidden_others, 0)], units, slots_of(upstream_full[0], tokens_up), True
        )
        d_others = jnp.stack(exchanged(turned[1:].transpose(1, 0, 2, 3), "dp")[1:])
        two_slots = slots_of(normed_full, jnp.stack(spread(normed_full, "dp")[1:]))
    down_piece = scattered(down_raw)
    first = turned.shape[0] - 2
    gate_raw = raw_piece([feed_slots(first, d_others, 0)], units, two_slots, True)
    gate_piece = scattered(gate_raw)
    layer_out = own_half(stream_mid + sum_head(feed_part[None]), local_width).astype(jnp.bfloat16)
    if not fused:
        d_two = sum_head(d_two_part[None])
        d_stream = (
            upstream_full.astype(jnp.float32)
            + scale_two * gain_two * d_two
            - stream_mid
            * scale_two
            * scale_two
            * scale_two
            * (jnp.sum(d_two * gain_two * stream_mid, axis=-1, keepdims=True) / full_width)
        )
        grad_second = own_half(jnp.sum(d_two * stream_mid * scale_two, axis=(0, 1)), local_width)
        residual_full = d_stream.astype(jnp.bfloat16)
        d_head_out = jnp.einsum(
            "rsd,cd->rsc", residual_full, output_weight, preferred_element_type=jnp.float32
        )
    if fused:
        (
            *mix_sources, grad_kernels, d_beta_logit, grad_gain_part, out_others, res_others,
            up_others,
        ) = mixer_backward(
            d_head_out[0], mixed, head_gain, pres, rims, convs, beta_logit, live_col,
            query, key, value, wy, inverse, entering, ends, [gate_raw, down_piece],
            head_out[0], residual_full[0], turned, per_step, spans, ways, 4,
        )
    else:
        d_mixed, d_fresh, d_ends, grad_gain_part = mixer_back_local(
            d_head_out[0], mixed, head_gain, query, key, wy, per_step
        )
        leaving = chain_state(jnp.swapaxes(ends[:, :, :HEAD_DIM], 1, 2), d_ends, True)
        *d_pres, tails, d_rims, grad_kernels, d_beta_logit = mixer_back(
            pres, rims, convs, beta_logit, live_col, query, key, value, wy, inverse,
            entering, d_mixed, d_fresh, leaving, per_step,
        )
        tails = (tails + passed_along(d_rims, "seq", -1)).astype(jnp.bfloat16)
        mix_sources = [
            jnp.concatenate([part[: local_len - 8], tail], 0) for part, tail in zip(d_pres, tails)
        ]
    grad_gain_part = grad_gain_part[0]
    if fused:
        up_raw = raw_piece([feed_slots(1, up_others, 0)], units, two_slots, True)
    else:
        up_raw = raw_piece([feed_slots(2, d_others, 1)], units, two_slots, True)
    up_piece = scattered(up_raw)
    share_width = channels // ways
    residual = residual_full[0]
    if fused:
        d_one_part, *mix_others, one_far = back_projection(
            mix_sources, d_beta_logit, weights, beta_weight, normed_one[0], ways, [up_raw], 5,
        )
    else:
        *mix_others, out_others = [
            jnp.stack(exchanged(part.reshape(local_len, ways, -1).transpose(1, 0, 2), "dp")[1:])
            for part in mix_sources + [head_out[0]]
        ]
        res_others = jnp.stack(spread(residual, "dp")[1:])

    def column_slots(own, others):
        if fused:
            first = [(own, (local_len, share_width), lambda at: (0, at))]
        else:
            mine = lax.dynamic_slice_in_dim(
                own, lax.axis_index("dp") * share_width, share_width, 1
            )
            first = [(mine, (local_len, share_width), lambda at: (0, 0))]
        return first + [
            (others, (1, local_len, share_width), lambda at, by=by: (by, 0, 0))
            for by in range(ways - 1)
        ]

    if fused:
        one_slots = slots_of(normed_one[0], one_near)[: ways - 1]
        one_slots += slots_of(normed_one[0], one_far)[1:2]
    else:
        one_slots = slots_of(normed_one[0], jnp.stack(spread(normed_one[0], "dp")[1:]))
    out_raw = raw_piece(
        [column_slots(head_out[0], out_others)], share_width, slots_of(residual, res_others), False,
        [gate_piece],
    )
    mix_raw = raw_piece(
        [column_slots(own, others) for own, others in zip(mix_sources, mix_others)],
        3 * share_width, one_slots, False, [out_raw],
    )
    d_logit_low = d_beta_logit.astype(jnp.bfloat16)
    if not fused:
        d_one_part = jnp.dot(d_logit_low, beta_weight.T, preferred_element_type=jnp.float32)
        for part, weight in zip(mix_sources, (query_weight, key_weight, value_weight)):
            d_one_part = d_one_part + jnp.dot(
                part, weight.T, preferred_element_type=jnp.float32
            )
    grad_beta_part = lax.dot_general(
        d_logit_low, normed_one[0], (((0,), (0,)), ((), ())), preferred_element_type=jnp.float32
    )
    d_one = sum_head(d_one_part[None])
    grad_tokens = own_half(
        d_stream
        + scale_one * gain_one * d_one
        - stream_full
        * scale_one
        * scale_one
        * scale_one
        * (jnp.sum(d_one * gain_one * stream_full, axis=-1, keepdims=True) / full_width),
        local_width,
    )
    grad_first = own_half(jnp.sum(d_one * stream_full * scale_one, axis=(0, 1)), local_width)
    lane = 128
    sizes = [HEAD_DIM, local_width, local_width, grad_kernels.size, grad_beta_part.size]
    parts = [grad_gain_part, grad_first, grad_second, grad_kernels, grad_beta_part]
    shares = [
        jnp.pad(part.reshape(-1, lane), ((0, -(size // lane) % 8), (0, 0)))
        for part, size in zip(parts, sizes)
    ]
    small = jnp.concatenate(shares, 0)
    starts = [0]
    for part in shares:
        starts.append(starts[-1] + part.shape[0])
    share = lax.axis_index("dp") * spans + lax.axis_index("seq")
    rows = full_width // (ways * spans)
    if fused:
        *finished, small = finished_gradients(
            out_raw, mix_raw, [down_piece, gate_piece, up_piece], small, 6
        )
        results = widened(
            finished, [False, True, True, False, True, True, True],
            small, starts, channels, query_conv.shape[0], local_heads, full_width,
        )
        down, gate, up, out, *mix = results[:7]
        gain_total, grad_first, grad_second = [part.reshape(-1) for part in results[7:10]]
        kernel_sum, grad_beta = results[10:13], results[13].T
    else:
        small = sum_doubling(small, ("dp", "seq"))
        gain_total = sum_doubling(small[0], ("head",))
        totals = [
            small[start : start + size // lane].reshape(part.shape)
            for start, size, part in zip(starts, sizes, parts)
        ]
        grad_first, grad_second, kernel_sum, beta_sum = totals[1:]
        grad_beta = lax.dynamic_slice_in_dim(beta_sum, share * rows, rows, 1).T
        feed = to_owner(jnp.concatenate([down_piece, gate_piece, up_piece], 0))
        down, gate, up = [
            feed[:, place * units : (place + 1) * units].reshape(-1, rows).astype(jnp.float32)
            for place in range(3)
        ]
        gate, up = gate.T, up.T
        out = to_owner(scattered(out_raw)).reshape(-1, rows).astype(jnp.float32)
        mix = to_owner(scattered(mix_raw)).astype(jnp.float32)
        third = mix.shape[1] // 3
        mix = [mix[:, i * third : (i + 1) * third].reshape(-1, rows).T for i in range(3)]
    return (
        layer_out,
        grad_tokens,
        grad_first,
        mix[0],
        mix[1],
        mix[2],
        grad_beta,
        kernel_sum[0],
        kernel_sum[1],
        kernel_sum[2],
        gain_total,
        out,
        grad_second,
        gate,
        up,
        down,
    )


def solution(mesh):
    placed = (
        P("dp", "seq", "head"),
        P("dp"),
        P("head"),
        P(None, "head"),
        P(None, "head"),
        P(None, "head"),
        P(None, "head"),
        P(None, "head"),
        P(None, "head"),
        P(None, "head"),
        P(),
        P("head", None),
        P("head"),
        P(None, "head"),
        P(None, "head"),
        P("head", None),
        P("dp", "seq", "head"),
    )
    return jax.shard_map(
        shards,
        mesh=mesh,
        in_specs=placed,
        out_specs=(
            P("dp", "seq", "head"),
            P("dp", "seq", "head"),
            P("head"),
            P(("dp", "seq"), "head"),
            P(("dp", "seq"), "head"),
            P(("dp", "seq"), "head"),
            P(("dp", "seq"), "head"),
            P(None, "head"),
            P(None, "head"),
            P(None, "head"),
            P(),
            P("head", ("dp", "seq")),
            P("head"),
            P(("dp", "seq"), "head"),
            P(("dp", "seq"), "head"),
            P("head", ("dp", "seq")),
        ),
        check_vma=False,
    )
```

```python
import functools

import jax
import jax.numpy as jnp
from jax import lax
from jax.experimental import pallas as pl
from jax.experimental.pallas import tpu as pltpu
from jax.sharding import PartitionSpec as P

HEAD_DIM = 128


HIGH = lax.Precision.HIGHEST
EPSILON = 1e-05
UNIT_EPSILON = 1e-06
VMEM = 56 * 1024 * 1024
SHORT = pl.CostEstimate(flops=0, bytes_accessed=0, transcendentals=0)


def passed_along(value, axis, by):
    peers = lax.axis_size(axis)
    pairs = [(i, i + by) for i in range(peers) if 0 <= i + by < peers]
    return lax.ppermute(value, axis, pairs)


def swap_pairs(axis, by):
    peers = lax.axis_size(axis)
    return [(i, i ^ by) for i in range(peers)]


def exchanged(values, axis):
    peers = lax.axis_size(axis)
    own = lax.axis_index(axis)
    parts = [lax.dynamic_index_in_dim(values, own, 0, keepdims=False)]
    for by in range(1, peers):
        out = lax.dynamic_index_in_dim(values, own ^ by, 0, keepdims=False)
        parts.append(lax.ppermute(out, axis, swap_pairs(axis, by)))
    return parts


def spread(value, axis):
    peers = lax.axis_size(axis)
    return [value] + [
        lax.ppermute(value, axis, swap_pairs(axis, by)) for by in range(1, peers)
    ]


def in_order(parts, axis):
    stacked = jnp.stack(parts, 0)
    own = lax.axis_index(axis)
    return [
        lax.dynamic_index_in_dim(stacked, own ^ k, 0, keepdims=False) for k in range(len(parts))
    ]


def gather_head(value, axis):
    if lax.axis_size("head") == 2:
        other = lax.ppermute(value, "head", [(0, 1), (1, 0)])
        first = lax.axis_index("head") == 0
        return jnp.concatenate(
            [jnp.where(first, value, other), jnp.where(first, other, value)], axis
        )
    return lax.all_gather(value, "head", axis=axis, tiled=True)


def swapped(value):
    return lax.ppermute(value, "head", [(0, 1), (1, 0)])


def sum_head(value):
    low = value.astype(jnp.bfloat16)
    if lax.axis_size("head") == 2:
        other = lax.ppermute(low, "head", [(0, 1), (1, 0)])
        return low.astype(jnp.float32) + other.astype(jnp.float32)
    return lax.psum(low, "head").astype(jnp.float32)


def sum_doubling(value, axes):
    for axis in axes:
        by = 1
        while by < lax.axis_size(axis):
            value = value + lax.ppermute(value, axis, swap_pairs(axis, by))
            by *= 2
    return value


def own_half(value, width):
    return lax.dynamic_slice_in_dim(value, lax.axis_index("head") * width, width, value.ndim - 1)


def chain_state(maps, shifts, reverse):
    peers = lax.axis_size("seq")
    by = -1 if reverse else 1
    states = [passed_along(shifts.astype(jnp.bfloat16), "seq", by)]
    for step in range(peers - 2):
        out = (
            jnp.einsum("hij,hjk->hik", maps, states[-1].astype(jnp.float32), precision=HIGH)
            + shifts
        )
        states.append(passed_along(out.astype(jnp.bfloat16), "seq", by))
    return states[-1]


def inverse_rms(values):
    return lax.rsqrt(jnp.mean(values * values, axis=-1, keepdims=True) + EPSILON)


MESH = pl.DeviceIdType.MESH


def partner(own, by):
    other = own
    bit = 1
    while bit <= by:
        if by & bit:
            other = other + bit - 2 * bit * ((own // bit) % 2)
        bit *= 2
    return other


def place(name, index):
    return {name: index}


def meet(devices):
    barrier = pltpu.get_barrier_semaphore()
    for device in devices:
        pl.semaphore_signal(barrier, inc=1, device_id=device, device_id_type=MESH)
    pl.semaphore_wait(barrier, len(devices))


class Halves:
    def __init__(
        self, ways, source, out, sends, receives, hand_sends, hand_receives, distances=None
    ):
        own = lax.axis_index("dp")
        core = lax.axis_index("head")
        width = source.shape[1] // 2
        mine = pl.ds(pl.multiple_of(core * width, width), width)
        distances = distances or list(range(1, ways))
        self.peers = [place("dp", partner(own, by)) for by in distances]
        self.other = place("head", 1 - core)
        self.first = [
            pltpu.make_async_remote_copy(
                src_ref=source.at[:, mine],
                dst_ref=out.at[slot, :, mine],
                send_sem=sends.at[slot],
                recv_sem=receives.at[slot],
                device_id=peer,
                device_id_type=MESH,
            )
            for slot, peer in enumerate(self.peers)
        ]
        self.second = [
            pltpu.make_async_remote_copy(
                src_ref=out.at[slot, :, mine],
                dst_ref=out.at[slot, :, mine],
                send_sem=hand_sends.at[slot],
                recv_sem=hand_receives.at[slot],
                device_id=self.other,
                device_id_type=MESH,
            )
            for slot in range(len(distances))
        ]

    def devices(self):
        return self.peers + [self.other]

    def start(self):
        for copy in self.first:
            copy.start()

    def hand_on(self):
        for copy, hand in zip(self.first, self.second):
            copy.wait_recv()
            hand.start()

    def finish(self):
        for copy, hand in zip(self.first, self.second):
            copy.wait_send()
            hand.wait()


def column_copies(ways, source, out, sends, receives):
    own = lax.axis_index("dp")
    width = source.shape[1] // ways
    copies = []
    for by in range(1, ways):
        peer = partner(own, by)
        copies.append(
            pltpu.make_async_remote_copy(
                src_ref=source.at[:, pl.ds(pl.multiple_of(peer * width, width), width)],
                dst_ref=out.at[by - 1],
                send_sem=sends.at[by - 1],
                recv_sem=receives.at[by - 1],
                device_id=place("dp", peer),
                device_id_type=MESH,
            )
        )
    return copies


def halves(a):
    top = a.astype(jnp.bfloat16)
    return top, (a - top.astype(jnp.float32)).astype(jnp.bfloat16)


def dot_low(a, b, dims=(1, 0)):
    return lax.dot_general(
        a, b, (((dims[0],), (dims[1],)), ((), ())), preferred_element_type=jnp.float32
    )


def dot_left(a, b, dims=(1, 0)):
    top, rest = halves(a)
    return dot_low(top, b, dims) + dot_low(rest, b, dims)


def dot_right(a, b, dims=(1, 0)):
    top, rest = halves(b)
    return dot_low(a, top, dims) + dot_low(a, rest, dims)


def dot_both(a, b, dims=(1, 0)):
    a_top, a_rest = halves(a)
    b_top, b_rest = halves(b)
    return dot_low(a_top, b_top, dims) + (
        dot_low(a_top, b_rest, dims) + dot_low(a_rest, b_top, dims)
    )


def grid_marks(size):
    row = lax.broadcasted_iota(jnp.int32, (size, size), 0)
    col = lax.broadcasted_iota(jnp.int32, (size, size), 1)
    return row, col


def unit_lower_inverses(tiles):
    size = tiles[0].shape[0]
    row, col = grid_marks(size)
    unit = (row == col).astype(jnp.float32)
    base = 8
    near = (row // base == col // base) & (row > col)
    cores = [jnp.where(near, tile, 0.0) for tile in tiles]
    squares = [dot_both(core, core) for core in cores]
    fourths = [dot_both(square, square) for square in squares]
    found = [dot_both(unit - core, unit + square) for core, square in zip(cores, squares)]
    found = [dot_both(part, unit + fourth) for part, fourth in zip(found, fourths)]
    while base < size:
        wide = 2 * base
        near = (row // wide == col // wide) & (row // base > col // base)
        links = [jnp.where(near, tile, 0.0) for tile in tiles]
        steps = [dot_both(part, link) for part, link in zip(found, links)]
        found = [part - dot_both(step, part) for part, step in zip(found, steps)]
        base = wide
    return found


def lower_inverses(systems, tile):
    size = systems[0].shape[0]
    if size <= tile:
        return unit_lower_inverses(systems)
    half = size // 2
    diagonals = [s[:half, :half] for s in systems] + [s[half:, half:] for s in systems]
    found = lower_inverses(diagonals, tile)
    firsts, seconds = found[: len(systems)], found[len(systems) :]
    steps = [dot_both(second, s[half:, :half]) for second, s in zip(seconds, systems)]
    corners = [-dot_both(step, first) for step, first in zip(steps, firsts)]
    empty = jnp.zeros((half, half), jnp.float32)
    return [
        jnp.concatenate(
            [jnp.concatenate([first, empty], 1), jnp.concatenate([corner, second], 1)], 0
        )
        for first, corner, second in zip(firsts, corners, seconds)
    ]


RIM = 16


def conv_sum(ext, pre, rim, weights, taps, length):
    ext[:RIM, :] = rim.astype(jnp.float32)
    ext[RIM : RIM + length, :] = pre.astype(jnp.float32)
    first = RIM - taps + 1
    summed = weights[0:1, :] * ext[first : first + length, :]
    for tap in range(1, taps):
        summed = summed + weights[tap : tap + 1, :] * ext[first + tap : first + tap + length, :]
    return summed


def head_columns(refs, index):
    span = slice(index * HEAD_DIM, (index + 1) * HEAD_DIM)
    return [ref[:, span] for ref in refs]


def unit_scale(rows):
    return lax.rsqrt(jnp.sum(rows * rows, axis=-1, keepdims=True) + UNIT_EPSILON)


def column_of(values, index):
    lane = lax.broadcasted_iota(jnp.int32, values.shape, 1)
    return jnp.sum(jnp.where(lane == index, values, 0.0), axis=-1, keepdims=True)


def row_of(values, index):
    place = lax.broadcasted_iota(jnp.int32, values.shape, 0)
    return jnp.sum(jnp.where(place == index, values, 0.0), axis=0, keepdims=True)


def local_part(pres, rims, weights, logit, logit_t, live, live_t, ext, first, taps):
    length = live.shape[0]
    row, col = grid_marks(length)
    heads = range(pres[0].shape[1] // HEAD_DIM)
    queries, keys, values, systems, beta_rows = [], [], [], [], []
    for i in heads:
        span = slice(i * HEAD_DIM, (i + 1) * HEAD_DIM)
        active = []
        for pre, rim, weight in zip(pres, rims, weights):
            summed = conv_sum(
                ext, pre[:, span], rim[:, span], weight[:, span].astype(jnp.float32), taps, length
            )
            active.append(summed * jax.nn.sigmoid(summed))
        q, k, v = active
        q = (q * unit_scale(q)).astype(jnp.bfloat16)
        k = (k * unit_scale(k) * live).astype(jnp.bfloat16)
        v = v.astype(jnp.bfloat16)
        beta = jax.nn.sigmoid(column_of(logit, first + i)) * live
        beta_rows.append(jax.nn.sigmoid(row_of(logit_t, first + i)) * live_t)
        gram = dot_low(k, k, (1, 1))
        systems.append(jnp.where(row > col, beta * gram, 0.0))
        queries.append(q)
        keys.append(k)
        values.append(v)
    inverses = lower_inverses(systems, 128)
    wys = [
        dot_left(inverse * beta_row, jnp.concatenate([k, v], 1))
        for inverse, beta_row, k, v in zip(inverses, beta_rows, keys, values)
    ]
    wide = (HEAD_DIM, 2 * HEAD_DIM)
    place = lax.broadcasted_iota(jnp.int32, wide, 1)
    unit = (lax.broadcasted_iota(jnp.int32, wide, 0) == place).astype(jnp.float32)
    found = []
    for i in heads:
        ends = dot_right(keys[i], wys[i], (0, 0))
        ends = unit + jnp.where(place < HEAD_DIM, -ends, ends)
        scores = jnp.where(row >= col, dot_low(queries[i], keys[i], (1, 1)), 0.0)
        seen = dot_both(scores, wys[i])
        mix = jnp.concatenate(
            [queries[i].astype(jnp.float32) - seen[:, :HEAD_DIM], seen[:, HEAD_DIM:]], 1
        )
        found.append((queries[i], keys[i], values[i], wys[i], inverses[i], mix, ends))
    return found


def finish_part(mix, state, gain):
    mixed = mix[:, HEAD_DIM:] + dot_left(mix[:, :HEAD_DIM], state)
    scale = lax.rsqrt(jnp.mean(mixed * mixed, axis=-1, keepdims=True) + EPSILON)
    return mixed, (mixed * scale * gain).astype(jnp.bfloat16)


def back_local_part(d_out, mixed, gain, q, k, wy):
    row, col = grid_marks(q.shape[0])
    scale = lax.rsqrt(jnp.mean(mixed * mixed, axis=-1, keepdims=True) + EPSILON)
    weighted = gain * d_out
    inner = jnp.sum(weighted * mixed, axis=-1, keepdims=True)
    d_mixed = scale * weighted - mixed * (scale * scale * scale * inner / HEAD_DIM)
    gain_row = jnp.sum(d_out * mixed * scale, axis=0, keepdims=True)
    scores_t = jnp.where(col >= row, dot_low(k, q, (1, 1)), 0.0)
    d_fresh = dot_both(scores_t, d_mixed)
    d_end = dot_right(q, d_mixed, (0, 0)) - dot_both(wy[:, :HEAD_DIM], d_fresh, (0, 0))
    return d_mixed, d_fresh, d_end, gain_row


def back_part(q, k, v, wy, inverse, entering, leaving, d_mixed, d_fresh, logit, live):
    row, col = grid_marks(q.shape[0])
    d_fresh = d_fresh + dot_low(k, leaving)
    fresh = wy[:, HEAD_DIM:] - dot_left(wy[:, :HEAD_DIM], entering)
    d_scores = jnp.where(row >= col, dot_both(d_mixed, fresh, (1, 1)), 0.0)
    d_q = dot_left(d_mixed, entering, (1, 1)) + dot_left(d_scores, k)
    d_k = dot_left(d_scores, q, (0, 0)) + dot_left(fresh, leaving, (1, 1))
    d_wy = jnp.concatenate([-dot_left(d_fresh, entering, (1, 1)), d_fresh], 1)
    d_rhs = dot_both(inverse, d_wy, (0, 0))
    edges = jnp.where(row > col, -dot_both(d_rhs, wy, (1, 1)), 0.0)
    sig = jax.nn.sigmoid(logit)
    beta = sig * live
    both = jnp.concatenate([k, v], 1).astype(jnp.float32)
    gram = dot_low(k, k, (1, 1))
    d_beta = jnp.sum(d_rhs * both, axis=-1, keepdims=True) + jnp.sum(
        edges * gram, axis=-1, keepdims=True
    )
    scaled = beta * edges
    d_k = d_k + beta * d_rhs[:, :HEAD_DIM] + dot_left(scaled, k) + dot_left(scaled, k, (0, 0))
    d_v = beta * d_rhs[:, HEAD_DIM:]
    d_logit = d_beta * live * sig * (1.0 - sig)
    return d_q, d_k * live, d_v, d_logit


def back_conv_part(part, pre, rim, weight, grad, taps, ext, ext_back):
    length = pre.shape[0]
    weight = weight.astype(jnp.float32)
    summed = conv_sum(ext, pre, rim, weight, taps, length)
    gate = jax.nn.sigmoid(summed)
    if part < 2:
        active = summed * gate
        scale = unit_scale(active)
        inner = jnp.sum(active * grad, axis=-1, keepdims=True)
        grad = scale * grad - active * (scale * scale * scale * inner)
    d_conv = grad * gate * (1.0 + summed * (1.0 - gate))
    first = RIM - taps + 1
    rows = [
        jnp.sum(d_conv * ext[first + tap : first + tap + length, :], axis=0, keepdims=True)
        for tap in range(taps)
    ]
    ext_back[:8, :] = jnp.zeros((8, HEAD_DIM), jnp.float32)
    ext_back[8 : 8 + length, :] = d_conv
    ext_back[8 + length :, :] = jnp.zeros((8, HEAD_DIM), jnp.float32)
    own = jnp.zeros((length, HEAD_DIM), jnp.float32)
    before = jnp.zeros((8, HEAD_DIM), jnp.float32)
    for tap in range(taps):
        shift = taps - 1 - tap
        own = own + weight[tap : tap + 1, :] * ext_back[8 + shift : 8 + shift + length, :]
        before = before + weight[tap : tap + 1, :] * ext_back[shift : shift + 8, :]
    return own, before, jnp.concatenate(rows, 0)


def mixer_local_kernel(per_step, taps, *refs):
    pres, rims, weights = refs[:3], refs[3:6], refs[6:9]
    logit, logit_t, live, live_t = refs[9:13]
    q_out, k_out, v_out, wy_out, inv_out, mix_out, end_out, ext = refs[13:]
    found = local_part(
        pres, rims, weights, logit[...], logit_t[...], live[...], live_t[...], ext,
        pl.program_id(0) * per_step, taps,
    )
    for i, (q, k, v, wy, inverse, mix, ends) in enumerate(found):
        span = slice(i * HEAD_DIM, (i + 1) * HEAD_DIM)
        q_out[:, span] = q
        k_out[:, span] = k
        v_out[:, span] = v
        wy_out[i] = wy
        inv_out[i] = inverse
        mix_out[i] = mix
        end_out[i] = ends


def mixer_finish_kernel(per_step, mix, state, gain, mixed_out, head_out):
    for i in range(per_step):
        span = slice(i * HEAD_DIM, (i + 1) * HEAD_DIM)
        mixed_out[:, span], head_out[:, span] = finish_part(mix[i], state[i], gain[...])


def mixer_back_local_kernel(
    per_step, d_head, mixed_ref, gain_ref, q_ref, k_ref, wy,
    d_mixed_out, d_fresh_out, end_out, gain_out,
):
    gain_total = jnp.zeros((1, HEAD_DIM), jnp.float32)
    for i in range(per_step):
        d_out, mixed, q, k = head_columns((d_head, mixed_ref, q_ref, k_ref), i)
        d_mixed_out[i], d_fresh_out[i], end_out[i], gain_row = back_local_part(
            d_out, mixed, gain_ref[...], q, k, wy[i]
        )
        gain_total += gain_row

    @pl.when(pl.program_id(0) == 0)
    def _():
        gain_out[...] = jnp.zeros_like(gain_out)

    gain_out[...] += jnp.broadcast_to(gain_total, gain_out.shape)


def mixer_back_kernel(per_step, taps, *refs):
    pre_refs, rim_refs, weight_refs, (logit, live) = refs[:3], refs[3:6], refs[6:9], refs[9:11]
    (q_ref, k_ref, v_ref, wy, inv, state, d_mixed_ref, d_fresh_ref, d_state) = refs[11:20]
    d_q_out, d_k_out, d_v_out, tail_out, rim_out, conv_out, d_logit_out, ext, ext_back = refs[20:]
    length = live.shape[0]
    step = pl.program_id(0)

    @pl.when(step == 0)
    def _():
        d_logit_out[...] = jnp.zeros_like(d_logit_out)

    for i in range(per_step):
        q, k, v = head_columns((q_ref, k_ref, v_ref), i)
        *grads, d_logit = back_part(
            q, k, v, wy[i], inv[i], state[i], d_state[i], d_mixed_ref[i], d_fresh_ref[i],
            column_of(logit[...], step * per_step + i), live[...],
        )
        lane = lax.broadcasted_iota(jnp.int32, d_logit_out.shape, 1)
        d_logit_out[...] += jnp.where(lane == step * per_step + i, d_logit, 0.0)
        span = slice(i * HEAD_DIM, (i + 1) * HEAD_DIM)
        outs = (d_q_out, d_k_out, d_v_out)
        for part in range(3):
            own, before, rows = back_conv_part(
                part, pre_refs[part][:, span], rim_refs[part][:, span],
                weight_refs[part][:, span], grads[part], taps, ext, ext_back,
            )
            conv_out[part, :, span] = rows
            outs[part][:, span] = own.astype(jnp.bfloat16)
            tail_out[part, :, span] = own[length - 8 :, :]
            rim_out[part, :, span] = before


def mixer_specs(length, heads, per_step):
    width = per_step * HEAD_DIM

    def flat(rows):
        return pl.BlockSpec((rows, width), lambda h: (0, h))

    def whole(*shape):
        return pl.BlockSpec(shape, lambda h: (0,) * len(shape))

    def by_head(*shape):
        return pl.BlockSpec((per_step,) + shape, lambda h: (h,) + (0,) * len(shape))

    return flat, whole, by_head


def mixer_call(kernel, heads, per_step, ins, outs, scratch, flops, args):
    moved = sum(a.size * a.dtype.itemsize for a in args)
    return pl.pallas_call(
        kernel,
        grid=(heads // per_step,),
        in_specs=ins,
        out_specs=[spec for spec, _ in outs],
        out_shape=[shape for _, shape in outs],
        scratch_shapes=scratch,
        compiler_params=pltpu.CompilerParams(vmem_limit_bytes=VMEM),
        cost_estimate=SHORT,
    )(*args)


def f32(*shape):
    return jax.ShapeDtypeStruct(shape, jnp.float32)


def b16(*shape):
    return jax.ShapeDtypeStruct(shape, jnp.bfloat16)


def mixer_local(pres, rims, convs, logit, live, per_step):
    length, channels = pres[0].shape
    heads = channels // HEAD_DIM
    taps = convs[0].shape[0]
    flat, whole, by_head = mixer_specs(length, heads, per_step)
    args = (*pres, *rims, *convs, logit, logit.T, live, live.T)
    return mixer_call(
        functools.partial(mixer_local_kernel, per_step, taps),
        heads,
        per_step,
        [flat(length)] * 3
        + [flat(RIM)] * 3
        + [flat(taps)] * 3
        + [whole(length, heads), whole(heads, length), whole(length, 1), whole(1, length)],
        [(flat(length), b16(length, channels))] * 3
        + [
            (by_head(length, 2 * HEAD_DIM), f32(heads, length, 2 * HEAD_DIM)),
            (by_head(length, length), f32(heads, length, length)),
            (by_head(length, 2 * HEAD_DIM), f32(heads, length, 2 * HEAD_DIM)),
            (by_head(HEAD_DIM, 2 * HEAD_DIM), f32(heads, HEAD_DIM, 2 * HEAD_DIM)),
        ],
        [pltpu.VMEM((RIM + length, HEAD_DIM), jnp.float32)],
        heads * 2 * length**3 * 30,
        args,
    )


def mixer_finish(mix, state, gain, per_step):
    heads, length, _ = mix.shape
    flat, whole, by_head = mixer_specs(length, heads, per_step)
    return mixer_call(
        functools.partial(mixer_finish_kernel, per_step),
        heads,
        per_step,
        [by_head(length, 2 * HEAD_DIM), by_head(HEAD_DIM, HEAD_DIM), whole(1, HEAD_DIM)],
        [
            (flat(length), f32(length, heads * HEAD_DIM)),
            (flat(length), b16(length, heads * HEAD_DIM)),
        ],
        [],
        heads * 2 * length**3,
        (mix, state, gain),
    )


def mixer_back_local(d_head, mixed, gain, q, k, wy, per_step):
    heads, length, _ = wy.shape
    flat, whole, by_head = mixer_specs(length, heads, per_step)
    return mixer_call(
        functools.partial(mixer_back_local_kernel, per_step),
        heads,
        per_step,
        [flat(length)] * 2 + [whole(1, HEAD_DIM)] + [flat(length)] * 2 + [by_head(length, 2 * HEAD_DIM)],
        [
            (by_head(length, HEAD_DIM), f32(heads, length, HEAD_DIM)),
            (by_head(length, HEAD_DIM), f32(heads, length, HEAD_DIM)),
            (by_head(HEAD_DIM, HEAD_DIM), f32(heads, HEAD_DIM, HEAD_DIM)),
            (whole(8, HEAD_DIM), f32(8, HEAD_DIM)),
        ],
        [],
        heads * 2 * length**3 * 5,
        (d_head, mixed, gain, q, k, wy),
    )


def mixer_back(pres, rims, convs, logit, live, q, k, v, wy, inv, state, d_mixed, d_fresh, d_state, per_step):
    length, channels = pres[0].shape
    heads = channels // HEAD_DIM
    taps = convs[0].shape[0]
    flat, whole, by_head = mixer_specs(length, heads, per_step)
    three = pl.BlockSpec((3, 8, per_step * HEAD_DIM), lambda h: (0, 0, h))
    return mixer_call(
        functools.partial(mixer_back_kernel, per_step, taps),
        heads,
        per_step,
        [flat(length)] * 3
        + [flat(RIM)] * 3
        + [flat(taps)] * 3
        + [whole(length, heads), whole(length, 1)]
        + [flat(length)] * 3
        + [
            by_head(length, 2 * HEAD_DIM),
            by_head(length, length),
            by_head(HEAD_DIM, HEAD_DIM),
            by_head(length, HEAD_DIM),
            by_head(length, HEAD_DIM),
            by_head(HEAD_DIM, HEAD_DIM),
        ],
        [(flat(length), b16(length, channels))] * 3
        + [
            (three, f32(3, 8, channels)),
            (three, f32(3, 8, channels)),
            (
                pl.BlockSpec((3, taps, per_step * HEAD_DIM), lambda h: (0, 0, h)),
                f32(3, taps, channels),
            ),
            (whole(length, heads), f32(length, heads)),
        ],
        [
            pltpu.VMEM((RIM + length, HEAD_DIM), jnp.float32),
            pltpu.VMEM((16 + length, HEAD_DIM), jnp.float32),
        ],
        heads * 2 * length**3 * 20,
        (*pres, *rims, *convs, logit, live, q, k, v, wy, inv, state, d_mixed, d_fresh, d_state),
    )


def mixer_forward_kernel(per_step, taps, spans, ways, *refs):
    pres, weights = refs[:3], refs[3:6]
    logit, logit_t, live, live_t, gain = refs[6:11]
    sources, normed = refs[11:14], refs[14]
    q_out, k_out, v_out, wy_out, inv_out, end_out, mixed_out, head_out, state_out, rim_out = refs[
        15:25
    ]
    normed_others = refs[25]
    ext, mix_all, rims, arriving, leaving, sends, receives, rim_sends, rim_receives = refs[26:35]
    halves = Halves(ways, normed, normed_others, *refs[35:], distances=list(range(1, ways - 1)))
    step = pl.program_id(0)
    position = lax.axis_index("seq")
    pairs = arriving.shape[0]
    length = live.shape[0]
    width = per_step * HEAD_DIM
    last = spans - 1
    after = place("seq", position + 1)

    def rim_copy(part):
        return pltpu.make_async_remote_copy(
            src_ref=sources[part].at[length - RIM :, :],
            dst_ref=rims.at[part],
            send_sem=rim_sends.at[part],
            recv_sem=rim_receives.at[part],
            device_id=after,
            device_id_type=MESH,
        )

    def state_copy(pair, i):
        return pltpu.make_async_remote_copy(
            src_ref=leaving.at[pair, i],
            dst_ref=arriving.at[pair, i],
            send_sem=sends.at[pair * per_step + i],
            recv_sem=receives.at[pair * per_step + i],
            device_id=after,
            device_id_type=MESH,
        )

    @pl.when(step == 0)
    def _():
        meet(
            [place("seq", (position + last) % spans), place("seq", (position + 1) % spans)]
            + halves.devices()
        )

        @pl.when(position != last)
        def _():
            for part in range(3):
                rim_copy(part).start()

        halves.start()

        @pl.when(position == 0)
        def _():
            rims[...] = jnp.zeros_like(rims)
            arriving[...] = jnp.zeros_like(arriving)

        @pl.when(position != 0)
        def _():
            for part in range(3):
                rim_copy(part).wait_recv()

        rim_out[...] = rims[...]

    @pl.when(step < pairs)
    def _():
        here = pl.ds(pl.multiple_of(step * width, width), width)
        found = local_part(
            pres, [rims[part, :, here] for part in range(3)], weights, logit[...], logit_t[...],
            live[...], live_t[...], ext, step * per_step, taps,
        )
        for i, (q, k, v, wy, inverse, mix, ends) in enumerate(found):
            span = slice(i * HEAD_DIM, (i + 1) * HEAD_DIM)
            q_out[:, span] = q
            k_out[:, span] = k
            v_out[:, span] = v
            wy_out[i] = wy
            inv_out[i] = inverse
            mix_all[step * per_step + i] = mix
            end_out[step * per_step + i] = ends

    pair = step - position

    @pl.when((pair >= 0) & (pair < pairs))
    def _():
        for i in range(per_step):

            @pl.when(position != 0)
            def _():
                state_copy(pair, i).wait_recv()

            ends = end_out[pair * per_step + i]
            moved = dot_left(ends[:, :HEAD_DIM], arriving[pair, i])
            leaving[pair, i] = (moved + ends[:, HEAD_DIM:]).astype(jnp.bfloat16)

            @pl.when(position != last)
            def _():
                state_copy(pair, i).start()

        for i in range(per_step):
            here = pl.ds(pl.multiple_of(pair * width + i * HEAD_DIM, HEAD_DIM), HEAD_DIM)
            state = arriving[pair, i]
            state_out[pair * per_step + i] = state
            mixed, head = finish_part(
                mix_all[pair * per_step + i], state, gain[...].astype(jnp.float32)
            )
            mixed_out[:, here] = mixed
            head_out[:, here] = head

    @pl.when(step == pairs)
    def _():
        halves.hand_on()

    @pl.when(step == pl.num_programs(0) - 1)
    def _():
        @pl.when(position != last)
        def _():
            for part in range(3):
                rim_copy(part).wait_send()
            for index in range(pairs):
                for i in range(per_step):
                    state_copy(index, i).wait_send()

        halves.finish()


def mixer_forward(
    pres, convs, logit, logit_t, live, live_t, gain, normed, per_step, spans, ways, number
):
    length, channels = pres[0].shape
    heads = channels // HEAD_DIM
    pairs = heads // per_step
    taps = convs[0].shape[0]
    width = per_step * HEAD_DIM
    wide = (heads, length, 2 * HEAD_DIM)
    states = (heads, HEAD_DIM, HEAD_DIM)

    def at(step):
        return jnp.minimum(step, pairs - 1)

    def flat(rows):
        return pl.BlockSpec((rows, width), lambda s: (0, at(s)))

    def by_head(*shape):
        return pl.BlockSpec((per_step,) + shape, lambda s: (at(s),) + (0,) * len(shape))

    def whole(*shape):
        return pl.BlockSpec(shape, lambda s: (0,) * len(shape))

    anywhere = pl.BlockSpec(memory_space=pl.ANY)
    return pl.pallas_call(
        functools.partial(mixer_forward_kernel, per_step, taps, spans, ways),
        grid=(pairs + spans - 1,),
        in_specs=[flat(length)] * 3
        + [flat(taps)] * 3
        + [whole(length, heads), whole(heads, length), whole(length, 1), whole(1, length)]
        + [whole(1, HEAD_DIM)]
        + [anywhere] * 4,
        out_specs=[flat(length)] * 3
        + [
            by_head(length, 2 * HEAD_DIM),
            by_head(length, length),
            whole(heads, HEAD_DIM, 2 * HEAD_DIM),
            whole(length, channels),
            whole(length, channels),
            whole(*states),
            whole(3, RIM, channels),
            anywhere,
        ],
        out_shape=[b16(length, channels)] * 3
        + [
            f32(*wide),
            f32(heads, length, length),
            f32(heads, HEAD_DIM, 2 * HEAD_DIM),
            f32(length, channels),
            b16(length, channels),
            b16(*states),
            b16(3, RIM, channels),
            b16(ways - 2, *normed.shape),
        ],
        scratch_shapes=[
            pltpu.VMEM((RIM + length, HEAD_DIM), jnp.float32),
            pltpu.VMEM(wide, jnp.float32),
            pltpu.VMEM((3, RIM, channels), jnp.bfloat16),
            pltpu.VMEM((pairs, per_step, HEAD_DIM, HEAD_DIM), jnp.bfloat16),
            pltpu.VMEM((pairs, per_step, HEAD_DIM, HEAD_DIM), jnp.bfloat16),
            pltpu.SemaphoreType.DMA((heads,)),
            pltpu.SemaphoreType.DMA((heads,)),
            pltpu.SemaphoreType.DMA((3,)),
            pltpu.SemaphoreType.DMA((3,)),
        ]
        + [pltpu.SemaphoreType.DMA((ways - 2,))] * 4,
        compiler_params=pltpu.CompilerParams(
            collective_id=number, has_side_effects=True, vmem_limit_bytes=VMEM
        ),
        cost_estimate=SHORT,
    )(*pres, *convs, logit, logit_t, live, live_t, gain, *pres, normed)


def mixer_backward_kernel(per_step, taps, spans, ways, tokens, *refs):
    d_head, mixed_ref, q_one, k_one, wy_one, gain = refs[:6]
    pres, weights = refs[6:9], refs[9:12]
    q_ref, k_ref, v_ref, wy, inv = refs[12:17]
    logit, live, state, ends, rims = refs[17:22]
    head_source, residual, up_source = refs[22 + tokens : 25 + tokens]
    d_q_out, d_k_out, d_v_out, conv_out, d_logit_out, gain_out = refs[25 + tokens : 31 + tokens]
    head_others, res_others, up_others = refs[31 + tokens : 34 + tokens]
    (
        d_mixed_all, d_fresh_all, d_end_all, arriving, sending, tails, rim_out, rim_in,
        ext, ext_back, sends, receives, rim_sends, rim_receives,
    ) = refs[34 + tokens : 48 + tokens]
    col_sends, col_receives, up_sends, up_receives, *half_sems = refs[48 + tokens :]
    halves = Halves(ways, residual, res_others, *half_sems)
    columns = row_copies(ways, (1, 2), up_source, up_others, up_sends, up_receives)
    columns += column_copies(ways, head_source, head_others, col_sends, col_receives)
    step = pl.program_id(0)
    position = lax.axis_index("seq")
    pairs = arriving.shape[0]
    length = live.shape[0]
    last = spans - 1
    before_here = place("seq", position - 1)

    def state_copy(pair):
        return pltpu.make_async_remote_copy(
            src_ref=sending.at[pair],
            dst_ref=arriving.at[pair],
            send_sem=sends.at[pair],
            recv_sem=receives.at[pair],
            device_id=before_here,
            device_id_type=MESH,
        )

    def rim_copy():
        return pltpu.make_async_remote_copy(
            src_ref=rim_out,
            dst_ref=rim_in,
            send_sem=rim_sends.at[0],
            recv_sem=rim_receives.at[0],
            device_id=before_here,
            device_id_type=MESH,
        )

    @pl.when(step == 0)
    def _():
        meet(
            [place("seq", (position + last) % spans), place("seq", (position + 1) % spans)]
            + halves.devices()
        )
        for copy in columns:
            copy.start()
        halves.start()
        d_logit_out[...] = jnp.zeros_like(d_logit_out)
        gain_out[...] = jnp.zeros_like(gain_out)

        @pl.when(position == last)
        def _():
            arriving[...] = jnp.zeros_like(arriving)
            rim_in[...] = jnp.zeros_like(rim_in)

    @pl.when(step < pairs)
    def _():
        for i in range(per_step):
            d_out, mixed, q, k = head_columns((d_head, mixed_ref, q_one, k_one), i)
            d_mixed, d_fresh, d_end, gain_row = back_local_part(
                d_out, mixed, gain[...].astype(jnp.float32), q, k, wy_one[i]
            )
            d_mixed_all[step * per_step + i] = d_mixed
            d_fresh_all[step * per_step + i] = d_fresh
            d_end_all[step * per_step + i] = d_end
            gain_out[...] += jnp.broadcast_to(gain_row, gain_out.shape)

    pair = step - (last - position)

    @pl.when((pair >= 0) & (pair < pairs))
    def _():
        @pl.when(position != last)
        def _():
            state_copy(pair).wait_recv()

        for i in range(per_step):
            head = pair * per_step + i
            moved = dot_left(ends[head, :, :HEAD_DIM], arriving[pair, i], (0, 0))
            sending[pair, i] = (moved + d_end_all[head]).astype(jnp.bfloat16)

        @pl.when(position != 0)
        def _():
            state_copy(pair).start()

    ready = step - last

    @pl.when(ready >= 0)
    def _():
        outs = (d_q_out, d_k_out, d_v_out)
        for i in range(per_step):
            head = ready * per_step + i
            here = pl.ds(pl.multiple_of(head * HEAD_DIM, HEAD_DIM), HEAD_DIM)
            q, k, v = head_columns((q_ref, k_ref, v_ref), i)
            *grads, d_logit = back_part(
                q, k, v, wy[i], inv[i], state[head], arriving[ready, i],
                d_mixed_all[head], d_fresh_all[head], column_of(logit[...], head), live[...],
            )
            lane = lax.broadcasted_iota(jnp.int32, d_logit_out.shape, 1)
            d_logit_out[...] += jnp.where(lane == head, d_logit, 0.0)
            span = slice(i * HEAD_DIM, (i + 1) * HEAD_DIM)
            for part in range(3):
                own, before, rows = back_conv_part(
                    part, pres[part][:, span], rims[part, :, here],
                    weights[part][:, span], grads[part], taps, ext, ext_back,
                )
                conv_out[part, :, here] = rows
                outs[part][:, here] = own.astype(jnp.bfloat16)
                tails[part, :, here] = own[length - 16 :, :]
                rim_out[part, :, here] = before

    @pl.when(step == pl.num_programs(0) - 1)
    def _():
        @pl.when(position != 0)
        def _():
            rim_copy().start()

        halves.hand_on()

        @pl.when(position != last)
        def _():
            rim_copy().wait_recv()

        for part, out in enumerate((d_q_out, d_k_out, d_v_out)):
            joined = tails[part] + jnp.concatenate(
                [jnp.zeros_like(rim_in[part]), rim_in[part]], 0
            )
            out[length - 16 :, :] = joined.astype(jnp.bfloat16)

        @pl.when(position != 0)
        def _():
            rim_copy().wait_send()
            for index in range(pairs):
                state_copy(index).wait_send()

        for copy in columns:
            copy.wait()
        halves.finish()


def mixer_backward(
    d_head, mixed, gain, pres, rims, convs, logit, live, q, k, v, wy, inv, state, ends, tokens,
    head_out, residual, turned, per_step, spans, ways, number,
):
    length, channels = pres[0].shape
    heads = channels // HEAD_DIM
    pairs = heads // per_step
    taps = convs[0].shape[0]
    width = per_step * HEAD_DIM
    lag = spans - 1

    def early(step):
        return jnp.minimum(step, pairs - 1)

    def late(step):
        return jnp.maximum(step - lag, 0)

    def flat(rows, at):
        return pl.BlockSpec((rows, width), lambda s: (0, at(s)))

    def by_head(at, *shape):
        return pl.BlockSpec((per_step,) + shape, lambda s: (at(s),) + (0,) * len(shape))

    def whole(*shape):
        return pl.BlockSpec(shape, lambda s: (0,) * len(shape))

    wide = (length, 2 * HEAD_DIM)
    states = (pairs, per_step, HEAD_DIM, HEAD_DIM)
    return pl.pallas_call(
        functools.partial(mixer_backward_kernel, per_step, taps, spans, ways, len(tokens)),
        grid=(pairs + lag,),
        in_specs=[flat(length, early)] * 4
        + [by_head(early, *wide), whole(1, HEAD_DIM)]
        + [flat(length, late)] * 3
        + [flat(taps, late)] * 3
        + [flat(length, late)] * 3
        + [by_head(late, *wide), by_head(late, length, length)]
        + [whole(length, heads), whole(length, 1), whole(heads, HEAD_DIM, HEAD_DIM)]
        + [whole(heads, HEAD_DIM, 2 * HEAD_DIM), whole(3, RIM, channels)]
        + [pl.BlockSpec(memory_space=pl.ANY)] * (len(tokens) + 3),
        out_specs=[whole(length, channels)] * 3
        + [whole(3, taps, channels), whole(length, heads), whole(8, HEAD_DIM)]
        + [pl.BlockSpec(memory_space=pl.ANY)] * 3,
        out_shape=[b16(length, channels)] * 3
        + [f32(3, taps, channels), f32(length, heads), f32(8, HEAD_DIM)]
        + [b16(ways - 1, length, channels // ways)]
        + [b16(ways - 1, *residual.shape), b16(ways - 1, 1, *turned.shape[2:])],
        scratch_shapes=[
            pltpu.VMEM((heads, length, HEAD_DIM), jnp.float32),
            pltpu.VMEM((heads, length, HEAD_DIM), jnp.float32),
            pltpu.VMEM((heads, HEAD_DIM, HEAD_DIM), jnp.float32),
            pltpu.VMEM(states, jnp.bfloat16),
            pltpu.VMEM(states, jnp.bfloat16),
            pltpu.VMEM((3, 16, channels), jnp.float32),
            pltpu.VMEM((3, 8, channels), jnp.float32),
            pltpu.VMEM((3, 8, channels), jnp.float32),
            pltpu.VMEM((RIM + length, HEAD_DIM), jnp.float32),
            pltpu.VMEM((16 + length, HEAD_DIM), jnp.float32),
            pltpu.SemaphoreType.DMA((pairs,)),
            pltpu.SemaphoreType.DMA((pairs,)),
            pltpu.SemaphoreType.DMA((1,)),
            pltpu.SemaphoreType.DMA((1,)),
        ]
        + [pltpu.SemaphoreType.DMA((ways - 1,))] * 8,
        compiler_params=pltpu.CompilerParams(
            collective_id=number, has_side_effects=True, vmem_limit_bytes=VMEM
        ),
        cost_estimate=SHORT,
    )(
        d_head, mixed, q, k, wy, gain, *pres, *convs, q, k, v, wy, inv, logit, live, state, ends,
        rims, *tokens, head_out, residual, turned,
    )


def feed_kernel(
    x_ref, d_ref, gate_w, up_w, down_w, token, feed_out, d_x_out, turned_out, feed_sum, d_x_sum
):
    step = pl.program_id(0)
    x = x_ref[...]
    d_out = d_ref[...]
    gate = dot_low(x, gate_w[...])
    up = dot_low(x, up_w[...])
    d_hidden = dot_low(d_out, down_w[...], (1, 1))
    sig = jax.nn.sigmoid(gate)
    hidden = (gate * sig * up).astype(jnp.bfloat16)
    d_gate = (d_hidden * up * sig * (1.0 + gate * (1.0 - sig))).astype(jnp.bfloat16)
    d_up = (d_hidden * gate * sig).astype(jnp.bfloat16)
    for place, part in enumerate((hidden, d_gate, d_up)):
        turned_out[place] = part.T
    feed = dot_low(hidden, down_w[...])
    d_x = dot_low(d_gate, gate_w[...], (1, 1)) + dot_low(d_up, up_w[...], (1, 1))

    @pl.when(step == 0)
    def _():
        feed_sum[...] = feed
        d_x_sum[...] = d_x

    @pl.when(step > 0)
    def _():
        feed_sum[...] += feed
        d_x_sum[...] += d_x

    @pl.when(step == pl.num_programs(0) - 1)
    def _():
        feed_out[...] = feed_sum[...].astype(jnp.bfloat16)
        d_x_out[...] = d_x_sum[...].astype(jnp.bfloat16)


def feed_forward(x, d_out, gate_weight, up_weight, down_weight, token):
    length, width = x.shape
    units = gate_weight.shape[1]
    tile = 256 if units % 256 == 0 else units
    whole = pl.BlockSpec((length, width), lambda f: (0, 0))
    column = pl.BlockSpec((width, tile), lambda f: (0, f))
    return pl.pallas_call(
        feed_kernel,
        grid=(units // tile,),
        in_specs=[whole, whole, column, column]
        + [pl.BlockSpec((tile, width), lambda f: (f, 0)), pl.BlockSpec(memory_space=pl.ANY)],
        out_specs=[whole, whole, pl.BlockSpec((3, tile, length), lambda f: (0, f, 0))],
        out_shape=[b16(length, width), b16(length, width), b16(3, units, length)],
        scratch_shapes=[pltpu.VMEM((length, width), jnp.float32)] * 2,
        compiler_params=pltpu.CompilerParams(vmem_limit_bytes=VMEM),
        cost_estimate=SHORT,
    )(x, d_out, gate_weight, up_weight, down_weight, token)


def back_projection_kernel(ways, *refs):
    sources, d_logit, weights, beta_w = refs[:3], refs[3], refs[4:7], refs[7]
    shared, normed = refs[8:11], refs[11]
    out, others, normed_far = refs[-15], refs[-14:-11], refs[-11]
    sends, receives = refs[-10:-7], refs[-7:-4]
    far = Halves(ways, normed, normed_far, *refs[-4:], distances=[ways - 1])
    step = pl.program_id(0)
    copies = [
        copy
        for part in range(3)
        for copy in column_copies(ways, shared[part], others[part], sends[part], receives[part])
    ]

    @pl.when(step == 0)
    def _():
        own = lax.axis_index("dp")
        meet([place("dp", partner(own, by)) for by in range(1, ways)] + [far.other])
        for copy in copies:
            copy.start()
        far.start()

    total = dot_low(d_logit[...].astype(jnp.bfloat16), beta_w[...])
    for source, weight in zip(sources, weights):
        total = total + dot_low(source[...], weight[...], (1, 1))
    out[...] = total.astype(jnp.bfloat16)

    @pl.when(step == pl.num_programs(0) - 1)
    def _():
        far.hand_on()
        for copy in copies:
            copy.wait()
        far.finish()


def back_projection(sources, d_logit, weights, beta_weight, normed, ways, tokens, number):
    length, channels = sources[0].shape
    width, heads = beta_weight.shape
    tile = width // 4
    anywhere = pl.BlockSpec(memory_space=pl.ANY)
    return pl.pallas_call(
        functools.partial(back_projection_kernel, ways),
        grid=(width // tile,),
        in_specs=[pl.BlockSpec((length, channels), lambda n: (0, 0))] * 3
        + [pl.BlockSpec((length, heads), lambda n: (0, 0))]
        + [pl.BlockSpec((tile, channels), lambda n: (n, 0))] * 3
        + [pl.BlockSpec((heads, tile), lambda n: (0, n))]
        + [anywhere] * (4 + len(tokens)),
        out_specs=[pl.BlockSpec((length, tile), lambda n: (0, n))] + [anywhere] * 4,
        out_shape=[b16(length, width)]
        + [b16(ways - 1, length, channels // ways)] * 3
        + [b16(1, *normed.shape)],
        scratch_shapes=[pltpu.SemaphoreType.DMA((ways - 1,))] * 6
        + [pltpu.SemaphoreType.DMA((1,))] * 4,
        compiler_params=pltpu.CompilerParams(
            collective_id=number, has_side_effects=True, vmem_limit_bytes=VMEM
        ),
        cost_estimate=SHORT,
    )(*sources, d_logit, *weights, beta_weight.T, *sources, normed, *tokens)


def project_kernel(lengths, tokens, first_gain, second_gain, q_w, k_w, v_w, beta_w, *refs):
    q_out, k_out, v_out, logit_out, logit_t_out, stream_out, normed_out, gains_out = refs[:8]
    live_out, live_t_out, arriving, gains, gains_in, sends, receives = refs[8:]
    step = pl.program_id(0)
    half = tokens.shape[1]

    @pl.when(step == 0)
    def _():
        core = lax.axis_index("head")
        other = place("head", 1 - core)
        mine = pl.ds(pl.multiple_of(core * half, half), half)
        theirs = pl.ds(pl.multiple_of((1 - core) * half, half), half)
        row = lax.broadcasted_iota(jnp.int32, gains.shape, 0)
        first, second = [
            jnp.concatenate(
                [part[...].astype(jnp.float32)[i : i + 1] for i in range(part.shape[0])], 1
            )
            for part in (first_gain, second_gain)
        ]
        gains[...] = jnp.where(row == 0, first, second).astype(jnp.bfloat16)
        meet([other])
        copies = [
            pltpu.make_async_remote_copy(
                src_ref=source, dst_ref=target, send_sem=sends.at[index],
                recv_sem=receives.at[index], device_id=other, device_id_type=MESH,
            )
            for index, (source, target) in enumerate(((tokens, arriving), (gains, gains_in)))
        ]
        for copy in copies:
            copy.start()
        left = lengths[0] - lax.axis_index("seq") * tokens.shape[0]
        for axis, out in ((0, live_out), (1, live_t_out)):
            index = lax.broadcasted_iota(jnp.int32, out.shape, axis)
            out[...] = jnp.where(index < left, 1.0, 0.0)
        stream_out[:, mine] = tokens[...]
        gains_out[:, mine] = gains[...]
        for copy in copies:
            copy.wait()
        stream_out[:, theirs] = arriving[...]
        gains_out[:, theirs] = gains_in[...]
        stream = stream_out[...].astype(jnp.float32)
        scale = lax.rsqrt(jnp.mean(stream * stream, axis=-1, keepdims=True) + EPSILON)
        gain = gains_out[...].astype(jnp.float32)[0:1]
        normed_out[...] = (stream * scale * gain).astype(jnp.bfloat16)
        logit_out[...] = dot_low(normed_out[...], beta_w[...], (1, 1))
        logit_t_out[...] = dot_low(beta_w[...], normed_out[...], (1, 1))

    for part, (weight, out) in enumerate(((q_w, q_out), (k_w, k_out), (v_w, v_out))):

        @pl.when(step // 2 == part)
        def _():
            out[...] = dot_low(normed_out[...], weight[...]).astype(jnp.bfloat16)


def projected(lengths, tokens, first_gain, second_gain, weights, beta_weight, number):
    length, half = tokens.shape
    width, channels = weights[0].shape
    heads = beta_weight.shape[1]
    tile = channels // 2

    def whole(*shape):
        return pl.BlockSpec(shape, lambda s: (0,) * len(shape))

    def tiles(rows, part):
        return pl.BlockSpec((rows, tile), lambda s: (0, jnp.clip(s - 2 * part, 0, 1)))

    return pl.pallas_call(
        project_kernel,
        grid=(6,),
        in_specs=[pl.BlockSpec(memory_space=pltpu.SMEM), whole(length, half)]
        + [whole(half // 128, 128)] * 2
        + [tiles(width, part) for part in range(3)]
        + [whole(heads, width)],
        out_specs=[tiles(length, part) for part in range(3)]
        + [whole(length, heads), whole(heads, length), whole(length, width)]
        + [whole(length, width), whole(16, width), whole(length, 1), whole(1, length)],
        out_shape=[b16(length, channels)] * 3
        + [f32(length, heads), f32(heads, length), b16(length, width)]
        + [b16(length, width), b16(16, width), f32(length, 1), f32(1, length)],
        scratch_shapes=[
            pltpu.VMEM((length, half), jnp.bfloat16),
            pltpu.VMEM((16, half), jnp.bfloat16),
            pltpu.VMEM((16, half), jnp.bfloat16),
            pltpu.SemaphoreType.DMA((2,)),
            pltpu.SemaphoreType.DMA((2,)),
        ],
        compiler_params=pltpu.CompilerParams(
            collective_id=number, has_side_effects=True, vmem_limit_bytes=VMEM
        ),
        cost_estimate=SHORT,
    )(
        lengths, tokens, first_gain.reshape(-1, 128), second_gain.reshape(-1, 128), *weights,
        beta_weight.T,
    )


def units_kernel(
    ways, steps, head_ref, out_w, stream_ref, gains, d_own, d_other, live, gate_w, up_w, down_w,
    plane, turned_out, d_gate_out, d_up_out, hidden_out, stream_out, normed_out, own_out, others,
    plane_out, part_low, arriving, turned_hidden, d_ref, sends, receives, hidden_sends,
    hidden_receives, plane_sems, out_tiles, load_sems,
):
    plane_copy = pltpu.make_async_remote_copy(
        src_ref=plane, dst_ref=plane_out, send_sem=plane_sems.at[0], recv_sem=plane_sems.at[1],
        device_id=place("head", 1 - lax.axis_index("head")), device_id_type=MESH,
    )
    own = lax.axis_index("dp")
    tile = hidden_out.shape[1]
    part_rows = tile // ways

    def hidden_copy(step, by):
        peer = partner(own, by)
        start = pl.multiple_of(step * tile + peer * part_rows, part_rows)
        return pltpu.make_async_remote_copy(
            src_ref=turned_hidden.at[pl.ds(start, part_rows), :],
            dst_ref=others.at[
                by - 1, pl.ds(pl.multiple_of(step * part_rows, part_rows), part_rows), :
            ],
            send_sem=hidden_sends.at[(by - 1) * steps + step],
            recv_sem=hidden_receives.at[(by - 1) * steps + step],
            device_id=place("dp", peer),
            device_id_type=MESH,
        )

    @pl.when(pl.program_id(0) == 0)
    def _():
        other = place("head", 1 - lax.axis_index("head"))
        block = out_tiles.shape[2]
        loads = [
            pltpu.make_async_copy(
                out_w.at[:, index * block : (index + 1) * block],
                out_tiles.at[index],
                load_sems.at[index],
            )
            for index in range(out_tiles.shape[0])
        ]
        for load in loads:
            load.start()
        meet([other] + [place("dp", partner(own, by)) for by in range(1, ways)])
        pieces = part_low.shape[0]
        width = part_low.shape[2]
        copies = []
        for piece in range(pieces):
            loads[piece].wait()
            part_low[piece] = dot_low(head_ref[...], out_tiles[piece]).astype(jnp.bfloat16)
            copy = pltpu.make_async_remote_copy(
                src_ref=part_low.at[piece], dst_ref=arriving.at[piece],
                send_sem=sends.at[piece], recv_sem=receives.at[piece],
                device_id=other, device_id_type=MESH,
            )
            copy.start()
            copies.append(copy)
        core = lax.axis_index("head")
        half = d_own.shape[1]
        plane_copy.start()
        for place_of, part in ((core, d_own), (1 - core, d_other)):
            masked = part[...].astype(jnp.float32) * live[...]
            here = pl.ds(pl.multiple_of(place_of * half, half), half)
            d_ref[:, here] = masked.astype(jnp.bfloat16)
        squares = 0.0
        for piece, copy in enumerate(copies):
            span = slice(piece * width, (piece + 1) * width)
            copy.wait()
            both = part_low[piece].astype(jnp.float32) + arriving[piece].astype(jnp.float32)
            stream = stream_ref[:, span].astype(jnp.float32) + both
            stream_out[:, span] = stream
            squares = squares + jnp.sum(stream * stream, axis=-1, keepdims=True)
        scale = lax.rsqrt(squares / (pieces * width) + EPSILON)
        gain = gains[...].astype(jnp.float32)[1:2]
        normed_out[...] = (stream_out[...] * scale * gain).astype(jnp.bfloat16)

    x = normed_out[...]
    gate = dot_low(x, gate_w[...])
    up = dot_low(x, up_w[...])
    d_hidden = dot_low(d_ref[...], down_w[...], (1, 1))
    sig = jax.nn.sigmoid(gate)
    hidden = (gate * sig * up).astype(jnp.bfloat16)
    d_gate = (d_hidden * up * sig * (1.0 + gate * (1.0 - sig))).astype(jnp.bfloat16)
    d_up = (d_hidden * gate * sig).astype(jnp.bfloat16)
    for index, (part, out) in enumerate(
        ((hidden, hidden_out), (d_gate, d_gate_out), (d_up, d_up_out))
    ):
        out[...] = part
        if index > 0:
            turned_out[index - 1] = part.T
    step = pl.program_id(0)
    live_hidden = (hidden.astype(jnp.float32) * live[...]).astype(jnp.bfloat16)
    turned_hidden[pl.ds(pl.multiple_of(step * tile, tile), tile), :] = live_hidden.T
    for by in range(1, ways):
        hidden_copy(step, by).start()
    own_out[pl.ds(pl.multiple_of(step * part_rows, part_rows), part_rows), :] = turned_hidden[
        pl.ds(pl.multiple_of(step * tile + own * part_rows, part_rows), part_rows), :
    ]

    @pl.when(step == steps - 1)
    def _():
        for index in range(steps):
            for by in range(1, ways):
                hidden_copy(index, by).wait()
        plane_copy.wait()


def hidden_units(
    head_out, out_weight, stream, gains, d_own, d_other, live, gate_weight, up_weight,
    down_weight, plane, number,
):
    ways = lax.axis_size("dp")
    length, width = stream.shape
    channels = head_out.shape[1]
    units = gate_weight.shape[1]
    tile = 256
    whole = pl.BlockSpec((length, width), lambda f: (0, 0))
    column = pl.BlockSpec((width, tile), lambda f: (0, f))
    flat = pl.BlockSpec((length, tile), lambda f: (0, f))
    chunk = units // ways
    return pl.pallas_call(
        functools.partial(units_kernel, ways, units // tile),
        grid=(units // tile,),
        in_specs=[
            pl.BlockSpec((length, channels), lambda f: (0, 0)),
            pl.BlockSpec(memory_space=pl.ANY),
            whole,
            pl.BlockSpec((16, width), lambda f: (0, 0)),
            pl.BlockSpec((length, width // 2), lambda f: (0, 0)),
            pl.BlockSpec((length, width // 2), lambda f: (0, 0)),
            pl.BlockSpec((length, 1), lambda f: (0, 0)),
            column,
            column,
        ]
        + [pl.BlockSpec((tile, width), lambda f: (f, 0)), pl.BlockSpec(memory_space=pl.ANY)],
        out_specs=[pl.BlockSpec((2, tile, length), lambda f: (0, f, 0))]
        + [flat] * 3
        + [whole] * 2
        + [pl.BlockSpec((chunk, length), lambda f: (0, 0))]
        + [pl.BlockSpec(memory_space=pl.ANY)] * 2,
        out_shape=[b16(2, units, length)]
        + [b16(length, units)] * 3
        + [f32(length, width), b16(length, width)]
        + [b16(chunk, length), b16(ways - 1, chunk, length), b16(*plane.shape)],
        scratch_shapes=[pltpu.VMEM((4, length, width // 4), jnp.bfloat16)] * 2
        + [pltpu.VMEM((units, length), jnp.bfloat16), pltpu.VMEM((length, width), jnp.bfloat16)]
        + [pltpu.SemaphoreType.DMA((4,))] * 2
        + [pltpu.SemaphoreType.DMA(((ways - 1) * (units // tile),))] * 2
        + [pltpu.SemaphoreType.DMA((2,))]
        + [pltpu.VMEM((4, channels, width // 4), jnp.bfloat16), pltpu.SemaphoreType.DMA((4,))],
        compiler_params=pltpu.CompilerParams(
            collective_id=number, has_side_effects=True, vmem_limit_bytes=VMEM
        ),
        cost_estimate=SHORT,
    )(
        head_out, out_weight, stream, gains, d_own, d_other, live, gate_weight, up_weight,
        down_weight, plane,
    )


def row_copies(ways, entries, source, out, sends, receives):
    own = lax.axis_index("dp")
    copies = []
    for by in range(1, ways):
        peer = partner(own, by)
        copies.append(
            pltpu.make_async_remote_copy(
                src_ref=source.at[entries[0] : entries[1], peer],
                dst_ref=out.at[by - 1],
                send_sem=sends.at[by - 1],
                recv_sem=receives.at[by - 1],
                device_id=place("dp", peer),
                device_id_type=MESH,
            )
        )
    return copies


def feed_back_kernel(ways, entries, *refs):
    d_gate, d_up, hidden, gate_w, up_w, down_w = refs[:6]
    up_own, up_other, live, gains, source, normed, stream_in, out_w_in = refs[6:14]
    feed_out, d_stream_out, low_out, d_head_out, second_out, others, normed_others = refs[-20:-13]
    d_x, arriving, masked, stream_ref, out_w = refs[-13:-8]
    swap_sems, load_sems = refs[-8:-6]
    sends, receives = refs[-6:-4]
    halves = Halves(ways, normed, normed_others, *refs[-4:])
    copies = row_copies(ways, entries, source, others, sends, receives)
    step = pl.program_id(0)
    tile = feed_out.shape[1]
    width = d_x.shape[1]
    loads = [
        pltpu.make_async_copy(stream_in, stream_ref, load_sems.at[0]),
        pltpu.make_async_copy(out_w_in, out_w, load_sems.at[1]),
    ]

    @pl.when(step == 0)
    def _():
        meet(halves.devices())
        halves.start()
        for copy in copies + loads:
            copy.start()

    d_tile = dot_low(d_gate[...], gate_w[...], (1, 1)) + dot_low(d_up[...], up_w[...], (1, 1))
    d_x[:, pl.ds(pl.multiple_of(step * tile, tile), tile)] = d_tile.astype(jnp.bfloat16)
    feed_out[...] = dot_low(hidden[...], down_w[...]).astype(jnp.bfloat16)

    @pl.when(step == pl.num_programs(0) - 1)
    def _():
        swap = pltpu.make_async_remote_copy(
            src_ref=d_x, dst_ref=arriving, send_sem=swap_sems.at[0], recv_sem=swap_sems.at[1],
            device_id=halves.other, device_id_type=MESH,
        )
        swap.start()
        core = lax.axis_index("head")
        half = up_own.shape[1]
        for place_of, part in ((core, up_own), (1 - core, up_other)):
            here = pl.ds(pl.multiple_of(place_of * half, half), half)
            masked[:, here] = (part[...].astype(jnp.float32) * live[...]).astype(jnp.bfloat16)
        for copy in loads:
            copy.wait()
        swap.wait()
        d_two = d_x[...].astype(jnp.float32) + arriving[...].astype(jnp.float32)
        stream = stream_ref[...]
        scale = lax.rsqrt(jnp.mean(stream * stream, axis=-1, keepdims=True) + EPSILON)
        weighted = gains[...].astype(jnp.float32)[1:2] * d_two
        inner = jnp.sum(weighted * stream, axis=-1, keepdims=True)
        d_stream = (
            masked[...].astype(jnp.float32)
            + scale * weighted
            - stream * (scale * scale * scale * inner / width)
        )
        second_out[...] = jnp.sum(d_two * stream * scale, axis=0, keepdims=True)
        d_stream_out[...] = d_stream
        low_out[...] = d_stream.astype(jnp.bfloat16)
        d_head_out[...] = dot_low(low_out[...], out_w[...], (1, 1))
        halves.hand_on()
        for copy in copies:
            copy.wait()
        halves.finish()


def feed_back(
    d_gate, d_up, hidden, weights, up_own, up_other, live, gains, source, entries, normed, stream,
    out_weight, tokens, number,
):
    ways = lax.axis_size("dp")
    length, units = hidden.shape
    width = normed.shape[1]
    channels = out_weight.shape[0]
    tile = width // 8
    anywhere = pl.BlockSpec(memory_space=pl.ANY)
    row = pl.BlockSpec((tile, units), lambda n: (n, 0))
    out = pl.BlockSpec((length, tile), lambda n: (0, n))

    def whole(*shape):
        return pl.BlockSpec(shape, lambda n: (0,) * len(shape))

    return pl.pallas_call(
        functools.partial(feed_back_kernel, ways, entries),
        grid=(8,),
        in_specs=[whole(length, units)] * 3
        + [row, row, pl.BlockSpec((units, tile), lambda n: (0, n))]
        + [whole(length, width // 2)] * 2
        + [whole(length, 1), whole(16, width)]
        + [anywhere] * (4 + len(tokens)),
        out_specs=[out, whole(length, width), whole(length, width), whole(length, channels)]
        + [whole(1, width), anywhere, anywhere],
        out_shape=[
            b16(length, width), f32(length, width), b16(length, width), f32(length, channels),
            f32(1, width),
            b16(ways - 1, entries[1] - entries[0], *source.shape[2:]),
            b16(ways - 1, length, width),
        ],
        scratch_shapes=[pltpu.VMEM((length, width), jnp.bfloat16)] * 3
        + [pltpu.VMEM((length, width), jnp.float32), pltpu.VMEM(out_weight.shape, jnp.bfloat16)]
        + [pltpu.SemaphoreType.DMA((2,))] * 2
        + [pltpu.SemaphoreType.DMA((ways - 1,))] * 6,
        compiler_params=pltpu.CompilerParams(
            collective_id=number, has_side_effects=True, vmem_limit_bytes=VMEM
        ),
        cost_estimate=SHORT,
    )(
        d_gate, d_up, hidden, *weights, up_own, up_other, live, gains, source, normed, stream,
        out_weight, *tokens,
    )


def pieces_kernel(groups, slots, ways, turned, at, *refs):
    lefts = refs[: groups * slots]
    rights = refs[groups * slots : (groups + ways) * slots]
    out, left_all, right_all = refs[-3:]
    length = rights[0].shape[-2]
    rows = rights[0].shape[-1]
    count = left_all.shape[0] // groups

    @pl.when(pl.program_id(0) == 0)
    def _():
        for group in range(groups):
            for slot in range(slots):
                block = lefts[group * slots + slot][...]
                block = block.reshape(block.shape[-2:])
                left_all[
                    group * count : (group + 1) * count, slot * length : (slot + 1) * length
                ] = block if turned else block.T

    for slot in range(slots):
        for way in range(ways):
            right = rights[slot * ways + way][...]
            right_all[
                slot * length : (slot + 1) * length, way * rows : (way + 1) * rows
            ] = right.reshape(right.shape[-2:])
    out[0] = dot_low(left_all[...], right_all[...]).astype(jnp.bfloat16)


def span_pieces(lefts, count, rights, length, width, spans, turned, tokens=()):
    groups = len(lefts)
    lefts = [left for group in lefts for left in group]
    slots = len(rights)
    ways = lax.axis_size("dp")
    rows = width // (ways * spans)

    def left_block(block, at_place):
        return pl.BlockSpec(block, lambda s, at: at_place(at[0]))

    def right_block(block, at_place, column):
        return pl.BlockSpec(
            block + (rows,), lambda s, at: tuple(at_place(at[0])) + (column(s),)
        )

    rights = [right for slot in rights for right in slot]

    return pl.pallas_call(
        functools.partial(pieces_kernel, groups, slots, ways, turned),
        grid_spec=pltpu.PrefetchScalarGridSpec(
            num_scalar_prefetch=1,
            grid=(spans,),
            in_specs=[left_block(block, where) for _, block, where in lefts]
            + [right_block(block, where, column) for _, block, where, column in rights]
            + [pl.BlockSpec(memory_space=pl.ANY)] * len(tokens),
            out_specs=pl.BlockSpec((1, count, ways * rows), lambda s, at: (s, 0, 0)),
            scratch_shapes=[
                pltpu.VMEM((count, slots * length), jnp.bfloat16),
                pltpu.VMEM((slots * length, ways * rows), jnp.bfloat16),
            ],
        ),
        out_shape=b16(spans, count, ways * rows),
        compiler_params=pltpu.CompilerParams(vmem_limit_bytes=VMEM),
        cost_estimate=SHORT,
    )(
        lax.axis_index("dp")[None],
        *[array for array, _, _ in lefts],
        *[array for array, _, _, _ in rights],
        *tokens,
    )


def widen_kernel(count, turned, starts, share_of, ways, *refs):
    small = refs[count]
    outs = refs[count + 1 :]
    chunk = refs[0].shape[0] // ways
    part = 256 // ways
    for way in range(ways):
        for tile in range(chunk // part):
            start = way * chunk + tile * part
            to = tile * 256 + way * part
            outs[0][to : to + part, :] = refs[0][start : start + part, :].astype(jnp.float32)
    for index in range(1, count):
        whole = refs[index][...].astype(jnp.float32)
        outs[index][...] = whole.T if turned[index] else whole
    gain, first, second, taps, beta = outs[count], *outs[count + 1 : count + 3], outs[count + 3 : -1], outs[-1]
    gain[...] = small[starts[0] : starts[0] + 1, :]
    first[...] = small[starts[1] : starts[1] + first.shape[0], :]
    second[...] = small[starts[2] : starts[2] + second.shape[0], :]
    row = starts[3]
    for out in taps:
        high, wide = out.shape
        for tap in range(high):
            for lane in range(wide // 128):
                out[tap : tap + 1, lane * 128 : (lane + 1) * 128] = small[row : row + 1, :]
                row += 1
    heads = beta.shape[0]
    width = share_of[1] // 128
    share = lax.axis_index("dp") * share_of[0] + lax.axis_index("seq")
    rows = [small[pl.ds(starts[4] + head * width + share, 1), :] for head in range(heads)]
    beta[...] = jnp.concatenate(rows, 0)


def widened(arrays, turned, small, starts, channels, taps, heads, width):
    inside = pl.BlockSpec(memory_space=pltpu.VMEM)
    shapes = [
        f32(*(array.shape[::-1] if turn else array.shape)) for array, turn in zip(arrays, turned)
    ]
    shapes += [f32(1, 128), f32(width // 256, 128), f32(width // 256, 128)]
    shapes += [f32(taps, channels)] * 3 + [f32(heads, 128)]
    return pl.pallas_call(
        functools.partial(
            widen_kernel, len(arrays), turned, starts, (lax.axis_size("seq"), width),
            lax.axis_size("dp"),
        ),
        out_shape=shapes,
        in_specs=[inside] * (len(arrays) + 1),
        out_specs=[inside] * len(shapes),
        compiler_params=pltpu.CompilerParams(vmem_limit_bytes=VMEM),
        cost_estimate=SHORT,
    )(*arrays, small)


def doublings(size):
    return [1 << bit for bit in range(size.bit_length() - 1)]


def finish_kernel(spans, ways, fed, split, *refs):
    out_raw, mix_raw, small = refs[:3]
    pieces, refs = refs[3 : 3 + fed], refs[3 + fed :]
    stages, small_out, refs = refs[: 4 + fed], refs[4 + fed], refs[5 + fed :]
    received, handed, totals, *refs = refs
    sends, receives, owner_sends, owner_receives, own_sems = refs[:5]
    small_in, small_sent, small_sends, small_receives = refs[5:]
    own = lax.axis_index("dp")
    core = lax.axis_index("head")
    position = lax.axis_index("seq")
    last = spans - 1
    rounds = spans - 1
    whole = out_raw.shape[1]
    count = whole // split
    groups = split + mix_raw.shape[1] // count
    rows = stages[0].shape[1]
    peers = [partner(own, by) for by in range(1, ways)]

    def raw_at(group, shard):
        if group < split:
            return out_raw.at[shard, group * count : (group + 1) * count, :]
        return mix_raw.at[shard, (group - split) * count : (group - split + 1) * count, :]

    def line_copy(way, turn, group, src):
        step = 1 if way == 0 else -1
        slot = (way * rounds + turn) * groups + group
        return pltpu.make_async_remote_copy(
            src_ref=src,
            dst_ref=received.at[way, turn, group],
            send_sem=sends.at[slot],
            recv_sem=receives.at[slot],
            device_id=place("seq", position + step),
            device_id_type=MESH,
        )

    def owner_copies(index, source):
        high = source.shape[0]
        turn = core * (ways // 2) if index == 0 else 0

        def block_of(peer):
            start = ((peer + turn) % ways) * rows
            return source.at[:, pl.ds(pl.multiple_of(start, rows), rows)]

        if index < fed:
            stage, start = stages[index], own * high
        else:
            stage = stages[fed + (index - fed) // split]
            start = own * whole + (index - fed) % split * high
        mine = stage.at[pl.ds(pl.multiple_of(start, high), high), :]
        copies = []
        for by, peer in enumerate(peers):
            copies.append(
                pltpu.make_async_remote_copy(
                    src_ref=block_of(peer),
                    dst_ref=mine,
                    send_sem=owner_sends.at[index * (ways - 1) + by],
                    recv_sem=owner_receives.at[index * (ways - 1) + by],
                    device_id=place("dp", peer),
                    device_id_type=MESH,
                )
            )
        here = pltpu.make_async_copy(block_of(own), mine, own_sems.at[index])
        return copies + [here]

    partners = [place("dp", partner(own, by)) for by in doublings(ways)]
    partners += [place("seq", partner(position, by)) for by in doublings(spans)]
    partners += [place("head", 1 - lax.axis_index("head"))]

    def small_copy(turn):
        high = 8 if turn == len(partners) - 1 else small.shape[0]
        return pltpu.make_async_remote_copy(
            src_ref=small_sent.at[turn, :high, :],
            dst_ref=small_in.at[turn, :high, :],
            send_sem=small_sends.at[turn],
            recv_sem=small_receives.at[turn],
            device_id=partners[turn],
            device_id_type=MESH,
        )

    def small_turn(turn):
        if turn == 0:
            small_sent[0] = small[...]
        else:
            small_copy(turn - 1).wait_recv()
            if turn < len(partners):
                small_sent[turn] = small_sent[turn - 1] + small_in[turn - 1]
            else:
                small_out[...] = small_sent[turn - 1]
                small_out[:8, :] = small_sent[turn - 1, :8, :] + small_in[turn - 1, :8, :]
        if turn < len(partners):
            small_copy(turn).start()

    meet(
        [place("seq", (position + last) % spans), place("seq", (position + 1) % spans)]
        + [place("seq", partner(position, by)) for by in doublings(spans)[1:]]
        + [place("dp", peer) for peer in peers]
        + partners[-1:]
    )
    small_turn(0)
    along = (position, last - position)

    ahead = 6

    def source_send(way, index):
        turn, group = index // groups, index % groups
        shard = last - turn if way == 0 else turn
        if index >= ahead:
            before = index - ahead
            line_copy(way, before // groups, before % groups, totals.at[0]).wait_send()
        line_copy(way, turn, group, raw_at(group, shard)).start()

    for way in range(2):

        @pl.when(along[way] == 0)
        def _():
            for index in range(ahead):
                source_send(way, index)

    fed_copies = [owner_copies(index, piece) for index, piece in enumerate(pieces)]
    for copies in fed_copies:
        for copy in copies:
            copy.start()

    for way in range(2):

        @pl.when(along[way] == 0)
        def _():
            for index in range(ahead, groups + ahead):
                source_send(way, index)

    at_end = (position == 0) | (position == last)

    def finish(group):
        for way in range(2):

            @pl.when(along[way] >= 1)
            def _():
                line_copy(way, rounds - 1, group, totals.at[group]).wait_recv()

        total = raw_at(group, position)[...].astype(jnp.float32)
        for way in range(2):
            arrived = received[way, rounds - 1, group].astype(jnp.float32)
            total = total + jnp.where(along[way] >= 1, arrived, 0.0)
        totals[group] = total.astype(jnp.bfloat16)
        for copy in owner_copies(fed + group, totals.at[group]):
            copy.start()

    for turn in range(1, rounds):
        for group in range(groups):
            for way in range(2):
                if turn * groups + group + ahead < rounds * groups:

                    @pl.when(along[way] == 0)
                    def _():
                        source_send(way, turn * groups + group + ahead)

                shard = last - turn + position if way == 0 else turn - along[1]

                @pl.when((along[way] >= 1) & (along[way] <= turn))
                def _():
                    line_copy(way, turn - 1, group, handed.at[way, turn - 1, group]).wait_recv()
                    term = raw_at(group, shard)[...].astype(jnp.float32)
                    term = term + received[way, turn - 1, group].astype(jnp.float32)
                    handed[way, turn - 1, group] = term.astype(jnp.bfloat16)
                    line_copy(way, turn, group, handed.at[way, turn - 1, group]).start()

            if turn == rounds - 1:

                @pl.when(at_end)
                def _():
                    finish(group)

        small_turn(turn)

    later = list(range(rounds, len(partners) + 1))

    @pl.when(at_end)
    def _():
        for turn in later:
            small_turn(turn)

    @pl.when(jnp.logical_not(at_end))
    def _():
        done = 0
        for group in range(groups):
            finish(group)
            while done < len(later) and (group + 1) * len(later) >= (done + 1) * groups:
                small_turn(later[done])
                done += 1

    sources = list(pieces) + [totals.at[group] for group in range(groups)]
    for index, source in enumerate(sources):
        for copy in owner_copies(index, source):
            copy.wait()

    for turn in range(rounds):
        for way in range(2):

            @pl.when((along[way] >= 1) & (along[way] <= turn))
            def _():
                for group in range(groups):
                    line_copy(way, turn, group, totals.at[group]).wait_send()

    for way in range(2):

        @pl.when(along[way] == 0)
        def _():
            for group in range(groups - ahead, groups):
                line_copy(way, rounds - 1, group, totals.at[group]).wait_send()

    for turn in range(len(partners)):
        small_copy(turn).wait_send()


def finished_gradients(out_raw, mix_raw, pieces, small, number):
    spans, ways = lax.axis_size("seq"), lax.axis_size("dp")
    split = 2
    _, whole, wide = out_raw.shape
    count = whole // split
    grads = 1 + mix_raw.shape[1] // whole
    groups = grads * split
    rows = wide // ways
    fed = len(pieces)
    highs = [ways * piece.shape[0] for piece in pieces] + [ways * whole] * grads
    inside = pl.BlockSpec(memory_space=pltpu.VMEM)
    shapes = [b16(high, rows) for high in highs]
    lines = (2, spans - 1, groups, count, wide)
    turns = len(doublings(ways)) + len(doublings(spans)) + 1
    return pl.pallas_call(
        functools.partial(finish_kernel, spans, ways, fed, split),
        out_shape=shapes + [f32(*small.shape)],
        in_specs=[inside] * 3 + [pl.BlockSpec(memory_space=pl.ANY)] * fed,
        out_specs=[inside] * (len(shapes) + 1),
        scratch_shapes=[
            pltpu.VMEM(lines, jnp.bfloat16),
            pltpu.VMEM((2, spans - 2, groups, count, wide), jnp.bfloat16),
            pltpu.VMEM((groups, count, wide), jnp.bfloat16),
        ]
        + [pltpu.SemaphoreType.DMA((2 * (spans - 1) * groups,))] * 2
        + [pltpu.SemaphoreType.DMA(((fed + groups) * (ways - 1),))] * 2
        + [pltpu.SemaphoreType.DMA((fed + groups,))]
        + [pltpu.VMEM((turns,) + small.shape, jnp.float32)] * 2
        + [pltpu.SemaphoreType.DMA((turns,))] * 2,
        compiler_params=pltpu.CompilerParams(
            collective_id=number, has_side_effects=True, vmem_limit_bytes=VMEM
        ),
        cost_estimate=SHORT,
    )(out_raw, mix_raw, small, *pieces)


def shards(
    tokens_in,
    lengths,
    first_gain,
    query_weight,
    key_weight,
    value_weight,
    beta_weight,
    query_conv,
    key_conv,
    value_conv,
    mixer_gain,
    output_weight,
    second_gain,
    gate_weight,
    up_weight,
    down_weight,
    upstream,
):
    num_rows, local_len, local_width = tokens_in.shape
    full_width = query_weight.shape[0]
    channels = query_weight.shape[1]
    local_heads = beta_weight.shape[1]
    groups = lax.axis_size("head")
    ways = lax.axis_size("dp")
    spans = lax.axis_size("seq")
    positions = lax.axis_index("seq") * local_len + jnp.arange(local_len, dtype=jnp.int32)
    live_mask = (positions[None, :] < lengths[:, None]).astype(jnp.float32)
    live_low = live_mask[..., None].astype(jnp.bfloat16)
    fused = groups == 2
    weights = [query_weight, key_weight, value_weight]
    if fused:
        (
            *pres, beta_logit, logit_turned, gathered, normed_one, gains, live_col, live_row,
        ) = projected(
            lengths, tokens_in[0], first_gain, second_gain, weights, beta_weight, 7
        )
        upstream_other = swapped(upstream[0])
        upstream_other, beta_logit = lax.optimization_barrier((upstream_other, beta_logit))
        first = lax.axis_index("head") == 0
        upstream_full = live_low * jnp.concatenate(
            [
                jnp.where(first, upstream, upstream_other[None]),
                jnp.where(first, upstream_other[None], upstream),
            ],
            2,
        )
        half_up = lax.all_gather(upstream[0], "dp", axis=0, tiled=True)
    else:
        gains = jnp.stack([first_gain, second_gain] + [first_gain] * 14)
        masked_up = upstream[0] * live_low[0]
        everything = gather_head(jnp.concatenate([tokens_in[0], masked_up, gains], 0), 1)
        gathered = everything[:local_len]
        upstream_full = everything[None, local_len : 2 * local_len]
        gains = everything[2 * local_len :]
        scale_one = inverse_rms(gathered.astype(jnp.float32))
        normed_one = (
            gathered.astype(jnp.float32) * scale_one * gains[0].astype(jnp.float32)
        ).astype(jnp.bfloat16)
        pres = [
            jnp.dot(normed_one, weight, preferred_element_type=jnp.float32).astype(jnp.bfloat16)
            for weight in weights
        ]
        beta_logit = jnp.dot(normed_one, beta_weight, preferred_element_type=jnp.float32)
        tokens_up = jnp.stack(spread(upstream_full[0], "dp")[1:])

    def scattered(pieces):
        return lax.psum_scatter(pieces, "seq", scatter_dimension=0, tiled=False)

    def to_owner(piece):
        c = piece.shape[0]
        blocks = piece.reshape(c, ways, -1).transpose(1, 0, 2)
        return jnp.stack(in_order(exchanged(blocks, "dp"), "dp"), 0)

    per_step = 2 if local_heads % 2 == 0 else 1
    gain_one, gain_two = gains[0].astype(jnp.float32), gains[1].astype(jnp.float32)
    stream_full = gathered[None].astype(jnp.float32)
    scale_one = inverse_rms(stream_full)
    normed_one = normed_one[None]
    convs = [query_conv, key_conv, value_conv]
    if not fused:
        live_col = live_mask[0][:, None]
    head_gain = mixer_gain[None, :] if fused else mixer_gain.astype(jnp.float32)[None, :]
    if fused:
        (
            query, key, value, wy, inverse, ends, mixed, head_out, entering, rims, one_near,
        ) = mixer_forward(
            pres, convs, beta_logit, logit_turned, live_col, live_row, head_gain, normed_one[0],
            per_step, spans, ways, 1,
        )
    else:
        rims = passed_along(jnp.stack([pre[local_len - RIM :, :] for pre in pres]), "seq", 1)
        rims = [rims[0], rims[1], rims[2]]
        query, key, value, wy, inverse, mix, ends = mixer_local(
            pres, rims, convs, beta_logit, live_col, per_step
        )
        entering = chain_state(ends[:, :, :HEAD_DIM], ends[:, :, HEAD_DIM:], False)
        mixed, head_out = mixer_finish(mix, entering, head_gain, per_step)
    head_out = head_out[None]
    if fused:
        (
            turned, d_gate, d_up, hidden, stream_mid, normed_two, own_hidden, hidden_others,
            other_up,
        ) = hidden_units(
            head_out[0], output_weight, gathered, gains, upstream[0], upstream_other, live_col,
            gate_weight, up_weight, down_weight, half_up, 8,
        )
        stream_mid, normed_two = stream_mid[None], normed_two[None]
    else:
        mixer_part = jnp.dot(head_out, output_weight, preferred_element_type=jnp.float32)
        stream_mid = stream_full + sum_head(mixer_part)
        normed_two = (stream_mid * inverse_rms(stream_mid) * gain_two).astype(jnp.bfloat16)
        feed_part, d_two_part, turned = feed_forward(
            normed_two[0], upstream_full[0], gate_weight, up_weight, down_weight, normed_two
        )
    scale_two = inverse_rms(stream_mid)
    units = turned.shape[1] // ways
    turned = turned.reshape(-1, ways, units, local_len)

    def raw_piece(lefts, count, rights, is_turned, tokens=()):
        return span_pieces(
            lefts, count, rights, local_len, full_width, spans, is_turned, tokens
        )

    def slots_of(own, others):
        slots = [(own, (local_len,), lambda at: (0,))] + [
            (others, (1, local_len), lambda at, by=by: (by, 0)) for by in range(ways - 1)
        ]
        return [
            [slot + ((lambda s, way=way: way * spans + s),) for way in range(ways)]
            for slot in slots
        ]

    def halves_of(same, other):
        half = ways // 2
        return [
            [
                (
                    same if way < half else other,
                    (local_len,),
                    lambda at, by=by: (at ^ by,),
                    lambda s, way=way: (way % half) * spans + s,
                )
                for way in range(ways)
            ]
            for by in range(ways)
        ]

    def feed_slots(which, others, index):
        own = [(turned, (1, 1, units, local_len), lambda at: (which, at, 0, 0))]
        return own + [
            (others, (1, 1, units, local_len), lambda at, by=by: (by, index, 0, 0))
            for by in range(ways - 1)
        ]

    normed_full = normed_two[0]
    if fused:
        hidden_slots = [(own_hidden, (units, local_len), lambda at: (0, 0))] + [
            (hidden_others, (1, units, local_len), lambda at, by=by: (by, 0, 0))
            for by in range(ways - 1)
        ]
        down_raw = raw_piece(
            [hidden_slots], units, halves_of(half_up, other_up), True
        )
        feed_part, d_stream, residual, d_head_out, second_row, d_others, two_others = feed_back(
            d_gate, d_up, hidden, [gate_weight, up_weight, down_weight], upstream[0],
            upstream_other, live_col, gains, turned, (0, 1), normed_full, stream_mid[0],
            output_weight, [down_raw], 3,
        )
        d_stream, residual_full, d_head_out = d_stream[None], residual[None], d_head_out[None]
        grad_second = own_half(second_row[0], local_width)
        two_slots = slots_of(normed_full, two_others)
    else:
        hidden_others = jnp.stack(exchanged(turned[:1].transpose(1, 0, 2, 3), "dp")[1:])
        down_raw = raw_piece(
            [feed_slots(0, hidden_others, 0)], units, slots_of(upstream_full[0], tokens_up), True
        )
        d_others = jnp.stack(exchanged(turned[1:].transpose(1, 0, 2, 3), "dp")[1:])
        two_slots = slots_of(normed_full, jnp.stack(spread(normed_full, "dp")[1:]))
    down_piece = scattered(down_raw)
    first = turned.shape[0] - 2
    gate_raw = raw_piece([feed_slots(first, d_others, 0)], units, two_slots, True)
    gate_piece = scattered(gate_raw)
    layer_out = own_half(stream_mid + sum_head(feed_part[None]), local_width).astype(jnp.bfloat16)
    if not fused:
        d_two = sum_head(d_two_part[None])
        d_stream = (
            upstream_full.astype(jnp.float32)
            + scale_two * gain_two * d_two
            - stream_mid
            * scale_two
            * scale_two
            * scale_two
            * (jnp.sum(d_two * gain_two * stream_mid, axis=-1, keepdims=True) / full_width)
        )
        grad_second = own_half(jnp.sum(d_two * stream_mid * scale_two, axis=(0, 1)), local_width)
        residual_full = d_stream.astype(jnp.bfloat16)
        d_head_out = jnp.einsum(
            "rsd,cd->rsc", residual_full, output_weight, preferred_element_type=jnp.float32
        )
    if fused:
        (
            *mix_sources, grad_kernels, d_beta_logit, grad_gain_part, out_others, res_others,
            up_others,
        ) = mixer_backward(
            d_head_out[0], mixed, head_gain, pres, rims, convs, beta_logit, live_col,
            query, key, value, wy, inverse, entering, ends, [gate_raw, down_piece],
            head_out[0], residual_full[0], turned, per_step, spans, ways, 4,
        )
    else:
        d_mixed, d_fresh, d_ends, grad_gain_part = mixer_back_local(
            d_head_out[0], mixed, head_gain, query, key, wy, per_step
        )
        leaving = chain_state(jnp.swapaxes(ends[:, :, :HEAD_DIM], 1, 2), d_ends, True)
        *d_pres, tails, d_rims, grad_kernels, d_beta_logit = mixer_back(
            pres, rims, convs, beta_logit, live_col, query, key, value, wy, inverse,
            entering, d_mixed, d_fresh, leaving, per_step,
        )
        tails = (tails + passed_along(d_rims, "seq", -1)).astype(jnp.bfloat16)
        mix_sources = [
            jnp.concatenate([part[: local_len - 8], tail], 0) for part, tail in zip(d_pres, tails)
        ]
    grad_gain_part = grad_gain_part[0]
    if fused:
        up_raw = raw_piece([feed_slots(1, up_others, 0)], units, two_slots, True)
    else:
        up_raw = raw_piece([feed_slots(2, d_others, 1)], units, two_slots, True)
    up_piece = scattered(up_raw)
    share_width = channels // ways
    residual = residual_full[0]
    if fused:
        d_one_part, *mix_others, one_far = back_projection(
            mix_sources, d_beta_logit, weights, beta_weight, normed_one[0], ways, [up_raw], 5,
        )
    else:
        *mix_others, out_others = [
            jnp.stack(exchanged(part.reshape(local_len, ways, -1).transpose(1, 0, 2), "dp")[1:])
            for part in mix_sources + [head_out[0]]
        ]
        res_others = jnp.stack(spread(residual, "dp")[1:])

    def column_slots(own, others):
        if fused:
            first = [(own, (local_len, share_width), lambda at: (0, at))]
        else:
            mine = lax.dynamic_slice_in_dim(
                own, lax.axis_index("dp") * share_width, share_width, 1
            )
            first = [(mine, (local_len, share_width), lambda at: (0, 0))]
        return first + [
            (others, (1, local_len, share_width), lambda at, by=by: (by, 0, 0))
            for by in range(ways - 1)
        ]

    if fused:
        one_slots = slots_of(normed_one[0], one_near)[: ways - 1]
        one_slots += slots_of(normed_one[0], one_far)[1:2]
    else:
        one_slots = slots_of(normed_one[0], jnp.stack(spread(normed_one[0], "dp")[1:]))
    out_raw = raw_piece(
        [column_slots(head_out[0], out_others)], share_width, slots_of(residual, res_others), False,
        [gate_piece],
    )
    mix_raw = raw_piece(
        [column_slots(own, others) for own, others in zip(mix_sources, mix_others)],
        3 * share_width, one_slots, False, [out_raw],
    )
    d_logit_low = d_beta_logit.astype(jnp.bfloat16)
    if not fused:
        d_one_part = jnp.dot(d_logit_low, beta_weight.T, preferred_element_type=jnp.float32)
        for part, weight in zip(mix_sources, (query_weight, key_weight, value_weight)):
            d_one_part = d_one_part + jnp.dot(
                part, weight.T, preferred_element_type=jnp.float32
            )
    grad_beta_part = lax.dot_general(
        d_logit_low, normed_one[0], (((0,), (0,)), ((), ())), preferred_element_type=jnp.float32
    )
    d_one = sum_head(d_one_part[None])
    grad_tokens = own_half(
        d_stream
        + scale_one * gain_one * d_one
        - stream_full
        * scale_one
        * scale_one
        * scale_one
        * (jnp.sum(d_one * gain_one * stream_full, axis=-1, keepdims=True) / full_width),
        local_width,
    )
    grad_first = own_half(jnp.sum(d_one * stream_full * scale_one, axis=(0, 1)), local_width)
    lane = 128
    sizes = [HEAD_DIM, local_width, local_width, grad_kernels.size, grad_beta_part.size]
    parts = [grad_gain_part, grad_first, grad_second, grad_kernels, grad_beta_part]
    shares = [
        jnp.pad(part.reshape(-1, lane), ((0, -(size // lane) % 8), (0, 0)))
        for part, size in zip(parts, sizes)
    ]
    small = jnp.concatenate(shares, 0)
    starts = [0]
    for part in shares:
        starts.append(starts[-1] + part.shape[0])
    share = lax.axis_index("dp") * spans + lax.axis_index("seq")
    rows = full_width // (ways * spans)
    if fused:
        *finished, small = finished_gradients(
            out_raw, mix_raw, [down_piece, gate_piece, up_piece], small, 6
        )
        results = widened(
            finished, [False, True, True, False, True, True, True],
            small, starts, channels, query_conv.shape[0], local_heads, full_width,
        )
        down, gate, up, out, *mix = results[:7]
        gain_total, grad_first, grad_second = [part.reshape(-1) for part in results[7:10]]
        kernel_sum, grad_beta = results[10:13], results[13].T
    else:
        small = sum_doubling(small, ("dp", "seq"))
        gain_total = sum_doubling(small[0], ("head",))
        totals = [
            small[start : start + size // lane].reshape(part.shape)
            for start, size, part in zip(starts, sizes, parts)
        ]
        grad_first, grad_second, kernel_sum, beta_sum = totals[1:]
        grad_beta = lax.dynamic_slice_in_dim(beta_sum, share * rows, rows, 1).T
        feed = to_owner(jnp.concatenate([down_piece, gate_piece, up_piece], 0))
        down, gate, up = [
            feed[:, place * units : (place + 1) * units].reshape(-1, rows).astype(jnp.float32)
            for place in range(3)
        ]
        gate, up = gate.T, up.T
        out = to_owner(scattered(out_raw)).reshape(-1, rows).astype(jnp.float32)
        mix = to_owner(scattered(mix_raw)).astype(jnp.float32)
        third = mix.shape[1] // 3
        mix = [mix[:, i * third : (i + 1) * third].reshape(-1, rows).T for i in range(3)]
    return (
        layer_out,
        grad_tokens,
        grad_first,
        mix[0],
        mix[1],
        mix[2],
        grad_beta,
        kernel_sum[0],
        kernel_sum[1],
        kernel_sum[2],
        gain_total,
        out,
        grad_second,
        gate,
        up,
        down,
    )


def solution(mesh):
    placed = (
        P("dp", "seq", "head"),
        P("dp"),
        P("head"),
        P(None, "head"),
        P(None, "head"),
        P(None, "head"),
        P(None, "head"),
        P(None, "head"),
        P(None, "head"),
        P(None, "head"),
        P(),
        P("head", None),
        P("head"),
        P(None, "head"),
        P(None, "head"),
        P("head", None),
        P("dp", "seq", "head"),
    )
    return jax.shard_map(
        shards,
        mesh=mesh,
        in_specs=placed,
        out_specs=(
            P("dp", "seq", "head"),
            P("dp", "seq", "head"),
            P("head"),
            P(("dp", "seq"), "head"),
            P(("dp", "seq"), "head"),
            P(("dp", "seq"), "head"),
            P(("dp", "seq"), "head"),
            P(None, "head"),
            P(None, "head"),
            P(None, "head"),
            P(),
            P("head", ("dp", "seq")),
            P("head"),
            P(("dp", "seq"), "head"),
            P(("dp", "seq"), "head"),
            P("head", ("dp", "seq")),
        ),
        check_vma=False,
    )
```
